32 devices in a mesh: dp: 8 (over z, y), shard: 4 (over x, core).
Axes of the slice: x: 2, y: 2, z: 4, core: 2. Of those that a mesh axis runs over, the one named last changes fastest.
Arguments:
- images: bfloat16 [2, 160, 12, 12, 256], P(None, ('dp', 'shard')), may hold values from -6 to 6
- bucket: int32 [8], P('dp'), may hold values from 0 to 2
- counts: int32 [2, 32], P(None, ('dp', 'shard')), may hold values from 2 to 5, as said below
- balance: int32 [2, 160], P(None, ('dp', 'shard')), may hold values from 1 to 4
- labels: int32 [2, 160], P(None, ('dp', 'shard')), may hold values from 0 to 999
- step: int32 [1], replicated, may hold values from 2 to 20
- expand_w: float32 [2, 256, 3072], P(None, 'shard'), may hold values from -0.375 to 0.375
- expand_m: float32 [2, 256, 3072], P(None, 'shard'), may hold values from -6.1035156e-05 to 6.1035156e-05
- expand_v: float32 [2, 256, 3072], P(None, 'shard'), may hold values from 3.4375e-11 to 5.625e-10
- expand_e: float32 [2, 256, 3072], P(None, 'shard'), may hold values from -0.375 to 0.375
- chan_w: float32 [2, 137, 1536], P(None, None, 'shard'), may hold values from -0.75 to 0.75
- chan_m: float32 [2, 137, 1536], P(None, None, 'shard'), may hold values from -6.1035156e-05 to 6.1035156e-05
- chan_v: float32 [2, 137, 1536], P(None, None, 'shard'), may hold values from 3.4375e-11 to 5.625e-10
- chan_e: float32 [2, 137, 1536], P(None, None, 'shard'), may hold values from -0.75 to 0.75
- head_w: float32 [256, 1280], P(None, 'shard'), may hold values from -0.375 to 0.375
- head_m: float32 [256, 1280], P(None, 'shard'), may hold values from -6.1035156e-05 to 6.1035156e-05
- head_v: float32 [256, 1280], P(None, 'shard'), may hold values from 5e-11 to 8.125e-10
- head_e: float32 [256, 1280], P(None, 'shard'), may hold values from -0.375 to 0.375
- class_w: float32 [1280, 1000], P('shard'), may hold values from -0.3125 to 0.3125
- class_m: float32 [1280, 1000], P('shard'), may hold values from -0.0007324219 to 0.0007324219
- class_v: float32 [1280, 1000], P('shard'), may hold values from 6.25e-09 to 1e-07
- class_e: float32 [1280, 1000], P('shard'), may hold values from -0.3125 to 0.3125
- gain_w: float32 [4, 5018], P('shard'), may hold values from 0.25 to 1.75
- gain_m: float32 [4, 5018], P('shard'), may hold values from -0.00010681152 to 0.00010681152
- gain_v: float32 [4, 5018], P('shard'), may hold values from 1.40625e-10 to 2.25e-09
- gain_e: float32 [4, 5018], P('shard'), may hold values from 0.25 to 1.75
Outputs:
- loss: float32 [], replicated
- expand_new: float32 [2, 256, 3072], P(None, 'shard')
- expand_first: float32 [2, 256, 3072], P(None, 'shard')
- expand_second: float32 [2, 256, 3072], P(None, 'shard')
- expand_avg: float32 [2, 256, 3072], P(None, 'shard')
- chan_new: float32 [2, 137, 1536], P(None, None, 'shard')
- chan_first: float32 [2, 137, 1536], P(None, None, 'shard')
- chan_second: float32 [2, 137, 1536], P(None, None, 'shard')
- chan_avg: float32 [2, 137, 1536], P(None, None, 'shard')
- head_new: float32 [256, 1280], P(None, 'shard')
- head_first: float32 [256, 1280], P(None, 'shard')
- head_second: float32 [256, 1280], P(None, 'shard')
- head_avg: float32 [256, 1280], P(None, 'shard')
- class_new: float32 [1280, 1000], P('shard')
- class_first: float32 [1280, 1000], P('shard')
- class_second: float32 [1280, 1000], P('shard')
- class_avg: float32 [1280, 1000], P('shard')
- gain_new: float32 [4, 5018], P('shard')
- gain_first: float32 [4, 5018], P('shard')
- gain_second: float32 [4, 5018], P('shard')
- gain_avg: float32 [4, 5018], P('shard')
- norms: float32 [2, 12], replicated
The draws below stay inside these ranges and needn't reach their ends.
Inputs may be any that keep to these rules, and one draw needn't show every extreme that they name: `bucket`: 0, 1, 2 stand for images of 7 x 7, 10 x 10 and 12 x 12 pixels at the upper left of each slot. A device's valid images are its first counts slots; in every micro-batch some device holds 5 images.
All inputs are finite; a program needn't handle non-finite values.
Results may differ from the reference program's by a relative error of at most 0.01065.
The reference program's roundings to bfloat16 on the way (of `low` and `scaled`) count: a program that leaves them out, or rounds other values in their place, can miss the bound.
Values may be sent and summed in bfloat16 or wider, within the bound.
A program may use at most 448 MiB of HBM per device.

```python
import math
import jax
import jax.numpy as jnp
from jax import lax

C = 256
E = 1536
SE = 64
HEAD = 1280
CLASSES = 1000
L = 2
MB = 2
S = 12
IMG = 5
R = 137
RANKS = 32
GROUPS = 8
IMGS = 160
G = 20072
N_SHARD = 4


def draw_counts(key, part):
    lowest = max(1, IMG // 2)
    base = jax.random.randint(jax.random.fold_in(key, 11), (MB, RANKS), lowest, IMG + 1)
    chosen = jax.random.randint(jax.random.fold_in(key, 12), (MB,), 0, RANKS)
    return jnp.where(jnp.arange(RANKS)[None, :] == chosen[:, None], IMG, base).astype(jnp.int32)


def draw_images(key, part):
    key = jax.random.fold_in(key, 21)
    shape = (MB, IMGS, S, S, C)
    base = jax.random.normal(jax.random.fold_in(key, 1), shape, jnp.float32)
    factor = jnp.exp(jax.random.uniform(jax.random.fold_in(key, 2), (MB, 1, 1, 1, C), jnp.float32, -0.5, 0.4))
    offset = jax.random.uniform(jax.random.fold_in(key, 3), (MB, 1, 1, 1, C), jnp.float32, -0.5, 0.5)
    return jnp.clip(base * factor + offset, -6.0, 6.0).astype(jnp.bfloat16)


def set_ends(values, own_key, smallest, top_value):
    longest = values.shape.index(max(values.shape))
    spots = []
    for shift in (0, 1):
        where = [jax.random.randint(jax.random.fold_in(own_key, axis), (), 0, length) for axis, length in enumerate(values.shape)]
        where[longest] = (where[longest] + shift) % values.shape[longest]
        spots.append(tuple(where))
    return values.at[spots[0]].set(smallest).at[spots[1]].set(top_value)


def levels(rng, extent, cuts, smallest, largest):
    def one(position, shards_of):
        draws = jax.random.uniform(jax.random.fold_in(jax.random.fold_in(rng, 6), position), (shards_of,), jnp.float32, smallest / len(cuts), largest / len(cuts))
        return jnp.repeat(jnp.exp(draws), extent[position] // shards_of).reshape((-1,) + (1,) * (len(extent) - position - 1))

    level = one(*cuts[0])
    for cut in cuts[1:]:
        level = level * one(*cut)
    return level


def noise(key, extent, scale, bound, pieces=(), held_as=jnp.bfloat16):
    values = scale * jax.random.normal(key, extent, jnp.float32)
    if pieces:
        values = values * levels(key, extent, pieces, -0.22, 0.18)
    return jnp.clip(values, -bound, bound).astype(held_as)


def setup_inputs(seed: int = 0) -> dict:
    streams_of = jax.random.split(jax.random.key(seed), 27)
    images = draw_images(jax.random.fold_in(streams_of[26], 71), 0)
    bucket = set_ends(jax.random.randint(streams_of[1], (GROUPS,), 0, 3), jax.random.fold_in(streams_of[1], 1), 0, 2).astype(jnp.int32)
    counts = draw_counts(jax.random.fold_in(streams_of[26], 71), 0)
    balance = set_ends(jax.random.randint(streams_of[3], (MB, IMGS), 1, 5), jax.random.fold_in(streams_of[3], 1), 1, 4).astype(jnp.int32)
    labels = set_ends(jax.random.randint(streams_of[4], (MB, IMGS), 0, CLASSES), jax.random.fold_in(streams_of[4], 1), 0, CLASSES - 1).astype(jnp.int32)
    step = jax.random.randint(streams_of[5], (1,), 2, 21).astype(jnp.int32)
    expand_w = noise(streams_of[6], (L, C, 2 * E), C ** -0.5, 0.375, ((1, 4),), jnp.float32)
    expand_m = noise(streams_of[7], (L, C, 2 * E), (0.00017 * (RANKS * MB * IMG) ** -0.5), 6.103515625e-05, ((1, 4),), jnp.float32)
    expand_v = jnp.clip(jnp.exp(math.log(5.624999910303075e-10) - 2.7950616 * jax.random.uniform(streams_of[8], (L, C, 2 * E), jnp.float32) ** levels(streams_of[8], (L, C, 2 * E), ((1, 4),), -0.2, 0.2)), 3.43749993747533e-11, 5.624999910303075e-10)
    expand_e = noise(streams_of[9], (L, C, 2 * E), C ** -0.5, 0.375, ((1, 4),), jnp.float32)
    chan_w = noise(streams_of[10], (L, R, E), SE ** -0.5, 0.75, ((2, 4),), jnp.float32)
    chan_m = noise(streams_of[11], (L, R, E), (0.00017 * (RANKS * MB * IMG) ** -0.5), 6.103515625e-05, ((2, 4),), jnp.float32)
    chan_v = jnp.clip(jnp.exp(math.log(5.624999910303075e-10) - 2.7950616 * jax.random.uniform(streams_of[12], (L, R, E), jnp.float32) ** levels(streams_of[12], (L, R, E), ((2, 4),), -0.2, 0.2)), 3.43749993747533e-11, 5.624999910303075e-10)
    chan_e = noise(streams_of[13], (L, R, E), SE ** -0.5, 0.75, ((2, 4),), jnp.float32)
    head_w = noise(streams_of[14], (C, HEAD), C ** -0.5, 0.375, ((1, 4),), jnp.float32)
    head_m = noise(streams_of[15], (C, HEAD), (0.0002 * (RANKS * MB * IMG) ** -0.5), 6.103515625e-05, ((1, 4),), jnp.float32)
    head_v = jnp.clip(jnp.exp(math.log(8.125000117154002e-10) - 2.7880929 * jax.random.uniform(streams_of[16], (C, HEAD), jnp.float32) ** levels(streams_of[16], (C, HEAD), ((1, 4),), -0.2, 0.2)), 5.00000006675716e-11, 8.125000117154002e-10)
    head_e = noise(streams_of[17], (C, HEAD), C ** -0.5, 0.375, ((1, 4),), jnp.float32)
    class_w = noise(streams_of[18], (HEAD, CLASSES), (HEAD // 4) ** -0.5, 0.3125, ((0, 4),), jnp.float32)
    class_m = noise(streams_of[19], (HEAD, CLASSES), (0.0022 * (RANKS * MB * IMG) ** -0.5), 0.0007324219, ((0, 4),), jnp.float32)
    class_v = jnp.clip(jnp.exp(math.log(1.0000000116860974e-07) - 2.7725887 * jax.random.uniform(streams_of[20], (HEAD, CLASSES), jnp.float32) ** levels(streams_of[20], (HEAD, CLASSES), ((0, 4),), -0.2, 0.2)), 6.250000073038109e-09, 1.0000000116860974e-07)
    class_e = noise(streams_of[21], (HEAD, CLASSES), (HEAD // 4) ** -0.5, 0.3125, ((0, 4),), jnp.float32)
    gain_w = jnp.clip(1.0 + 0.15 * jax.random.normal(streams_of[22], (N_SHARD, G // N_SHARD), jnp.float32), 0.25, 1.75)
    gain_m = noise(streams_of[23], (N_SHARD, G // N_SHARD), (0.00033 * (RANKS * MB * IMG) ** -0.5), 0.00010681152, ((0, 4),), jnp.float32)
    gain_v = jnp.clip(jnp.exp(math.log(2.24999996412123e-09) - 2.7725887 * jax.random.uniform(streams_of[24], (N_SHARD, G // N_SHARD), jnp.float32) ** levels(streams_of[24], (N_SHARD, G // N_SHARD), ((0, 4),), -0.2, 0.2)), 1.4062499775757686e-10, 2.24999996412123e-09)
    gain_e = jnp.clip(1.0 + 0.15 * jax.random.normal(streams_of[25], (N_SHARD, G // N_SHARD), jnp.float32), 0.25, 1.75)
    return {"images": images, "bucket": bucket, "counts": counts, "balance": balance, "labels": labels, "step": step, "expand_w": expand_w, "expand_m": expand_m, "expand_v": expand_v, "expand_e": expand_e, "chan_w": chan_w, "chan_m": chan_m, "chan_v": chan_v, "chan_e": chan_e, "head_w": head_w, "head_m": head_m, "head_v": head_v, "head_e": head_e, "class_w": class_w, "class_m": class_m, "class_v": class_v, "class_e": class_e, "gain_w": gain_w, "gain_m": gain_m, "gain_v": gain_v, "gain_e": gain_e}


EPS_NORM = 1e-05
BETA_ONE = 0.9
BETA_TWO = 0.99
EPS_ADAM = 1e-08
DECAY = 0.01
RATE = 0.3
KEEP = 0.9

@jax.custom_vjp
def low(v):
    return lax.optimization_barrier(v.astype(jnp.bfloat16)).astype(jnp.float32)

@jax.custom_vjp
def low_back(v):
    return v

def low_keep(v):
    return (low(v), None)

def low_pass(kept, grad):
    return (grad,)

def back_keep(v):
    return (v, None)

def back_low(kept, grad):
    return (low(grad),)
low.defvjp(low_keep, low_pass)
low_back.defvjp(back_keep, back_low)

def matmul(left, right):
    return jnp.dot(left, right, precision=lax.Precision.HIGHEST, preferred_element_type=jnp.float32)

def matmul_bt(left, right):
    return lax.dot_general(left, right, (((1,), (1,)), ((), ())), precision=lax.Precision.HIGHEST, preferred_element_type=jnp.float32)

def batch_norm(value, mask, gain, shift, count):
    mean = lax.optimization_barrier(jnp.sum(mask * value, 0)) / count
    var = lax.optimization_barrier(jnp.sum(mask * value * value, 0)) / count - mean * mean
    return mask * (gain * ((value - mean) * lax.rsqrt(var + EPS_NORM)) + shift)

def spread(first, taps):
    image = jax.nn.silu(first).reshape(-1, S, S, first.shape[-1])
    padded = jnp.pad(image, ((0, 0), (1, 1), (1, 1), (0, 0)))
    total = jnp.zeros_like(image)
    for offset in range(9):
        total = total + padded[:, offset // 3:offset // 3 + S, offset % 3:offset % 3 + S, :] * taps[offset]
    return total.reshape(first.shape)

def pool(value, area):
    return lax.optimization_barrier(jnp.sum(value.reshape(area.shape[0], S * S, value.shape[-1]), 1)) / area[:, None]

def excite(second, se_part, excite_bias, squeeze_bias, area):
    active = jax.nn.silu(second)
    pooled = pool(active, area)
    squeezed = jax.nn.silu(matmul_bt(pooled, se_part[:SE]) + squeeze_bias)
    gate = jax.nn.sigmoid(matmul(squeezed, se_part[SE:]) + excite_bias)
    shaped = active.reshape(area.shape[0], S * S, active.shape[-1])
    return (shaped * gate[:, None, :]).reshape(second.shape)

def unpack_gains(gains):
    rows = gains.shape[0]
    widths = []
    for layer in range(L):
        widths = widths + [E, E, E, E, E, C, C, SE]
    widths = widths + [HEAD, HEAD, CLASSES]
    parts = []
    start = 0
    for width in widths:
        piece = width // rows
        parts.append(gains[:, start:start + piece].reshape(-1))
        start = start + piece
    return parts

def block(hidden, mats, chan, gains, mask, area, count):
    gain_one, shift_one, gain_two, shift_two, excite_bias, gain_three, shift_three, squeeze_bias = gains
    pre = low_back(matmul(low(hidden), mats[:, :E]))
    first = batch_norm(pre, mask, gain_one, shift_one, count)
    mixed = spread(first, chan[:9])
    second = batch_norm(mixed, mask, gain_two, shift_two, count)
    scaled = excite(second, chan[9:], excite_bias, squeeze_bias, area)
    out = low_back(matmul_bt(low(scaled), mats[:, E:]))
    return hidden + batch_norm(out, mask, gain_three, shift_three, count)

def forward(params, rows, mask, area, count):
    mats, chan, head, classes, gains = params
    parts = unpack_gains(gains)
    hidden = rows
    for layer in range(L):
        hidden = jax.checkpoint(block)(hidden, mats[layer], chan[layer], parts[8 * layer:8 * layer + 8], mask, area, count)
    head_gain, head_shift, class_bias = parts[8 * L:8 * L + 3]
    feat = low_back(matmul(low(hidden), head))
    pooled = pool(jax.nn.silu(batch_norm(feat, mask, head_gain, head_shift, count)), area)
    return low_back(matmul(low(pooled), classes) + class_bias)

def layout(bucket, counts, index):
    image = jnp.arange(IMGS)
    rank = image // IMG
    code = bucket[rank // N_SHARD]
    side = jnp.where(code == 0, 7, jnp.where(code == 1, 10, 12))
    valid = (image % IMG < counts[index, rank]).astype(jnp.float32)
    spot = jnp.arange(S * S)
    inside = ((spot[None, :] // S < side[:, None]) & (spot[None, :] % S < side[:, None])).astype(jnp.float32)
    mask = (valid[:, None] * inside).reshape(-1, 1)
    return (mask, (side * side).astype(jnp.float32), valid)

def mats_groups(value):
    rows = lax.optimization_barrier(jnp.sum(value * value, 1))
    half = rows.shape[1] // 2
    return jnp.stack([lax.optimization_barrier(jnp.sum(rows[:, :half], 1)), lax.optimization_barrier(jnp.sum(rows[:, half:], 1))], 1).reshape(-1)

def chan_groups(value):
    rows = lax.optimization_barrier(jnp.sum(value * value, 2))
    return jnp.stack([lax.optimization_barrier(jnp.sum(rows[:, :9], 1)), lax.optimization_barrier(jnp.sum(rows[:, 9:9 + SE], 1)), lax.optimization_barrier(jnp.sum(rows[:, 9 + SE:], 1))], 1).reshape(-1)

def mats_factor(ratio, value):
    paired = ratio.reshape(-1, 2)
    column = jnp.arange(value.shape[2])
    return jnp.where(column[None, :] < value.shape[2] // 2, paired[:, 0:1], paired[:, 1:2])[:, None, :]

def chan_factor(ratio, value):
    triple = ratio.reshape(-1, 3)
    row = jnp.arange(value.shape[1])[None, :]
    return jnp.where(row < 9, triple[:, 0:1], jnp.where(row < 9 + SE, triple[:, 1:2], triple[:, 2:3]))[:, :, None]

def adapt(first, second, grad, first_fix, second_fix):
    new_first = BETA_ONE * first + (1.0 - BETA_ONE) * grad
    new_second = BETA_TWO * second + (1.0 - BETA_TWO) * grad * grad
    update = new_first / first_fix / (jnp.sqrt(new_second / second_fix) + EPS_ADAM)
    return (new_first, new_second, update)

def reference(images, bucket, counts, balance, labels, step, expand_w, expand_m, expand_v, expand_e, chan_w, chan_m, chan_v, chan_e, head_w, head_m, head_v, head_e, class_w, class_m, class_v, class_e, gain_w, gain_m, gain_v, gain_e):
    weights = (expand_w, chan_w, head_w, class_w, gain_w)
    averaged = (expand_e, chan_e, head_e, class_e, gain_e)
    setups = [layout(bucket, counts, index) for index in range(MB)]
    total_weight = jnp.float32(0.0)
    for index in range(MB):
        total_weight = total_weight + jnp.sum(setups[index][2] * balance[index].astype(jnp.float32))
    averaged_low = tuple((low(item) for item in averaged))
    targets = []
    for index in range(MB):
        mask, area, valid = setups[index]
        rows = images[index].astype(jnp.float32).reshape(-1, C)
        targets.append(jax.nn.log_softmax(forward(averaged_low, rows, mask, area, jnp.sum(mask))))

    def objective(params):
        lowered = tuple((low(item) for item in params))
        total = jnp.float32(0.0)
        for index in range(MB):
            mask, area, valid = setups[index]
            rows = images[index].astype(jnp.float32).reshape(-1, C)
            logp = jax.nn.log_softmax(forward(lowered, rows, mask, area, jnp.sum(mask)))
            onehot = (labels[index][:, None] == jnp.arange(CLASSES)[None, :]).astype(jnp.float32)
            target = targets[index]
            per = -lax.optimization_barrier(jnp.sum(onehot * logp, 1)) + lax.optimization_barrier(jnp.sum(jnp.exp(target) * (target - logp), 1))
            coef = valid * balance[index].astype(jnp.float32) / total_weight
            total = total + jnp.sum(coef * per)
        return total
    loss, pull = jax.vjp(objective, weights)
    grads, = pull(jnp.float32(1.0))
    power = step[0].astype(jnp.float32)
    first_fix = 1.0 - jnp.power(jnp.float32(BETA_ONE), power)
    second_fix = 1.0 - jnp.power(jnp.float32(BETA_TWO), power)
    firsts = (expand_m, chan_m, head_m, class_m, gain_m)
    seconds = (expand_v, chan_v, head_v, class_v, gain_v)
    states = [adapt(firsts[item], seconds[item], grads[item], first_fix, second_fix) for item in range(5)]
    updates = [states[item][2] + DECAY * weights[item] for item in range(4)]
    weight_sq = jnp.concatenate([mats_groups(expand_w), chan_groups(chan_w), jnp.sum(head_w * head_w)[None], jnp.sum(class_w * class_w)[None]])
    update_sq = jnp.concatenate([mats_groups(updates[0]), chan_groups(updates[1]), jnp.sum(updates[2] * updates[2])[None], jnp.sum(updates[3] * updates[3])[None]])
    ratio = jnp.sqrt(weight_sq) / jnp.sqrt(update_sq)
    count_mats = 2 * L
    count_chan = 3 * L
    factors = [mats_factor(ratio[:count_mats], expand_w), chan_factor(ratio[count_mats:count_mats + count_chan], chan_w), ratio[count_mats + count_chan], ratio[count_mats + count_chan + 1]]
    result = [loss]
    for item in range(5):
        if item < 4:
            fresh = weights[item] - RATE * factors[item] * updates[item]
        else:
            fresh = weights[item] - RATE * states[item][2]
        result = result + [fresh, states[item][0], states[item][1], KEEP * averaged[item] + (1.0 - KEEP) * fresh]
    norms = jnp.stack([jnp.sqrt(weight_sq), jnp.sqrt(update_sq)])
    return tuple(result + [norms])
```

```python
import functools

import jax
import jax.numpy as jnp
from jax import lax
from jax.experimental import pallas as pl
from jax.experimental.pallas import tpu as pltpu
from jax.sharding import PartitionSpec as P

C = 256
E = 1536
SE = 64
HEAD = 1280
CLASSES = 1000
L = 2
S = 12


EPS_NORM = 1e-05
BETA_ONE = 0.9
BETA_TWO = 0.99
EPS_ADAM = 1e-08
DECAY = 0.01
RATE = 0.3
KEEP = 0.9


def contract(left, right, left_dim, right_dim):
    return lax.dot_general(
        left, right, (((left_dim,), (right_dim,)), ((), ())), preferred_element_type=jnp.float32
    )


def matmul(left, right):
    return jnp.dot(left, right, precision=lax.Precision.HIGHEST, preferred_element_type=jnp.float32)


def matmul_bt(left, right):
    return lax.dot_general(
        left,
        right,
        (((1,), (1,)), ((), ())),
        precision=lax.Precision.HIGHEST,
        preferred_element_type=jnp.float32,
    )


def norm_stats(values, masks, counts):
    sums_first = jnp.stack([jnp.sum(masks[0] * values[0], 0)])
    sums_second = jnp.stack([jnp.sum(masks[0] * values[0] * values[0], 0)])
    sums = lax.psum((sums_first, sums_second), ("dp", "shard"))
    mean = sums[0][0] / counts[0]
    scale = lax.rsqrt(sums[1][0] / counts[0] - mean * mean + EPS_NORM)
    result = [(mean, scale)]
    return result


def norm_apply(value, mask, gain, shift, mean, scale):
    return mask * (gain * ((value - mean) * scale) + shift)


def norm_back(grads, values, masks, gains, stats, counts):
    units = (values[0] - stats[0][0]) * stats[0][1]
    inners = masks[0] * grads[0] * gains[0]
    sums_first = jnp.stack([jnp.sum(inners, 0)])
    sums_second = jnp.stack([jnp.sum(inners * units, 0)])
    sums = lax.psum((sums_first, sums_second), ("dp", "shard"))
    gain_grad = jnp.sum(masks[0] * grads[0] * units, 0)
    shift_grad = jnp.sum(masks[0] * grads[0], 0)
    back = (
        masks[0] * stats[0][1] * (inners - sums[0][0] / counts[0] - units * sums[1][0] / counts[0])
    )
    result = [(back, gain_grad, shift_grad)]
    return result


def spread(first, taps):
    image = jax.nn.silu(first).reshape(-1, S, S, first.shape[-1])
    padded = jnp.pad(image, ((0, 0), (1, 1), (1, 1), (0, 0)))
    total = jnp.zeros_like(image)
    for offset in range(9):
        total = (
            total
            + padded[:, offset // 3 : offset // 3 + S, offset % 3 : offset % 3 + S, :]
            * taps[offset]
        )
    return total.reshape(first.shape)


def pool(value, area):
    return jnp.sum(value.reshape(area.shape[0], S * S, value.shape[-1]), 1) / area[:, None]


def excite(second, se_part, excite_bias, squeeze_bias, area):
    active = jax.nn.silu(second)
    pooled = pool(active, area)
    squeezed = jax.nn.silu(matmul_bt(pooled, se_part[:SE]) + squeeze_bias)
    gate = jax.nn.sigmoid(matmul(squeezed, se_part[SE:]) + excite_bias)
    shaped = active.reshape(area.shape[0], S * S, active.shape[-1])
    return (shaped * gate[:, None, :]).reshape(second.shape)


def unpack_gains(gains):
    rows = gains.shape[0]
    widths = []
    for layer in range(L):
        widths = widths + [E, E, E, E, E, C, C, SE]
    widths = widths + [HEAD, HEAD, CLASSES]
    parts = []
    start = 0
    for width in widths:
        piece = width // rows
        parts.append(gains[:, start : start + piece].reshape(-1))
        start = start + piece
    return parts


def pack_gains(vectors, rows):
    return jnp.concatenate([vector.reshape(rows, -1) for vector in vectors], 1)


def block_forward(hiddens, mats, chans, gainsets, masks, area, counts):
    width = mats[0].shape[1] // 2
    hidden_lows = [h.astype(jnp.bfloat16) for h in hiddens]
    pres = [jnp.dot(hidden_lows[0], mats[0][:, :width], preferred_element_type=jnp.float32)]
    stats_one = norm_stats(pres, masks, counts)
    firsts = norm_apply(
        pres[0], masks[0], gainsets[0][0], gainsets[0][1], stats_one[0][0], stats_one[0][1]
    )
    mixeds = [spread(firsts, chans[0][:9].astype(jnp.float32))]
    stats_two = norm_stats(mixeds, masks, counts)
    seconds = norm_apply(
        mixeds[0], masks[0], gainsets[0][2], gainsets[0][3], stats_two[0][0], stats_two[0][1]
    )
    scaleds = excite(
        seconds, chans[0][9:].astype(jnp.float32), gainsets[0][4], gainsets[0][7], area
    ).astype(jnp.bfloat16)
    outs = [contract(scaleds, mats[0][:, width:], 1, 1)]
    stats_three = norm_stats(outs, masks, counts)
    fresh = [
        hiddens[0]
        + norm_apply(
            outs[0], masks[0], gainsets[0][5], gainsets[0][6], stats_three[0][0], stats_three[0][1]
        )
    ]
    kept = [
        (
            hidden_lows[0],
            pres[0],
            stats_one[0],
            mixeds[0],
            stats_two[0],
            scaleds,
            outs[0],
            stats_three[0],
        )
    ]
    return (fresh, kept)


def block_backward(grad_hiddens, mats, chans, gainsets, kepts, masks, area, counts):
    width = mats[0].shape[1] // 2
    backs_three = norm_back(
        grad_hiddens, [kepts[0][6]], masks, [gainsets[0][5]], [kepts[0][7]], counts
    )
    k = 0
    hidden_low, pre, stats_one, mixed, stats_two, scaled, out, stats_three = kepts[k]
    grad_out_low = backs_three[k][0].astype(jnp.bfloat16)
    grad_project = contract(grad_out_low, scaled, 0, 0)
    grad_scaled = jnp.dot(grad_out_low, mats[k][:, width:], preferred_element_type=jnp.float32)
    second = norm_apply(mixed, masks[k], gainsets[k][2], gainsets[k][3], stats_two[0], stats_two[1])
    excite_part = lambda value, se_part, bias_x, bias_r: excite(
        value, se_part, bias_x, bias_r, area
    )
    unused, pull = jax.vjp(
        excite_part, second, chans[k][9:].astype(jnp.float32), gainsets[k][4], gainsets[k][7]
    )
    grad_second, grad_se, grad_excite_bias, grad_squeeze_bias = pull(grad_scaled)
    grad_seconds = [grad_second]
    middle = [(grad_project, grad_se, grad_excite_bias, grad_squeeze_bias)]
    backs_two = norm_back(
        grad_seconds, [kepts[0][3]], masks, [gainsets[0][2]], [kepts[0][4]], counts
    )
    k = 0
    pre = kepts[k][1]
    stats_one = kepts[k][2]
    first = norm_apply(pre, masks[k], gainsets[k][0], gainsets[k][1], stats_one[0], stats_one[1])
    unused, pull = jax.vjp(spread, first, chans[k][:9].astype(jnp.float32))
    grad_first, grad_taps = pull(backs_two[k][0])
    grad_firsts = [grad_first]
    taps_grads = [grad_taps]
    backs_one = norm_back(
        grad_firsts, [kepts[0][1]], masks, [gainsets[0][0]], [kepts[0][2]], counts
    )
    k = 0
    grad_pre_low = backs_one[k][0].astype(jnp.bfloat16)
    grad_expand = contract(kepts[k][0], grad_pre_low, 0, 0)
    grad_below = grad_hiddens[k] + contract(grad_pre_low, mats[k][:, :width], 1, 1)
    grad_project, grad_se, grad_excite_bias, grad_squeeze_bias = middle[k]
    grad_mats = jnp.concatenate([grad_expand, grad_project], 1)
    grad_chan = jnp.concatenate([taps_grads[k], grad_se], 0)
    grad_gains = [
        backs_one[k][1],
        backs_one[k][2],
        backs_two[k][1],
        backs_two[k][2],
        grad_excite_bias,
        backs_three[k][1],
        backs_three[k][2],
        grad_squeeze_bias,
    ]
    result = [(grad_below, grad_mats, grad_chan, grad_gains)]
    return result


def run_forward(models, rows_list, masks, area, counts):
    gainsets_all = [unpack_gains(m[4].astype(jnp.float32)) for m in models]
    layers = models[0][0].shape[0]
    hiddens = rows_list
    kept_blocks = []
    for layer in range(layers):
        hiddens, kept = block_forward(
            hiddens,
            [m[0][layer] for m in models],
            [m[1][layer] for m in models],
            [g[8 * layer : 8 * layer + 8] for g in gainsets_all],
            masks,
            area,
            counts,
        )
        kept_blocks.append(kept)
    heads = [g[8 * layers : 8 * layers + 3] for g in gainsets_all]
    hidden_lows = [h.astype(jnp.bfloat16) for h in hiddens]
    feats = [jnp.dot(hidden_lows[0], models[0][2], preferred_element_type=jnp.float32)]
    stats_head = norm_stats(feats, masks, counts)
    normed = norm_apply(
        feats[0], masks[0], heads[0][0], heads[0][1], stats_head[0][0], stats_head[0][1]
    )
    pooled_low = pool(jax.nn.silu(normed), area).astype(jnp.bfloat16)
    logits_all = [
        jnp.dot(pooled_low, models[0][3], preferred_element_type=jnp.float32) + heads[0][2]
    ]
    kept_heads = [(hidden_lows[0], feats[0], stats_head[0], pooled_low)]
    return (logits_all, kept_blocks, kept_heads)


def head_backward(grad_logits_all, model, kept_heads, masks, area, counts):
    count_all = len(grad_logits_all)
    layers = model[0].shape[0]
    gains = unpack_gains(model[4].astype(jnp.float32))
    head_gain, head_shift, class_bias = gains[8 * layers : 8 * layers + 3]
    k = 0
    hidden_low, feat, stats_head, pooled_low = kept_heads[k]
    grad_low = grad_logits_all[k].astype(jnp.bfloat16)
    grad_classes = contract(pooled_low, grad_low, 0, 0)
    grad_class_bias = jnp.sum(grad_low.astype(jnp.float32), 0)
    grad_pooled = contract(grad_low, model[3], 1, 1)
    normed = norm_apply(feat, masks[k], head_gain, head_shift, stats_head[0], stats_head[1])
    unused, pull = jax.vjp(lambda value: pool(jax.nn.silu(value), area), normed)
    (grad_normed,) = pull(grad_pooled)
    grad_normeds = [grad_normed]
    partial_heads = [(grad_classes, grad_class_bias)]
    backs = norm_back(
        grad_normeds, [kept_heads[0][1]], masks, [head_gain] * count_all, [kept_heads[0][2]], counts
    )
    k = 0
    grad_feat_low = backs[k][0].astype(jnp.bfloat16)
    grad_head = contract(kept_heads[k][0], grad_feat_low, 0, 0)
    grad_hidden = contract(grad_feat_low, model[2], 1, 1)
    head_tail = [backs[k][1], backs[k][2], partial_heads[k][1]]
    result = [(grad_hidden, grad_head, partial_heads[k][0], head_tail)]
    return result


IMGS = 5
ROWS = S * S
BATCHES = 2
HALF = IMGS * ROWS
FULL = BATCHES * HALF
SLOTS = BATCHES * IMGS
LANES = 128
EC = E // LANES
HC = HEAD // LANES
GAP = 16
TILE = 48
OFFSETS = [S * (a - 1) + (c - 1) for a in range(3) for c in range(3)]
MESH = pl.DeviceIdType.MESH
F32 = jnp.float32
BF16 = jnp.bfloat16


class Sum:
    def __init__(self, near, far, total, sems, sizes, rows):
        self.near, self.far, self.total = near, far, total
        self.sems = sems
        self.n_dp, self.n_sh = sizes
        self.rows = rows

    def copy_near(self, step, slot, target):
        d = lax.axis_index("dp")
        return pltpu.make_async_remote_copy(
            self.near.at[slot], self.near.at[slot],
            self.sems[0].at[step], self.sems[1].at[slot],
            device_id=(d, target), device_id_type=MESH)

    def copy_far(self, step, slot, target):
        s = lax.axis_index("shard")
        return pltpu.make_async_remote_copy(
            self.far.at[slot], self.far.at[slot],
            self.sems[2].at[step], self.sems[3].at[slot],
            device_id=(target, s), device_id_type=MESH)

    def start(self, stage):
        s = lax.axis_index("shard")
        self.near[s] = stage[0 : self.rows]
        for j in range(1, self.n_sh):
            self.copy_near(j, s, lax.rem(s + j, self.n_sh)).start()

    def middle(self):
        s, d = lax.axis_index("shard"), lax.axis_index("dp")
        for j in range(1, self.n_sh):
            self.copy_near(j, lax.rem(s + j, self.n_sh), s).wait_recv()
        for j in range(1, self.n_sh):
            self.copy_near(j, s, s).wait_send()
        part = self.near[0]
        for j in range(1, self.n_sh):
            part = part + self.near[j]
        self.far[d] = part

        def send(j, carry):
            self.copy_far(j, d, lax.rem(d + j, self.n_dp)).start()
            return carry

        lax.fori_loop(1, self.n_dp, send, 0)

    def finish(self):
        d = lax.axis_index("dp")

        def arrive(j, carry):
            self.copy_far(j, lax.rem(d + j, self.n_dp), d).wait_recv()
            self.copy_far(j, d, d).wait_send()
            return carry

        lax.fori_loop(1, self.n_dp, arrive, 0)
        part = self.far[0]
        for j in range(1, self.n_dp):
            part = part + self.far[j]
        self.total[0 : self.rows] = part


def sum_scratch(sizes, rows):
    n_dp, n_sh = sizes
    return [
        pltpu.VMEM((n_sh, rows, LANES), F32),
        pltpu.VMEM((n_dp, rows, LANES), F32),
        pltpu.SemaphoreType.DMA((n_sh,)),
        pltpu.SemaphoreType.DMA((n_sh,)),
        pltpu.SemaphoreType.DMA((n_dp,)),
        pltpu.SemaphoreType.DMA((n_dp,)),
    ]


def greet(sizes):
    n_dp, n_sh = sizes
    d, s = lax.axis_index("dp"), lax.axis_index("shard")
    gate = pltpu.get_barrier_semaphore()
    for j in range(1, n_sh):
        pl.semaphore_signal(gate, inc=1, device_id=(d, lax.rem(s + j, n_sh)), device_id_type=MESH)

    def signal(j, carry):
        pl.semaphore_signal(gate, inc=1, device_id=(lax.rem(d + j, n_dp), s), device_id_type=MESH)
        return carry

    lax.fori_loop(1, n_dp, signal, 0)
    pl.semaphore_wait(gate, n_sh + n_dp - 2)


def repeat(count, body, hook=None):
    def step(i, carry):
        if hook is not None:

            @pl.when(i == hook[0])
            def _():
                hook[1]()

        body(i)
        return carry

    lax.fori_loop(0, count, step, 0)


def lanes(c, width=LANES):
    return pl.ds(pl.multiple_of(c * width, width), width)


def coefs(total, row, count, gain, shift):
    mean = total[pl.ds(row, 1), :] / count
    square = total[pl.ds(row + 1, 1), :] / count
    scale = gain * lax.rsqrt(square - mean * mean + EPS_NORM)
    return scale, shift - mean * scale


def act_half(half):
    return half + half * jnp.tanh(half)


def forward_kernel(sizes, *refs):
    (images, mask, edge_l, edge_r, area, firstrow, wexp, headt, taps, squeeze, excite, gain_e, gain_c, gain_h, gain_s,
     pre_s, mixed_s, feat_s, out_s, low_s, pool_s, unit_s, gate_s, tot_e, tot_c, tot_h, pooled_h,
     pre, hid, out_t, low_t, scaled, pads, stages, totals, cnt, pool_t, gate_t) = refs[:38]
    rest = list(refs[38:])
    save_sems = rest.pop(0)
    sums = []
    for m in range(2):
        group = []
        for rows in (56, 48, 8, 40):
            near, far = rest[0], rest[1]
            group.append((near, far, rest[2:6], rows))
            rest = rest[6:]
        sums.append(group)

    greet(sizes)

    def low(m, layer):
        return low_s.at[layer] if m == 0 else low_t

    def out(m, layer):
        return out_s.at[layer] if m == 0 else out_t

    def total_ref(m, kind, layer):
        if m == 0:
            return (tot_e.at[layer, 0], tot_e.at[layer, 1], tot_c.at[layer], tot_h)[kind]
        return totals.at[kind]

    def summer(m, kind, layer):
        near, far, sems, rows = sums[m][kind]
        if kind == 0 and layer == 1:
            pass
        return Sum(near, far, total_ref(m, kind, layer), sems, sizes, rows)

    def save(src, dst, index):
        return pltpu.make_async_copy(src, dst, save_sems.at[index])

    for slot in range(SLOTS):
        pads[slot, 0:GAP, :] = jnp.zeros((GAP, LANES), F32)
        pads[slot, GAP + ROWS : 2 * GAP + ROWS, :] = jnp.zeros((GAP, LANES), F32)

    def load_rows(i):
        rows = pl.ds(pl.multiple_of(i * ROWS, ROWS), ROWS)
        for half in range(2):
            cols = slice(half * LANES, half * LANES + LANES)
            value = images[rows, cols].astype(F32) * mask[rows, :]
            hid[0, rows, cols] = value
            hid[1, rows, cols] = value
            low_s[0, rows, cols] = value.astype(BF16)
            low_t[rows, cols] = value.astype(BF16)

    repeat(SLOTS, load_rows)

    def update(m, layer):
        tot = total_ref(m, 2, layer)
        for half in range(2):
            cols = slice(half * LANES, half * LANES + LANES)
            for b in range(BATCHES):
                scale, shift = coefs(tot, 4 * half + 2 * b, cnt[b : b + 1, :], gain_c[m, layer, 0:1, cols], gain_c[m, layer, 1:2, cols])

                def one(i):
                    rows = pl.ds(pl.multiple_of(b * HALF + i * ROWS, ROWS), ROWS)
                    value = hid[m, rows, cols] + mask[rows, :] * (out(m, layer)[rows, cols] * scale + shift)
                    hid[m, rows, cols] = value
                    low(m, layer + 1)[rows, cols] = value.astype(BF16)

                repeat(IMGS, one)

    def put_sums(stage, chunk, b, value):
        stage[pl.ds(4 * chunk + 2 * b, 1), :] = jnp.sum(value, 0, keepdims=True)
        stage[pl.ds(4 * chunk + 2 * b + 1, 1), :] = jnp.sum(value * value, 0, keepdims=True)

    def expand(m, layer, hook=None):
        stage = stages.at[m]

        def body(c):
            weight = wexp[m, layer, :, lanes(c, 256)]
            for b in range(BATCHES):
                value = jnp.dot(low(m, layer)[b * HALF : (b + 1) * HALF, :], weight, preferred_element_type=F32)
                for half in range(2):
                    piece = value[:, half * LANES : (half + 1) * LANES]
                    pre[m, 2 * c + half, b * HALF : (b + 1) * HALF, :] = piece
                    put_sums(stage, 2 * c + half, b, piece)
            if m == 0:
                for half in range(2):
                    save(pre.at[0, 2 * c + half], pre_s.at[layer, 2 * c + half], 2 * c + half).start()

        repeat(E // 256, body, hook)

    def depthwise(m, layer, hook=None):
        stage = stages.at[m]
        tot = total_ref(m, 0, layer)

        def body(c):
            if m == 0:
                save(pre.at[0, c], pre_s.at[layer, c], c).wait()
            tap = [taps[m, layer, k : k + 1, lanes(c)] for k in range(9)]
            for b in range(BATCHES):
                scale, shift = coefs(tot, 4 * c + 2 * b, cnt[b : b + 1, :], gain_e[m, layer, 0:1, lanes(c)], gain_e[m, layer, 1:2, lanes(c)])
                scale, shift = 0.5 * scale, 0.5 * shift
                for i in range(IMGS):
                    slot = b * IMGS + i
                    rows = slice(slot * ROWS, (slot + 1) * ROWS)
                    half = mask[rows, :] * (pre[m, c, rows, :] * scale + shift)
                    pads[slot, GAP : GAP + ROWS, :] = act_half(half)
                first = jnp.zeros((8, LANES), F32)
                second = jnp.zeros((8, LANES), F32)
                for i in range(IMGS):
                    slot = b * IMGS + i
                    for t in range(ROWS // TILE):
                        start = GAP + t * TILE
                        near = [pads[slot, start + o : start + o + TILE, :] for o in OFFSETS]
                        left = near[0] * tap[0] + near[3] * tap[3] + near[6] * tap[6]
                        mid = near[1] * tap[1] + near[4] * tap[4] + near[7] * tap[7]
                        right = near[2] * tap[2] + near[5] * tap[5] + near[8] * tap[8]
                        rows = slice(slot * ROWS + t * TILE, slot * ROWS + (t + 1) * TILE)
                        value = mask[rows, :] * (mid + edge_l[0:TILE, :] * left + edge_r[0:TILE, :] * right)
                        pre[m, c, rows, :] = value
                        first = first + jnp.sum(value.reshape(TILE // 8, 8, LANES), 0)
                        second = second + jnp.sum((value * value).reshape(TILE // 8, 8, LANES), 0)
                stage[pl.ds(4 * c + 2 * b, 1), :] = jnp.sum(first, 0, keepdims=True)
                stage[pl.ds(4 * c + 2 * b + 1, 1), :] = jnp.sum(second, 0, keepdims=True)
            if m == 0:
                save(pre.at[0, c], mixed_s.at[layer, c], c).start()

        repeat(EC, body, hook)

    def pooling(m, layer, hook=None):
        tot = total_ref(m, 1, layer)
        pool = pool_s.at[layer] if m == 0 else pool_t

        def body(c):
            if m == 0:
                save(pre.at[0, c], mixed_s.at[layer, c], c).wait()
            for b in range(BATCHES):
                scale, shift = coefs(tot, 4 * c + 2 * b, cnt[b : b + 1, :], gain_e[m, layer, 2:3, lanes(c)], gain_e[m, layer, 3:4, lanes(c)])
                scale, shift = 0.5 * scale, 0.5 * shift
                for i in range(IMGS):
                    slot = b * IMGS + i
                    rows = slice(slot * ROWS, (slot + 1) * ROWS)
                    value = act_half(mask[rows, :] * (pre[m, c, rows, :] * scale + shift))
                    pre[m, c, rows, :] = value
                    pool[slot : slot + 1, lanes(c)] = jnp.sum(value, 0, keepdims=True) / area[0:1, :]

        repeat(EC, body, hook)

    def project(m, layer):
        pool = pool_s.at[layer] if m == 0 else pool_t
        gate = gate_s.at[layer] if m == 0 else gate_t
        units = matmul_bt(pool[...], squeeze[m, layer]) + gain_s[m, layer]
        if m == 0:
            unit_s[layer] = units
        gate[...] = jax.nn.sigmoid(matmul(jax.nn.silu(units), excite[m, layer]) + gain_e[m, layer, 4:5, :])

        def body(c):
            for i in range(SLOTS):
                rows = slice(i * ROWS, (i + 1) * ROWS)
                scaled[rows, lanes(c)] = (pre[m, c, rows, :] * gate[i : i + 1, lanes(c)]).astype(BF16)

        repeat(EC, body)
        stage = stages.at[m]
        for b in range(BATCHES):
            rows = slice(b * HALF, (b + 1) * HALF)
            value = contract(scaled[rows, :], wexp[m, layer, :, E : 2 * E], 1, 1)
            out(m, layer)[rows, :] = value
            for half in range(2):
                put_sums(stage, half, b, value[:, half * LANES : (half + 1) * LANES])

    def features(m, hook=None):
        stage = stages.at[m]

        def body(c):
            weight = headt[m, pl.ds(pl.multiple_of(c * 256, 256), 256), :]
            for b in range(BATCHES):
                value = contract(low(m, L)[b * HALF : (b + 1) * HALF, :], weight, 1, 1)
                for half in range(2):
                    piece = value[:, half * LANES : (half + 1) * LANES]
                    pre[m, 2 * c + half, b * HALF : (b + 1) * HALF, :] = piece
                    put_sums(stage, 2 * c + half, b, piece)
            if m == 0:
                for half in range(2):
                    save(pre.at[0, 2 * c + half], feat_s.at[2 * c + half], 2 * c + half).start()

        repeat(HEAD // 256, body, hook)

    def head_pool(m, hook=None):
        tot = total_ref(m, 3, 0)

        def body(c):
            for b in range(BATCHES):
                scale, shift = coefs(tot, 4 * c + 2 * b, cnt[b : b + 1, :], gain_h[m, 0:1, lanes(c)], gain_h[m, 1:2, lanes(c)])
                scale, shift = 0.5 * scale, 0.5 * shift
                for i in range(IMGS):
                    slot = b * IMGS + i
                    rows = slice(slot * ROWS, (slot + 1) * ROWS)
                    value = act_half(mask[rows, :] * (pre[m, c, rows, :] * scale + shift))
                    pooled_h[m, slot : slot + 1, lanes(c)] = jnp.sum(value, 0, keepdims=True) / area[0:1, :]

        repeat(HC, body, hook)

    for m in range(2):
        stages[m] = jnp.zeros((56, LANES), F32)
    pool_s[...] = jnp.zeros(pool_s.shape, F32)
    pool_t[...] = jnp.zeros(pool_t.shape, F32)
    pooled_h[...] = jnp.zeros(pooled_h.shape, F32)
    stages[0, 48:56, :] = firstrow[...]
    pending = None
    for layer in range(L):
        s_one, t_one = summer(0, 0, layer), summer(1, 0, layer)
        s_two, t_two = summer(0, 1, layer), summer(1, 1, layer)
        s_three, t_three = summer(0, 2, layer), summer(1, 2, layer)
        if layer > 0:
            update(0, layer - 1)
        expand(0, layer, None if pending is None else (2, pending.middle))
        s_one.start(stages.at[0])
        if layer > 0:
            pending.finish()
            update(1, layer - 1)
        expand(1, layer, (4, s_one.middle))
        t_one.start(stages.at[1])
        s_one.finish()
        if layer == 0:
            cnt[...] = tot_e[0, 0, 48:56, :]
        depthwise(0, layer, (2, t_one.middle))
        s_two.start(stages.at[0])
        t_one.finish()
        depthwise(1, layer, (5, s_two.middle))
        t_two.start(stages.at[1])
        s_two.finish()
        pooling(0, layer, (5, t_two.middle))
        project(0, layer)
        s_three.start(stages.at[0])
        t_two.finish()
        pooling(1, layer, (6, s_three.middle))
        project(1, layer)
        t_three.start(stages.at[1])
        s_three.finish()
        pending = t_three
    s_head, t_head = summer(0, 3, 0), summer(1, 3, 0)
    update(0, L - 1)
    features(0, (2, pending.middle))
    s_head.start(stages.at[0])
    pending.finish()
    update(1, L - 1)
    features(1, (4, s_head.middle))
    t_head.start(stages.at[1])
    s_head.finish()
    head_pool(0, (3, t_head.middle))
    t_head.finish()
    head_pool(1)
    for c in range(HC):
        save(pre.at[0, c], feat_s.at[c], c).wait()


def run_forward_all(sizes, inputs):
    sds = jax.ShapeDtypeStruct
    vm = pl.BlockSpec(memory_space=pltpu.VMEM)
    hbm = pl.BlockSpec(memory_space=pl.ANY)
    outs = [
        (sds((L, EC, FULL, LANES), F32), hbm),
        (sds((L, EC, FULL, LANES), F32), hbm),
        (sds((HC, FULL, LANES), F32), hbm),
        (sds((L, FULL, C), F32), vm),
        (sds((L + 1, FULL, C), BF16), vm),
        (sds((L, 16, E), F32), vm),
        (sds((L, 16, SE), F32), vm),
        (sds((L, 16, E), F32), vm),
        (sds((L, 2, 56, LANES), F32), vm),
        (sds((L, 8, LANES), F32), vm),
        (sds((40, LANES), F32), vm),
        (sds((2, 16, HEAD), F32), vm),
    ]
    scratch = [
        pltpu.VMEM((2, EC, FULL, LANES), F32),
        pltpu.VMEM((2, FULL, C), F32),
        pltpu.VMEM((FULL, C), F32),
        pltpu.VMEM((FULL, C), BF16),
        pltpu.VMEM((FULL, E), BF16),
        pltpu.VMEM((SLOTS, ROWS + 2 * GAP, LANES), F32),
        pltpu.VMEM((2, 56, LANES), F32),
        pltpu.VMEM((4, 56, LANES), F32),
        pltpu.VMEM((8, LANES), F32),
        pltpu.VMEM((16, E), F32),
        pltpu.VMEM((16, E), F32),
        pltpu.SemaphoreType.DMA((EC,)),
    ]
    for m in range(2):
        for rows in (56, 48, 8, 40):
            scratch = scratch + sum_scratch(sizes, rows)
    return pl.pallas_call(
        functools.partial(forward_kernel, sizes),
        out_shape=[o[0] for o in outs],
        in_specs=[vm] * len(inputs),
        out_specs=[o[1] for o in outs],
        scratch_shapes=scratch,
        compiler_params=pltpu.CompilerParams(collective_id=1, has_side_effects=True, vmem_limit_bytes=63 * 2**20),
        name="forward",
    )(*inputs)


def objective(logits, target, onehot, coef):
    logp = jax.nn.log_softmax(logits)
    per = -jnp.sum(onehot * logp, 1) + jnp.sum(jnp.exp(target) * (target - logp), 1)
    return jnp.sum(coef * per)


def own_slice(value, dim, parts, place):
    width = value.shape[dim] // parts
    return lax.dynamic_slice_in_dim(value, place * width, width, dim)


def mats_groups(value):
    rows = jnp.sum(value * value, 1)
    half = rows.shape[1] // 2
    return jnp.stack([jnp.sum(rows[:, :half], 1), jnp.sum(rows[:, half:], 1)], 1).reshape(-1)


def chan_groups(value):
    rows = jnp.sum(value * value, 2)
    return jnp.stack(
        [jnp.sum(rows[:, :9], 1), jnp.sum(rows[:, 9 : 9 + SE], 1), jnp.sum(rows[:, 9 + SE :], 1)], 1
    ).reshape(-1)


def mats_factor(ratio, value):
    paired = ratio.reshape(-1, 2)
    column = jnp.arange(value.shape[2])
    return jnp.where(column[None, :] < value.shape[2] // 2, paired[:, 0:1], paired[:, 1:2])[
        :, None, :
    ]


def chan_factor(ratio, value):
    triple = ratio.reshape(-1, 3)
    row = jnp.arange(value.shape[1])[None, :]
    return jnp.where(
        row < 9, triple[:, 0:1], jnp.where(row < 9 + SE, triple[:, 1:2], triple[:, 2:3])
    )[:, :, None]


def adapt(first, second, grad, first_fix, second_fix):
    new_first = BETA_ONE * first + (1.0 - BETA_ONE) * grad
    new_second = BETA_TWO * second + (1.0 - BETA_TWO) * grad * grad
    update = new_first / first_fix / (jnp.sqrt(new_second / second_fix) + EPS_ADAM)
    return (new_first, new_second, update)


def per_device(
    images,
    bucket,
    counts,
    balance,
    labels,
    step,
    expand_w,
    expand_m,
    expand_v,
    expand_e,
    chan_w,
    chan_m,
    chan_v,
    chan_e,
    head_w,
    head_m,
    head_v,
    head_e,
    class_w,
    class_m,
    class_v,
    class_e,
    gain_w,
    gain_m,
    gain_v,
    gain_e,
):
    full = (
        lax.all_gather(expand_w.astype(jnp.bfloat16), "shard", axis=1, tiled=True),
        lax.all_gather(chan_w.astype(jnp.bfloat16), "shard", axis=2, tiled=True),
        lax.all_gather(head_w.astype(jnp.bfloat16), "shard", axis=1, tiled=True),
        lax.all_gather(class_w.astype(jnp.bfloat16), "shard", axis=0, tiled=True),
        lax.all_gather(gain_w.astype(jnp.bfloat16), "shard", axis=0, tiled=True),
        lax.all_gather(expand_e.astype(jnp.bfloat16), "shard", axis=1, tiled=True),
        lax.all_gather(chan_e.astype(jnp.bfloat16), "shard", axis=2, tiled=True),
        lax.all_gather(head_e.astype(jnp.bfloat16), "shard", axis=1, tiled=True),
        lax.all_gather(class_e.astype(jnp.bfloat16), "shard", axis=0, tiled=True),
        lax.all_gather(gain_e.astype(jnp.bfloat16), "shard", axis=0, tiled=True),
    )
    model = full[:5]
    shadow = full[5:]
    batches = images.shape[0]
    slots = images.shape[1]
    code = bucket[0]
    side = jnp.where(code == 0, 7, jnp.where(code == 1, 10, 12))
    spot = jnp.arange(S * S)
    inside = ((spot // S < side) & (spot % S < side)).astype(jnp.float32)
    area_value = (side * side).astype(jnp.float32)
    area = jnp.full((slots,), area_value)
    valid = (jnp.arange(slots)[None, :] < counts).astype(jnp.float32)
    weighted = valid * balance.astype(jnp.float32)
    pixels, weight_sums = lax.psum(
        (jnp.sum(valid, 1) * area_value, jnp.sum(weighted, 1)), ("dp", "shard")
    )
    total_weight = jnp.sum(weight_sums)
    layers = model[0].shape[0]
    rows_all = [
        images[index].astype(jnp.float32).reshape(-1, images.shape[-1]) for index in range(batches)
    ]
    masks_all = [
        (valid[index][:, None] * inside[None, :]).reshape(-1, 1) for index in range(batches)
    ]
    counts_all = [pixels[index] for index in range(batches)]
    backward_groups = [[index] for index in range(batches)]
    sizes = (lax.axis_size("dp"), lax.axis_size("shard"))
    both = [jnp.stack([model[item], shadow[item]]) for item in range(5)]
    spot_l = (spot % S > 0).astype(F32)[:, None]
    spot_r = (spot % S < S - 1).astype(F32)[:, None]
    spread_l = jnp.broadcast_to(spot_l, (S * S, LANES))
    spread_r = jnp.broadcast_to(spot_r, (S * S, LANES))
    mask_all = jnp.broadcast_to(jnp.concatenate(masks_all, 0), (FULL, LANES))
    own = jnp.concatenate([jnp.sum(valid, 1) * area_value, jnp.sum(weighted, 1), jnp.zeros((4,), F32)])
    chan_f = both[1].astype(F32)
    gains_f = both[4].astype(F32)
    n_sh = sizes[1]
    block_width = gains_f.shape[2] - 2 * (HEAD // n_sh) - CLASSES // n_sh
    blocks = gains_f[:, :, :block_width].reshape(2, n_sh, L, -1)
    wide = 5 * E // n_sh
    vec_e = blocks[..., :wide].reshape(2, n_sh, L, 5, E // n_sh).transpose(0, 2, 3, 1, 4).reshape(2, L, 5, E)
    vec_c = blocks[..., wide : wide + 2 * C // n_sh].reshape(2, n_sh, L, 2, C // n_sh).transpose(0, 2, 3, 1, 4).reshape(2, L, 2, C)
    vec_s = blocks[..., wide + 2 * C // n_sh :].transpose(0, 2, 1, 3).reshape(2, L, 1, SE)
    heads_f = gains_f[:, :, block_width : block_width + 2 * HEAD // n_sh]
    vec_h = heads_f.reshape(2, n_sh, 2, HEAD // n_sh).transpose(0, 2, 1, 3).reshape(2, 2, HEAD)
    class_bias = gains_f[:, :, block_width + 2 * HEAD // n_sh :].reshape(2, CLASSES)
    inputs = [
        images.reshape(FULL, C), mask_all, spread_l, spread_r, jnp.full((1, LANES), area_value),
        jnp.broadcast_to(own[:, None], (8, LANES)), both[0], both[2].transpose(0, 2, 1),
        chan_f[:, :, :9], chan_f[:, :, 9 : 9 + SE], chan_f[:, :, 9 + SE :], vec_e, vec_c, vec_h, vec_s,
    ]
    (pre_s, mixed_s, feat_s, out_s, low_s, pool_s, unit_s, gate_s, tot_e, tot_c, tot_h, pooled_h) = run_forward_all(sizes, inputs)
    logits = [jnp.dot(pooled_h[m, :SLOTS].astype(BF16), both[3][m], preferred_element_type=F32) + class_bias[m] for m in range(2)]
    main_logits = [logits[0][b * IMGS : (b + 1) * IMGS] for b in range(2)]
    targets = [jax.nn.log_softmax(logits[1][b * IMGS : (b + 1) * IMGS]) for b in range(2)]

    def plain(value, b):
        return value[:, b * HALF : (b + 1) * HALF].transpose(1, 0, 2).reshape(HALF, -1)

    def stats(tot, b, chunks):
        pairs = tot[: 4 * chunks].reshape(chunks, 2, 2, LANES)[:, b]
        mean = pairs[:, 0].reshape(-1) / counts_all[b]
        return (mean, lax.rsqrt(pairs[:, 1].reshape(-1) / counts_all[b] - mean * mean + EPS_NORM))

    main_blocks = []
    main_heads = []
    for b in range(2):
        rows = slice(b * HALF, (b + 1) * HALF)
        kept = []
        for layer in range(layers):
            mixed = plain(mixed_s[layer], b)
            st = stats(tot_e[layer, 1], b, EC)
            second = norm_apply(mixed, masks_all[b], vec_e[0, layer, 2], vec_e[0, layer, 3], st[0], st[1])
            act = jax.nn.silu(second).reshape(IMGS, ROWS, E) * gate_s[layer, b * IMGS : (b + 1) * IMGS][:, None, :]
            kept.append((low_s[layer, rows], plain(pre_s[layer], b), stats(tot_e[layer, 0], b, EC), mixed, st,
                         act.reshape(HALF, E).astype(BF16), out_s[layer, rows], stats(tot_c[layer], b, 2)))
        main_blocks.append(kept)
        main_heads.append((low_s[layers, rows], plain(feat_s, b), stats(tot_h, b, HC), pooled_h[0, b * IMGS : (b + 1) * IMGS].astype(BF16)))
    grad_mats = jnp.zeros(model[0].shape, jnp.float32)
    grad_chan = jnp.zeros(model[1].shape, jnp.float32)
    grad_head = jnp.zeros(model[2].shape, jnp.float32)
    grad_class = jnp.zeros(model[3].shape, jnp.float32)
    grad_gain = jnp.zeros(model[4].shape, jnp.float32)
    loss = jnp.float32(0.0)
    gain_list = unpack_gains(model[4].astype(jnp.float32))
    for group in backward_groups:
        grad_logits_all = []
        for index in group:
            onehot = (
                labels[index][:, None] == jnp.arange(main_logits[index].shape[1])[None, :]
            ).astype(jnp.float32)
            coef = weighted[index] / total_weight
            target = targets[index]
            part, pull = jax.vjp(
                lambda value: objective(value, target, onehot, coef), main_logits[index]
            )
            (grad_logits,) = pull(jnp.float32(1.0))
            loss = loss + part
            grad_logits_all.append(grad_logits)
        masks = [masks_all[index] for index in group]
        group_counts = [counts_all[index] for index in group]
        head_parts = head_backward(
            grad_logits_all,
            model,
            [main_heads[index] for index in group],
            masks,
            area,
            group_counts,
        )
        grad_hiddens = [item[0] for item in head_parts]
        mats_parts = [[None] * layers for index in group]
        chan_parts = [[None] * layers for index in group]
        gain_parts = [[None] * layers for index in group]
        for layer in reversed(range(layers)):
            size = len(group)
            backs = block_backward(
                grad_hiddens,
                [model[0][layer]] * size,
                [model[1][layer]] * size,
                [gain_list[8 * layer : 8 * layer + 8]] * size,
                [main_blocks[index][layer] for index in group],
                masks,
                area,
                group_counts,
            )
            grad_hiddens = [item[0] for item in backs]
            place = 0
            mats_parts[place][layer] = backs[place][1]
            chan_parts[place][layer] = backs[place][2]
            gain_parts[place][layer] = backs[place][3]
        place = 0
        grad_mats = grad_mats + jnp.stack(mats_parts[place])
        grad_chan = grad_chan + jnp.stack(chan_parts[place])
        grad_head = grad_head + head_parts[place][1]
        grad_class = grad_class + head_parts[place][2]
        vectors = []
        for layer in range(layers):
            vectors = vectors + gain_parts[place][layer]
        vectors = vectors + head_parts[place][3]
        grad_gain = grad_gain + pack_gains(vectors, grad_gain.shape[0])
    shards = lax.axis_size("shard")
    loss_spread = jnp.full((shards,), loss)
    summed = lax.psum(
        (loss_spread, grad_mats, grad_chan, grad_head, grad_class, grad_gain), ("dp", "shard")
    )
    place = lax.axis_index("shard")
    owned = (
        summed[0][0:1],
        own_slice(summed[1], 1, shards, place),
        own_slice(summed[2], 2, shards, place),
        own_slice(summed[3], 1, shards, place),
        own_slice(summed[4], 0, shards, place),
        own_slice(summed[5], 0, shards, place),
    )
    total_loss = owned[0][0]
    power = step[0].astype(jnp.float32)
    first_fix = 1.0 - jnp.power(jnp.float32(BETA_ONE), power)
    second_fix = 1.0 - jnp.power(jnp.float32(BETA_TWO), power)
    weights = (expand_w, chan_w, head_w, class_w, gain_w)
    firsts = (expand_m, chan_m, head_m, class_m, gain_m)
    seconds = (expand_v, chan_v, head_v, class_v, gain_v)
    averaged = (expand_e, chan_e, head_e, class_e, gain_e)
    states = [
        adapt(firsts[item], seconds[item], owned[item + 1], first_fix, second_fix)
        for item in range(5)
    ]
    updates = [states[item][2] + DECAY * weights[item] for item in range(4)]
    local_weight_sq = jnp.concatenate(
        [
            mats_groups(expand_w),
            chan_groups(chan_w),
            jnp.sum(head_w * head_w)[None],
            jnp.sum(class_w * class_w)[None],
        ]
    )
    local_update_sq = jnp.concatenate(
        [
            mats_groups(updates[0]),
            chan_groups(updates[1]),
            jnp.sum(updates[2] * updates[2])[None],
            jnp.sum(updates[3] * updates[3])[None],
        ]
    )
    weight_sq, update_sq = lax.psum((local_weight_sq, local_update_sq), "shard")
    ratio = jnp.sqrt(weight_sq) / jnp.sqrt(update_sq)
    count_mats = 2 * layers
    count_chan = 3 * layers
    factors = [
        mats_factor(ratio[:count_mats], expand_w),
        chan_factor(ratio[count_mats : count_mats + count_chan], chan_w),
        ratio[count_mats + count_chan],
        ratio[count_mats + count_chan + 1],
    ]
    result = [total_loss]
    for item in range(5):
        if item < 4:
            fresh = weights[item] - RATE * factors[item] * updates[item]
        else:
            fresh = weights[item] - RATE * states[item][2]
        result = result + [
            fresh,
            states[item][0],
            states[item][1],
            KEEP * averaged[item] + (1.0 - KEEP) * fresh,
        ]
    norms = jnp.stack([jnp.sqrt(weight_sq), jnp.sqrt(update_sq)])
    return tuple(result + [norms])


def solution(mesh):
    in_specs = (
        P(None, ("dp", "shard"), None, None, None),
        P("dp"),
        P(None, ("dp", "shard")),
        P(None, ("dp", "shard")),
        P(None, ("dp", "shard")),
        P(),
        P(None, "shard", None),
        P(None, "shard", None),
        P(None, "shard", None),
        P(None, "shard", None),
        P(None, None, "shard"),
        P(None, None, "shard"),
        P(None, None, "shard"),
        P(None, None, "shard"),
        P(None, "shard"),
        P(None, "shard"),
        P(None, "shard"),
        P(None, "shard"),
        P("shard", None),
        P("shard", None),
        P("shard", None),
        P("shard", None),
        P("shard", None),
        P("shard", None),
        P("shard", None),
        P("shard", None),
    )
    out_specs = (
        P(),
        P(None, "shard", None),
        P(None, "shard", None),
        P(None, "shard", None),
        P(None, "shard", None),
        P(None, None, "shard"),
        P(None, None, "shard"),
        P(None, None, "shard"),
        P(None, None, "shard"),
        P(None, "shard"),
        P(None, "shard"),
        P(None, "shard"),
        P(None, "shard"),
        P("shard", None),
        P("shard", None),
        P("shard", None),
        P("shard", None),
        P("shard", None),
        P("shard", None),
        P("shard", None),
        P("shard", None),
        P(),
    )
    return jax.shard_map(
        per_device, mesh=mesh, in_specs=in_specs, out_specs=out_specs, check_vma=False
    )
```

```python
import functools

import jax
import jax.numpy as jnp
from jax import lax
from jax.experimental import pallas as pl
from jax.experimental.pallas import tpu as pltpu
from jax.sharding import PartitionSpec as P

C = 256
E = 1536
SE = 64
HEAD = 1280
CLASSES = 1000
L = 2
S = 12


EPS_NORM = 1e-05
BETA_ONE = 0.9
BETA_TWO = 0.99
EPS_ADAM = 1e-08
DECAY = 0.01
RATE = 0.3
KEEP = 0.9


def contract(left, right, left_dim, right_dim):
    return lax.dot_general(
        left, right, (((left_dim,), (right_dim,)), ((), ())), preferred_element_type=jnp.float32
    )


def matmul(left, right):
    return jnp.dot(left, right, precision=lax.Precision.HIGHEST, preferred_element_type=jnp.float32)


def matmul_bt(left, right):
    return lax.dot_general(
        left,
        right,
        (((1,), (1,)), ((), ())),
        precision=lax.Precision.HIGHEST,
        preferred_element_type=jnp.float32,
    )


def matmul_tb(left, right):
    return lax.dot_general(
        left,
        right,
        (((0,), (0,)), ((), ())),
        precision=lax.Precision.HIGHEST,
        preferred_element_type=jnp.float32,
    )


def pack_gains(vectors, rows):
    return jnp.concatenate([vector.reshape(rows, -1) for vector in vectors], 1)


IMGS = 5
ROWS = S * S
BATCHES = 2
HALF = IMGS * ROWS
FULL = BATCHES * HALF
SLOTS = BATCHES * IMGS
LANES = 128
EC = E // LANES
HC = HEAD // LANES
GAP = 16
TILE = 48
TILE_BACK = 48
OFFSETS = [S * (a - 1) + (c - 1) for a in range(3) for c in range(3)]
MESH = pl.DeviceIdType.MESH
F32 = jnp.float32
BF16 = jnp.bfloat16


class Sum:
    def __init__(self, near, far, total, sems, sizes, rows):
        self.near, self.far, self.total = near, far, total
        self.sems = sems
        self.n_dp, self.n_sh = sizes
        self.rows = rows

    def copy_near(self, step, slot, target):
        d = lax.axis_index("dp")
        return pltpu.make_async_remote_copy(
            self.near.at[slot], self.near.at[slot],
            self.sems[0].at[step], self.sems[1].at[slot],
            device_id=(d, target), device_id_type=MESH)

    def copy_far(self, step, slot, target):
        s = lax.axis_index("shard")
        return pltpu.make_async_remote_copy(
            self.far.at[slot], self.far.at[slot],
            self.sems[2].at[step], self.sems[3].at[slot],
            device_id=(target, s), device_id_type=MESH)

    def start(self, stage):
        s = lax.axis_index("shard")
        self.near[s] = stage[0 : self.rows]
        for j in range(1, self.n_sh):
            self.copy_near(j, s, lax.rem(s + j, self.n_sh)).start()

    def middle(self):
        s, d = lax.axis_index("shard"), lax.axis_index("dp")
        for j in range(1, self.n_sh):
            self.copy_near(j, lax.rem(s + j, self.n_sh), s).wait_recv()
        for j in range(1, self.n_sh):
            self.copy_near(j, s, s).wait_send()
        part = self.near[0]
        for j in range(1, self.n_sh):
            part = part + self.near[j]
        self.far[d] = part

        def send(j, carry):
            self.copy_far(j, d, lax.rem(d + j, self.n_dp)).start()
            return carry

        lax.fori_loop(1, self.n_dp, send, 0)

    def finish(self):
        d = lax.axis_index("dp")

        def arrive(j, carry):
            self.copy_far(j, lax.rem(d + j, self.n_dp), d).wait_recv()
            self.copy_far(j, d, d).wait_send()
            return carry

        lax.fori_loop(1, self.n_dp, arrive, 0)
        part = self.far[0]
        for j in range(1, self.n_dp):
            part = part + self.far[j]
        self.total[0 : self.rows] = part


def sum_scratch(sizes, rows):
    n_dp, n_sh = sizes
    return [
        pltpu.VMEM((n_sh, rows, LANES), F32),
        pltpu.VMEM((n_dp, rows, LANES), F32),
        pltpu.SemaphoreType.DMA((n_sh,)),
        pltpu.SemaphoreType.DMA((n_sh,)),
        pltpu.SemaphoreType.DMA((n_dp,)),
        pltpu.SemaphoreType.DMA((n_dp,)),
    ]


def greet(sizes):
    n_dp, n_sh = sizes
    d, s = lax.axis_index("dp"), lax.axis_index("shard")
    gate = pltpu.get_barrier_semaphore()
    for j in range(1, n_sh):
        pl.semaphore_signal(gate, inc=1, device_id=(d, lax.rem(s + j, n_sh)), device_id_type=MESH)

    def signal(j, carry):
        pl.semaphore_signal(gate, inc=1, device_id=(lax.rem(d + j, n_dp), s), device_id_type=MESH)
        return carry

    lax.fori_loop(1, n_dp, signal, 0)
    pl.semaphore_wait(gate, n_sh + n_dp - 2)


def repeat(count, body, hook=None):
    def step(i, carry):
        if hook is not None:

            @pl.when(i == hook[0])
            def _():
                hook[1]()

        body(i)
        return carry

    lax.fori_loop(0, count, step, 0)


def lanes(c, width=LANES):
    return pl.ds(pl.multiple_of(c * width, width), width)


def coefs(total, row, count, gain, shift):
    mean = total[pl.ds(row, 1), :] / count
    square = total[pl.ds(row + 1, 1), :] / count
    scale = gain * lax.rsqrt(square - mean * mean + EPS_NORM)
    return scale, shift - mean * scale


def act_half(half):
    return half + half * jnp.tanh(half)


def forward_kernel(sizes, *refs):
    (images, mask, edge_l, edge_r, area, firstrow, wexp, headt, taps, squeeze, excite, gain_e, gain_c, gain_h, gain_s,
     pre_s, mixed_s, feat_s, out_s, low_s, pool_s, unit_s, gate_s, tot_e, tot_c, tot_h, pooled_h,
     pre, hid, out_t, low_t, scaled, pads, stages, totals, cnt, pool_t, gate_t) = refs[:38]
    rest = list(refs[38:])
    save_sems = rest.pop(0)
    sums = []
    for m in range(2):
        group = []
        for rows in (56, 48, 8, 40):
            near, far = rest[0], rest[1]
            group.append((near, far, rest[2:6], rows))
            rest = rest[6:]
        sums.append(group)

    greet(sizes)

    def low(m, layer):
        return low_s.at[layer] if m == 0 else low_t

    def out(m, layer):
        return out_s.at[layer] if m == 0 else out_t

    def total_ref(m, kind, layer):
        if m == 0:
            return (tot_e.at[layer, 0], tot_e.at[layer, 1], tot_c.at[layer], tot_h)[kind]
        return totals.at[kind]

    def summer(m, kind, layer):
        near, far, sems, rows = sums[m][kind]
        return Sum(near, far, total_ref(m, kind, layer), sems, sizes, rows)

    def save(src, dst, index):
        return pltpu.make_async_copy(src, dst, save_sems.at[index])

    for slot in range(SLOTS):
        pads[slot, 0:GAP, :] = jnp.zeros((GAP, LANES), F32)
        pads[slot, GAP + ROWS : 2 * GAP + ROWS, :] = jnp.zeros((GAP, LANES), F32)

    def load_rows(i):
        rows = pl.ds(pl.multiple_of(i * ROWS, ROWS), ROWS)
        for half in range(2):
            cols = slice(half * LANES, half * LANES + LANES)
            value = images[rows, cols].astype(F32) * mask[rows, :]
            hid[0, rows, cols] = value
            hid[1, rows, cols] = value
            low_s[0, rows, cols] = value.astype(BF16)
            low_t[rows, cols] = value.astype(BF16)

    repeat(SLOTS, load_rows)

    def update(m, layer):
        tot = total_ref(m, 2, layer)
        for half in range(2):
            cols = slice(half * LANES, half * LANES + LANES)
            for b in range(BATCHES):
                scale, shift = coefs(tot, 4 * half + 2 * b, cnt[b : b + 1, :], gain_c[m, layer, 0:1, cols], gain_c[m, layer, 1:2, cols])

                def one(i):
                    rows = pl.ds(pl.multiple_of(b * HALF + i * ROWS, ROWS), ROWS)
                    value = hid[m, rows, cols] + mask[rows, :] * (out(m, layer)[rows, cols] * scale + shift)
                    hid[m, rows, cols] = value
                    low(m, layer + 1)[rows, cols] = value.astype(BF16)

                repeat(IMGS, one)

    def put_sums(stage, chunk, b, value):
        stage[pl.ds(4 * chunk + 2 * b, 1), :] = jnp.sum(value, 0, keepdims=True)
        stage[pl.ds(4 * chunk + 2 * b + 1, 1), :] = jnp.sum(value * value, 0, keepdims=True)

    def expand(m, layer, hook=None):
        stage = stages.at[m]

        def body(c):
            weight = wexp[m, layer, :, lanes(c, 256)]
            for b in range(BATCHES):
                value = jnp.dot(low(m, layer)[b * HALF : (b + 1) * HALF, :], weight, preferred_element_type=F32)
                for half in range(2):
                    piece = value[:, half * LANES : (half + 1) * LANES]
                    pre[m, 2 * c + half, b * HALF : (b + 1) * HALF, :] = piece
                    put_sums(stage, 2 * c + half, b, piece)
            if m == 0:
                for half in range(2):
                    save(pre.at[0, 2 * c + half], pre_s.at[layer, 2 * c + half], 2 * c + half).start()

        repeat(E // 256, body, hook)

    def depthwise(m, layer, hook=None):
        stage = stages.at[m]
        tot = total_ref(m, 0, layer)

        def body(c):
            if m == 0:
                save(pre.at[0, c], pre_s.at[layer, c], c).wait()
            tap = [taps[m, layer, k : k + 1, lanes(c)] for k in range(9)]
            for b in range(BATCHES):
                scale, shift = coefs(tot, 4 * c + 2 * b, cnt[b : b + 1, :], gain_e[m, layer, 0:1, lanes(c)], gain_e[m, layer, 1:2, lanes(c)])
                scale, shift = 0.5 * scale, 0.5 * shift
                for i in range(IMGS):
                    slot = b * IMGS + i
                    rows = slice(slot * ROWS, (slot + 1) * ROWS)
                    half = mask[rows, :] * (pre[m, c, rows, :] * scale + shift)
                    pads[slot, GAP : GAP + ROWS, :] = act_half(half)
                first = jnp.zeros((8, LANES), F32)
                second = jnp.zeros((8, LANES), F32)
                for i in range(IMGS):
                    slot = b * IMGS + i
                    for t in range(ROWS // TILE):
                        start = GAP + t * TILE
                        near = [pads[slot, start + o : start + o + TILE, :] for o in OFFSETS]
                        left = near[0] * tap[0] + near[3] * tap[3] + near[6] * tap[6]
                        mid = near[1] * tap[1] + near[4] * tap[4] + near[7] * tap[7]
                        right = near[2] * tap[2] + near[5] * tap[5] + near[8] * tap[8]
                        rows = slice(slot * ROWS + t * TILE, slot * ROWS + (t + 1) * TILE)
                        value = mask[rows, :] * (mid + edge_l[0:TILE, :] * left + edge_r[0:TILE, :] * right)
                        pre[m, c, rows, :] = value
                        first = first + jnp.sum(value.reshape(TILE // 8, 8, LANES), 0)
                        second = second + jnp.sum((value * value).reshape(TILE // 8, 8, LANES), 0)
                stage[pl.ds(4 * c + 2 * b, 1), :] = jnp.sum(first, 0, keepdims=True)
                stage[pl.ds(4 * c + 2 * b + 1, 1), :] = jnp.sum(second, 0, keepdims=True)
            if m == 0:
                save(pre.at[0, c], mixed_s.at[layer, c], c).start()

        repeat(EC, body, hook)

    def pooling(m, layer, hook=None):
        tot = total_ref(m, 1, layer)
        pool = pool_s.at[layer] if m == 0 else pool_t

        def body(c):
            if m == 0:
                save(pre.at[0, c], mixed_s.at[layer, c], c).wait()
            for b in range(BATCHES):
                scale, shift = coefs(tot, 4 * c + 2 * b, cnt[b : b + 1, :], gain_e[m, layer, 2:3, lanes(c)], gain_e[m, layer, 3:4, lanes(c)])
                scale, shift = 0.5 * scale, 0.5 * shift
                for i in range(IMGS):
                    slot = b * IMGS + i
                    rows = slice(slot * ROWS, (slot + 1) * ROWS)
                    value = act_half(mask[rows, :] * (pre[m, c, rows, :] * scale + shift))
                    pre[m, c, rows, :] = value
                    pool[b * 8 + i : b * 8 + i + 1, lanes(c)] = jnp.sum(value, 0, keepdims=True) / area[0:1, :]

        repeat(EC, body, hook)

    def project(m, layer):
        pool = pool_s.at[layer] if m == 0 else pool_t
        gate = gate_s.at[layer] if m == 0 else gate_t
        units = matmul_bt(pool[...], squeeze[m, layer]) + gain_s[m, layer]
        if m == 0:
            unit_s[layer] = units
        gate[...] = jax.nn.sigmoid(matmul(jax.nn.silu(units), excite[m, layer]) + gain_e[m, layer, 4:5, :])

        def body(c):
            for b in range(BATCHES):
                for i in range(IMGS):
                    rows = slice(b * HALF + i * ROWS, b * HALF + (i + 1) * ROWS)
                    scaled[rows, lanes(c)] = (pre[m, c, rows, :] * gate[b * 8 + i : b * 8 + i + 1, lanes(c)]).astype(BF16)

        repeat(EC, body)
        stage = stages.at[m]
        for b in range(BATCHES):
            rows = slice(b * HALF, (b + 1) * HALF)
            value = contract(scaled[rows, :], wexp[m, layer, :, E : 2 * E], 1, 1)
            out(m, layer)[rows, :] = value
            for half in range(2):
                put_sums(stage, half, b, value[:, half * LANES : (half + 1) * LANES])

    def features(m, hook=None):
        stage = stages.at[m]

        def body(c):
            weight = headt[m, pl.ds(pl.multiple_of(c * 256, 256), 256), :]
            for b in range(BATCHES):
                value = contract(low(m, L)[b * HALF : (b + 1) * HALF, :], weight, 1, 1)
                for half in range(2):
                    piece = value[:, half * LANES : (half + 1) * LANES]
                    pre[m, 2 * c + half, b * HALF : (b + 1) * HALF, :] = piece
                    put_sums(stage, 2 * c + half, b, piece)
            if m == 0:
                for half in range(2):
                    save(pre.at[0, 2 * c + half], feat_s.at[2 * c + half], 2 * c + half).start()

        repeat(HEAD // 256, body, hook)

    def head_pool(m, hook=None):
        tot = total_ref(m, 3, 0)

        def body(c):
            for b in range(BATCHES):
                scale, shift = coefs(tot, 4 * c + 2 * b, cnt[b : b + 1, :], gain_h[m, 0:1, lanes(c)], gain_h[m, 1:2, lanes(c)])
                scale, shift = 0.5 * scale, 0.5 * shift
                for i in range(IMGS):
                    slot = b * IMGS + i
                    rows = slice(slot * ROWS, (slot + 1) * ROWS)
                    value = act_half(mask[rows, :] * (pre[m, c, rows, :] * scale + shift))
                    pooled_h[m, b * 8 + i : b * 8 + i + 1, lanes(c)] = jnp.sum(value, 0, keepdims=True) / area[0:1, :]

        repeat(HC, body, hook)

    for m in range(2):
        stages[m] = jnp.zeros((56, LANES), F32)
    pool_s[...] = jnp.zeros(pool_s.shape, F32)
    pool_t[...] = jnp.zeros(pool_t.shape, F32)
    pooled_h[...] = jnp.zeros(pooled_h.shape, F32)
    stages[0, 48:56, :] = firstrow[...]
    pending = None
    for layer in range(L):
        s_one, t_one = summer(0, 0, layer), summer(1, 0, layer)
        s_two, t_two = summer(0, 1, layer), summer(1, 1, layer)
        s_three, t_three = summer(0, 2, layer), summer(1, 2, layer)
        if layer > 0:
            update(0, layer - 1)
        expand(0, layer, None if pending is None else (2, pending.middle))
        s_one.start(stages.at[0])
        if layer > 0:
            pending.finish()
            update(1, layer - 1)
        expand(1, layer, (4, s_one.middle))
        t_one.start(stages.at[1])
        s_one.finish()
        if layer == 0:
            cnt[...] = tot_e[0, 0, 48:56, :]
        depthwise(0, layer, (2, t_one.middle))
        s_two.start(stages.at[0])
        t_one.finish()
        depthwise(1, layer, (5, s_two.middle))
        t_two.start(stages.at[1])
        s_two.finish()
        pooling(0, layer, (5, t_two.middle))
        project(0, layer)
        s_three.start(stages.at[0])
        t_two.finish()
        pooling(1, layer, (6, s_three.middle))
        project(1, layer)
        t_three.start(stages.at[1])
        s_three.finish()
        pending = t_three
    s_head, t_head = summer(0, 3, 0), summer(1, 3, 0)
    update(0, L - 1)
    features(0, (2, pending.middle))
    s_head.start(stages.at[0])
    pending.finish()
    update(1, L - 1)
    features(1, (4, s_head.middle))
    t_head.start(stages.at[1])
    s_head.finish()
    head_pool(0, (3, t_head.middle))
    t_head.finish()
    head_pool(1)
    for c in range(HC):
        save(pre.at[0, c], feat_s.at[c], c).wait()


def run_forward_all(sizes, inputs):
    sds = jax.ShapeDtypeStruct
    vm = pl.BlockSpec(memory_space=pltpu.VMEM)
    hbm = pl.BlockSpec(memory_space=pl.ANY)
    outs = [
        (sds((L, EC, FULL, LANES), F32), hbm),
        (sds((L, EC, FULL, LANES), F32), hbm),
        (sds((HC, FULL, LANES), F32), hbm),
        (sds((L, FULL, C), F32), vm),
        (sds((L + 1, FULL, C), BF16), vm),
        (sds((L, 16, E), F32), vm),
        (sds((L, 16, SE), F32), vm),
        (sds((L, 16, E), F32), vm),
        (sds((L, 2, 56, LANES), F32), vm),
        (sds((L, 8, LANES), F32), vm),
        (sds((40, LANES), F32), vm),
        (sds((2, 16, HEAD), F32), vm),
    ]
    scratch = [
        pltpu.VMEM((2, EC, FULL, LANES), F32),
        pltpu.VMEM((2, FULL, C), F32),
        pltpu.VMEM((FULL, C), F32),
        pltpu.VMEM((FULL, C), BF16),
        pltpu.VMEM((FULL, E), BF16),
        pltpu.VMEM((SLOTS, ROWS + 2 * GAP, LANES), F32),
        pltpu.VMEM((2, 56, LANES), F32),
        pltpu.VMEM((4, 56, LANES), F32),
        pltpu.VMEM((8, LANES), F32),
        pltpu.VMEM((16, E), F32),
        pltpu.VMEM((16, E), F32),
        pltpu.SemaphoreType.DMA((EC,)),
    ]
    for m in range(2):
        for rows in (56, 48, 8, 40):
            scratch = scratch + sum_scratch(sizes, rows)
    return pl.pallas_call(
        functools.partial(forward_kernel, sizes),
        out_shape=[o[0] for o in outs],
        in_specs=[vm] * len(inputs),
        out_specs=[o[1] for o in outs],
        scratch_shapes=scratch,
        compiler_params=pltpu.CompilerParams(collective_id=1, has_side_effects=True, vmem_limit_bytes=63 * 2**20),
        name="forward",
    )(*inputs)


def backward_kernel(sizes, *refs):
    (dpool_h, mask, edge_l, edge_r, area, wexp, headt, taps, squeeze, excite, gain_e, gain_c, gain_h,
     pre_s, mixed_s, feat_s, out_s, low_s, pool_s, unit_s, gate_s, tot_e, tot_c, tot_h,
     g_exp, g_taps, g_sq, g_ex, g_exb, g_sqb, g_head, back_e, back_c, back_h,
     pre, mixed, grad, grad_hid, low_out, low_pre, pads_x, pads_g, slope, dgate, dpool, stages, load_sems) = refs[:47]
    rest = list(refs[47:])
    sums = []
    for b in range(BATCHES):
        group = []
        for rows in (24, 24, 8, 24):
            group.append((rest[0], rest[1], rest[2:6], rows))
            rest = rest[6:]
        sums.append(group)

    greet(sizes)

    def back_ref(b, kind, layer):
        return (back_e.at[layer, b, 0], back_e.at[layer, b, 1], back_c.at[layer, b], back_h.at[b])[kind]

    def summer(b, kind, layer):
        near, far, sems, rows = sums[b][kind]
        return Sum(near, far, back_ref(b, kind, layer), sems, sizes, rows)

    def load(b, kind, layer):
        rows = slice(b * HALF, (b + 1) * HALF)
        if kind == 0:
            return pltpu.make_async_copy(pre_s.at[layer, :, rows], pre.at[b], load_sems.at[b, 0])
        if kind == 1:
            return pltpu.make_async_copy(mixed_s.at[layer, :, rows], mixed.at[b], load_sems.at[b, 1])
        return pltpu.make_async_copy(feat_s.at[:, rows], pre.at[b, 0:HC], load_sems.at[b, 0])

    for b in range(BATCHES):
        load(b, 2, 0).start()
    for b in range(BATCHES):
        load(b, 1, L - 1).start()
    for slot in range(IMGS):
        for pads in (pads_x, pads_g):
            pads[slot, 0:GAP, :] = jnp.zeros((GAP, LANES), F32)
            pads[slot, GAP + ROWS : 2 * GAP + ROWS, :] = jnp.zeros((GAP, LANES), F32)
    dgate[...] = jnp.zeros(dgate.shape, F32)
    stages[...] = jnp.zeros(stages.shape, F32)

    def forward_total(kind, layer):
        return (tot_e.at[layer, 0], tot_e.at[layer, 1], tot_c.at[layer], tot_h)[kind]

    def moments(b, kind, layer, c):
        tot = forward_total(kind, layer)
        count = tot_e[0, 0, 48 + b : 49 + b, :]
        mean = tot[pl.ds(4 * c + 2 * b, 1), :] / count
        square = tot[pl.ds(4 * c + 2 * b + 1, 1), :] / count
        return mean, lax.rsqrt(square - mean * mean + EPS_NORM)

    def half_coefs(b, kind, layer, c, gain, shift):
        mean, scale = moments(b, kind, layer, c)
        scale = scale * gain
        return 0.5 * scale, 0.5 * (shift - mean * scale)

    def back_coefs(b, kind, layer, c, gain):
        mean, scale = moments(b, kind, layer, c)
        count = tot_e[0, 0, 48 + b : 49 + b, :]
        back = back_ref(b, kind, layer)
        plain = back[pl.ds(2 * c, 1), :]
        cross = scale * (back[pl.ds(2 * c + 1, 1), :] - mean * plain)
        first = scale * gain
        third = -first * scale * cross / count
        return first, -first * plain / count - mean * third, third

    def fold(value):
        return jnp.sum(value.reshape(value.shape[0] // 8, 8, LANES), 0)

    def put(stage, c, first, second):
        stage[pl.ds(2 * c, 1), :] = jnp.sum(first, 0, keepdims=True)
        stage[pl.ds(2 * c + 1, 1), :] = jnp.sum(second, 0, keepdims=True)

    def image(b, i):
        return slice(i * ROWS, (i + 1) * ROWS), slice(b * HALF + i * ROWS, b * HALF + (i + 1) * ROWS)

    def bend(half):
        t = jnp.tanh(half)
        return half + half * t, (0.5 + 0.5 * t) * (1.0 + half * (1.0 - t))

    def head_first(b, hook=None):
        stage = stages.at[b]

        def body(c):
            scale, shift = half_coefs(b, 3, 0, c, gain_h[0:1, lanes(c)], gain_h[1:2, lanes(c)])
            first = jnp.zeros((8, LANES), F32)
            second = jnp.zeros((8, LANES), F32)
            for i in range(IMGS):
                rows, full = image(b, i)
                x = pre[b, c, rows, :]
                half = mask[full, :] * (x * scale + shift)
                value = mask[full, :] * dpool_h[b * 8 + i : b * 8 + i + 1, lanes(c)] * bend(half)[1]
                grad[b, c, rows, :] = value
                first = first + fold(value)
                second = second + fold(value * x)
            put(stage, c, first, second)

        repeat(HC, body, hook)

    def norm_back_rows(b, kind, layer, c, gain, source):
        one, two, three = back_coefs(b, kind, layer, c, gain)
        for i in range(IMGS):
            rows, full = image(b, i)
            value = mask[full, :] * (one * grad[b, c, rows, :] + two + three * source[b, c, rows, :])
            low_pre[rows, lanes(c)] = value.astype(BF16)

    def put_hidden_sums(b, layer):
        stage = stages.at[b]
        for half in range(2):
            cols = slice(half * LANES, (half + 1) * LANES)
            first = jnp.zeros((8, LANES), F32)
            second = jnp.zeros((8, LANES), F32)
            for i in range(IMGS):
                full = image(b, i)[1]
                value = grad_hid[full, cols]
                first = first + fold(value)
                second = second + fold(value * out_s[layer, full, cols])
            put(stage, half, first, second)

    def add(ref, index, value, b):
        if b == 0:
            ref[index] = value
        else:
            ref[index] = ref[index] + value

    def head_second(b, hook=None):
        mine = slice(b * HALF, (b + 1) * HALF)

        def body(c):
            for half in range(2):
                norm_back_rows(b, 3, 0, 2 * c + half, gain_h[0:1, lanes(2 * c + half)], pre)
            rows = pl.ds(pl.multiple_of(c * 256, 256), 256)
            add(g_head, (rows, slice(None)), contract(low_pre[:, lanes(c, 256)], low_s[L, mine, :], 0, 0), b)

        repeat(HEAD // 256, body, hook)
        grad_hid[mine, :] = jnp.dot(low_pre[:, 0:HEAD], headt[...], preferred_element_type=F32)
        put_hidden_sums(b, L - 1)

    def block_gate(b, layer, hook=None):
        mine = slice(b * HALF, (b + 1) * HALF)
        eight = slice(b * 8, b * 8 + 8)
        for half in range(2):
            cols = slice(half * LANES, (half + 1) * LANES)
            one, two, three = back_coefs(b, 2, layer, half, gain_c[layer, 0:1, cols])
            for i in range(IMGS):
                rows, full = image(b, i)
                low_out[rows, cols] = (mask[full, :] * (one * grad_hid[full, cols] + two + three * out_s[layer, full, cols])).astype(BF16)

        def body(c):
            value = jnp.dot(low_out[...], wexp[layer, :, lanes(E // 256 + c, 256)], preferred_element_type=F32)
            for part in range(2):
                k = 2 * c + part
                scale, shift = half_coefs(b, 1, layer, k, gain_e[layer, 2:3, lanes(k)], gain_e[layer, 3:4, lanes(k)])
                for i in range(IMGS):
                    rows, full = image(b, i)
                    act = act_half(mask[full, :] * (mixed[b, k, rows, :] * scale + shift))
                    piece = value[rows, part * LANES : (part + 1) * LANES]
                    grad[b, k, rows, :] = piece
                    dgate[i : i + 1, lanes(k)] = jnp.sum(fold(piece * act), 0, keepdims=True)
                    low_pre[rows, lanes(k)] = (act * gate_s[layer, b * 8 + i : b * 8 + i + 1, lanes(k)]).astype(BF16)
            add(g_exp, (layer, slice(None), lanes(E // 256 + c, 256)), contract(low_out[...], low_pre[:, lanes(c, 256)], 0, 0), b)

        repeat(E // 256, body, hook)
        gate = gate_s[layer, eight, :]
        units = unit_s[layer, eight, :]
        sig = jax.nn.sigmoid(units)
        inner = dgate[...] * gate * (1.0 - gate)
        add(g_exb, layer, jnp.broadcast_to(jnp.sum(inner, 0, keepdims=True), (8, E)), b)
        add(g_ex, layer, matmul_tb(units * sig, inner), b)
        outer = matmul_bt(inner, excite[layer]) * (sig * (1.0 + units * (1.0 - sig)))
        add(g_sqb, layer, jnp.broadcast_to(jnp.sum(outer, 0, keepdims=True), (8, SE)), b)
        add(g_sq, layer, matmul_tb(outer, pool_s[layer, eight, :]), b)
        dpool[...] = matmul(outer, squeeze[layer])

    def block_second(b, layer, hook=None):
        stage = stages.at[b]

        def body(c):
            scale, shift = half_coefs(b, 1, layer, c, gain_e[layer, 2:3, lanes(c)], gain_e[layer, 3:4, lanes(c)])
            first = jnp.zeros((8, LANES), F32)
            second = jnp.zeros((8, LANES), F32)
            for i in range(IMGS):
                rows, full = image(b, i)
                x = mixed[b, c, rows, :]
                half = mask[full, :] * (x * scale + shift)
                gate = gate_s[layer, b * 8 + i : b * 8 + i + 1, lanes(c)]
                value = mask[full, :] * (grad[b, c, rows, :] * gate + dpool[i : i + 1, lanes(c)] / area[0:1, :]) * bend(half)[1]
                grad[b, c, rows, :] = value
                first = first + fold(value)
                second = second + fold(value * x)
            put(stage, c, first, second)

        repeat(EC, body, hook)

    def block_spread(b, layer, hook=None):
        stage = stages.at[b]

        def body(c):
            scale, shift = half_coefs(b, 0, layer, c, gain_e[layer, 0:1, lanes(c)], gain_e[layer, 1:2, lanes(c)])
            one, two, three = back_coefs(b, 1, layer, c, gain_e[layer, 2:3, lanes(c)])
            tap = [taps[layer, k : k + 1, lanes(c)] for k in range(9)]
            for i in range(IMGS):
                rows, full = image(b, i)
                act, der = bend(mask[full, :] * (pre[b, c, rows, :] * scale + shift))
                pads_x[i, GAP : GAP + ROWS, :] = act
                slope[rows, :] = mask[full, :] * der
                pads_g[i, GAP : GAP + ROWS, :] = mask[full, :] * (one * grad[b, c, rows, :] + two + three * mixed[b, c, rows, :])
            first = jnp.zeros((8, LANES), F32)
            second = jnp.zeros((8, LANES), F32)
            total = [jnp.zeros((8, LANES), F32) for k in range(9)]
            for i in range(IMGS):
                for t in range(ROWS // TILE_BACK):
                    start = GAP + t * TILE_BACK
                    rows = slice(i * ROWS + t * TILE_BACK, i * ROWS + (t + 1) * TILE_BACK)
                    g = [pads_g[i, start - o : start - o + TILE_BACK, :] for o in OFFSETS]
                    left, right = edge_l[0:TILE_BACK, :], edge_r[0:TILE_BACK, :]
                    wide = (g[1] * tap[1] + g[4] * tap[4] + g[7] * tap[7]
                            + right * (g[0] * tap[0] + g[3] * tap[3] + g[6] * tap[6])
                            + left * (g[2] * tap[2] + g[5] * tap[5] + g[8] * tap[8]))
                    value = wide * slope[rows, :]
                    grad[b, c, rows, :] = value
                    first = first + fold(value)
                    second = second + fold(value * pre[b, c, rows, :])
                    center = g[4]
                    sides = (center * left, center, center * right)
                    for k in range(9):
                        o = OFFSETS[k]
                        total[k] = total[k] + fold(sides[k % 3] * pads_x[i, start + o : start + o + TILE_BACK, :])
            put(stage, c, first, second)
            for k in range(9):
                add(g_taps, (layer, slice(k, k + 1), lanes(c)), jnp.sum(total[k], 0, keepdims=True), b)

        repeat(EC, body, hook)

    def block_expand(b, layer, hook=None):
        mine = slice(b * HALF, (b + 1) * HALF)

        def body(c):
            for part in range(2):
                norm_back_rows(b, 0, layer, 2 * c + part, gain_e[layer, 0:1, lanes(2 * c + part)], pre)
            add(g_exp, (layer, slice(None), lanes(c, 256)), contract(low_s[layer, mine, :], low_pre[:, lanes(c, 256)], 0, 0), b)

        repeat(E // 256, body, hook)
        if layer > 0:
            grad_hid[mine, :] = grad_hid[mine, :] + contract(low_pre[...], wexp[layer, :, 0:E], 1, 1)
            put_hidden_sums(b, layer - 1)

    heads = [summer(b, 3, 0) for b in range(BATCHES)]
    load(0, 2, 0).wait()
    head_first(0)
    heads[0].start(stages.at[0])
    load(1, 2, 0).wait()
    head_first(1, (5, heads[0].middle))
    heads[1].start(stages.at[1])
    thirds = [summer(b, 2, L - 1) for b in range(BATCHES)]
    heads[0].finish()
    head_second(0, (2, heads[1].middle))
    load(0, 0, L - 1).start()
    thirds[0].start(stages.at[0])
    heads[1].finish()
    head_second(1, (3, thirds[0].middle))
    load(1, 0, L - 1).start()
    thirds[1].start(stages.at[1])
    for layer in reversed(range(L)):
        twos = [summer(b, 1, layer) for b in range(BATCHES)]
        ones = [summer(b, 0, layer) for b in range(BATCHES)]
        thirds[0].finish()
        load(0, 1, layer).wait()
        block_gate(0, layer, (3, thirds[1].middle))
        block_second(0, layer)
        twos[0].start(stages.at[0])
        thirds[1].finish()
        load(1, 1, layer).wait()
        block_gate(1, layer, (3, twos[0].middle))
        block_second(1, layer)
        twos[1].start(stages.at[1])
        twos[0].finish()
        load(0, 0, layer).wait()
        block_spread(0, layer, (4, twos[1].middle))
        if layer > 0:
            load(0, 1, layer - 1).start()
        ones[0].start(stages.at[0])
        twos[1].finish()
        load(1, 0, layer).wait()
        block_spread(1, layer, (4, ones[0].middle))
        if layer > 0:
            load(1, 1, layer - 1).start()
        ones[1].start(stages.at[1])
        ones[0].finish()
        block_expand(0, layer, (3, ones[1].middle))
        if layer > 0:
            load(0, 0, layer - 1).start()
            thirds = [summer(b, 2, layer - 1) for b in range(BATCHES)]
            thirds[0].start(stages.at[0])
        ones[1].finish()
        block_expand(1, layer, None if layer == 0 else (3, thirds[0].middle))
        if layer > 0:
            load(1, 0, layer - 1).start()
            thirds[1].start(stages.at[1])


def run_backward_all(sizes, inputs):
    sds = jax.ShapeDtypeStruct
    vm = pl.BlockSpec(memory_space=pltpu.VMEM)
    hbm = pl.BlockSpec(memory_space=pl.ANY)
    outs = [
        sds((L, C, 2 * E), F32),
        sds((L, 9, E), F32),
        sds((L, SE, E), F32),
        sds((L, SE, E), F32),
        sds((L, 8, E), F32),
        sds((L, 8, SE), F32),
        sds((HEAD, C), F32),
        sds((L, BATCHES, 2, 24, LANES), F32),
        sds((L, BATCHES, 8, LANES), F32),
        sds((BATCHES, 24, LANES), F32),
    ]
    scratch = [
        pltpu.VMEM((BATCHES, EC, HALF, LANES), F32),
        pltpu.VMEM((BATCHES, EC, HALF, LANES), F32),
        pltpu.VMEM((BATCHES, EC, HALF, LANES), F32),
        pltpu.VMEM((FULL, C), F32),
        pltpu.VMEM((HALF, C), BF16),
        pltpu.VMEM((HALF, E), BF16),
        pltpu.VMEM((IMGS, ROWS + 2 * GAP, LANES), F32),
        pltpu.VMEM((IMGS, ROWS + 2 * GAP, LANES), F32),
        pltpu.VMEM((HALF, LANES), F32),
        pltpu.VMEM((8, E), F32),
        pltpu.VMEM((8, E), F32),
        pltpu.VMEM((BATCHES, 24, LANES), F32),
        pltpu.SemaphoreType.DMA((BATCHES, 2)),
    ]
    for b in range(BATCHES):
        for rows in (24, 24, 8, 24):
            scratch = scratch + sum_scratch(sizes, rows)
    specs = [vm] * 13 + [hbm] * 3 + [vm] * 8
    return pl.pallas_call(
        functools.partial(backward_kernel, sizes),
        out_shape=outs,
        in_specs=specs,
        out_specs=[vm] * len(outs),
        scratch_shapes=scratch,
        compiler_params=pltpu.CompilerParams(collective_id=2, has_side_effects=True, vmem_limit_bytes=63 * 2**20),
        name="backward",
    )(*inputs)


def objective(logits, target, onehot, coef):
    logp = jax.nn.log_softmax(logits)
    per = -jnp.sum(onehot * logp, 1) + jnp.sum(jnp.exp(target) * (target - logp), 1)
    return jnp.sum(coef * per)


def own_slice(value, dim, parts, place):
    width = value.shape[dim] // parts
    return lax.dynamic_slice_in_dim(value, place * width, width, dim)


def mats_groups(value):
    rows = jnp.sum(value * value, 1)
    half = rows.shape[1] // 2
    return jnp.stack([jnp.sum(rows[:, :half], 1), jnp.sum(rows[:, half:], 1)], 1).reshape(-1)


def chan_groups(value):
    rows = jnp.sum(value * value, 2)
    return jnp.stack(
        [jnp.sum(rows[:, :9], 1), jnp.sum(rows[:, 9 : 9 + SE], 1), jnp.sum(rows[:, 9 + SE :], 1)], 1
    ).reshape(-1)


def mats_factor(ratio, value):
    paired = ratio.reshape(-1, 2)
    column = jnp.arange(value.shape[2])
    return jnp.where(column[None, :] < value.shape[2] // 2, paired[:, 0:1], paired[:, 1:2])[
        :, None, :
    ]


def chan_factor(ratio, value):
    triple = ratio.reshape(-1, 3)
    row = jnp.arange(value.shape[1])[None, :]
    return jnp.where(
        row < 9, triple[:, 0:1], jnp.where(row < 9 + SE, triple[:, 1:2], triple[:, 2:3])
    )[:, :, None]


def adapt(first, second, grad, first_fix, second_fix):
    new_first = BETA_ONE * first + (1.0 - BETA_ONE) * grad
    new_second = BETA_TWO * second + (1.0 - BETA_TWO) * grad * grad
    update = new_first / first_fix / (jnp.sqrt(new_second / second_fix) + EPS_ADAM)
    return (new_first, new_second, update)


def per_device(
    images,
    bucket,
    counts,
    balance,
    labels,
    step,
    expand_w,
    expand_m,
    expand_v,
    expand_e,
    chan_w,
    chan_m,
    chan_v,
    chan_e,
    head_w,
    head_m,
    head_v,
    head_e,
    class_w,
    class_m,
    class_v,
    class_e,
    gain_w,
    gain_m,
    gain_v,
    gain_e,
):
    sizes = (lax.axis_size("dp"), lax.axis_size("shard"))
    n_sh = sizes[1]
    weights = (expand_w, chan_w, head_w, class_w, gain_w)
    firsts = (expand_m, chan_m, head_m, class_m, gain_m)
    seconds = (expand_v, chan_v, head_v, class_v, gain_v)
    averaged = (expand_e, chan_e, head_e, class_e, gain_e)
    axes = (1, 2, 1, 0, 0)
    both = [
        jnp.stack(
            [
                lax.all_gather(item.astype(BF16), "shard", axis=axes[k], tiled=True)
                for item in (weights[k], averaged[k])
            ]
        )
        for k in range(5)
    ]
    code = bucket[0]
    side = jnp.where(code == 0, 7, jnp.where(code == 1, 10, 12))
    spot = jnp.arange(S * S)
    inside = ((spot // S < side) & (spot % S < side)).astype(F32)
    area_value = (side * side).astype(F32)
    valid = (jnp.arange(IMGS)[None, :] < counts).astype(F32)
    weighted = valid * balance.astype(F32)
    mask_all = jnp.broadcast_to(
        (valid[:, :, None] * inside[None, None, :]).reshape(FULL, 1), (FULL, LANES)
    )
    spread_l = jnp.broadcast_to((spot % S > 0).astype(F32)[:, None], (ROWS, LANES))
    spread_r = jnp.broadcast_to((spot % S < S - 1).astype(F32)[:, None], (ROWS, LANES))
    own = jnp.concatenate(
        [jnp.sum(valid, 1) * area_value, jnp.sum(weighted, 1), jnp.zeros((4,), F32)]
    )
    area = jnp.full((1, LANES), area_value)
    chan_f = both[1].astype(F32)
    gains_f = both[4].astype(F32)
    block_width = gains_f.shape[2] - 2 * (HEAD // n_sh) - CLASSES // n_sh
    blocks = gains_f[:, :, :block_width].reshape(2, n_sh, L, -1)
    wide = 5 * E // n_sh
    vec_e = (
        blocks[..., :wide].reshape(2, n_sh, L, 5, E // n_sh).transpose(0, 2, 3, 1, 4)
    ).reshape(2, L, 5, E)
    vec_c = (
        blocks[..., wide : wide + 2 * C // n_sh]
        .reshape(2, n_sh, L, 2, C // n_sh)
        .transpose(0, 2, 3, 1, 4)
    ).reshape(2, L, 2, C)
    vec_s = blocks[..., wide + 2 * C // n_sh :].transpose(0, 2, 1, 3).reshape(2, L, 1, SE)
    heads_f = gains_f[:, :, block_width : block_width + 2 * HEAD // n_sh]
    vec_h = heads_f.reshape(2, n_sh, 2, HEAD // n_sh).transpose(0, 2, 1, 3).reshape(2, 2, HEAD)
    class_bias = gains_f[:, :, block_width + 2 * HEAD // n_sh :].reshape(2, CLASSES)
    headt = both[2].transpose(0, 2, 1)
    taps, squeeze, excite = chan_f[:, :, :9], chan_f[:, :, 9 : 9 + SE], chan_f[:, :, 9 + SE :]
    saved = run_forward_all(
        sizes,
        [
            images.reshape(FULL, C), mask_all, spread_l, spread_r, area,
            jnp.broadcast_to(own[:, None], (8, LANES)), both[0], headt,
            taps, squeeze, excite, vec_e, vec_c, vec_h, vec_s,
        ],
    )
    pooled_h, kept = saved[11], saved[:11]
    tot_e, tot_c, tot_h = kept[8:11]
    total_weight = tot_e[0, 0, 50, 0] + tot_e[0, 0, 51, 0]
    pooled_low = pooled_h.reshape(2, BATCHES, 8, HEAD)[:, :, :IMGS].reshape(2, SLOTS, HEAD).astype(BF16)
    logits = [
        jnp.dot(pooled_low[m], both[3][m], preferred_element_type=F32) + class_bias[m]
        for m in range(2)
    ]
    onehot = (labels.reshape(SLOTS, 1) == jnp.arange(CLASSES)[None, :]).astype(F32)
    coef = weighted.reshape(SLOTS) / total_weight
    target = jax.nn.log_softmax(logits[1])
    loss, pull = jax.vjp(lambda value: objective(value, target, onehot, coef), logits[0])
    grad_low = pull(jnp.float32(1.0))[0].astype(BF16)
    grad_class = contract(pooled_low[0], grad_low, 0, 0)
    grad_class_bias = jnp.sum(grad_low.astype(F32), 0)
    grad_pooled = contract(grad_low, both[3][0], 1, 1) / area_value
    dpool_h = jnp.pad(grad_pooled.reshape(BATCHES, IMGS, HEAD), ((0, 0), (0, 3), (0, 0))).reshape(16, HEAD)
    (g_exp, g_taps, g_sq, g_ex, g_exb, g_sqb, g_head, back_e, back_c, back_h) = run_backward_all(
        sizes,
        [
            dpool_h, mask_all, spread_l, spread_r, area, both[0][0], headt[0],
            taps[0], squeeze[0], excite[0], vec_e[0], vec_c[0], vec_h[0], *kept,
        ],
    )
    g_chan = jnp.concatenate([g_taps, g_sq, g_ex], 1)
    summed = lax.psum(
        (loss, g_exp, g_chan, g_head, grad_class, g_exb[:, 0], g_sqb[:, 0], grad_class_bias),
        ("dp", "shard"),
    )
    place = lax.axis_index("shard")

    def norm_grads(tot, back, chunks):
        count = tot_e[0, 0, 48 : 48 + BATCHES, :1]
        forth = tot[: 4 * chunks].reshape(chunks, BATCHES, 2, LANES).transpose(1, 2, 0, 3).reshape(BATCHES, 2, -1)
        mean = forth[:, 0] / count
        scale = lax.rsqrt(forth[:, 1] / count - mean * mean + EPS_NORM)
        pairs = back[:, : 2 * chunks].reshape(BATCHES, chunks, 2, LANES).transpose(0, 2, 1, 3).reshape(BATCHES, 2, -1)
        cross = scale * (pairs[:, 1] - mean * pairs[:, 0])
        return [jnp.sum(cross, 0), jnp.sum(pairs[:, 0], 0)]

    vectors = []
    for layer in range(L):
        vectors = vectors + norm_grads(tot_e[layer, 0], back_e[layer, :, 0], EC)
        vectors = vectors + norm_grads(tot_e[layer, 1], back_e[layer, :, 1], EC)
        vectors = vectors + [summed[5][layer]]
        vectors = vectors + norm_grads(tot_c[layer], back_c[layer], 2)
        vectors = vectors + [summed[6][layer]]
    vectors = vectors + norm_grads(tot_h, back_h, HC) + [summed[7]]
    owned = (
        own_slice(summed[1], 1, n_sh, place),
        own_slice(summed[2], 2, n_sh, place),
        own_slice(summed[3], 0, n_sh, place).T,
        own_slice(summed[4], 0, n_sh, place),
        own_slice(pack_gains(vectors, n_sh), 0, n_sh, place),
    )
    total_loss = summed[0]
    power = step[0].astype(F32)
    first_fix = 1.0 - jnp.power(jnp.float32(BETA_ONE), power)
    second_fix = 1.0 - jnp.power(jnp.float32(BETA_TWO), power)
    states = [
        adapt(firsts[item], seconds[item], owned[item], first_fix, second_fix) for item in range(5)
    ]
    updates = [states[item][2] + DECAY * weights[item] for item in range(4)]
    local_weight_sq = jnp.concatenate(
        [
            mats_groups(expand_w),
            chan_groups(chan_w),
            jnp.sum(head_w * head_w)[None],
            jnp.sum(class_w * class_w)[None],
        ]
    )
    local_update_sq = jnp.concatenate(
        [
            mats_groups(updates[0]),
            chan_groups(updates[1]),
            jnp.sum(updates[2] * updates[2])[None],
            jnp.sum(updates[3] * updates[3])[None],
        ]
    )
    weight_sq, update_sq = lax.psum((local_weight_sq, local_update_sq), "shard")
    ratio = jnp.sqrt(weight_sq) / jnp.sqrt(update_sq)
    count_mats = 2 * L
    count_chan = 3 * L
    factors = [
        mats_factor(ratio[:count_mats], expand_w),
        chan_factor(ratio[count_mats : count_mats + count_chan], chan_w),
        ratio[count_mats + count_chan],
        ratio[count_mats + count_chan + 1],
    ]
    result = [total_loss]
    for item in range(5):
        if item < 4:
            fresh = weights[item] - RATE * factors[item] * updates[item]
        else:
            fresh = weights[item] - RATE * states[item][2]
        result = result + [
            fresh,
            states[item][0],
            states[item][1],
            KEEP * averaged[item] + (1.0 - KEEP) * fresh,
        ]
    norms = jnp.stack([jnp.sqrt(weight_sq), jnp.sqrt(update_sq)])
    return tuple(result + [norms])


def solution(mesh):
    in_specs = (
        P(None, ("dp", "shard"), None, None, None),
        P("dp"),
        P(None, ("dp", "shard")),
        P(None, ("dp", "shard")),
        P(None, ("dp", "shard")),
        P(),
        P(None, "shard", None),
        P(None, "shard", None),
        P(None, "shard", None),
        P(None, "shard", None),
        P(None, None, "shard"),
        P(None, None, "shard"),
        P(None, None, "shard"),
        P(None, None, "shard"),
        P(None, "shard"),
        P(None, "shard"),
        P(None, "shard"),
        P(None, "shard"),
        P("shard", None),
        P("shard", None),
        P("shard", None),
        P("shard", None),
        P("shard", None),
        P("shard", None),
        P("shard", None),
        P("shard", None),
    )
    out_specs = (
        P(),
        P(None, "shard", None),
        P(None, "shard", None),
        P(None, "shard", None),
        P(None, "shard", None),
        P(None, None, "shard"),
        P(None, None, "shard"),
        P(None, None, "shard"),
        P(None, None, "shard"),
        P(None, "shard"),
        P(None, "shard"),
        P(None, "shard"),
        P(None, "shard"),
        P("shard", None),
        P("shard", None),
        P("shard", None),
        P("shard", None),
        P("shard", None),
        P("shard", None),
        P("shard", None),
        P("shard", None),
        P(),
    )
    return jax.shard_map(
        per_device, mesh=mesh, in_specs=in_specs, out_specs=out_specs, check_vma=False
    )
```

```python
import functools

import jax
import jax.numpy as jnp
from jax import lax
from jax.experimental import pallas as pl
from jax.experimental.pallas import tpu as pltpu
from jax.sharding import PartitionSpec as P

C = 256
E = 1536
SE = 64
HEAD = 1280
CLASSES = 1000
L = 2
S = 12


EPS_NORM = 1e-05
BETA_ONE = 0.9
BETA_TWO = 0.99
EPS_ADAM = 1e-08
DECAY = 0.01
RATE = 0.3
KEEP = 0.9


def contract(left, right, left_dim, right_dim):
    return lax.dot_general(
        left, right, (((left_dim,), (right_dim,)), ((), ())), preferred_element_type=jnp.float32
    )


def matmul(left, right):
    return jnp.dot(left, right, precision=lax.Precision.HIGHEST, preferred_element_type=jnp.float32)


def matmul_bt(left, right):
    return lax.dot_general(
        left,
        right,
        (((1,), (1,)), ((), ())),
        precision=lax.Precision.HIGHEST,
        preferred_element_type=jnp.float32,
    )


def matmul_tb(left, right):
    return lax.dot_general(
        left,
        right,
        (((0,), (0,)), ((), ())),
        precision=lax.Precision.HIGHEST,
        preferred_element_type=jnp.float32,
    )


def pack_gains(vectors, rows):
    return jnp.concatenate([vector.reshape(rows, -1) for vector in vectors], 1)


IMGS = 5
ROWS = S * S
BATCHES = 2
HALF = IMGS * ROWS
FULL = BATCHES * HALF
SLOTS = BATCHES * IMGS
LANES = 128
EC = E // LANES
HC = HEAD // LANES
GAP = 16
TILE = 48
TILE_BACK = 48
OFFSETS = [S * (a - 1) + (c - 1) for a in range(3) for c in range(3)]
MESH = pl.DeviceIdType.MESH
F32 = jnp.float32
BF16 = jnp.bfloat16


class Sum:
    def __init__(self, near, far, total, sems, sizes, rows):
        self.near, self.far, self.total = near, far, total
        self.sems = sems
        self.n_dp, self.n_sh = sizes
        self.rows = rows

    def copy_near(self, step, slot, target):
        d = lax.axis_index("dp")
        return pltpu.make_async_remote_copy(
            self.near.at[slot], self.near.at[slot],
            self.sems[0].at[step], self.sems[1].at[slot],
            device_id=(d, target), device_id_type=MESH)

    def copy_far(self, step, slot, target):
        s = lax.axis_index("shard")
        return pltpu.make_async_remote_copy(
            self.far.at[slot], self.far.at[slot],
            self.sems[2].at[step], self.sems[3].at[slot],
            device_id=(target, s), device_id_type=MESH)

    def start(self, stage):
        s = lax.axis_index("shard")
        self.near[s] = stage[0 : self.rows]
        for j in range(1, self.n_sh):
            self.copy_near(j, s, lax.rem(s + j, self.n_sh)).start()

    def middle(self):
        s, d = lax.axis_index("shard"), lax.axis_index("dp")
        for j in range(1, self.n_sh):
            self.copy_near(j, lax.rem(s + j, self.n_sh), s).wait_recv()
        for j in range(1, self.n_sh):
            self.copy_near(j, s, s).wait_send()
        part = self.near[0]
        for j in range(1, self.n_sh):
            part = part + self.near[j]
        self.far[d] = part

        def send(j, carry):
            self.copy_far(j, d, lax.rem(d + j, self.n_dp)).start()
            return carry

        lax.fori_loop(1, self.n_dp, send, 0)

    def finish(self):
        d = lax.axis_index("dp")

        def arrive(j, carry):
            self.copy_far(j, lax.rem(d + j, self.n_dp), d).wait_recv()
            self.copy_far(j, d, d).wait_send()
            return carry

        lax.fori_loop(1, self.n_dp, arrive, 0)
        part = self.far[0]
        for j in range(1, self.n_dp):
            part = part + self.far[j]
        self.total[0 : self.rows] = part


def sum_scratch(sizes, rows):
    n_dp, n_sh = sizes
    return [
        pltpu.VMEM((n_sh, rows, LANES), F32),
        pltpu.VMEM((n_dp, rows, LANES), F32),
        pltpu.SemaphoreType.DMA((n_sh,)),
        pltpu.SemaphoreType.DMA((n_sh,)),
        pltpu.SemaphoreType.DMA((n_dp,)),
        pltpu.SemaphoreType.DMA((n_dp,)),
    ]


def greet(sizes):
    n_dp, n_sh = sizes
    d, s = lax.axis_index("dp"), lax.axis_index("shard")
    gate = pltpu.get_barrier_semaphore()
    for j in range(1, n_sh):
        pl.semaphore_signal(gate, inc=1, device_id=(d, lax.rem(s + j, n_sh)), device_id_type=MESH)

    def signal(j, carry):
        pl.semaphore_signal(gate, inc=1, device_id=(lax.rem(d + j, n_dp), s), device_id_type=MESH)
        return carry

    lax.fori_loop(1, n_dp, signal, 0)
    pl.semaphore_wait(gate, n_sh + n_dp - 2)


def repeat(count, body, hook=None):
    def step(i, carry):
        if hook is not None:

            @pl.when(i == hook[0])
            def _():
                hook[1]()

        body(i)
        return carry

    lax.fori_loop(0, count, step, 0)


def lanes(c, width=LANES):
    return pl.ds(pl.multiple_of(c * width, width), width)


def coefs(total, row, count, gain, shift):
    mean = total[pl.ds(row, 1), :] / count
    square = total[pl.ds(row + 1, 1), :] / count
    scale = gain * lax.rsqrt(square - mean * mean + EPS_NORM)
    return scale, shift - mean * scale


def act_half(half):
    return half + half * jnp.tanh(half)


def forward_kernel(sizes, *refs):
    (images, mask, edge_l, edge_r, area, firstrow, wexp, headt, taps, squeeze, excite, gain_e, gain_c, gain_h, gain_s,
     pre_s, mixed_s, feat_s, out_s, low_s, pool_s, unit_s, gate_s, tot_e, tot_c, tot_h, pooled_h,
     pre, hid, out_t, low_t, scaled, pads, stages, totals, cnt, pool_t, gate_t) = refs[:38]
    rest = list(refs[38:])
    save_sems = rest.pop(0)
    sums = []
    for m in range(2):
        group = []
        for rows in (56, 48, 8, 40):
            near, far = rest[0], rest[1]
            group.append((near, far, rest[2:6], rows))
            rest = rest[6:]
        sums.append(group)

    greet(sizes)

    def low(m, layer):
        return low_s.at[layer] if m == 0 else low_t

    def out(m, layer):
        return out_s.at[layer] if m == 0 else out_t

    def total_ref(m, kind, layer):
        if m == 0:
            return (tot_e.at[layer, 0], tot_e.at[layer, 1], tot_c.at[layer], tot_h)[kind]
        return totals.at[kind]

    def summer(m, kind, layer):
        near, far, sems, rows = sums[m][kind]
        return Sum(near, far, total_ref(m, kind, layer), sems, sizes, rows)

    def save(src, dst, index):
        return pltpu.make_async_copy(src, dst, save_sems.at[index])

    for slot in range(SLOTS):
        pads[slot, 0:GAP, :] = jnp.zeros((GAP, LANES), F32)
        pads[slot, GAP + ROWS : 2 * GAP + ROWS, :] = jnp.zeros((GAP, LANES), F32)

    def load_rows(i):
        rows = pl.ds(pl.multiple_of(i * ROWS, ROWS), ROWS)
        for half in range(2):
            cols = slice(half * LANES, half * LANES + LANES)
            value = images[rows, cols].astype(F32) * mask[rows, :]
            hid[0, rows, cols] = value
            hid[1, rows, cols] = value
            low_s[0, rows, cols] = value.astype(BF16)
            low_t[rows, cols] = value.astype(BF16)

    repeat(SLOTS, load_rows)

    def update(m, layer):
        tot = total_ref(m, 2, layer)
        for half in range(2):
            cols = slice(half * LANES, half * LANES + LANES)
            for b in range(BATCHES):
                scale, shift = coefs(tot, 4 * half + 2 * b, cnt[b : b + 1, :], gain_c[m, layer, 0:1, cols], gain_c[m, layer, 1:2, cols])

                def one(i):
                    rows = pl.ds(pl.multiple_of(b * HALF + i * ROWS, ROWS), ROWS)
                    value = hid[m, rows, cols] + mask[rows, :] * (out(m, layer)[rows, cols] * scale + shift)
                    hid[m, rows, cols] = value
                    low(m, layer + 1)[rows, cols] = value.astype(BF16)

                repeat(IMGS, one)

    def put_sums(stage, chunk, b, value):
        stage[pl.ds(4 * chunk + 2 * b, 1), :] = jnp.sum(value, 0, keepdims=True)
        stage[pl.ds(4 * chunk + 2 * b + 1, 1), :] = jnp.sum(value * value, 0, keepdims=True)

    def expand(m, layer, hook=None):
        stage = stages.at[m]

        def body(c):
            weight = wexp[m, layer, :, lanes(c, 256)]
            for b in range(BATCHES):
                value = jnp.dot(low(m, layer)[b * HALF : (b + 1) * HALF, :], weight, preferred_element_type=F32)
                for half in range(2):
                    piece = value[:, half * LANES : (half + 1) * LANES]
                    pre[m, 2 * c + half, b * HALF : (b + 1) * HALF, :] = piece
                    put_sums(stage, 2 * c + half, b, piece)
            if m == 0:
                for half in range(2):
                    save(pre.at[0, 2 * c + half], pre_s.at[layer, 2 * c + half], 2 * c + half).start()

        repeat(E // 256, body, hook)

    def depthwise(m, layer, hook=None):
        stage = stages.at[m]
        tot = total_ref(m, 0, layer)

        def body(c):
            if m == 0:
                save(pre.at[0, c], pre_s.at[layer, c], c).wait()
            tap = [taps[m, layer, k : k + 1, lanes(c)] for k in range(9)]
            for b in range(BATCHES):
                scale, shift = coefs(tot, 4 * c + 2 * b, cnt[b : b + 1, :], gain_e[m, layer, 0:1, lanes(c)], gain_e[m, layer, 1:2, lanes(c)])
                scale, shift = 0.5 * scale, 0.5 * shift
                for i in range(IMGS):
                    slot = b * IMGS + i
                    rows = slice(slot * ROWS, (slot + 1) * ROWS)
                    half = mask[rows, :] * (pre[m, c, rows, :] * scale + shift)
                    pads[slot, GAP : GAP + ROWS, :] = act_half(half)
                first = jnp.zeros((8, LANES), F32)
                second = jnp.zeros((8, LANES), F32)
                for i in range(IMGS):
                    slot = b * IMGS + i
                    for t in range(ROWS // TILE):
                        start = GAP + t * TILE
                        near = [pads[slot, start + o : start + o + TILE, :] for o in OFFSETS]
                        left = near[0] * tap[0] + near[3] * tap[3] + near[6] * tap[6]
                        mid = near[1] * tap[1] + near[4] * tap[4] + near[7] * tap[7]
                        right = near[2] * tap[2] + near[5] * tap[5] + near[8] * tap[8]
                        rows = slice(slot * ROWS + t * TILE, slot * ROWS + (t + 1) * TILE)
                        value = mask[rows, :] * (mid + edge_l[0:TILE, :] * left + edge_r[0:TILE, :] * right)
                        pre[m, c, rows, :] = value
                        first = first + jnp.sum(value.reshape(TILE // 8, 8, LANES), 0)
                        second = second + jnp.sum((value * value).reshape(TILE // 8, 8, LANES), 0)
                stage[pl.ds(4 * c + 2 * b, 1), :] = jnp.sum(first, 0, keepdims=True)
                stage[pl.ds(4 * c + 2 * b + 1, 1), :] = jnp.sum(second, 0, keepdims=True)
            if m == 0:
                save(pre.at[0, c], mixed_s.at[layer, c], c).start()

        repeat(EC, body, hook)

    def pooling(m, layer, hook=None):
        tot = total_ref(m, 1, layer)
        pool = pool_s.at[layer] if m == 0 else pool_t

        def body(c):
            if m == 0:
                save(pre.at[0, c], mixed_s.at[layer, c], c).wait()
            for b in range(BATCHES):
                scale, shift = coefs(tot, 4 * c + 2 * b, cnt[b : b + 1, :], gain_e[m, layer, 2:3, lanes(c)], gain_e[m, layer, 3:4, lanes(c)])
                scale, shift = 0.5 * scale, 0.5 * shift
                for i in range(IMGS):
                    slot = b * IMGS + i
                    rows = slice(slot * ROWS, (slot + 1) * ROWS)
                    value = act_half(mask[rows, :] * (pre[m, c, rows, :] * scale + shift))
                    pre[m, c, rows, :] = value
                    pool[b * 8 + i : b * 8 + i + 1, lanes(c)] = jnp.sum(value, 0, keepdims=True) / area[0:1, :]

        repeat(EC, body, hook)

    def project(m, layer):
        pool = pool_s.at[layer] if m == 0 else pool_t
        gate = gate_s.at[layer] if m == 0 else gate_t
        units = matmul_bt(pool[...], squeeze[m, layer]) + gain_s[m, layer]
        if m == 0:
            unit_s[layer] = units
        gate[...] = jax.nn.sigmoid(matmul(jax.nn.silu(units), excite[m, layer]) + gain_e[m, layer, 4:5, :])

        def body(c):
            for b in range(BATCHES):
                for i in range(IMGS):
                    rows = slice(b * HALF + i * ROWS, b * HALF + (i + 1) * ROWS)
                    scaled[rows, lanes(c)] = (pre[m, c, rows, :] * gate[b * 8 + i : b * 8 + i + 1, lanes(c)]).astype(BF16)

        repeat(EC, body)
        stage = stages.at[m]
        for b in range(BATCHES):
            rows = slice(b * HALF, (b + 1) * HALF)
            value = contract(scaled[rows, :], wexp[m, layer, :, E : 2 * E], 1, 1)
            out(m, layer)[rows, :] = value
            for half in range(2):
                put_sums(stage, half, b, value[:, half * LANES : (half + 1) * LANES])

    def features(m, hook=None):
        stage = stages.at[m]

        def body(c):
            weight = headt[m, pl.ds(pl.multiple_of(c * 256, 256), 256), :]
            for b in range(BATCHES):
                value = contract(low(m, L)[b * HALF : (b + 1) * HALF, :], weight, 1, 1)
                for half in range(2):
                    piece = value[:, half * LANES : (half + 1) * LANES]
                    pre[m, 2 * c + half, b * HALF : (b + 1) * HALF, :] = piece
                    put_sums(stage, 2 * c + half, b, piece)
            if m == 0:
                for half in range(2):
                    save(pre.at[0, 2 * c + half], feat_s.at[2 * c + half], 2 * c + half).start()

        repeat(HEAD // 256, body, hook)

    def head_pool(m, hook=None):
        tot = total_ref(m, 3, 0)

        def body(c):
            for b in range(BATCHES):
                scale, shift = coefs(tot, 4 * c + 2 * b, cnt[b : b + 1, :], gain_h[m, 0:1, lanes(c)], gain_h[m, 1:2, lanes(c)])
                scale, shift = 0.5 * scale, 0.5 * shift
                for i in range(IMGS):
                    slot = b * IMGS + i
                    rows = slice(slot * ROWS, (slot + 1) * ROWS)
                    value = act_half(mask[rows, :] * (pre[m, c, rows, :] * scale + shift))
                    pooled_h[m, b * 8 + i : b * 8 + i + 1, lanes(c)] = jnp.sum(value, 0, keepdims=True) / area[0:1, :]

        repeat(HC, body, hook)

    for m in range(2):
        stages[m] = jnp.zeros((56, LANES), F32)
    pool_s[...] = jnp.zeros(pool_s.shape, F32)
    pool_t[...] = jnp.zeros(pool_t.shape, F32)
    pooled_h[...] = jnp.zeros(pooled_h.shape, F32)
    stages[0, 48:56, :] = firstrow[...]
    pending = None
    for layer in range(L):
        s_one, t_one = summer(0, 0, layer), summer(1, 0, layer)
        s_two, t_two = summer(0, 1, layer), summer(1, 1, layer)
        s_three, t_three = summer(0, 2, layer), summer(1, 2, layer)
        if layer > 0:
            update(0, layer - 1)
        expand(0, layer, None if pending is None else (2, pending.middle))
        s_one.start(stages.at[0])
        if layer > 0:
            pending.finish()
            update(1, layer - 1)
        expand(1, layer, (4, s_one.middle))
        t_one.start(stages.at[1])
        s_one.finish()
        if layer == 0:
            cnt[...] = tot_e[0, 0, 48:56, :]
        depthwise(0, layer, (2, t_one.middle))
        s_two.start(stages.at[0])
        t_one.finish()
        depthwise(1, layer, (5, s_two.middle))
        t_two.start(stages.at[1])
        s_two.finish()
        pooling(0, layer, (5, t_two.middle))
        project(0, layer)
        s_three.start(stages.at[0])
        t_two.finish()
        pooling(1, layer, (6, s_three.middle))
        project(1, layer)
        t_three.start(stages.at[1])
        s_three.finish()
        pending = t_three
    s_head, t_head = summer(0, 3, 0), summer(1, 3, 0)
    update(0, L - 1)
    features(0, (2, pending.middle))
    s_head.start(stages.at[0])
    pending.finish()
    update(1, L - 1)
    features(1, (4, s_head.middle))
    t_head.start(stages.at[1])
    s_head.finish()
    head_pool(0, (3, t_head.middle))
    t_head.finish()
    head_pool(1)
    for c in range(HC):
        save(pre.at[0, c], feat_s.at[c], c).wait()


def run_forward_all(sizes, inputs):
    sds = jax.ShapeDtypeStruct
    vm = pl.BlockSpec(memory_space=pltpu.VMEM)
    hbm = pl.BlockSpec(memory_space=pl.ANY)
    outs = [
        (sds((L, EC, FULL, LANES), F32), hbm),
        (sds((L, EC, FULL, LANES), F32), hbm),
        (sds((HC, FULL, LANES), F32), hbm),
        (sds((L, FULL, C), F32), vm),
        (sds((L + 1, FULL, C), BF16), vm),
        (sds((L, 16, E), F32), vm),
        (sds((L, 16, SE), F32), vm),
        (sds((L, 16, E), F32), vm),
        (sds((L, 2, 56, LANES), F32), vm),
        (sds((L, 8, LANES), F32), vm),
        (sds((40, LANES), F32), vm),
        (sds((2, 16, HEAD), F32), vm),
    ]
    scratch = [
        pltpu.VMEM((2, EC, FULL, LANES), F32),
        pltpu.VMEM((2, FULL, C), F32),
        pltpu.VMEM((FULL, C), F32),
        pltpu.VMEM((FULL, C), BF16),
        pltpu.VMEM((FULL, E), BF16),
        pltpu.VMEM((SLOTS, ROWS + 2 * GAP, LANES), F32),
        pltpu.VMEM((2, 56, LANES), F32),
        pltpu.VMEM((4, 56, LANES), F32),
        pltpu.VMEM((8, LANES), F32),
        pltpu.VMEM((16, E), F32),
        pltpu.VMEM((16, E), F32),
        pltpu.SemaphoreType.DMA((EC,)),
    ]
    for m in range(2):
        for rows in (56, 48, 8, 40):
            scratch = scratch + sum_scratch(sizes, rows)
    return pl.pallas_call(
        functools.partial(forward_kernel, sizes),
        out_shape=[o[0] for o in outs],
        in_specs=[vm] * len(inputs),
        out_specs=[o[1] for o in outs],
        scratch_shapes=scratch,
        compiler_params=pltpu.CompilerParams(collective_id=1, has_side_effects=True, vmem_limit_bytes=63 * 2**20),
        name="forward",
    )(*inputs)


CLASS_PAD = 1024
FACT = CLASS_PAD + 384
BACK_ROWS = ((24, 24, 8, 24), (40, 24, 8, 40))


def round_up(value, unit):
    return -(-value // unit) * unit


CHUNKS = 6
MATS = 2 * E // LANES * 8
CHAN = 3 * 18
AT_CHAN = L * MATS
AT_HEAD = AT_CHAN + L * CHAN
AT_END = AT_HEAD + 2 * HEAD // 4 // 8


def packed_blocks(sizes):
    return round_up(AT_END, CHUNKS * 2 * sizes[0])


def backward_kernel(sizes, *refs):
    (dpool_h, extra, mask, edge_l, edge_r, area, wexp, headt, taps, squeeze, excite, gain_e, gain_c, gain_h,
     pre_s, mixed_s, feat_s, out_s, low_s, pool_s, unit_s, gate_s, tot_e, tot_c, tot_h,
     packed, back_e, back_c, back_h,
     pre, mixed, grad, grad_hid, low_out, low_pre, pads_x, pads_g, slope, dgate, dpool, stages, load_sems,
     held, held_chan, held_exb, held_sqb, out_v, low_v, row_sems) = refs[:49]
    rest = list(refs[49:])
    n_dp, n_sh = sizes
    sums = []
    for b in range(BATCHES):
        group = []
        for rows in BACK_ROWS[b]:
            group.append((rest[0], rest[1], rest[2:6], rows))
            rest = rest[6:]
        sums.append(group)

    greet(sizes)

    def back_ref(b, kind, layer):
        return (back_e.at[layer, b, 0], back_e.at[layer, b, 1], back_c.at[layer, b], back_h.at[b])[kind]

    def summer(b, kind, layer):
        near, far, sems, rows = sums[b][kind]
        return Sum(near, far, back_ref(b, kind, layer), sems, sizes, rows)

    def load(b, kind, layer):
        rows = slice(b * HALF, (b + 1) * HALF)
        if kind == 0:
            return pltpu.make_async_copy(pre_s.at[layer, :, rows], pre.at[b], load_sems.at[b, 0])
        if kind == 1:
            return pltpu.make_async_copy(mixed_s.at[layer, :, rows], mixed.at[b], load_sems.at[b, 1])
        return pltpu.make_async_copy(feat_s.at[:, rows], pre.at[b, 0:HC], load_sems.at[b, 0])

    def load_out(layer):
        return pltpu.make_async_copy(out_s.at[layer], out_v, row_sems.at[0])

    def load_low(layer):
        return pltpu.make_async_copy(low_s.at[layer], low_v, row_sems.at[1])

    for b in range(BATCHES):
        load(b, 2, 0).start()
    load_low(L).start()
    load_out(L - 1).start()
    for b in range(BATCHES):
        load(b, 1, L - 1).start()
    for slot in range(IMGS):
        for pads in (pads_x, pads_g):
            pads[slot, 0:GAP, :] = jnp.zeros((GAP, LANES), F32)
            pads[slot, GAP + ROWS : 2 * GAP + ROWS, :] = jnp.zeros((GAP, LANES), F32)
    dgate[...] = jnp.zeros(dgate.shape, F32)
    stages[...] = jnp.zeros(stages.shape, F32)
    stages[1, 24:40, :] = extra[...]
    held_chan[...] = jnp.zeros(held_chan.shape, F32)
    spare = packed.shape[1] - AT_END
    if spare:
        packed[:, AT_END:] = jnp.zeros((n_sh, spare, 8, LANES), F32)

    def pack(first, c, value):
        for t in range(n_sh):
            for half in range(2):
                piece = value[64 * t : 64 * t + 64, half * LANES : (half + 1) * LANES]
                packed[t, pl.ds(first + 16 * c + 8 * half, 8)] = piece.reshape(8, 8, LANES)

    def pack_chan(layer):
        for k in range(EC):
            first = AT_CHAN + CHAN * layer + 18 * (k % 3)
            packed[k // 3, first : first + 18] = held_chan[:, k * LANES : (k + 1) * LANES].reshape(18, 8, LANES)

    def forward_total(kind, layer):
        return (tot_e.at[layer, 0], tot_e.at[layer, 1], tot_c.at[layer], tot_h)[kind]

    def moments(b, kind, layer, c):
        tot = forward_total(kind, layer)
        count = tot_e[0, 0, 48 + b : 49 + b, :]
        mean = tot[pl.ds(4 * c + 2 * b, 1), :] / count
        square = tot[pl.ds(4 * c + 2 * b + 1, 1), :] / count
        return mean, lax.rsqrt(square - mean * mean + EPS_NORM)

    def half_coefs(b, kind, layer, c, gain, shift):
        mean, scale = moments(b, kind, layer, c)
        scale = scale * gain
        return 0.5 * scale, 0.5 * (shift - mean * scale)

    def back_coefs(b, kind, layer, c, gain):
        mean, scale = moments(b, kind, layer, c)
        count = tot_e[0, 0, 48 + b : 49 + b, :]
        back = back_ref(b, kind, layer)
        plain = back[pl.ds(2 * c, 1), :]
        cross = scale * (back[pl.ds(2 * c + 1, 1), :] - mean * plain)
        first = scale * gain
        third = -first * scale * cross / count
        return first, -first * plain / count - mean * third, third

    def fold(value):
        return jnp.sum(value.reshape(value.shape[0] // 8, 8, LANES), 0)

    def put(stage, c, first, second):
        stage[pl.ds(2 * c, 1), :] = jnp.sum(first, 0, keepdims=True)
        stage[pl.ds(2 * c + 1, 1), :] = jnp.sum(second, 0, keepdims=True)

    def image(b, i):
        return slice(i * ROWS, (i + 1) * ROWS), slice(b * HALF + i * ROWS, b * HALF + (i + 1) * ROWS)

    def bend(half):
        t = jnp.tanh(half)
        return half + half * t, (0.5 + 0.5 * t) * (1.0 + half * (1.0 - t))

    def head_first(b, hook=None):
        stage = stages.at[b]

        def body(c):
            scale, shift = half_coefs(b, 3, 0, c, gain_h[0:1, lanes(c)], gain_h[1:2, lanes(c)])
            first = jnp.zeros((8, LANES), F32)
            second = jnp.zeros((8, LANES), F32)
            for i in range(IMGS):
                rows, full = image(b, i)
                x = pre[b, c, rows, :]
                half = mask[full, :] * (x * scale + shift)
                value = mask[full, :] * dpool_h[b * 8 + i : b * 8 + i + 1, lanes(c)] * bend(half)[1]
                grad[b, c, rows, :] = value
                first = first + fold(value)
                second = second + fold(value * x)
            put(stage, c, first, second)

        repeat(HC, body, hook)

    def norm_back_rows(b, kind, layer, c, gain, source):
        one, two, three = back_coefs(b, kind, layer, c, gain)
        for i in range(IMGS):
            rows, full = image(b, i)
            value = mask[full, :] * (one * grad[b, c, rows, :] + two + three * source[b, c, rows, :])
            low_pre[rows, lanes(c)] = value.astype(BF16)

    def put_hidden_sums(b, layer):
        stage = stages.at[b]
        for half in range(2):
            cols = slice(half * LANES, (half + 1) * LANES)
            first = jnp.zeros((8, LANES), F32)
            second = jnp.zeros((8, LANES), F32)
            for i in range(IMGS):
                full = image(b, i)[1]
                value = grad_hid[full, cols]
                first = first + fold(value)
                second = second + fold(value * out_v[full, cols])
            put(stage, half, first, second)

    def head_second(b, hook=None):
        mine = slice(b * HALF, (b + 1) * HALF)

        def body(c):
            for half in range(2):
                norm_back_rows(b, 3, 0, 2 * c + half, gain_h[0:1, lanes(2 * c + half)], pre)
            value = contract(low_pre[:, lanes(c, 256)], low_v[mine, :], 0, 0)
            if b == 0:
                held[c] = value
            else:
                value = value + held[c]
                for i in range(32):
                    row = 32 * c + i
                    for half in range(2):
                        packed[row // 40, AT_HEAD + 40 * half + lax.rem(row, 40)] = value[8 * i : 8 * i + 8, half * LANES : (half + 1) * LANES]

        repeat(HEAD // 256, body, hook)
        grad_hid[mine, :] = jnp.dot(low_pre[:, 0:HEAD], headt[...], preferred_element_type=F32)
        put_hidden_sums(b, L - 1)

    def block_gate(b, layer, hook=None):
        mine = slice(b * HALF, (b + 1) * HALF)
        eight = slice(b * 8, b * 8 + 8)
        for half in range(2):
            cols = slice(half * LANES, (half + 1) * LANES)
            one, two, three = back_coefs(b, 2, layer, half, gain_c[layer, 0:1, cols])
            for i in range(IMGS):
                rows, full = image(b, i)
                low_out[rows, cols] = (mask[full, :] * (one * grad_hid[full, cols] + two + three * out_v[full, cols])).astype(BF16)

        def body(c):
            value = jnp.dot(low_out[...], wexp[layer, :, lanes(E // 256 + c, 256)], preferred_element_type=F32)
            for part in range(2):
                k = 2 * c + part
                scale, shift = half_coefs(b, 1, layer, k, gain_e[layer, 2:3, lanes(k)], gain_e[layer, 3:4, lanes(k)])
                for i in range(IMGS):
                    rows, full = image(b, i)
                    act = act_half(mask[full, :] * (mixed[b, k, rows, :] * scale + shift))
                    piece = value[rows, part * LANES : (part + 1) * LANES]
                    grad[b, k, rows, :] = piece
                    dgate[i : i + 1, lanes(k)] = jnp.sum(fold(piece * act), 0, keepdims=True)
                    low_pre[rows, lanes(k)] = (act * gate_s[layer, b * 8 + i : b * 8 + i + 1, lanes(k)]).astype(BF16)
            value = contract(low_out[...], low_pre[:, lanes(c, 256)], 0, 0)
            if b == 0:
                held[c] = value
            else:
                pack(MATS * layer + MATS // 2, c, value + held[c])

        repeat(E // 256, body, hook)
        gate = gate_s[layer, eight, :]
        units = unit_s[layer, eight, :]
        sig = jax.nn.sigmoid(units)
        inner = dgate[...] * gate * (1.0 - gate)
        bias_x = jnp.sum(inner, 0, keepdims=True)
        grad_x = matmul_tb(units * sig, inner)
        outer = matmul_bt(inner, excite[layer]) * (sig * (1.0 + units * (1.0 - sig)))
        bias_r = jnp.sum(outer, 0, keepdims=True)
        grad_r = matmul_tb(outer, pool_s[layer, eight, :])
        if b == 0:
            held_exb[0:1, :] = bias_x
            held_chan[9 + SE : 9 + 2 * SE, :] = grad_x
            held_sqb[0:1, 0:SE] = bias_r
            held_chan[9 : 9 + SE, :] = grad_r
        else:
            bias_x = bias_x + held_exb[0:1, :]
            for k in range(EC):
                stages[1, 24 + k : 25 + k, :] = bias_x[:, k * LANES : (k + 1) * LANES]
            stages[1, 24 + EC : 25 + EC, 0:SE] = bias_r + held_sqb[0:1, 0:SE]
            held_chan[9 : 9 + SE, :] = held_chan[9 : 9 + SE, :] + grad_r
            held_chan[9 + SE : 9 + 2 * SE, :] = held_chan[9 + SE : 9 + 2 * SE, :] + grad_x
        dpool[...] = matmul(outer, squeeze[layer])

    def block_second(b, layer, hook=None):
        stage = stages.at[b]

        def body(c):
            scale, shift = half_coefs(b, 1, layer, c, gain_e[layer, 2:3, lanes(c)], gain_e[layer, 3:4, lanes(c)])
            first = jnp.zeros((8, LANES), F32)
            second = jnp.zeros((8, LANES), F32)
            for i in range(IMGS):
                rows, full = image(b, i)
                x = mixed[b, c, rows, :]
                half = mask[full, :] * (x * scale + shift)
                gate = gate_s[layer, b * 8 + i : b * 8 + i + 1, lanes(c)]
                value = mask[full, :] * (grad[b, c, rows, :] * gate + dpool[i : i + 1, lanes(c)] / area[0:1, :]) * bend(half)[1]
                grad[b, c, rows, :] = value
                first = first + fold(value)
                second = second + fold(value * x)
            put(stage, c, first, second)

        repeat(EC, body, hook)

    def block_spread(b, layer, hook=None):
        stage = stages.at[b]

        def body(c):
            scale, shift = half_coefs(b, 0, layer, c, gain_e[layer, 0:1, lanes(c)], gain_e[layer, 1:2, lanes(c)])
            one, two, three = back_coefs(b, 1, layer, c, gain_e[layer, 2:3, lanes(c)])
            tap = [taps[layer, k : k + 1, lanes(c)] for k in range(9)]
            for i in range(IMGS):
                rows, full = image(b, i)
                act, der = bend(mask[full, :] * (pre[b, c, rows, :] * scale + shift))
                pads_x[i, GAP : GAP + ROWS, :] = act
                slope[rows, :] = mask[full, :] * der
                pads_g[i, GAP : GAP + ROWS, :] = mask[full, :] * (one * grad[b, c, rows, :] + two + three * mixed[b, c, rows, :])
            first = jnp.zeros((8, LANES), F32)
            second = jnp.zeros((8, LANES), F32)
            total = [jnp.zeros((8, LANES), F32) for k in range(9)]
            for i in range(IMGS):
                for t in range(ROWS // TILE_BACK):
                    start = GAP + t * TILE_BACK
                    rows = slice(i * ROWS + t * TILE_BACK, i * ROWS + (t + 1) * TILE_BACK)
                    g = [pads_g[i, start - o : start - o + TILE_BACK, :] for o in OFFSETS]
                    left, right = edge_l[0:TILE_BACK, :], edge_r[0:TILE_BACK, :]
                    wide = (g[1] * tap[1] + g[4] * tap[4] + g[7] * tap[7]
                            + right * (g[0] * tap[0] + g[3] * tap[3] + g[6] * tap[6])
                            + left * (g[2] * tap[2] + g[5] * tap[5] + g[8] * tap[8]))
                    value = wide * slope[rows, :]
                    grad[b, c, rows, :] = value
                    first = first + fold(value)
                    second = second + fold(value * pre[b, c, rows, :])
                    center = g[4]
                    sides = (center * left, center, center * right)
                    for k in range(9):
                        o = OFFSETS[k]
                        total[k] = total[k] + fold(sides[k % 3] * pads_x[i, start + o : start + o + TILE_BACK, :])
            put(stage, c, first, second)
            for k in range(9):
                row = jnp.sum(total[k], 0, keepdims=True)
                if b == 0:
                    held_chan[k : k + 1, lanes(c)] = row
                else:
                    held_chan[k : k + 1, lanes(c)] = held_chan[k : k + 1, lanes(c)] + row

        repeat(EC, body, hook)
        if b == 1:
            pack_chan(layer)

    def block_expand(b, layer, hook=None):
        mine = slice(b * HALF, (b + 1) * HALF)

        def body(c):
            for part in range(2):
                norm_back_rows(b, 0, layer, 2 * c + part, gain_e[layer, 0:1, lanes(2 * c + part)], pre)
            value = contract(low_v[mine, :], low_pre[:, lanes(c, 256)], 0, 0)
            if b == 0:
                held[c] = value
            else:
                pack(MATS * layer, c, value + held[c])

        repeat(E // 256, body, hook)
        if layer > 0:
            grad_hid[mine, :] = grad_hid[mine, :] + contract(low_pre[...], wexp[layer, :, 0:E], 1, 1)
            put_hidden_sums(b, layer - 1)

    heads = [summer(b, 3, 0) for b in range(BATCHES)]
    load(0, 2, 0).wait()
    head_first(0)
    heads[0].start(stages.at[0])
    load(1, 2, 0).wait()
    head_first(1, (5, heads[0].middle))
    heads[1].start(stages.at[1])
    thirds = [summer(b, 2, L - 1) for b in range(BATCHES)]
    heads[0].finish()
    load_low(L).wait()
    load_out(L - 1).wait()
    head_second(0, (2, heads[1].middle))
    load(0, 0, L - 1).start()
    thirds[0].start(stages.at[0])
    heads[1].finish()
    head_second(1, (3, thirds[0].middle))
    load(1, 0, L - 1).start()
    thirds[1].start(stages.at[1])
    load_low(L - 1).start()
    for layer in reversed(range(L)):
        twos = [summer(b, 1, layer) for b in range(BATCHES)]
        ones = [summer(b, 0, layer) for b in range(BATCHES)]
        thirds[0].finish()
        load(0, 1, layer).wait()
        block_gate(0, layer, (3, thirds[1].middle))
        block_second(0, layer)
        twos[0].start(stages.at[0])
        thirds[1].finish()
        load(1, 1, layer).wait()
        block_gate(1, layer, (3, twos[0].middle))
        if layer > 0:
            load_out(layer - 1).start()
        block_second(1, layer)
        twos[1].start(stages.at[1])
        twos[0].finish()
        load(0, 0, layer).wait()
        block_spread(0, layer, (4, twos[1].middle))
        ones[0].start(stages.at[0])
        if layer > 0:
            load(0, 1, layer - 1).start()
        twos[1].finish()
        load(1, 0, layer).wait()
        block_spread(1, layer, (4, ones[0].middle))
        ones[1].start(stages.at[1])
        if layer > 0:
            load(1, 1, layer - 1).start()
        ones[0].finish()
        load_low(layer).wait()
        if layer > 0:
            load_out(layer - 1).wait()
        block_expand(0, layer, (3, ones[1].middle))
        if layer > 0:
            thirds = [summer(b, 2, layer - 1) for b in range(BATCHES)]
            thirds[0].start(stages.at[0])
            load(0, 0, layer - 1).start()
        ones[1].finish()
        block_expand(1, layer, None if layer == 0 else (3, thirds[0].middle))
        if layer > 0:
            thirds[1].start(stages.at[1])
            load(1, 0, layer - 1).start()
            load_low(layer - 1).start()


def run_backward_all(sizes, inputs):
    sds = jax.ShapeDtypeStruct
    vm = pl.BlockSpec(memory_space=pltpu.VMEM)
    hbm = pl.BlockSpec(memory_space=pl.ANY)
    n_dp, n_sh = sizes
    outs = [
        sds((n_sh, packed_blocks(sizes), 8, LANES), F32),
        sds((L, BATCHES, 2, 40, LANES), F32),
        sds((L, BATCHES, 8, LANES), F32),
        sds((BATCHES, 40, LANES), F32),
    ]
    scratch = [
        pltpu.VMEM((BATCHES, EC, HALF, LANES), F32),
        pltpu.VMEM((BATCHES, EC, HALF, LANES), F32),
        pltpu.VMEM((BATCHES, EC, HALF, LANES), F32),
        pltpu.VMEM((FULL, C), F32),
        pltpu.VMEM((HALF, C), BF16),
        pltpu.VMEM((HALF, E), BF16),
        pltpu.VMEM((IMGS, ROWS + 2 * GAP, LANES), F32),
        pltpu.VMEM((IMGS, ROWS + 2 * GAP, LANES), F32),
        pltpu.VMEM((HALF, LANES), F32),
        pltpu.VMEM((8, E), F32),
        pltpu.VMEM((8, E), F32),
        pltpu.VMEM((BATCHES, 40, LANES), F32),
        pltpu.SemaphoreType.DMA((BATCHES, 2)),
        pltpu.VMEM((E // 256, 256, 256), F32),
        pltpu.VMEM((144, E), F32),
        pltpu.VMEM((8, E), F32),
        pltpu.VMEM((8, LANES), F32),
        pltpu.VMEM((FULL, C), F32),
        pltpu.VMEM((FULL, C), BF16),
        pltpu.SemaphoreType.DMA((2,)),
    ]
    for b in range(BATCHES):
        for rows in BACK_ROWS[b]:
            scratch = scratch + sum_scratch(sizes, rows)
    specs = [vm] * 14 + [hbm] * 5 + [vm] * 6
    return pl.pallas_call(
        functools.partial(backward_kernel, sizes),
        out_shape=outs,
        in_specs=specs,
        out_specs=[vm] * len(outs),
        scratch_shapes=scratch,
        compiler_params=pltpu.CompilerParams(collective_id=2, has_side_effects=True, vmem_limit_bytes=63 * 2**20),
        name="backward",
    )(*inputs)


GROUPS = 12


def update_kernel(sizes, *refs):
    (packed, facts, fixes, *state) = refs[:19]
    state_in = [state[4 * k : 4 * k + 4] for k in range(4)]
    outs = refs[19:36]
    out_refs = [outs[4 * k : 4 * k + 4] for k in range(4)]
    norms = outs[16]
    peers = refs[36]
    (own, near, cross, side, line, full, gathered, g_class, turned, sums_near, ratios) = refs[37:48]
    boxes = [refs[48 + 5 * k : 53 + 5 * k] for k in range(4)]
    (core_s, core_r, x_s, x_r, y_s, y_r, z_s, z_r, zz_s, zz_r, yy_s, yy_r,
     fn_s, fn_r, ff_s, ff_r, nn_s, nn_r, load_sems, store_sems, misc) = refs[68:89]
    n_dp, n_sh = sizes
    d, s = lax.axis_index("dp"), lax.axis_index("shard")
    count = packed_blocks(sizes)
    chunk = count // CHUNKS
    half = chunk // 2
    n_z = n_dp // 2
    piece = half // n_z
    bit0, bit1 = lax.rem(s, 2), s // 2
    near_peer = s + 1 - 2 * bit0
    far_peer = s + 2 - 4 * bit1
    yb, zi = lax.rem(d, 2), d // 2
    y_peer = d + 1 - 2 * yb

    greet(sizes)

    def load_own(t):
        return pltpu.make_async_copy(packed.at[t], own.at[t], load_sems.at[16 + t])

    def load(k, i):
        return pltpu.make_async_copy(state_in[k][i], boxes[k][i], load_sems.at[4 * k + i])

    def store(k, i):
        source = boxes[k][(4, 1, 2, 3)[i]]
        return pltpu.make_async_copy(source, out_refs[k][i], store_sems.at[4 * k + i])

    def core_copy(k, i):
        rows = pl.ds(k * chunk, chunk)
        return pltpu.make_async_remote_copy(
            packed.at[2 * i + 1 - bit0, rows], near.at[i, rows], core_s.at[k, i], core_r.at[k, i],
            device_id=(d, near_peer), device_id_type=MESH)

    def x_copy(k):
        rows = pl.ds(k * chunk, chunk)
        return pltpu.make_async_remote_copy(
            own.at[far_peer, rows], cross.at[rows], x_s.at[k], x_r.at[k],
            device_id=(d, far_peer), device_id_type=MESH)

    def y_copy(k):
        rows = pl.ds(k * chunk + (1 - yb) * half, half)
        return pltpu.make_async_remote_copy(
            own.at[s, rows], side.at[k], y_s.at[k], y_r.at[k],
            device_id=(y_peer, s), device_id_type=MESH)

    def z_copy(k, step, source, target):
        rows = pl.ds(k * chunk + yb * half + target * piece, piece)
        return pltpu.make_async_remote_copy(
            own.at[s, rows], line.at[k, source], z_s.at[k, step], z_r.at[k, source],
            device_id=(2 * target + yb, s), device_id_type=MESH)

    def zz_copy(k, step, source, target):
        rows = pl.ds(k * (chunk // 2) + yb * (half // 2) + source * (piece // 2), piece // 2)
        return pltpu.make_async_remote_copy(
            full.at[rows], full.at[rows], zz_s.at[k, step], zz_r.at[k, source],
            device_id=(2 * target + yb, s), device_id_type=MESH)

    def yy_copy(k, b):
        rows = pl.ds(k * (chunk // 2) + b * (half // 2), half // 2)
        return pltpu.make_async_remote_copy(
            full.at[rows], full.at[rows], yy_s.at[k], yy_r.at[k],
            device_id=(y_peer, s), device_id_type=MESH)

    def over_z(action):
        def step(j, carry):
            action(j, lax.rem(zi + j, n_z))
            return carry

        lax.fori_loop(1, n_z, step, 0)

    def add_into(t, low, length, other, low_other, unit=8):
        def step(i, carry):
            rows = pl.ds(low + i * unit, unit)
            own[t, rows] = own[t, rows] + other(pl.ds(low_other + i * unit, unit))
            return carry

        lax.fori_loop(0, length // unit, step, 0)

    def stage_core(k):
        for i in range(2):
            core_copy(k, i).start()

    def stage_x(k):
        for i in range(2):
            core_copy(k, i).wait_recv()
        low = k * chunk
        add_into(far_peer, low, chunk, lambda rows: near[1 - bit1, rows], low)
        x_copy(k).start()
        add_into(s, low, chunk, lambda rows: near[bit1, rows], low)

    def stage_y(k):
        x_copy(k).wait_recv()
        low = k * chunk
        give = low + (1 - yb) * half
        keep = low + yb * half
        add_into(s, give, half, lambda rows: cross[rows], give)
        y_copy(k).start()
        add_into(s, keep, half, lambda rows: cross[rows], keep)

    def stage_z(k):
        y_copy(k).wait_recv()
        add_into(s, k * chunk + yb * half, half, lambda rows: side[k, rows], 0)
        over_z(lambda j, t: z_copy(k, j, zi, t).start())

    def stage_zz(k):
        over_z(lambda j, t: z_copy(k, j, t, zi).wait_recv())
        low = k * chunk + yb * half + zi * piece

        def step(i, carry):
            total = own[s, pl.ds(low + 2 * i, 2)]
            for j in range(1, n_z):
                total = total + line[k, lax.rem(zi + j, n_z), pl.ds(2 * i, 2)]
            full[low // 2 + i] = total.reshape(16, LANES).astype(BF16)
            return carry

        lax.fori_loop(0, piece // 2, step, 0)
        over_z(lambda j, t: zz_copy(k, j, zi, t).start())

    def stage_yy(k):
        over_z(lambda j, t: zz_copy(k, j, t, zi).wait_recv())
        yy_copy(k, yb).start()

    def stage_done(k):
        yy_copy(k, 1 - yb).wait_recv()

    def settle(k):
        for i in range(2):
            core_copy(k, i).wait_send()
        x_copy(k).wait_send()
        y_copy(k).wait_send()
        over_z(lambda j, t: z_copy(k, j, zi, t).wait_send())
        over_z(lambda j, t: zz_copy(k, j, zi, t).wait_send())
        yy_copy(k, yb).wait_send()

    def own_facts():
        return pltpu.make_async_copy(facts.at[s], peers.at[d, s], misc.at[0])

    def fact_near(step, source, target):
        return pltpu.make_async_remote_copy(
            facts.at[target], peers.at[d, source], fn_s.at[step], fn_r.at[source],
            device_id=(d, target), device_id_type=MESH)

    def fact_far(step, source, target):
        return pltpu.make_async_remote_copy(
            peers.at[source], peers.at[source], ff_s.at[step], ff_r.at[source],
            device_id=(target, s), device_id_type=MESH)

    def over_dp(action):
        def step(j, carry):
            action(j, lax.rem(d + j, n_dp))
            return carry

        lax.fori_loop(1, n_dp, step, 0)

    def facts_begin():
        own_facts().start()
        for j in range(1, n_sh):
            fact_near(j, s, lax.rem(s + j, n_sh)).start()

    def facts_second():
        for j in range(1, n_sh):
            fact_near(j, lax.rem(s + j, n_sh), s).wait_recv()
            fact_near(j, s, s).wait_send()
        own_facts().wait()
        over_dp(lambda j, t: fact_far(j, d, t).start())

    def facts_third():
        def arrive(j, t):
            fact_far(j, t, d).wait_recv()
            fact_far(j, d, d).wait_send()

        over_dp(arrive)
        for first in range(0, n_dp, 8):
            copy = pltpu.make_async_copy(peers.at[pl.ds(first, 8)], gathered, misc.at[1])
            copy.start()
            copy.wait()
            value = gathered[...].reshape(8 * n_sh * 16, FACT)
            product = contract(value[:, CLASS_PAD:], value[:, :CLASS_PAD], 0, 0)
            g_class[...] = product if first == 0 else g_class[...] + product

    sums_near[s] = jnp.zeros((24, LANES), F32)
    first_fix, second_fix = fixes[0:1, 0:1], fixes[1:2, 0:1]

    def note(row, value):
        square = value * value
        width = square.shape[1]
        line_sum = jnp.sum(square, 0, keepdims=True)
        total = jnp.zeros((1, LANES), F32)
        for low in range(0, width - width % LANES, LANES):
            total = total + line_sum[:, low : low + LANES]
        tail = width % LANES
        if tail:
            total = total + jnp.concatenate([line_sum[:, width - tail :], jnp.zeros((1, LANES - tail), F32)], 1)
        sums_near[s, row : row + 1, :] = sums_near[s, row : row + 1, :] + total

    def moments(k, index, grad):
        weight, first, second, unused, update = boxes[k]
        new_first = BETA_ONE * first[index] + (1.0 - BETA_ONE) * grad
        new_second = BETA_TWO * second[index] + (1.0 - BETA_TWO) * grad * grad
        first[index] = new_first
        second[index] = new_second
        value = new_first / first_fix / (jnp.sqrt(new_second / second_fix) + EPS_ADAM) + DECAY * weight[index]
        update[index] = value
        return value

    every = slice(None)

    def mats_index(layer, c):
        return (layer, every, lanes(c))

    def weights_squares():
        for layer in range(L):
            for part in range(2):

                def body(c):
                    note(2 * layer + part, boxes[0][0][mats_index(layer, c + part * EC)])

                repeat(EC, body)
            for kk in range(3):
                cols = slice(kk * LANES, (kk + 1) * LANES)
                note(2 * L + 3 * layer, boxes[1][0][layer, 0:9, cols])
                note(2 * L + 3 * layer + 1, boxes[1][0][layer, 9 : 9 + SE, cols])
                note(2 * L + 3 * layer + 2, boxes[1][0][layer, 9 + SE : 9 + 2 * SE, cols])
        note(5 * L, boxes[2][0][...])

        def body(i):
            note(5 * L + 1, boxes[3][0][pl.ds(pl.multiple_of(i * 40, 40), 40), :])

        repeat(8, body)

    def mats_moments(layer):
        for part in range(2):

            def body(c):
                panel = c + part * EC
                grad = full[pl.ds(layer * (MATS // 2) + 4 * panel, 4)].astype(F32).reshape(64, LANES)
                note(GROUPS + 2 * layer + part, moments(0, mats_index(layer, panel), grad))

            repeat(EC, body)

    def chan_moments():
        for layer in range(L):
            for kk in range(3):
                low = (AT_CHAN + CHAN * layer + 18 * kk) // 2
                grad = full[low : low + 9].astype(F32).reshape(144, LANES)[:137]
                value = moments(1, (layer, every, slice(kk * LANES, (kk + 1) * LANES)), grad)
                note(GROUPS + 2 * L + 3 * layer, value[0:9])
                note(GROUPS + 2 * L + 3 * layer + 1, value[9 : 9 + SE])
                note(GROUPS + 2 * L + 3 * layer + 2, value[9 + SE :])

    def head_moments():
        rows = HEAD // 4
        turned[rows:, :] = jnp.zeros((turned.shape[0] - rows, C), F32)
        for part in range(2):
            low = (AT_HEAD + part * (rows // 8)) // 2
            turned[0:rows, part * LANES : (part + 1) * LANES] = full[low : low + rows // 16].astype(F32).reshape(rows, LANES)
        grad = turned[...].T
        note(GROUPS + 5 * L, moments(2, (every, every), grad[:, :rows]))

    def class_moments():
        def body(i):
            rows = pl.ds(pl.multiple_of(i * 40, 40), 40)
            note(GROUPS + 5 * L + 1, moments(3, (rows, every), g_class[rows, :CLASSES]))

        repeat(8, body)

    def norm_copy(step, source, target):
        return pltpu.make_async_remote_copy(
            sums_near.at[source], sums_near.at[source], nn_s.at[step], nn_r.at[source],
            device_id=(d, target), device_id_type=MESH)

    def finish(k, index, factor):
        weight, unused, unused_two, average, update = boxes[k]
        fresh = weight[index] - RATE * factor * update[index]
        update[index] = fresh
        average[index] = KEEP * average[index] + (1.0 - KEEP) * fresh

    for k in range(CHUNKS):
        stage_core(k)
    for t in range(n_sh):
        load_own(t).start()
    facts_begin()
    for i in range(4):
        for k in range(4):
            load(k, i).start()
    for t in range(n_sh):
        load_own(t).wait()
    for tau in range(1, CHUNKS + 6):
        stages = (stage_x, stage_y, stage_z, stage_zz, stage_yy, stage_done)
        for age, stage in enumerate(stages):
            k = tau - 1 - age
            if 0 <= k < CHUNKS:
                stage(k)
        if tau == 1:
            facts_second()
            for k in range(4):
                load(k, 0).wait()
            weights_squares()
        if tau == 2:
            for i in range(1, 4):
                for k in range(4):
                    load(k, i).wait()
        if tau == CHUNKS:
            facts_third()
            class_moments()
            for i in (1, 2):
                store(3, i).start()
        if tau == CHUNKS + 2:
            mats_moments(0)
        if tau == CHUNKS + 4:
            mats_moments(1)
            for i in (1, 2):
                store(0, i).start()
    chan_moments()
    head_moments()
    for j in range(1, n_sh):
        norm_copy(j, s, lax.rem(s + j, n_sh)).start()
    for k in (1, 2):
        for i in (1, 2):
            store(k, i).start()
    for k in range(CHUNKS):
        settle(k)
    for j in range(1, n_sh):
        norm_copy(j, lax.rem(s + j, n_sh), s).wait_recv()
        norm_copy(j, s, s).wait_send()
    total = sums_near[0]
    for j in range(1, n_sh):
        total = total + sums_near[j]
    root = jnp.broadcast_to(jnp.sqrt(jnp.sum(total, 1, keepdims=True)), (24, LANES))
    norms[...] = root
    ratios[0:GROUPS, :] = root[0:GROUPS] / root[GROUPS : 2 * GROUPS]

    def ratio(row):
        return ratios[row : row + 1, 0:1]

    for layer in range(L):
        for part in range(2):

            def body(c):
                finish(0, mats_index(layer, c + part * EC), ratio(2 * layer + part))

            repeat(EC, body)
    for i in (0, 3):
        store(0, i).start()

    def body(i):
        finish(3, (pl.ds(pl.multiple_of(i * 40, 40), 40), every), ratio(5 * L + 1))

    repeat(8, body)
    for i in (0, 3):
        store(3, i).start()
    row = lax.broadcasted_iota(jnp.int32, (137, LANES), 0)
    for layer in range(L):
        low = 2 * L + 3 * layer
        factor = jnp.where(row < 9, ratio(low), jnp.where(row < 9 + SE, ratio(low + 1), ratio(low + 2)))
        for kk in range(3):
            finish(1, (layer, every, slice(kk * LANES, (kk + 1) * LANES)), factor)
    finish(2, (every, every), ratio(5 * L))
    for k in (1, 2):
        for i in (0, 3):
            store(k, i).start()
    for k in range(4):
        for i in range(4):
            store(k, i).wait()


def run_update(sizes, packed, facts, fixes, states):
    sds = jax.ShapeDtypeStruct
    vm = pl.BlockSpec(memory_space=pltpu.VMEM)
    hbm = pl.BlockSpec(memory_space=pl.ANY)
    n_dp, n_sh = sizes
    count = packed_blocks(sizes)
    chunk = count // CHUNKS
    n_z = n_dp // 2
    sem = pltpu.SemaphoreType.DMA
    outs = [sds(item.shape, F32) for group in states for item in group]
    outs = outs + [sds((2 * GROUPS, LANES), F32), sds((n_dp, n_sh, 16, FACT), BF16)]
    scratch = [
        pltpu.VMEM((n_sh, count, 8, LANES), F32),
        pltpu.VMEM((2, count, 8, LANES), F32),
        pltpu.VMEM((count, 8, LANES), F32),
        pltpu.VMEM((CHUNKS, chunk // 2, 8, LANES), F32),
        pltpu.VMEM((CHUNKS, n_z, chunk // 2 // n_z, 8, LANES), F32),
        pltpu.VMEM((count // 2, 16, LANES), BF16),
        pltpu.VMEM((8, n_sh, 16, FACT), BF16),
        pltpu.VMEM((FACT - CLASS_PAD, CLASS_PAD), F32),
        pltpu.VMEM((FACT - CLASS_PAD, C), F32),
        pltpu.VMEM((n_sh, 2 * GROUPS, LANES), F32),
        pltpu.VMEM((16, LANES), F32),
    ]
    for group in states:
        scratch = scratch + [pltpu.VMEM(group[0].shape, F32)] * 5
    scratch = scratch + [
        sem((CHUNKS, 2)), sem((CHUNKS, 2)), sem((CHUNKS,)), sem((CHUNKS,)), sem((CHUNKS,)), sem((CHUNKS,)),
        sem((CHUNKS, n_z)), sem((CHUNKS, n_z)), sem((CHUNKS, n_z)), sem((CHUNKS, n_z)), sem((CHUNKS,)), sem((CHUNKS,)),
        sem((n_sh,)), sem((n_sh,)), sem((n_dp,)), sem((n_dp,)), sem((n_sh,)), sem((n_sh,)),
        sem((20,)), sem((16,)), sem((2,)),
    ]
    return pl.pallas_call(
        functools.partial(update_kernel, sizes),
        out_shape=outs,
        in_specs=[hbm, hbm, vm] + [hbm] * 16,
        out_specs=[hbm] * 16 + [vm, hbm],
        scratch_shapes=scratch,
        compiler_params=pltpu.CompilerParams(collective_id=3, has_side_effects=True, vmem_limit_bytes=63 * 2**20),
        name="update",
    )(packed, facts, fixes, *[item for group in states for item in group])


def objective(logits, target, onehot, coef):
    logp = jax.nn.log_softmax(logits)
    per = -jnp.sum(onehot * logp, 1) + jnp.sum(jnp.exp(target) * (target - logp), 1)
    return jnp.sum(coef * per)


def own_slice(value, dim, parts, place):
    width = value.shape[dim] // parts
    return lax.dynamic_slice_in_dim(value, place * width, width, dim)


def adapt(first, second, grad, first_fix, second_fix):
    new_first = BETA_ONE * first + (1.0 - BETA_ONE) * grad
    new_second = BETA_TWO * second + (1.0 - BETA_TWO) * grad * grad
    update = new_first / first_fix / (jnp.sqrt(new_second / second_fix) + EPS_ADAM)
    return (new_first, new_second, update)


def per_device(
    images,
    bucket,
    counts,
    balance,
    labels,
    step,
    expand_w,
    expand_m,
    expand_v,
    expand_e,
    chan_w,
    chan_m,
    chan_v,
    chan_e,
    head_w,
    head_m,
    head_v,
    head_e,
    class_w,
    class_m,
    class_v,
    class_e,
    gain_w,
    gain_m,
    gain_v,
    gain_e,
):
    sizes = (lax.axis_size("dp"), lax.axis_size("shard"))
    n_sh = sizes[1]
    weights = (expand_w, chan_w, head_w, class_w, gain_w)
    firsts = (expand_m, chan_m, head_m, class_m, gain_m)
    seconds = (expand_v, chan_v, head_v, class_v, gain_v)
    averaged = (expand_e, chan_e, head_e, class_e, gain_e)
    axes = (1, 2, 1, 0, 0)
    both = [
        jnp.stack(
            [
                lax.all_gather(item.astype(BF16), "shard", axis=axes[k], tiled=True)
                for item in (weights[k], averaged[k])
            ]
        )
        for k in range(5)
    ]
    code = bucket[0]
    side = jnp.where(code == 0, 7, jnp.where(code == 1, 10, 12))
    spot = jnp.arange(S * S)
    inside = ((spot // S < side) & (spot % S < side)).astype(F32)
    area_value = (side * side).astype(F32)
    valid = (jnp.arange(IMGS)[None, :] < counts).astype(F32)
    weighted = valid * balance.astype(F32)
    mask_all = jnp.broadcast_to(
        (valid[:, :, None] * inside[None, None, :]).reshape(FULL, 1), (FULL, LANES)
    )
    spread_l = jnp.broadcast_to((spot % S > 0).astype(F32)[:, None], (ROWS, LANES))
    spread_r = jnp.broadcast_to((spot % S < S - 1).astype(F32)[:, None], (ROWS, LANES))
    own = jnp.concatenate(
        [jnp.sum(valid, 1) * area_value, jnp.sum(weighted, 1), jnp.zeros((4,), F32)]
    )
    area = jnp.full((1, LANES), area_value)
    chan_f = both[1].astype(F32)
    gains_f = both[4].astype(F32)
    block_width = gains_f.shape[2] - 2 * (HEAD // n_sh) - CLASSES // n_sh
    blocks = gains_f[:, :, :block_width].reshape(2, n_sh, L, -1)
    wide = 5 * E // n_sh
    vec_e = (
        blocks[..., :wide].reshape(2, n_sh, L, 5, E // n_sh).transpose(0, 2, 3, 1, 4)
    ).reshape(2, L, 5, E)
    vec_c = (
        blocks[..., wide : wide + 2 * C // n_sh]
        .reshape(2, n_sh, L, 2, C // n_sh)
        .transpose(0, 2, 3, 1, 4)
    ).reshape(2, L, 2, C)
    vec_s = blocks[..., wide + 2 * C // n_sh :].transpose(0, 2, 1, 3).reshape(2, L, 1, SE)
    heads_f = gains_f[:, :, block_width : block_width + 2 * HEAD // n_sh]
    vec_h = heads_f.reshape(2, n_sh, 2, HEAD // n_sh).transpose(0, 2, 1, 3).reshape(2, 2, HEAD)
    class_bias = gains_f[:, :, block_width + 2 * HEAD // n_sh :].reshape(2, CLASSES)
    headt = both[2].transpose(0, 2, 1)
    taps, squeeze, excite = chan_f[:, :, :9], chan_f[:, :, 9 : 9 + SE], chan_f[:, :, 9 + SE :]
    saved = run_forward_all(
        sizes,
        [
            images.reshape(FULL, C), mask_all, spread_l, spread_r, area,
            jnp.broadcast_to(own[:, None], (8, LANES)), both[0], headt,
            taps, squeeze, excite, vec_e, vec_c, vec_h, vec_s,
        ],
    )
    pooled_h, kept = saved[11], saved[:11]
    tot_e, tot_c, tot_h = kept[8:11]
    total_weight = tot_e[0, 0, 50, 0] + tot_e[0, 0, 51, 0]
    pooled_low = pooled_h.reshape(2, BATCHES, 8, HEAD)[:, :, :IMGS].reshape(2, SLOTS, HEAD).astype(BF16)
    logits = [
        jnp.dot(pooled_low[m], both[3][m], preferred_element_type=F32) + class_bias[m]
        for m in range(2)
    ]
    onehot = (labels.reshape(SLOTS, 1) == jnp.arange(CLASSES)[None, :]).astype(F32)
    coef = weighted.reshape(SLOTS) / total_weight
    target = jax.nn.log_softmax(logits[1])
    loss, pull = jax.vjp(lambda value: objective(value, target, onehot, coef), logits[0])
    grad_low = pull(jnp.float32(1.0))[0].astype(BF16)
    grad_class_bias = jnp.sum(grad_low.astype(F32), 0)
    grad_pooled = contract(grad_low, both[3][0], 1, 1) / area_value
    dpool_h = jnp.pad(grad_pooled.reshape(BATCHES, IMGS, HEAD), ((0, 0), (0, 3), (0, 0))).reshape(16, HEAD)
    extra = jnp.concatenate(
        [
            jnp.pad(grad_class_bias, (0, CLASS_PAD - CLASSES)).reshape(8, LANES),
            jnp.broadcast_to(loss, (8, LANES)),
        ]
    )
    pooled_parts = pooled_low[0].reshape(SLOTS, n_sh, HEAD // n_sh).transpose(1, 0, 2)
    pooled_parts = jnp.pad(pooled_parts, ((0, 0), (0, 6), (0, FACT - CLASS_PAD - HEAD // n_sh)))
    facts = jnp.concatenate(
        [
            jnp.broadcast_to(
                jnp.pad(grad_low, ((0, 6), (0, CLASS_PAD - CLASSES)))[None], (n_sh, 16, CLASS_PAD)
            ),
            pooled_parts,
        ],
        2,
    )
    (packed, back_e, back_c, back_h) = run_backward_all(
        sizes,
        [
            dpool_h, extra, mask_all, spread_l, spread_r, area, both[0][0], headt[0],
            taps[0], squeeze[0], excite[0], vec_e[0], vec_c[0], vec_h[0], *kept,
        ],
    )
    place = lax.axis_index("shard")

    def norm_grads(tot, back, chunks):
        count = tot_e[0, 0, 48 : 48 + BATCHES, :1]
        forth = tot[: 4 * chunks].reshape(chunks, BATCHES, 2, LANES).transpose(1, 2, 0, 3).reshape(BATCHES, 2, -1)
        mean = forth[:, 0] / count
        scale = lax.rsqrt(forth[:, 1] / count - mean * mean + EPS_NORM)
        pairs = back[:, : 2 * chunks].reshape(BATCHES, chunks, 2, LANES).transpose(0, 2, 1, 3).reshape(BATCHES, 2, -1)
        cross = scale * (pairs[:, 1] - mean * pairs[:, 0])
        return [jnp.sum(cross, 0), jnp.sum(pairs[:, 0], 0)]

    vectors = []
    for layer in range(L):
        vectors = vectors + norm_grads(tot_e[layer, 0], back_e[layer, :, 0], EC)
        vectors = vectors + norm_grads(tot_e[layer, 1], back_e[layer, :, 1], EC)
        vectors = vectors + [back_e[layer, 1, 0, 24 : 24 + EC].reshape(E)]
        vectors = vectors + norm_grads(tot_c[layer], back_c[layer], 2)
        vectors = vectors + [back_e[layer, 1, 0, 24 + EC, :SE]]
    vectors = vectors + norm_grads(tot_h, back_h, HC) + [back_h[1, 24:32].reshape(CLASS_PAD)[:CLASSES]]
    total_loss = back_h[1, 32, 0]
    power = step[0].astype(F32)
    first_fix = 1.0 - jnp.power(jnp.float32(BETA_ONE), power)
    second_fix = 1.0 - jnp.power(jnp.float32(BETA_TWO), power)
    fixes = jnp.broadcast_to(jnp.stack([first_fix, second_fix])[:, None], (2, LANES))
    new = run_update(
        sizes,
        packed,
        facts,
        fixes,
        [(weights[k], firsts[k], seconds[k], averaged[k]) for k in range(4)],
    )
    gain_grad = own_slice(pack_gains(vectors, n_sh), 0, n_sh, place)
    gain_first, gain_second, gain_update = adapt(gain_m, gain_v, gain_grad, first_fix, second_fix)
    gain_new = gain_w - RATE * gain_update
    gains_out = [gain_new, gain_first, gain_second, KEEP * gain_e + (1.0 - KEEP) * gain_new]
    norms = new[16][:, 0].reshape(2, GROUPS)
    return tuple([total_loss] + list(new[:16]) + gains_out + [norms])


def solution(mesh):
    in_specs = (
        P(None, ("dp", "shard"), None, None, None),
        P("dp"),
        P(None, ("dp", "shard")),
        P(None, ("dp", "shard")),
        P(None, ("dp", "shard")),
        P(),
        P(None, "shard", None),
        P(None, "shard", None),
        P(None, "shard", None),
        P(None, "shard", None),
        P(None, None, "shard"),
        P(None, None, "shard"),
        P(None, None, "shard"),
        P(None, None, "shard"),
        P(None, "shard"),
        P(None, "shard"),
        P(None, "shard"),
        P(None, "shard"),
        P("shard", None),
        P("shard", None),
        P("shard", None),
        P("shard", None),
        P("shard", None),
        P("shard", None),
        P("shard", None),
        P("shard", None),
    )
    out_specs = (
        P(),
        P(None, "shard", None),
        P(None, "shard", None),
        P(None, "shard", None),
        P(None, "shard", None),
        P(None, None, "shard"),
        P(None, None, "shard"),
        P(None, None, "shard"),
        P(None, None, "shard"),
        P(None, "shard"),
        P(None, "shard"),
        P(None, "shard"),
        P(None, "shard"),
        P("shard", None),
        P("shard", None),
        P("shard", None),
        P("shard", None),
        P("shard", None),
        P("shard", None),
        P("shard", None),
        P("shard", None),
        P(),
    )
    return jax.shard_map(
        per_device, mesh=mesh, in_specs=in_specs, out_specs=out_specs, check_vma=False
    )
```

```python
import functools

import jax
import jax.numpy as jnp
from jax import lax
from jax.experimental import pallas as pl
from jax.experimental.pallas import tpu as pltpu
from jax.sharding import PartitionSpec as P

C = 256
E = 1536
SE = 64
HEAD = 1280
CLASSES = 1000
L = 2
S = 12


EPS_NORM = 1e-05
BETA_ONE = 0.9
BETA_TWO = 0.99
EPS_ADAM = 1e-08
DECAY = 0.01
RATE = 0.3
KEEP = 0.9


def contract(left, right, left_dim, right_dim):
    return lax.dot_general(
        left, right, (((left_dim,), (right_dim,)), ((), ())), preferred_element_type=jnp.float32
    )


def matmul(left, right):
    return jnp.dot(left, right, precision=lax.Precision.HIGHEST, preferred_element_type=jnp.float32)


def matmul_bt(left, right):
    return lax.dot_general(
        left,
        right,
        (((1,), (1,)), ((), ())),
        precision=lax.Precision.HIGHEST,
        preferred_element_type=jnp.float32,
    )


def matmul_tb(left, right):
    return lax.dot_general(
        left,
        right,
        (((0,), (0,)), ((), ())),
        precision=lax.Precision.HIGHEST,
        preferred_element_type=jnp.float32,
    )


def pack_gains(vectors, rows):
    return jnp.concatenate([vector.reshape(rows, -1) for vector in vectors], 1)


IMGS = 5
ROWS = S * S
BATCHES = 2
HALF = IMGS * ROWS
FULL = BATCHES * HALF
SLOTS = BATCHES * IMGS
LANES = 128
EC = E // LANES
HC = HEAD // LANES
GAP = 16
TILE = 48
TILE_BACK = 48
CLASS_PAD = 1024
FACT = CLASS_PAD + 384
OFFSETS = [S * (a - 1) + (c - 1) for a in range(3) for c in range(3)]
MESH = pl.DeviceIdType.MESH
F32 = jnp.float32
BF16 = jnp.bfloat16


class Sum:
    def __init__(self, near, far, total, sems, sizes, rows):
        self.near, self.far, self.total = near, far, total
        self.sems = sems
        self.n_dp, self.n_sh = sizes
        self.rows = rows

    def copy_near(self, step, slot, target):
        d = lax.axis_index("dp")
        return pltpu.make_async_remote_copy(
            self.near.at[slot], self.near.at[slot],
            self.sems[0].at[step], self.sems[1].at[slot],
            device_id=(d, target), device_id_type=MESH)

    def copy_far(self, step, slot, target):
        s = lax.axis_index("shard")
        return pltpu.make_async_remote_copy(
            self.far.at[slot], self.far.at[slot],
            self.sems[2].at[step], self.sems[3].at[slot],
            device_id=(target, s), device_id_type=MESH)

    def start(self, stage):
        s = lax.axis_index("shard")
        self.near[s] = stage[0 : self.rows]
        for j in range(1, self.n_sh):
            self.copy_near(j, s, lax.rem(s + j, self.n_sh)).start()

    def middle(self):
        s, d = lax.axis_index("shard"), lax.axis_index("dp")
        for j in range(1, self.n_sh):
            self.copy_near(j, lax.rem(s + j, self.n_sh), s).wait_recv()
        for j in range(1, self.n_sh):
            self.copy_near(j, s, s).wait_send()
        part = self.near[0]
        for j in range(1, self.n_sh):
            part = part + self.near[j]
        self.far[d] = part

        def send(j, carry):
            self.copy_far(j, d, lax.rem(d + j, self.n_dp)).start()
            return carry

        lax.fori_loop(1, self.n_dp, send, 0)

    def finish(self):
        d = lax.axis_index("dp")

        def arrive(j, carry):
            self.copy_far(j, lax.rem(d + j, self.n_dp), d).wait_recv()
            self.copy_far(j, d, d).wait_send()
            return carry

        lax.fori_loop(1, self.n_dp, arrive, 0)
        part = self.far[0]
        for j in range(1, self.n_dp):
            part = part + self.far[j]
        self.total[0 : self.rows] = part


def sum_scratch(sizes, rows):
    n_dp, n_sh = sizes
    return [
        pltpu.VMEM((n_sh, rows, LANES), F32),
        pltpu.VMEM((n_dp, rows, LANES), F32),
        pltpu.SemaphoreType.DMA((n_sh,)),
        pltpu.SemaphoreType.DMA((n_sh,)),
        pltpu.SemaphoreType.DMA((n_dp,)),
        pltpu.SemaphoreType.DMA((n_dp,)),
    ]


def greet(sizes):
    n_dp, n_sh = sizes
    d, s = lax.axis_index("dp"), lax.axis_index("shard")
    gate = pltpu.get_barrier_semaphore()
    for j in range(1, n_sh):
        pl.semaphore_signal(gate, inc=1, device_id=(d, lax.rem(s + j, n_sh)), device_id_type=MESH)

    def signal(j, carry):
        pl.semaphore_signal(gate, inc=1, device_id=(lax.rem(d + j, n_dp), s), device_id_type=MESH)
        return carry

    lax.fori_loop(1, n_dp, signal, 0)
    pl.semaphore_wait(gate, n_sh + n_dp - 2)


def repeat(count, body, hook=None):
    def step(i, carry):
        if hook is not None:

            @pl.when(i == hook[0])
            def _():
                hook[1]()

        body(i)
        return carry

    lax.fori_loop(0, count, step, 0)


def lanes(c, width=LANES):
    return pl.ds(pl.multiple_of(c * width, width), width)


def coefs(total, row, count, gain, shift):
    mean = total[pl.ds(row, 1), :] / count
    square = total[pl.ds(row + 1, 1), :] / count
    scale = gain * lax.rsqrt(square - mean * mean + EPS_NORM)
    return scale, shift - mean * scale


def act_half(half):
    return half + half * jnp.tanh(half)


def forward_kernel(sizes, *refs):
    (images, mask, edge_l, edge_r, area, firstrow, vec_own, labels, weights_of, expand_w, expand_e, chan_w, chan_e,
     head_w, head_e, class_w, class_e,
     pre_s, mixed_s, feat_s, out_s, low_s, pool_s, unit_s, gate_s, tot_e, tot_c, tot_h,
     dpool_h, extra, facts, wexp_s, headt_s, chan_s, gain_e_s, gain_c_s, gain_h_s,
     pre, hid, out_t, low_t, scaled, pads, stages, totals, cnt, pool_t, gate_t, save_sems,
     wexp, chan, headt, classes, vecs, gain_e, gain_c, gain_h, gain_s, gain_k, pooled_h, bias_row,
     st_exp, st_chan, st_head, st_class, load_sems, sx, rx, sc, rc, sf, rf, out_sems) = refs[:73]
    rest = list(refs[73:])
    n_sh = sizes[1]
    sums = []
    for m in range(2):
        group = []
        for rows in (56, 48, 8, 40):
            near, far = rest[0], rest[1]
            group.append((near, far, rest[2:6], rows))
            rest = rest[6:]
        sums.append(group)

    d, s = lax.axis_index("dp"), lax.axis_index("shard")
    near_peer = s + 1 - 2 * lax.rem(s, 2)
    far_peer = s + 2 - 4 * (s // 2)
    far_near = near_peer + 2 - 4 * (s // 2)
    pieces = [("exp", 0, 0, 0), ("exp", 1, 0, 0), ("vec", 0, 0, 0), ("chan", 0, 0, 0), ("exp", 0, 0, 1), ("exp", 1, 0, 1),
              ("exp", 0, 1, 0), ("exp", 1, 1, 0), ("chan", 0, 1, 0), ("exp", 0, 1, 1), ("exp", 1, 1, 1),
              ("head", 0, 0, 0), ("class", 0, 0, 0), ("class", 1, 0, 0)]
    mats = [k for k, piece in enumerate(pieces) if piece[0] == "exp"]

    def region(k, source):
        kind, m, layer, half = pieces[k]
        if kind == "exp":
            return wexp.at[m, layer, pl.ds(pl.multiple_of(source * 64, 64), 64), half * E : (half + 1) * E]
        if kind == "chan":
            return chan.at[:, layer, :, pl.ds(pl.multiple_of(source * 384, 384), 384)]
        if kind == "vec":
            return vecs.at[source]
        if kind == "head":
            return headt.at[:, pl.ds(pl.multiple_of(source * 320, 320), 320), :]
        return classes.at[m, pl.ds(pl.multiple_of(source * 320, 320), 320), :]

    def loads(k):
        kind, m, layer, half = pieces[k]
        if kind == "exp":
            slot = mats.index(k) % 2
            source = (expand_w, expand_e)[m].at[layer, :, half * E : (half + 1) * E]
            return [pltpu.make_async_copy(source, st_exp.at[slot], load_sems.at[slot])]
        if kind == "chan":
            return [pltpu.make_async_copy((chan_w, chan_e)[i].at[:, layer], st_chan.at[i], load_sems.at[2 + i]) for i in range(2)]
        if kind == "head":
            return [pltpu.make_async_copy((head_w, head_e)[i], st_head.at[i], load_sems.at[4 + i]) for i in range(2)]
        if kind == "class":
            return [pltpu.make_async_copy((class_w, class_e)[m], st_class, load_sems.at[6])]
        return []

    def fetch(k):
        for copy in loads(k):
            copy.start()

    def cast(k):
        kind, m, layer, half = pieces[k]
        for copy in loads(k):
            copy.wait()
        if kind == "exp":
            order = mats.index(k)
            wexp[m, layer, pl.ds(pl.multiple_of(s * 64, 64), 64), half * E : (half + 1) * E] = st_exp[order % 2].astype(BF16)
            if order + 2 < len(mats):
                fetch(mats[order + 2])
        if kind == "chan":
            cols = pl.ds(pl.multiple_of(s * 384, 384), 384)
            for i in range(2):
                padded = jnp.concatenate([st_chan[i, 0:9, :], jnp.zeros((7, 384), F32)], 0)
                chan[i, layer, 0:16, cols] = padded.astype(BF16)
                chan[i, layer, 16:80, cols] = st_chan[i, 9 : 9 + SE, :].astype(BF16)
                chan[i, layer, 80:144, cols] = st_chan[i, 9 + SE : 9 + 2 * SE, :].astype(BF16)
            if layer == 0:
                fetch(pieces.index(("chan", 0, 1, 0)))
        if kind == "head":
            for i in range(2):
                headt[i, pl.ds(pl.multiple_of(s * 320, 320), 320), :] = st_head[i].astype(BF16)
        if kind == "class":
            classes[m, pl.ds(pl.multiple_of(s * 320, 320), 320), :] = st_class[...].astype(BF16)
            if m == 0:
                fetch(k + 1)
        if kind == "vec":
            vecs[s] = vec_own[...]

    def hop(k, source, target, send, receive):
        return pltpu.make_async_remote_copy(
            region(k, source), region(k, source), send.at[k], receive.at[k],
            device_id=(d, target), device_id_type=MESH)

    def offer(k):
        cast(k)
        hop(k, s, far_peer, sx, rx).start()
        hop(k, s, near_peer, sc, rc).start()

    def forward_on(k):
        hop(k, far_peer, s, sx, rx).wait_recv()
        hop(k, far_peer, near_peer, sf, rf).start()

    def ready(k):
        hop(k, near_peer, s, sc, rc).wait_recv()
        hop(k, far_near, s, sf, rf).wait_recv()

    def settle():
        for k in range(len(pieces)):
            hop(k, s, far_peer, sx, rx).wait_send()
            hop(k, s, near_peer, sc, rc).wait_send()
            hop(k, far_peer, near_peer, sf, rf).wait_send()

    def join(m, row, low, width):
        return jnp.concatenate([vecs[t, m, 0:16, :].astype(F32)[row : row + 1, low : low + width] for t in range(n_sh)], 1)

    def unpack_vectors():
        for m in range(2):
            for layer in range(L):
                for t in range(n_sh):
                    gain_e[m, layer, 0:5, 384 * t : 384 * t + 384] = vecs[t, m].astype(F32)[6 * layer : 6 * layer + 5, :]
                gain_c[m, layer, 0:1, :] = join(m, 6 * layer + 5, 0, 64)
                gain_c[m, layer, 1:2, :] = join(m, 6 * layer + 5, 64, 64)
                gain_s[m, layer, 0:1, :] = join(m, 6 * layer + 5, 128, 16)
            gain_h[m, 0:1, :] = join(m, 12, 0, 320)
            gain_h[m, 1:2, :] = join(m, 13, 0, 320)
            gain_k[m, 0:1, :] = join(m, 14, 0, 250)

    for k in (0, 1, 3, 11, 12):
        fetch(k)
    greet(sizes)
    for k in (0, 1, 2, 3):
        offer(k)

    def low(m, layer):
        return low_s.at[layer] if m == 0 else low_t

    def out(m, layer):
        return out_s.at[layer] if m == 0 else out_t

    def total_ref(m, kind, layer):
        if m == 0:
            return (tot_e.at[layer, 0], tot_e.at[layer, 1], tot_c.at[layer], tot_h)[kind]
        return totals.at[kind]

    def summer(m, kind, layer):
        near, far, sems, rows = sums[m][kind]
        return Sum(near, far, total_ref(m, kind, layer), sems, sizes, rows)

    def save(src, dst, index):
        return pltpu.make_async_copy(src, dst, save_sems.at[index])

    for slot in range(SLOTS):
        pads[slot, 0:GAP, :] = jnp.zeros((GAP, LANES), F32)
        pads[slot, GAP + ROWS : 2 * GAP + ROWS, :] = jnp.zeros((GAP, LANES), F32)

    def store_wexp(layer):
        return pltpu.make_async_copy(wexp.at[0, layer], wexp_s.at[layer], out_sems.at[layer])

    store_headt = pltpu.make_async_copy(headt.at[0], headt_s, out_sems.at[L])
    store_chan = pltpu.make_async_copy(chan.at[0], chan_s, out_sems.at[L + 1])

    def load_rows(i):
        rows = pl.ds(pl.multiple_of(i * ROWS, ROWS), ROWS)
        for half in range(2):
            cols = slice(half * LANES, half * LANES + LANES)
            value = images[rows, cols].astype(F32) * mask[rows, :]
            hid[0, rows, cols] = value
            hid[1, rows, cols] = value
            low_s[0, rows, cols] = value.astype(BF16)
            low_t[rows, cols] = value.astype(BF16)

    repeat(SLOTS, load_rows)

    def update(m, layer):
        tot = total_ref(m, 2, layer)
        for half in range(2):
            cols = slice(half * LANES, half * LANES + LANES)
            for b in range(BATCHES):
                scale, shift = coefs(tot, 4 * half + 2 * b, cnt[b : b + 1, :], gain_c[m, layer, 0:1, cols], gain_c[m, layer, 1:2, cols])

                def one(i):
                    rows = pl.ds(pl.multiple_of(b * HALF + i * ROWS, ROWS), ROWS)
                    value = hid[m, rows, cols] + mask[rows, :] * (out(m, layer)[rows, cols] * scale + shift)
                    hid[m, rows, cols] = value
                    low(m, layer + 1)[rows, cols] = value.astype(BF16)

                repeat(IMGS, one)

    def put_sums(stage, chunk, b, value):
        stage[pl.ds(4 * chunk + 2 * b, 1), :] = jnp.sum(value, 0, keepdims=True)
        stage[pl.ds(4 * chunk + 2 * b + 1, 1), :] = jnp.sum(value * value, 0, keepdims=True)

    def expand(m, layer, hook=None):
        stage = stages.at[m]

        def body(c):
            weight = wexp[m, layer, :, lanes(c, 256)]
            for b in range(BATCHES):
                value = jnp.dot(low(m, layer)[b * HALF : (b + 1) * HALF, :], weight, preferred_element_type=F32)
                for half in range(2):
                    piece = value[:, half * LANES : (half + 1) * LANES]
                    pre[m, 2 * c + half, b * HALF : (b + 1) * HALF, :] = piece
                    put_sums(stage, 2 * c + half, b, piece)
            if m == 0:
                for half in range(2):
                    save(pre.at[0, 2 * c + half], pre_s.at[layer, 2 * c + half], 2 * c + half).start()

        repeat(E // 256, body, hook)

    def depthwise(m, layer, hook=None):
        stage = stages.at[m]
        tot = total_ref(m, 0, layer)

        def body(c):
            if m == 0:
                save(pre.at[0, c], pre_s.at[layer, c], c).wait()
            tap_rows = chan[m, layer, 0:16, lanes(c)].astype(F32)
            tap = [tap_rows[k : k + 1, :] for k in range(9)]
            for b in range(BATCHES):
                scale, shift = coefs(tot, 4 * c + 2 * b, cnt[b : b + 1, :], gain_e[m, layer, 0:1, lanes(c)], gain_e[m, layer, 1:2, lanes(c)])
                scale, shift = 0.5 * scale, 0.5 * shift
                for i in range(IMGS):
                    slot = b * IMGS + i
                    rows = slice(slot * ROWS, (slot + 1) * ROWS)
                    half = mask[rows, :] * (pre[m, c, rows, :] * scale + shift)
                    pads[slot, GAP : GAP + ROWS, :] = act_half(half)
                first = jnp.zeros((8, LANES), F32)
                second = jnp.zeros((8, LANES), F32)
                for i in range(IMGS):
                    slot = b * IMGS + i
                    for t in range(ROWS // TILE):
                        start = GAP + t * TILE
                        near = [pads[slot, start + o : start + o + TILE, :] for o in OFFSETS]
                        left = near[0] * tap[0] + near[3] * tap[3] + near[6] * tap[6]
                        mid = near[1] * tap[1] + near[4] * tap[4] + near[7] * tap[7]
                        right = near[2] * tap[2] + near[5] * tap[5] + near[8] * tap[8]
                        rows = slice(slot * ROWS + t * TILE, slot * ROWS + (t + 1) * TILE)
                        value = mask[rows, :] * (mid + edge_l[0:TILE, :] * left + edge_r[0:TILE, :] * right)
                        pre[m, c, rows, :] = value
                        first = first + jnp.sum(value.reshape(TILE // 8, 8, LANES), 0)
                        second = second + jnp.sum((value * value).reshape(TILE // 8, 8, LANES), 0)
                stage[pl.ds(4 * c + 2 * b, 1), :] = jnp.sum(first, 0, keepdims=True)
                stage[pl.ds(4 * c + 2 * b + 1, 1), :] = jnp.sum(second, 0, keepdims=True)
            if m == 0:
                save(pre.at[0, c], mixed_s.at[layer, c], c).start()

        repeat(EC, body, hook)

    def pooling(m, layer, hook=None):
        tot = total_ref(m, 1, layer)
        pool = pool_s.at[layer] if m == 0 else pool_t

        def body(c):
            if m == 0:
                save(pre.at[0, c], mixed_s.at[layer, c], c).wait()
            for b in range(BATCHES):
                scale, shift = coefs(tot, 4 * c + 2 * b, cnt[b : b + 1, :], gain_e[m, layer, 2:3, lanes(c)], gain_e[m, layer, 3:4, lanes(c)])
                scale, shift = 0.5 * scale, 0.5 * shift
                for i in range(IMGS):
                    slot = b * IMGS + i
                    rows = slice(slot * ROWS, (slot + 1) * ROWS)
                    value = act_half(mask[rows, :] * (pre[m, c, rows, :] * scale + shift))
                    pre[m, c, rows, :] = value
                    pool[b * 8 + i : b * 8 + i + 1, lanes(c)] = jnp.sum(value, 0, keepdims=True) / area[0:1, :]

        repeat(EC, body, hook)

    def project(m, layer):
        pool = pool_s.at[layer] if m == 0 else pool_t
        gate = gate_s.at[layer] if m == 0 else gate_t
        units = matmul_bt(pool[...], chan[m, layer, 16:80, :].astype(F32)) + gain_s[m, layer, 0:1, :]
        if m == 0:
            unit_s[layer] = units
        gate[...] = jax.nn.sigmoid(matmul(jax.nn.silu(units), chan[m, layer, 80:144, :].astype(F32)) + gain_e[m, layer, 4:5, :])

        def body(c):
            for b in range(BATCHES):
                for i in range(IMGS):
                    rows = slice(b * HALF + i * ROWS, b * HALF + (i + 1) * ROWS)
                    scaled[rows, lanes(c)] = (pre[m, c, rows, :] * gate[b * 8 + i : b * 8 + i + 1, lanes(c)]).astype(BF16)

        repeat(EC, body)
        stage = stages.at[m]
        for b in range(BATCHES):
            rows = slice(b * HALF, (b + 1) * HALF)
            value = contract(scaled[rows, :], wexp[m, layer, :, E : 2 * E], 1, 1)
            out(m, layer)[rows, :] = value
            for half in range(2):
                put_sums(stage, half, b, value[:, half * LANES : (half + 1) * LANES])

    def features(m, hook=None):
        stage = stages.at[m]

        def body(c):
            weight = headt[m, pl.ds(pl.multiple_of(c * 256, 256), 256), :]
            for b in range(BATCHES):
                value = contract(low(m, L)[b * HALF : (b + 1) * HALF, :], weight, 1, 1)
                for half in range(2):
                    piece = value[:, half * LANES : (half + 1) * LANES]
                    pre[m, 2 * c + half, b * HALF : (b + 1) * HALF, :] = piece
                    put_sums(stage, 2 * c + half, b, piece)
            if m == 0:
                for half in range(2):
                    save(pre.at[0, 2 * c + half], feat_s.at[2 * c + half], 2 * c + half).start()

        repeat(HEAD // 256, body, hook)

    def head_pool(m, hook=None):
        tot = total_ref(m, 3, 0)

        def body(c):
            for b in range(BATCHES):
                scale, shift = coefs(tot, 4 * c + 2 * b, cnt[b : b + 1, :], gain_h[m, 0:1, lanes(c)], gain_h[m, 1:2, lanes(c)])
                scale, shift = 0.5 * scale, 0.5 * shift
                for i in range(IMGS):
                    slot = b * IMGS + i
                    rows = slice(slot * ROWS, (slot + 1) * ROWS)
                    value = act_half(mask[rows, :] * (pre[m, c, rows, :] * scale + shift))
                    pooled_h[m, b * 8 + i : b * 8 + i + 1, lanes(c)] = jnp.sum(value, 0, keepdims=True) / area[0:1, :]

        repeat(HC, body, hook)

    for m in range(2):
        stages[m] = jnp.zeros((56, LANES), F32)
    pool_s[...] = jnp.zeros(pool_s.shape, F32)
    pool_t[...] = jnp.zeros(pool_t.shape, F32)
    pooled_h[...] = jnp.zeros(pooled_h.shape, F32)
    stages[0, 48:56, :] = firstrow[...]
    pending = None
    forward_on(0)
    ready(0)
    for layer in range(L):
        s_one, t_one = summer(0, 0, layer), summer(1, 0, layer)
        s_two, t_two = summer(0, 1, layer), summer(1, 1, layer)
        s_three, t_three = summer(0, 2, layer), summer(1, 2, layer)
        if layer > 0:
            update(0, layer - 1)
            ready(6)
        expand(0, layer, None if pending is None else (2, pending.middle))
        s_one.start(stages.at[0])
        if layer == 0:
            forward_on(1)
            ready(1)
            forward_on(2)
            offer(4)
        else:
            forward_on(8)
            pending.finish()
            update(1, layer - 1)
            ready(7)
            offer(10)
        expand(1, layer, (4, s_one.middle))
        t_one.start(stages.at[1])
        if layer == 0:
            forward_on(3)
            ready(2)
            unpack_vectors()
            ready(3)
            offer(5)
        else:
            forward_on(9)
            ready(8)
            offer(11)
        s_one.finish()
        if layer == 0:
            cnt[...] = tot_e[0, 0, 48:56, :]
        depthwise(0, layer, (2, t_one.middle))
        s_two.start(stages.at[0])
        forward_on((4, 10)[layer])
        offer((6, 12)[layer])
        t_one.finish()
        depthwise(1, layer, (5, s_two.middle))
        t_two.start(stages.at[1])
        forward_on((5, 11)[layer])
        if layer == 0:
            offer(7)
        ready((4, 9)[layer])
        s_two.finish()
        pooling(0, layer, (5, t_two.middle))
        project(0, layer)
        s_three.start(stages.at[0])
        forward_on((6, 12)[layer])
        offer((8, 13)[layer])
        ready((5, 10)[layer])
        t_two.finish()
        pooling(1, layer, (6, s_three.middle))
        project(1, layer)
        t_three.start(stages.at[1])
        if layer == 0:
            forward_on(7)
            offer(9)
        s_three.finish()
        pending = t_three
    for layer in range(L):
        store_wexp(layer).start()
    s_head, t_head = summer(0, 3, 0), summer(1, 3, 0)
    update(0, L - 1)
    ready(11)
    features(0, (2, pending.middle))
    s_head.start(stages.at[0])
    pending.finish()
    update(1, L - 1)
    features(1, (4, s_head.middle))
    t_head.start(stages.at[1])
    forward_on(13)
    store_headt.start()
    store_chan.start()
    s_head.finish()
    head_pool(0, (3, t_head.middle))
    ready(12)
    t_head.finish()
    head_pool(1)
    ready(13)

    def class_logits(m):
        low_pool = pooled_h[m].astype(BF16)
        return jnp.dot(low_pool, classes[m], preferred_element_type=F32) + gain_k[m, 0:1, :]

    def log_softmax(value):
        value = value - jnp.max(value, 1, keepdims=True)
        return value - jnp.log(jnp.sum(jnp.exp(value), 1, keepdims=True))

    logp = log_softmax(class_logits(0))
    target = log_softmax(class_logits(1))
    expected = jnp.exp(target)
    hot = lax.broadcasted_iota(jnp.int32, (16, CLASSES), 1) == labels[...]
    total_weight = tot_e[0, 0, 50:51, :] + tot_e[0, 0, 51:52, :]
    coef = weights_of[:, 0:1] / total_weight[:, 0:1]
    per = jnp.sum(expected * (target - logp), 1, keepdims=True) - jnp.sum(jnp.where(hot, logp, 0.0), 1, keepdims=True)
    loss = jnp.sum(coef * per, 0, keepdims=True)
    slope = -coef * (jnp.where(hot, 1.0, 0.0) + expected)
    grad_low = (slope - jnp.exp(logp) * jnp.sum(slope, 1, keepdims=True)).astype(BF16)
    bias_row[...] = jnp.zeros(bias_row.shape, F32)
    bias_row[0:1, 0:CLASSES] = jnp.sum(grad_low.astype(F32), 0, keepdims=True)
    for k in range(8):
        extra[k : k + 1, :] = bias_row[0:1, k * LANES : (k + 1) * LANES]
    extra[8:16, :] = jnp.broadcast_to(loss, (8, LANES))
    dpool_h[...] = contract(grad_low, classes[0], 1, 1) / area[0:1, 0:1]
    facts[...] = jnp.zeros(facts.shape, BF16)
    low_pool = pooled_h[0].astype(BF16)
    for t in range(n_sh):
        facts[t, :, 0:CLASSES] = grad_low
        facts[t, :, CLASS_PAD : CLASS_PAD + 320] = low_pool[:, 320 * t : 320 * t + 320]
    gain_e_s[...] = gain_e[0]
    gain_c_s[...] = gain_c[0]
    gain_h_s[...] = gain_h[0]
    settle()
    for layer in range(L):
        store_wexp(layer).wait()
    store_headt.wait()
    store_chan.wait()
    for c in range(HC):
        save(pre.at[0, c], feat_s.at[c], c).wait()


def run_forward_all(sizes, inputs):
    sds = jax.ShapeDtypeStruct
    vm = pl.BlockSpec(memory_space=pltpu.VMEM)
    hbm = pl.BlockSpec(memory_space=pl.ANY)
    n_sh = sizes[1]
    outs = [
        (sds((L, EC, FULL, LANES), F32), hbm),
        (sds((L, EC, FULL, LANES), F32), hbm),
        (sds((HC, FULL, LANES), F32), hbm),
        (sds((L, FULL, C), F32), vm),
        (sds((L + 1, FULL, C), BF16), vm),
        (sds((L, 16, E), F32), vm),
        (sds((L, 16, SE), F32), vm),
        (sds((L, 16, E), F32), vm),
        (sds((L, 2, 56, LANES), F32), vm),
        (sds((L, 8, LANES), F32), vm),
        (sds((40, LANES), F32), vm),
        (sds((16, HEAD), F32), vm),
        (sds((16, LANES), F32), vm),
        (sds((n_sh, 16, FACT), BF16), vm),
        (sds((L, C, 2 * E), BF16), hbm),
        (sds((HEAD, C), BF16), hbm),
        (sds((L, 144, E), BF16), hbm),
        (sds((L, 8, E), F32), vm),
        (sds((L, 8, C), F32), vm),
        (sds((8, HEAD), F32), vm),
    ]
    scratch = [
        pltpu.VMEM((2, EC, FULL, LANES), F32),
        pltpu.VMEM((2, FULL, C), F32),
        pltpu.VMEM((FULL, C), F32),
        pltpu.VMEM((FULL, C), BF16),
        pltpu.VMEM((FULL, E), BF16),
        pltpu.VMEM((SLOTS, ROWS + 2 * GAP, LANES), F32),
        pltpu.VMEM((2, 56, LANES), F32),
        pltpu.VMEM((4, 56, LANES), F32),
        pltpu.VMEM((8, LANES), F32),
        pltpu.VMEM((16, E), F32),
        pltpu.VMEM((16, E), F32),
        pltpu.SemaphoreType.DMA((EC,)),
        pltpu.VMEM((2, L, C, 2 * E), BF16),
        pltpu.VMEM((2, L, 144, E), BF16),
        pltpu.VMEM((2, HEAD, C), BF16),
        pltpu.VMEM((2, HEAD, CLASSES), BF16),
        pltpu.VMEM((n_sh, 2, 16, 384), BF16),
        pltpu.VMEM((2, L, 8, E), F32),
        pltpu.VMEM((2, L, 8, C), F32),
        pltpu.VMEM((2, 8, HEAD), F32),
        pltpu.VMEM((2, L, 8, SE), F32),
        pltpu.VMEM((2, 8, CLASSES), F32),
        pltpu.VMEM((2, 16, HEAD), F32),
        pltpu.VMEM((8, CLASS_PAD), F32),
        pltpu.VMEM((2, 64, E), F32),
        pltpu.VMEM((2, 137, 384), F32),
        pltpu.VMEM((2, 320, C), F32),
        pltpu.VMEM((320, CLASSES), F32),
        pltpu.SemaphoreType.DMA((7,)),
    ]
    scratch = scratch + [pltpu.SemaphoreType.DMA((14,))] * 6 + [pltpu.SemaphoreType.DMA((L + 2,))]
    for m in range(2):
        for rows in (56, 48, 8, 40):
            scratch = scratch + sum_scratch(sizes, rows)
    return pl.pallas_call(
        functools.partial(forward_kernel, sizes),
        out_shape=[o[0] for o in outs],
        in_specs=[vm] * 9 + [hbm] * 8,
        out_specs=[o[1] for o in outs],
        scratch_shapes=scratch,
        compiler_params=pltpu.CompilerParams(collective_id=1, has_side_effects=True, vmem_limit_bytes=63 * 2**20),
        name="forward",
    )(*inputs)


BACK_ROWS = ((24, 24, 8, 24), (40, 24, 8, 40))


def round_up(value, unit):
    return -(-value // unit) * unit


CHUNKS = 6
MATS = 2 * E // LANES * 8
CHAN = 3 * 18
AT_CHAN = L * MATS
AT_HEAD = AT_CHAN + L * CHAN
AT_END = AT_HEAD + 2 * HEAD // 4 // 8


def packed_blocks(sizes):
    return round_up(AT_END, CHUNKS * 2 * sizes[0])


def backward_kernel(sizes, *refs):
    (dpool_h, extra, mask, edge_l, edge_r, area, wexp, headt, chan, gain_e, gain_c, gain_h,
     pre_s, mixed_s, feat_s, out_s, low_s, pool_s, unit_s, gate_s, tot_e, tot_c, tot_h,
     packed, back_e, back_c, back_h,
     pre, mixed, grad, grad_hid, low_out, low_pre, pads_x, pads_g, slope, dgate, dpool, stages, load_sems,
     held, held_chan, held_exb, held_sqb, out_v, low_v, row_sems) = refs[:47]
    rest = list(refs[47:])
    n_dp, n_sh = sizes
    sums = []
    for b in range(BATCHES):
        group = []
        for rows in BACK_ROWS[b]:
            group.append((rest[0], rest[1], rest[2:6], rows))
            rest = rest[6:]
        sums.append(group)

    greet(sizes)

    def back_ref(b, kind, layer):
        return (back_e.at[layer, b, 0], back_e.at[layer, b, 1], back_c.at[layer, b], back_h.at[b])[kind]

    def summer(b, kind, layer):
        near, far, sems, rows = sums[b][kind]
        return Sum(near, far, back_ref(b, kind, layer), sems, sizes, rows)

    def load(b, kind, layer):
        rows = slice(b * HALF, (b + 1) * HALF)
        if kind == 0:
            return pltpu.make_async_copy(pre_s.at[layer, :, rows], pre.at[b], load_sems.at[b, 0])
        if kind == 1:
            return pltpu.make_async_copy(mixed_s.at[layer, :, rows], mixed.at[b], load_sems.at[b, 1])
        return pltpu.make_async_copy(feat_s.at[:, rows], pre.at[b, 0:HC], load_sems.at[b, 0])

    def load_out(layer):
        return pltpu.make_async_copy(out_s.at[layer], out_v, row_sems.at[0])

    def load_low(layer):
        return pltpu.make_async_copy(low_s.at[layer], low_v, row_sems.at[1])

    for b in range(BATCHES):
        load(b, 2, 0).start()
    load_low(L).start()
    load_out(L - 1).start()
    for b in range(BATCHES):
        load(b, 1, L - 1).start()
    for slot in range(IMGS):
        for pads in (pads_x, pads_g):
            pads[slot, 0:GAP, :] = jnp.zeros((GAP, LANES), F32)
            pads[slot, GAP + ROWS : 2 * GAP + ROWS, :] = jnp.zeros((GAP, LANES), F32)
    dgate[...] = jnp.zeros(dgate.shape, F32)
    stages[...] = jnp.zeros(stages.shape, F32)
    stages[1, 24:40, :] = extra[...]
    held_chan[...] = jnp.zeros(held_chan.shape, F32)
    spare = packed.shape[1] - AT_END
    if spare:
        packed[:, AT_END:] = jnp.zeros((n_sh, spare, 8, LANES), F32)

    def pack(first, c, value):
        for t in range(n_sh):
            for half in range(2):
                piece = value[64 * t : 64 * t + 64, half * LANES : (half + 1) * LANES]
                packed[t, pl.ds(first + 16 * c + 8 * half, 8)] = piece.reshape(8, 8, LANES)

    def pack_chan(layer):
        for k in range(EC):
            first = AT_CHAN + CHAN * layer + 18 * (k % 3)
            packed[k // 3, first : first + 18] = held_chan[:, k * LANES : (k + 1) * LANES].reshape(18, 8, LANES)

    def forward_total(kind, layer):
        return (tot_e.at[layer, 0], tot_e.at[layer, 1], tot_c.at[layer], tot_h)[kind]

    def moments(b, kind, layer, c):
        tot = forward_total(kind, layer)
        count = tot_e[0, 0, 48 + b : 49 + b, :]
        mean = tot[pl.ds(4 * c + 2 * b, 1), :] / count
        square = tot[pl.ds(4 * c + 2 * b + 1, 1), :] / count
        return mean, lax.rsqrt(square - mean * mean + EPS_NORM)

    def half_coefs(b, kind, layer, c, gain, shift):
        mean, scale = moments(b, kind, layer, c)
        scale = scale * gain
        return 0.5 * scale, 0.5 * (shift - mean * scale)

    def back_coefs(b, kind, layer, c, gain):
        mean, scale = moments(b, kind, layer, c)
        count = tot_e[0, 0, 48 + b : 49 + b, :]
        back = back_ref(b, kind, layer)
        plain = back[pl.ds(2 * c, 1), :]
        cross = scale * (back[pl.ds(2 * c + 1, 1), :] - mean * plain)
        first = scale * gain
        third = -first * scale * cross / count
        return first, -first * plain / count - mean * third, third

    def fold(value):
        return jnp.sum(value.reshape(value.shape[0] // 8, 8, LANES), 0)

    def put(stage, c, first, second):
        stage[pl.ds(2 * c, 1), :] = jnp.sum(first, 0, keepdims=True)
        stage[pl.ds(2 * c + 1, 1), :] = jnp.sum(second, 0, keepdims=True)

    def image(b, i):
        return slice(i * ROWS, (i + 1) * ROWS), slice(b * HALF + i * ROWS, b * HALF + (i + 1) * ROWS)

    def bend(half):
        t = jnp.tanh(half)
        return half + half * t, (0.5 + 0.5 * t) * (1.0 + half * (1.0 - t))

    def head_first(b, hook=None):
        stage = stages.at[b]

        def body(c):
            scale, shift = half_coefs(b, 3, 0, c, gain_h[0:1, lanes(c)], gain_h[1:2, lanes(c)])
            first = jnp.zeros((8, LANES), F32)
            second = jnp.zeros((8, LANES), F32)
            for i in range(IMGS):
                rows, full = image(b, i)
                x = pre[b, c, rows, :]
                half = mask[full, :] * (x * scale + shift)
                value = mask[full, :] * dpool_h[b * 8 + i : b * 8 + i + 1, lanes(c)] * bend(half)[1]
                grad[b, c, rows, :] = value
                first = first + fold(value)
                second = second + fold(value * x)
            put(stage, c, first, second)

        repeat(HC, body, hook)

    def norm_back_rows(b, kind, layer, c, gain, source):
        one, two, three = back_coefs(b, kind, layer, c, gain)
        for i in range(IMGS):
            rows, full = image(b, i)
            value = mask[full, :] * (one * grad[b, c, rows, :] + two + three * source[b, c, rows, :])
            low_pre[rows, lanes(c)] = value.astype(BF16)

    def put_hidden_sums(b, layer):
        stage = stages.at[b]
        for half in range(2):
            cols = slice(half * LANES, (half + 1) * LANES)
            first = jnp.zeros((8, LANES), F32)
            second = jnp.zeros((8, LANES), F32)
            for i in range(IMGS):
                full = image(b, i)[1]
                value = grad_hid[full, cols]
                first = first + fold(value)
                second = second + fold(value * out_v[full, cols])
            put(stage, half, first, second)

    def head_second(b, hook=None):
        mine = slice(b * HALF, (b + 1) * HALF)

        def body(c):
            for half in range(2):
                norm_back_rows(b, 3, 0, 2 * c + half, gain_h[0:1, lanes(2 * c + half)], pre)
            value = contract(low_pre[:, lanes(c, 256)], low_v[mine, :], 0, 0)
            if b == 0:
                held[c] = value
            else:
                value = value + held[c]
                for i in range(32):
                    row = 32 * c + i
                    for half in range(2):
                        packed[row // 40, AT_HEAD + 40 * half + lax.rem(row, 40)] = value[8 * i : 8 * i + 8, half * LANES : (half + 1) * LANES]

        repeat(HEAD // 256, body, hook)
        grad_hid[mine, :] = jnp.dot(low_pre[:, 0:HEAD], headt[...], preferred_element_type=F32)
        put_hidden_sums(b, L - 1)

    def block_gate(b, layer, hook=None):
        mine = slice(b * HALF, (b + 1) * HALF)
        eight = slice(b * 8, b * 8 + 8)
        for half in range(2):
            cols = slice(half * LANES, (half + 1) * LANES)
            one, two, three = back_coefs(b, 2, layer, half, gain_c[layer, 0:1, cols])
            for i in range(IMGS):
                rows, full = image(b, i)
                low_out[rows, cols] = (mask[full, :] * (one * grad_hid[full, cols] + two + three * out_v[full, cols])).astype(BF16)

        def body(c):
            value = jnp.dot(low_out[...], wexp[layer, :, lanes(E // 256 + c, 256)], preferred_element_type=F32)
            for part in range(2):
                k = 2 * c + part
                scale, shift = half_coefs(b, 1, layer, k, gain_e[layer, 2:3, lanes(k)], gain_e[layer, 3:4, lanes(k)])
                for i in range(IMGS):
                    rows, full = image(b, i)
                    act = act_half(mask[full, :] * (mixed[b, k, rows, :] * scale + shift))
                    piece = value[rows, part * LANES : (part + 1) * LANES]
                    grad[b, k, rows, :] = piece
                    dgate[i : i + 1, lanes(k)] = jnp.sum(fold(piece * act), 0, keepdims=True)
                    low_pre[rows, lanes(k)] = (act * gate_s[layer, b * 8 + i : b * 8 + i + 1, lanes(k)]).astype(BF16)
            value = contract(low_out[...], low_pre[:, lanes(c, 256)], 0, 0)
            if b == 0:
                held[c] = value
            else:
                pack(MATS * layer + MATS // 2, c, value + held[c])

        repeat(E // 256, body, hook)
        gate = gate_s[layer, eight, :]
        units = unit_s[layer, eight, :]
        sig = jax.nn.sigmoid(units)
        inner = dgate[...] * gate * (1.0 - gate)
        bias_x = jnp.sum(inner, 0, keepdims=True)
        grad_x = matmul_tb(units * sig, inner)
        outer = matmul_bt(inner, chan[layer, 80:144, :].astype(F32)) * (sig * (1.0 + units * (1.0 - sig)))
        bias_r = jnp.sum(outer, 0, keepdims=True)
        grad_r = matmul_tb(outer, pool_s[layer, eight, :])
        if b == 0:
            held_exb[0:1, :] = bias_x
            held_chan[9 + SE : 9 + 2 * SE, :] = grad_x
            held_sqb[0:1, 0:SE] = bias_r
            held_chan[9 : 9 + SE, :] = grad_r
        else:
            bias_x = bias_x + held_exb[0:1, :]
            for k in range(EC):
                stages[1, 24 + k : 25 + k, :] = bias_x[:, k * LANES : (k + 1) * LANES]
            stages[1, 24 + EC : 25 + EC, 0:SE] = bias_r + held_sqb[0:1, 0:SE]
            held_chan[9 : 9 + SE, :] = held_chan[9 : 9 + SE, :] + grad_r
            held_chan[9 + SE : 9 + 2 * SE, :] = held_chan[9 + SE : 9 + 2 * SE, :] + grad_x
        dpool[...] = matmul(outer, chan[layer, 16:80, :].astype(F32))

    def block_second(b, layer, hook=None):
        stage = stages.at[b]

        def body(c):
            scale, shift = half_coefs(b, 1, layer, c, gain_e[layer, 2:3, lanes(c)], gain_e[layer, 3:4, lanes(c)])
            first = jnp.zeros((8, LANES), F32)
            second = jnp.zeros((8, LANES), F32)
            for i in range(IMGS):
                rows, full = image(b, i)
                x = mixed[b, c, rows, :]
                half = mask[full, :] * (x * scale + shift)
                gate = gate_s[layer, b * 8 + i : b * 8 + i + 1, lanes(c)]
                value = mask[full, :] * (grad[b, c, rows, :] * gate + dpool[i : i + 1, lanes(c)] / area[0:1, :]) * bend(half)[1]
                grad[b, c, rows, :] = value
                first = first + fold(value)
                second = second + fold(value * x)
            put(stage, c, first, second)

        repeat(EC, body, hook)

    def block_spread(b, layer, hook=None):
        stage = stages.at[b]

        def body(c):
            scale, shift = half_coefs(b, 0, layer, c, gain_e[layer, 0:1, lanes(c)], gain_e[layer, 1:2, lanes(c)])
            one, two, three = back_coefs(b, 1, layer, c, gain_e[layer, 2:3, lanes(c)])
            tap_rows = chan[layer, 0:16, lanes(c)].astype(F32)
            tap = [tap_rows[k : k + 1, :] for k in range(9)]
            for i in range(IMGS):
                rows, full = image(b, i)
                act, der = bend(mask[full, :] * (pre[b, c, rows, :] * scale + shift))
                pads_x[i, GAP : GAP + ROWS, :] = act
                slope[rows, :] = mask[full, :] * der
                pads_g[i, GAP : GAP + ROWS, :] = mask[full, :] * (one * grad[b, c, rows, :] + two + three * mixed[b, c, rows, :])
            first = jnp.zeros((8, LANES), F32)
            second = jnp.zeros((8, LANES), F32)
            total = [jnp.zeros((8, LANES), F32) for k in range(9)]
            for i in range(IMGS):
                for t in range(ROWS // TILE_BACK):
                    start = GAP + t * TILE_BACK
                    rows = slice(i * ROWS + t * TILE_BACK, i * ROWS + (t + 1) * TILE_BACK)
                    g = [pads_g[i, start - o : start - o + TILE_BACK, :] for o in OFFSETS]
                    left, right = edge_l[0:TILE_BACK, :], edge_r[0:TILE_BACK, :]
                    wide = (g[1] * tap[1] + g[4] * tap[4] + g[7] * tap[7]
                            + right * (g[0] * tap[0] + g[3] * tap[3] + g[6] * tap[6])
                            + left * (g[2] * tap[2] + g[5] * tap[5] + g[8] * tap[8]))
                    value = wide * slope[rows, :]
                    grad[b, c, rows, :] = value
                    first = first + fold(value)
                    second = second + fold(value * pre[b, c, rows, :])
                    center = g[4]
                    sides = (center * left, center, center * right)
                    for k in range(9):
                        o = OFFSETS[k]
                        total[k] = total[k] + fold(sides[k % 3] * pads_x[i, start + o : start + o + TILE_BACK, :])
            put(stage, c, first, second)
            for k in range(9):
                row = jnp.sum(total[k], 0, keepdims=True)
                if b == 0:
                    held_chan[k : k + 1, lanes(c)] = row
                else:
                    held_chan[k : k + 1, lanes(c)] = held_chan[k : k + 1, lanes(c)] + row

        repeat(EC, body, hook)
        if b == 1:
            pack_chan(layer)

    def block_expand(b, layer, hook=None):
        mine = slice(b * HALF, (b + 1) * HALF)

        def body(c):
            for part in range(2):
                norm_back_rows(b, 0, layer, 2 * c + part, gain_e[layer, 0:1, lanes(2 * c + part)], pre)
            value = contract(low_v[mine, :], low_pre[:, lanes(c, 256)], 0, 0)
            if b == 0:
                held[c] = value
            else:
                pack(MATS * layer, c, value + held[c])

        repeat(E // 256, body, hook)
        if layer > 0:
            grad_hid[mine, :] = grad_hid[mine, :] + contract(low_pre[...], wexp[layer, :, 0:E], 1, 1)
            put_hidden_sums(b, layer - 1)

    heads = [summer(b, 3, 0) for b in range(BATCHES)]
    load(0, 2, 0).wait()
    head_first(0)
    heads[0].start(stages.at[0])
    load(1, 2, 0).wait()
    head_first(1, (5, heads[0].middle))
    heads[1].start(stages.at[1])
    thirds = [summer(b, 2, L - 1) for b in range(BATCHES)]
    heads[0].finish()
    load_low(L).wait()
    load_out(L - 1).wait()
    head_second(0, (2, heads[1].middle))
    load(0, 0, L - 1).start()
    thirds[0].start(stages.at[0])
    heads[1].finish()
    head_second(1, (3, thirds[0].middle))
    load(1, 0, L - 1).start()
    thirds[1].start(stages.at[1])
    load_low(L - 1).start()
    for layer in reversed(range(L)):
        twos = [summer(b, 1, layer) for b in range(BATCHES)]
        ones = [summer(b, 0, layer) for b in range(BATCHES)]
        thirds[0].finish()
        load(0, 1, layer).wait()
        block_gate(0, layer, (3, thirds[1].middle))
        block_second(0, layer)
        twos[0].start(stages.at[0])
        thirds[1].finish()
        load(1, 1, layer).wait()
        block_gate(1, layer, (3, twos[0].middle))
        if layer > 0:
            load_out(layer - 1).start()
        block_second(1, layer)
        twos[1].start(stages.at[1])
        twos[0].finish()
        load(0, 0, layer).wait()
        block_spread(0, layer, (4, twos[1].middle))
        ones[0].start(stages.at[0])
        if layer > 0:
            load(0, 1, layer - 1).start()
        twos[1].finish()
        load(1, 0, layer).wait()
        block_spread(1, layer, (4, ones[0].middle))
        ones[1].start(stages.at[1])
        if layer > 0:
            load(1, 1, layer - 1).start()
        ones[0].finish()
        load_low(layer).wait()
        if layer > 0:
            load_out(layer - 1).wait()
        block_expand(0, layer, (3, ones[1].middle))
        if layer > 0:
            thirds = [summer(b, 2, layer - 1) for b in range(BATCHES)]
            thirds[0].start(stages.at[0])
            load(0, 0, layer - 1).start()
        ones[1].finish()
        block_expand(1, layer, None if layer == 0 else (3, thirds[0].middle))
        if layer > 0:
            thirds[1].start(stages.at[1])
            load(1, 0, layer - 1).start()
            load_low(layer - 1).start()


def run_backward_all(sizes, inputs):
    sds = jax.ShapeDtypeStruct
    vm = pl.BlockSpec(memory_space=pltpu.VMEM)
    hbm = pl.BlockSpec(memory_space=pl.ANY)
    n_dp, n_sh = sizes
    outs = [
        sds((n_sh, packed_blocks(sizes), 8, LANES), F32),
        sds((L, BATCHES, 2, 40, LANES), F32),
        sds((L, BATCHES, 8, LANES), F32),
        sds((BATCHES, 40, LANES), F32),
    ]
    scratch = [
        pltpu.VMEM((BATCHES, EC, HALF, LANES), F32),
        pltpu.VMEM((BATCHES, EC, HALF, LANES), F32),
        pltpu.VMEM((BATCHES, EC, HALF, LANES), F32),
        pltpu.VMEM((FULL, C), F32),
        pltpu.VMEM((HALF, C), BF16),
        pltpu.VMEM((HALF, E), BF16),
        pltpu.VMEM((IMGS, ROWS + 2 * GAP, LANES), F32),
        pltpu.VMEM((IMGS, ROWS + 2 * GAP, LANES), F32),
        pltpu.VMEM((HALF, LANES), F32),
        pltpu.VMEM((8, E), F32),
        pltpu.VMEM((8, E), F32),
        pltpu.VMEM((BATCHES, 40, LANES), F32),
        pltpu.SemaphoreType.DMA((BATCHES, 2)),
        pltpu.VMEM((E // 256, 256, 256), F32),
        pltpu.VMEM((144, E), F32),
        pltpu.VMEM((8, E), F32),
        pltpu.VMEM((8, LANES), F32),
        pltpu.VMEM((FULL, C), F32),
        pltpu.VMEM((FULL, C), BF16),
        pltpu.SemaphoreType.DMA((2,)),
    ]
    for b in range(BATCHES):
        for rows in BACK_ROWS[b]:
            scratch = scratch + sum_scratch(sizes, rows)
    specs = [vm] * 12 + [hbm] * 5 + [vm] * 6
    return pl.pallas_call(
        functools.partial(backward_kernel, sizes),
        out_shape=outs,
        in_specs=specs,
        out_specs=[vm] * len(outs),
        scratch_shapes=scratch,
        compiler_params=pltpu.CompilerParams(collective_id=2, has_side_effects=True, vmem_limit_bytes=63 * 2**20),
        name="backward",
    )(*inputs)


GROUPS = 12


def update_kernel(sizes, *refs):
    (packed, facts, fixes, *state) = refs[:19]
    state_in = [state[4 * k : 4 * k + 4] for k in range(4)]
    outs = refs[19:36]
    out_refs = [outs[4 * k : 4 * k + 4] for k in range(4)]
    norms = outs[16]
    peers = refs[36]
    (own, near, cross, side, line, full, gathered, g_class, sums_near, ratios) = refs[37:47]
    boxes = [refs[47 + 5 * k : 52 + 5 * k] for k in range(4)]
    (core_s, core_r, x_s, x_r, y_s, y_r, z_s, z_r, zz_s, zz_r, yy_s, yy_r,
     fn_s, fn_r, ff_s, ff_r, nn_s, nn_r, load_sems, store_sems, misc) = refs[67:88]
    n_dp, n_sh = sizes
    d, s = lax.axis_index("dp"), lax.axis_index("shard")
    count = packed_blocks(sizes)
    chunk = count // CHUNKS
    half = chunk // 2
    n_z = n_dp // 2
    piece = half // n_z
    bit0, bit1 = lax.rem(s, 2), s // 2
    near_peer = s + 1 - 2 * bit0
    far_peer = s + 2 - 4 * bit1
    yb, zi = lax.rem(d, 2), d // 2
    y_peer = d + 1 - 2 * yb

    greet(sizes)

    def load_own(t):
        return pltpu.make_async_copy(packed.at[t], own.at[t], load_sems.at[16 + t])

    def load(k, i):
        if k == 1:
            return [pltpu.make_async_copy(state_in[1][i].at[:, l], boxes[1][i].at[l], load_sems.at[2 * i + 24 + l]) for l in range(L)]
        return [pltpu.make_async_copy(state_in[k][i], boxes[k][i], load_sems.at[4 * k + i])]

    def store(k, i):
        source = boxes[k][(4, 1, 2, 3)[i]]
        if k == 1:
            return [pltpu.make_async_copy(source.at[l], out_refs[1][i].at[:, l], store_sems.at[2 * i + 16 + l]) for l in range(L)]
        return [pltpu.make_async_copy(source, out_refs[k][i], store_sems.at[4 * k + i])]

    def core_copy(k, i):
        rows = pl.ds(k * chunk, chunk)
        return pltpu.make_async_remote_copy(
            packed.at[2 * i + 1 - bit0, rows], near.at[i, rows], core_s.at[k, i], core_r.at[k, i],
            device_id=(d, near_peer), device_id_type=MESH)

    def x_copy(k):
        rows = pl.ds(k * chunk, chunk)
        return pltpu.make_async_remote_copy(
            own.at[far_peer, rows], cross.at[rows], x_s.at[k], x_r.at[k],
            device_id=(d, far_peer), device_id_type=MESH)

    def y_copy(k):
        rows = pl.ds(k * chunk + (1 - yb) * half, half)
        return pltpu.make_async_remote_copy(
            own.at[s, rows], side.at[k], y_s.at[k], y_r.at[k],
            device_id=(y_peer, s), device_id_type=MESH)

    def z_copy(k, step, source, target):
        rows = pl.ds(k * chunk + yb * half + target * piece, piece)
        return pltpu.make_async_remote_copy(
            own.at[s, rows], line.at[k, source], z_s.at[k, step], z_r.at[k, source],
            device_id=(2 * target + yb, s), device_id_type=MESH)

    def zz_copy(k, step, source, target):
        rows = pl.ds(k * (chunk // 2) + yb * (half // 2) + source * (piece // 2), piece // 2)
        return pltpu.make_async_remote_copy(
            full.at[rows], full.at[rows], zz_s.at[k, step], zz_r.at[k, source],
            device_id=(2 * target + yb, s), device_id_type=MESH)

    def yy_copy(k, b):
        rows = pl.ds(k * (chunk // 2) + b * (half // 2), half // 2)
        return pltpu.make_async_remote_copy(
            full.at[rows], full.at[rows], yy_s.at[k], yy_r.at[k],
            device_id=(y_peer, s), device_id_type=MESH)

    def over_z(action):
        def step(j, carry):
            action(j, lax.rem(zi + j, n_z))
            return carry

        lax.fori_loop(1, n_z, step, 0)

    def add_into(t, low, length, other, low_other, unit=8):
        def step(i, carry):
            rows = pl.ds(low + i * unit, unit)
            own[t, rows] = own[t, rows] + other(pl.ds(low_other + i * unit, unit))
            return carry

        lax.fori_loop(0, length // unit, step, 0)

    def stage_core(k):
        for i in range(2):
            core_copy(k, i).start()

    def stage_x(k):
        for i in range(2):
            core_copy(k, i).wait_recv()
        low = k * chunk
        add_into(far_peer, low, chunk, lambda rows: near[1 - bit1, rows], low)
        x_copy(k).start()
        add_into(s, low, chunk, lambda rows: near[bit1, rows], low)

    def stage_y(k):
        x_copy(k).wait_recv()
        low = k * chunk
        give = low + (1 - yb) * half
        keep = low + yb * half
        add_into(s, give, half, lambda rows: cross[rows], give)
        y_copy(k).start()
        add_into(s, keep, half, lambda rows: cross[rows], keep)

    def stage_z(k):
        y_copy(k).wait_recv()
        add_into(s, k * chunk + yb * half, half, lambda rows: side[k, rows], 0)
        over_z(lambda j, t: z_copy(k, j, zi, t).start())

    def stage_zz(k):
        over_z(lambda j, t: z_copy(k, j, t, zi).wait_recv())
        low = k * chunk + yb * half + zi * piece

        def step(i, carry):
            total = own[s, pl.ds(low + 2 * i, 2)]
            for j in range(1, n_z):
                total = total + line[k, lax.rem(zi + j, n_z), pl.ds(2 * i, 2)]
            full[low // 2 + i] = total.reshape(16, LANES).astype(BF16)
            return carry

        lax.fori_loop(0, piece // 2, step, 0)
        over_z(lambda j, t: zz_copy(k, j, zi, t).start())

    def stage_yy(k):
        over_z(lambda j, t: zz_copy(k, j, t, zi).wait_recv())
        yy_copy(k, yb).start()

    def stage_done(k):
        yy_copy(k, 1 - yb).wait_recv()

    def settle(k):
        for i in range(2):
            core_copy(k, i).wait_send()
        x_copy(k).wait_send()
        y_copy(k).wait_send()
        over_z(lambda j, t: z_copy(k, j, zi, t).wait_send())
        over_z(lambda j, t: zz_copy(k, j, zi, t).wait_send())
        yy_copy(k, yb).wait_send()

    def own_facts():
        return pltpu.make_async_copy(facts.at[s], peers.at[d, s], misc.at[0])

    def fact_near(step, source, target):
        return pltpu.make_async_remote_copy(
            facts.at[target], peers.at[d, source], fn_s.at[step], fn_r.at[source],
            device_id=(d, target), device_id_type=MESH)

    def fact_far(step, source, target):
        return pltpu.make_async_remote_copy(
            peers.at[source], peers.at[source], ff_s.at[step], ff_r.at[source],
            device_id=(target, s), device_id_type=MESH)

    def over_dp(action):
        def step(j, carry):
            action(j, lax.rem(d + j, n_dp))
            return carry

        lax.fori_loop(1, n_dp, step, 0)

    def facts_begin():
        own_facts().start()
        for j in range(1, n_sh):
            fact_near(j, s, lax.rem(s + j, n_sh)).start()

    def facts_second():
        for j in range(1, n_sh):
            fact_near(j, lax.rem(s + j, n_sh), s).wait_recv()
            fact_near(j, s, s).wait_send()
        own_facts().wait()
        over_dp(lambda j, t: fact_far(j, d, t).start())

    def facts_third():
        def arrive(j, t):
            fact_far(j, t, d).wait_recv()
            fact_far(j, d, d).wait_send()

        over_dp(arrive)
        for first in range(0, n_dp, 8):
            copy = pltpu.make_async_copy(peers.at[pl.ds(first, 8)], gathered, misc.at[1])
            copy.start()
            copy.wait()
            value = gathered[...].reshape(8 * n_sh * 16, FACT)
            product = contract(value[:, CLASS_PAD:], value[:, :CLASS_PAD], 0, 0)
            g_class[...] = product if first == 0 else g_class[...] + product

    sums_near[s] = jnp.zeros((24, LANES), F32)
    first_fix, second_fix = fixes[0:1, 0:1], fixes[1:2, 0:1]

    def note(row, value):
        square = value * value
        width = square.shape[1]
        line_sum = jnp.sum(square, 0, keepdims=True)
        total = jnp.zeros((1, LANES), F32)
        for low in range(0, width - width % LANES, LANES):
            total = total + line_sum[:, low : low + LANES]
        tail = width % LANES
        if tail:
            total = total + jnp.concatenate([line_sum[:, width - tail :], jnp.zeros((1, LANES - tail), F32)], 1)
        sums_near[s, row : row + 1, :] = sums_near[s, row : row + 1, :] + total

    def moments(k, index, grad):
        weight, first, second, unused, update = boxes[k]
        new_first = BETA_ONE * first[index] + (1.0 - BETA_ONE) * grad
        new_second = BETA_TWO * second[index] + (1.0 - BETA_TWO) * grad * grad
        first[index] = new_first
        second[index] = new_second
        value = new_first / first_fix / (jnp.sqrt(new_second / second_fix) + EPS_ADAM) + DECAY * weight[index]
        update[index] = value
        return value

    every = slice(None)

    def mats_index(layer, c):
        return (layer, every, lanes(c))

    def weights_squares():
        for layer in range(L):
            for part in range(2):

                def body(c):
                    note(2 * layer + part, boxes[0][0][mats_index(layer, c + part * EC)])

                repeat(EC, body)
            for kk in range(3):
                cols = slice(kk * LANES, (kk + 1) * LANES)
                note(2 * L + 3 * layer, boxes[1][0][layer, 0:9, cols])
                note(2 * L + 3 * layer + 1, boxes[1][0][layer, 9 : 9 + SE, cols])
                note(2 * L + 3 * layer + 2, boxes[1][0][layer, 9 + SE : 9 + 2 * SE, cols])
        note(5 * L, boxes[2][0][...])

        def body(i):
            note(5 * L + 1, boxes[3][0][pl.ds(pl.multiple_of(i * 40, 40), 40), :])

        repeat(8, body)

    def mats_moments(layer):
        for part in range(2):

            def body(c):
                panel = c + part * EC
                grad = full[pl.ds(layer * (MATS // 2) + 4 * panel, 4)].astype(F32).reshape(64, LANES)
                note(GROUPS + 2 * layer + part, moments(0, mats_index(layer, panel), grad))

            repeat(EC, body)

    def chan_moments():
        for layer in range(L):
            for kk in range(3):
                low = (AT_CHAN + CHAN * layer + 18 * kk) // 2
                grad = full[low : low + 9].astype(F32).reshape(144, LANES)[:137]
                value = moments(1, (layer, every, slice(kk * LANES, (kk + 1) * LANES)), grad)
                note(GROUPS + 2 * L + 3 * layer, value[0:9])
                note(GROUPS + 2 * L + 3 * layer + 1, value[9 : 9 + SE])
                note(GROUPS + 2 * L + 3 * layer + 2, value[9 + SE :])

    def head_moments():
        rows = HEAD // 4
        for part in range(2):
            low = (AT_HEAD + part * (rows // 8)) // 2
            grad = full[low : low + rows // 16].astype(F32).reshape(rows, LANES)
            note(GROUPS + 5 * L, moments(2, (every, slice(part * LANES, (part + 1) * LANES)), grad))

    def class_moments():
        def body(i):
            rows = pl.ds(pl.multiple_of(i * 40, 40), 40)
            note(GROUPS + 5 * L + 1, moments(3, (rows, every), g_class[rows, :CLASSES]))

        repeat(8, body)

    def norm_copy(step, source, target):
        return pltpu.make_async_remote_copy(
            sums_near.at[source], sums_near.at[source], nn_s.at[step], nn_r.at[source],
            device_id=(d, target), device_id_type=MESH)

    def finish(k, index, factor):
        weight, unused, unused_two, average, update = boxes[k]
        fresh = weight[index] - RATE * factor * update[index]
        update[index] = fresh
        average[index] = KEEP * average[index] + (1.0 - KEEP) * fresh

    for k in range(CHUNKS):
        stage_core(k)
    for t in range(n_sh):
        load_own(t).start()
    facts_begin()
    for i in range(4):
        for k in range(4):
            for copy in load(k, i):
                copy.start()
    for t in range(n_sh):
        load_own(t).wait()
    for tau in range(1, CHUNKS + 6):
        stages = (stage_x, stage_y, stage_z, stage_zz, stage_yy, stage_done)
        for age, stage in enumerate(stages):
            k = tau - 1 - age
            if 0 <= k < CHUNKS:
                stage(k)
        if tau == 1:
            facts_second()
            for k in range(4):
                for copy in load(k, 0):
                    copy.wait()
            weights_squares()
        if tau == 2:
            for i in range(1, 4):
                for k in range(4):
                    for copy in load(k, i):
                        copy.wait()
        if tau == CHUNKS:
            facts_third()
            class_moments()
            for i in (1, 2):
                for copy in store(3, i):
                    copy.start()
        if tau == CHUNKS + 2:
            mats_moments(0)
        if tau == CHUNKS + 4:
            mats_moments(1)
            for i in (1, 2):
                for copy in store(0, i):
                    copy.start()
    chan_moments()
    head_moments()
    for j in range(1, n_sh):
        norm_copy(j, s, lax.rem(s + j, n_sh)).start()
    for k in (1, 2):
        for i in (1, 2):
            for copy in store(k, i):
                copy.start()
    for k in range(CHUNKS):
        settle(k)
    for j in range(1, n_sh):
        norm_copy(j, lax.rem(s + j, n_sh), s).wait_recv()
        norm_copy(j, s, s).wait_send()
    total = sums_near[0]
    for j in range(1, n_sh):
        total = total + sums_near[j]
    root = jnp.broadcast_to(jnp.sqrt(jnp.sum(total, 1, keepdims=True)), (24, LANES))
    norms[...] = root
    ratios[0:GROUPS, :] = root[0:GROUPS] / root[GROUPS : 2 * GROUPS]

    def ratio(row):
        return ratios[row : row + 1, 0:1]

    for layer in range(L):
        for part in range(2):

            def body(c):
                finish(0, mats_index(layer, c + part * EC), ratio(2 * layer + part))

            repeat(EC, body)
    for i in (0, 3):
        for copy in store(0, i):
            copy.start()

    def body(i):
        finish(3, (pl.ds(pl.multiple_of(i * 40, 40), 40), every), ratio(5 * L + 1))

    repeat(8, body)
    for i in (0, 3):
        for copy in store(3, i):
            copy.start()
    row = lax.broadcasted_iota(jnp.int32, (137, LANES), 0)
    for layer in range(L):
        low = 2 * L + 3 * layer
        factor = jnp.where(row < 9, ratio(low), jnp.where(row < 9 + SE, ratio(low + 1), ratio(low + 2)))
        for kk in range(3):
            finish(1, (layer, every, slice(kk * LANES, (kk + 1) * LANES)), factor)
    finish(2, (every, every), ratio(5 * L))
    for k in (1, 2):
        for i in (0, 3):
            for copy in store(k, i):
                copy.start()
    for k in range(4):
        for i in range(4):
            for copy in store(k, i):
                copy.wait()


def run_update(sizes, packed, facts, fixes, states):
    sds = jax.ShapeDtypeStruct
    vm = pl.BlockSpec(memory_space=pltpu.VMEM)
    hbm = pl.BlockSpec(memory_space=pl.ANY)
    n_dp, n_sh = sizes
    count = packed_blocks(sizes)
    chunk = count // CHUNKS
    n_z = n_dp // 2
    sem = pltpu.SemaphoreType.DMA
    outs = [sds(item.shape, F32) for group in states for item in group]
    outs = outs + [sds((2 * GROUPS, LANES), F32), sds((n_dp, n_sh, 16, FACT), BF16)]
    scratch = [
        pltpu.VMEM((n_sh, count, 8, LANES), F32),
        pltpu.VMEM((2, count, 8, LANES), F32),
        pltpu.VMEM((count, 8, LANES), F32),
        pltpu.VMEM((CHUNKS, chunk // 2, 8, LANES), F32),
        pltpu.VMEM((CHUNKS, n_z, chunk // 2 // n_z, 8, LANES), F32),
        pltpu.VMEM((count // 2, 16, LANES), BF16),
        pltpu.VMEM((8, n_sh, 16, FACT), BF16),
        pltpu.VMEM((FACT - CLASS_PAD, CLASS_PAD), F32),
        pltpu.VMEM((n_sh, 2 * GROUPS, LANES), F32),
        pltpu.VMEM((16, LANES), F32),
    ]
    for k, group in enumerate(states):
        shape = group[0].shape if k != 1 else (L, 137, 384)
        scratch = scratch + [pltpu.VMEM(shape, F32)] * 5
    scratch = scratch + [
        sem((CHUNKS, 2)), sem((CHUNKS, 2)), sem((CHUNKS,)), sem((CHUNKS,)), sem((CHUNKS,)), sem((CHUNKS,)),
        sem((CHUNKS, n_z)), sem((CHUNKS, n_z)), sem((CHUNKS, n_z)), sem((CHUNKS, n_z)), sem((CHUNKS,)), sem((CHUNKS,)),
        sem((n_sh,)), sem((n_sh,)), sem((n_dp,)), sem((n_dp,)), sem((n_sh,)), sem((n_sh,)),
        sem((32,)), sem((24,)), sem((2,)),
    ]
    return pl.pallas_call(
        functools.partial(update_kernel, sizes),
        out_shape=outs,
        in_specs=[hbm, hbm, vm] + [hbm] * 16,
        out_specs=[hbm] * 16 + [vm, hbm],
        scratch_shapes=scratch,
        compiler_params=pltpu.CompilerParams(collective_id=3, has_side_effects=True, vmem_limit_bytes=63 * 2**20),
        name="update",
    )(packed, facts, fixes, *[item for group in states for item in group])


def own_slice(value, dim, parts, place):
    width = value.shape[dim] // parts
    return lax.dynamic_slice_in_dim(value, place * width, width, dim)


def own_vectors(gains, n_sh):
    line = gains.astype(BF16)[0]
    wide, narrow = E // n_sh, (2 * C + SE) // n_sh
    rows = []
    start = 0
    for width in ([wide] * 5 + [narrow]) * L + [HEAD // n_sh] * 2 + [CLASSES // n_sh]:
        rows.append(jnp.pad(line[start : start + width], (0, wide - width)))
        start = start + width
    return jnp.stack(rows + [jnp.zeros((wide,), BF16)])


def adapt(first, second, grad, first_fix, second_fix):
    new_first = BETA_ONE * first + (1.0 - BETA_ONE) * grad
    new_second = BETA_TWO * second + (1.0 - BETA_TWO) * grad * grad
    update = new_first / first_fix / (jnp.sqrt(new_second / second_fix) + EPS_ADAM)
    return (new_first, new_second, update)


def per_device(
    images,
    bucket,
    counts,
    balance,
    labels,
    step,
    expand_w,
    expand_m,
    expand_v,
    expand_e,
    chan_w,
    chan_m,
    chan_v,
    chan_e,
    head_w,
    head_m,
    head_v,
    head_e,
    class_w,
    class_m,
    class_v,
    class_e,
    gain_w,
    gain_m,
    gain_v,
    gain_e,
):
    sizes = (lax.axis_size("dp"), lax.axis_size("shard"))
    n_sh = sizes[1]
    code = bucket[0]
    side = jnp.where(code == 0, 7, jnp.where(code == 1, 10, 12))
    spot = jnp.arange(S * S)
    inside = ((spot // S < side) & (spot % S < side)).astype(F32)
    area_value = (side * side).astype(F32)
    valid = (jnp.arange(IMGS)[None, :] < counts).astype(F32)
    weighted = valid * balance.astype(F32)
    mask_all = jnp.broadcast_to(
        (valid[:, :, None] * inside[None, None, :]).reshape(FULL, 1), (FULL, LANES)
    )
    spread_l = jnp.broadcast_to((spot % S > 0).astype(F32)[:, None], (ROWS, LANES))
    spread_r = jnp.broadcast_to((spot % S < S - 1).astype(F32)[:, None], (ROWS, LANES))
    own = jnp.concatenate(
        [jnp.sum(valid, 1) * area_value, jnp.sum(weighted, 1), jnp.zeros((4,), F32)]
    )
    area = jnp.full((1, LANES), area_value)
    vec_own = jnp.stack([own_vectors(gain_w, n_sh), own_vectors(gain_e, n_sh)])
    rows16 = lambda value: jnp.pad(value, ((0, 0), (0, 8 - IMGS))).reshape(16, 1)
    turned = lambda value: value.transpose(1, 0, 2)
    saved = run_forward_all(
        sizes,
        [
            images.reshape(FULL, C), mask_all, spread_l, spread_r, area,
            jnp.broadcast_to(own[:, None], (8, LANES)), vec_own, rows16(labels),
            jnp.broadcast_to(rows16(weighted), (16, LANES)),
            expand_w, expand_e, turned(chan_w), turned(chan_e), head_w.T, head_e.T, class_w, class_e,
        ],
    )
    kept = saved[:11]
    tot_e, tot_c, tot_h = kept[8:11]
    dpool_h, extra, facts, wexp_s, headt_s, chan_s, vec_e, vec_c, vec_h = saved[11:]
    (packed, back_e, back_c, back_h) = run_backward_all(
        sizes,
        [
            dpool_h, extra, mask_all, spread_l, spread_r, area, wexp_s, headt_s, chan_s,
            vec_e, vec_c, vec_h, *kept,
        ],
    )
    place = lax.axis_index("shard")

    def norm_grads(tot, back, chunks):
        count = tot_e[0, 0, 48 : 48 + BATCHES, :1]
        forth = tot[: 4 * chunks].reshape(chunks, BATCHES, 2, LANES).transpose(1, 2, 0, 3).reshape(BATCHES, 2, -1)
        mean = forth[:, 0] / count
        scale = lax.rsqrt(forth[:, 1] / count - mean * mean + EPS_NORM)
        pairs = back[:, : 2 * chunks].reshape(BATCHES, chunks, 2, LANES).transpose(0, 2, 1, 3).reshape(BATCHES, 2, -1)
        cross = scale * (pairs[:, 1] - mean * pairs[:, 0])
        return [jnp.sum(cross, 0), jnp.sum(pairs[:, 0], 0)]

    vectors = []
    for layer in range(L):
        vectors = vectors + norm_grads(tot_e[layer, 0], back_e[layer, :, 0], EC)
        vectors = vectors + norm_grads(tot_e[layer, 1], back_e[layer, :, 1], EC)
        vectors = vectors + [back_e[layer, 1, 0, 24 : 24 + EC].reshape(E)]
        vectors = vectors + norm_grads(tot_c[layer], back_c[layer], 2)
        vectors = vectors + [back_e[layer, 1, 0, 24 + EC, :SE]]
    vectors = vectors + norm_grads(tot_h, back_h, HC) + [back_h[1, 24:32].reshape(CLASS_PAD)[:CLASSES]]
    total_loss = back_h[1, 32, 0]
    power = step[0].astype(F32)
    first_fix = 1.0 - jnp.power(jnp.float32(BETA_ONE), power)
    second_fix = 1.0 - jnp.power(jnp.float32(BETA_TWO), power)
    fixes = jnp.broadcast_to(jnp.stack([first_fix, second_fix])[:, None], (2, LANES))
    new = run_update(
        sizes,
        packed,
        facts,
        fixes,
        [
            (expand_w, expand_m, expand_v, expand_e),
            tuple(turned(item) for item in (chan_w, chan_m, chan_v, chan_e)),
            tuple(item.T for item in (head_w, head_m, head_v, head_e)),
            (class_w, class_m, class_v, class_e),
        ],
    )
    gain_grad = own_slice(pack_gains(vectors, n_sh), 0, n_sh, place)
    gain_first, gain_second, gain_update = adapt(gain_m, gain_v, gain_grad, first_fix, second_fix)
    gain_new = gain_w - RATE * gain_update
    gains_out = [gain_new, gain_first, gain_second, KEEP * gain_e + (1.0 - KEEP) * gain_new]
    norms = new[16][:, 0].reshape(2, GROUPS)
    shaped = list(new[:4]) + [turned(item) for item in new[4:8]] + [item.T for item in new[8:12]] + list(new[12:16])
    return tuple([total_loss] + shaped + gains_out + [norms])


def solution(mesh):
    in_specs = (
        P(None, ("dp", "shard"), None, None, None),
        P("dp"),
        P(None, ("dp", "shard")),
        P(None, ("dp", "shard")),
        P(None, ("dp", "shard")),
        P(),
        P(None, "shard", None),
        P(None, "shard", None),
        P(None, "shard", None),
        P(None, "shard", None),
        P(None, None, "shard"),
        P(None, None, "shard"),
        P(None, None, "shard"),
        P(None, None, "shard"),
        P(None, "shard"),
        P(None, "shard"),
        P(None, "shard"),
        P(None, "shard"),
        P("shard", None),
        P("shard", None),
        P("shard", None),
        P("shard", None),
        P("shard", None),
        P("shard", None),
        P("shard", None),
        P("shard", None),
    )
    out_specs = (
        P(),
        P(None, "shard", None),
        P(None, "shard", None),
        P(None, "shard", None),
        P(None, "shard", None),
        P(None, None, "shard"),
        P(None, None, "shard"),
        P(None, None, "shard"),
        P(None, None, "shard"),
        P(None, "shard"),
        P(None, "shard"),
        P(None, "shard"),
        P(None, "shard"),
        P("shard", None),
        P("shard", None),
        P("shard", None),
        P("shard", None),
        P("shard", None),
        P("shard", None),
        P("shard", None),
        P("shard", None),
        P(),
    )
    return jax.shard_map(
        per_device, mesh=mesh, in_specs=in_specs, out_specs=out_specs, check_vma=False
    )
```

```python
import functools

import jax
import jax.numpy as jnp
from jax import lax
from jax.experimental import pallas as pl
from jax.experimental.pallas import tpu as pltpu
from jax.sharding import PartitionSpec as P
import numpy as np

C = 256
E = 1536
SE = 64
HEAD = 1280
CLASSES = 1000
L = 2
S = 12


EPS_NORM = 1e-05
BETA_ONE = 0.9
BETA_TWO = 0.99
EPS_ADAM = 1e-08
DECAY = 0.01
RATE = 0.3
KEEP = 0.9


def contract(left, right, left_dim, right_dim):
    return lax.dot_general(
        left, right, (((left_dim,), (right_dim,)), ((), ())), preferred_element_type=jnp.float32
    )


def matmul(left, right):
    return jnp.dot(left, right, precision=lax.Precision.HIGHEST, preferred_element_type=jnp.float32)


def matmul_bt(left, right):
    return lax.dot_general(
        left,
        right,
        (((1,), (1,)), ((), ())),
        precision=lax.Precision.HIGHEST,
        preferred_element_type=jnp.float32,
    )


def matmul_tb(left, right):
    return lax.dot_general(
        left,
        right,
        (((0,), (0,)), ((), ())),
        precision=lax.Precision.HIGHEST,
        preferred_element_type=jnp.float32,
    )


def pack_gains(vectors, rows):
    return jnp.concatenate([vector.reshape(rows, -1) for vector in vectors], 1)


IMGS = 5
ROWS = S * S
BATCHES = 2
HALF = IMGS * ROWS
FULL = BATCHES * HALF
SLOTS = BATCHES * IMGS
LANES = 128
EC = E // LANES
HC = HEAD // LANES
GAP = 16
TILE = 48
TILE_BACK = 48
CLASS_PAD = 1024
FACT = CLASS_PAD + 384
OFFSETS = [S * (a - 1) + (c - 1) for a in range(3) for c in range(3)]
MESH = pl.DeviceIdType.MESH
F32 = jnp.float32
BF16 = jnp.bfloat16


def split(value):
    high = value.astype(BF16).astype(F32)
    rest = value - high
    middle = rest.astype(BF16).astype(F32)
    return jnp.concatenate([high, middle, rest - middle], 0)


def exact(value, low_weight, dim):
    rows = value.shape[0]
    parts = contract(split(value).astype(BF16), low_weight, 1, dim)
    return parts[0:rows] + parts[rows : 2 * rows] + parts[2 * rows : 3 * rows]


def exact_outer(left, right):
    rows = left.shape[0]
    l, r = split(left), split(right)
    pick = lambda value, order: jnp.concatenate([value[k * rows : (k + 1) * rows] for k in order], 0).astype(BF16)
    return contract(pick(l, (0, 0, 1, 1, 0, 2)), pick(r, (0, 1, 0, 1, 2, 0)), 0, 0)


def tables():
    spot = np.arange(ROWS)
    rows = [spot % S > 0, spot % S < S - 1, spot // S, spot % S]
    return np.broadcast_to(np.stack(rows).astype(np.float32)[:, :, None], (4, ROWS, LANES))


def fill_mask(mask, table, bucket, counts):
    code = bucket[0]
    side = jnp.where(code == 0, 7, jnp.where(code == 1, 10, 12)).astype(F32)
    inside = jnp.where((table[2] < side) & (table[3] < side), 1.0, 0.0)
    for b in range(BATCHES):
        for i in range(IMGS):
            low = b * HALF + i * ROWS
            mask[low : low + ROWS, :] = inside * jnp.where(i < counts[b, 0], 1.0, 0.0)
    return side * side


class Sum:
    def __init__(self, near, far, total, sems, sizes, rows):
        self.near, self.far, self.total = near, far, total
        self.sems = sems
        self.n_dp, self.n_sh = sizes
        self.rows = rows

    def copy_near(self, step, slot, target):
        d = lax.axis_index("dp")
        return pltpu.make_async_remote_copy(
            self.near.at[slot], self.near.at[slot],
            self.sems[0].at[step], self.sems[1].at[slot],
            device_id=(d, target), device_id_type=MESH)

    def copy_far(self, step, slot, target):
        s = lax.axis_index("shard")
        return pltpu.make_async_remote_copy(
            self.far.at[slot], self.far.at[slot],
            self.sems[2].at[step], self.sems[3].at[slot],
            device_id=(target, s), device_id_type=MESH)

    def start(self, stage):
        s = lax.axis_index("shard")
        self.near[s] = stage[0 : self.rows]
        for j in range(1, self.n_sh):
            self.copy_near(j, s, lax.rem(s + j, self.n_sh)).start()

    def middle(self):
        s, d = lax.axis_index("shard"), lax.axis_index("dp")
        for j in range(1, self.n_sh):
            self.copy_near(j, lax.rem(s + j, self.n_sh), s).wait_recv()
        for j in range(1, self.n_sh):
            self.copy_near(j, s, s).wait_send()
        part = self.near[0]
        for j in range(1, self.n_sh):
            part = part + self.near[j]
        self.far[d] = part

        def send(j, carry):
            self.copy_far(j, d, lax.rem(d + j, self.n_dp)).start()
            return carry

        lax.fori_loop(1, self.n_dp, send, 0)

    def finish(self):
        d = lax.axis_index("dp")

        def arrive(j, carry):
            self.copy_far(j, lax.rem(d + j, self.n_dp), d).wait_recv()
            self.copy_far(j, d, d).wait_send()
            return carry

        lax.fori_loop(1, self.n_dp, arrive, 0)
        part = self.far[0]
        for j in range(1, self.n_dp):
            part = part + self.far[j]
        self.total[0 : self.rows] = part


def sum_scratch(sizes, rows):
    n_dp, n_sh = sizes
    return [
        pltpu.VMEM((n_sh, rows, LANES), F32),
        pltpu.VMEM((n_dp, rows, LANES), F32),
        pltpu.SemaphoreType.DMA((n_sh,)),
        pltpu.SemaphoreType.DMA((n_sh,)),
        pltpu.SemaphoreType.DMA((n_dp,)),
        pltpu.SemaphoreType.DMA((n_dp,)),
    ]


def greet(sizes):
    n_dp, n_sh = sizes
    d, s = lax.axis_index("dp"), lax.axis_index("shard")
    gate = pltpu.get_barrier_semaphore()
    for j in range(1, n_sh):
        pl.semaphore_signal(gate, inc=1, device_id=(d, lax.rem(s + j, n_sh)), device_id_type=MESH)

    def signal(j, carry):
        pl.semaphore_signal(gate, inc=1, device_id=(lax.rem(d + j, n_dp), s), device_id_type=MESH)
        return carry

    lax.fori_loop(1, n_dp, signal, 0)
    pl.semaphore_wait(gate, n_sh + n_dp - 2)


def repeat(count, body, hook=None):
    def step(i, carry):
        if hook is not None:

            @pl.when(i == hook[0])
            def _():
                hook[1]()

        body(i)
        return carry

    lax.fori_loop(0, count, step, 0)


def lanes(c, width=LANES):
    return pl.ds(pl.multiple_of(c * width, width), width)


def coefs(total, row, count, gain, shift):
    mean = total[pl.ds(row, 1), :] / count
    square = total[pl.ds(row + 1, 1), :] / count
    scale = gain * lax.rsqrt(square - mean * mean + EPS_NORM)
    return scale, shift - mean * scale


def act_half(half):
    return half + half * jnp.tanh(half)


def forward_kernel(sizes, *refs):
    (images, table, bucket, counts, balance, labels, vec_w, vec_e, expand_w, expand_e, chan_w, chan_e,
     head_w, head_e, class_w, class_e,
     pre_s, mixed_s, feat_s, out_s, low_s, pool_s, unit_s, gate_s, tot_e, tot_c, tot_h,
     dpool_h, extra, facts, wexp_s, headt_s, chan_s, gain_e_s, gain_c_s, gain_h_s,
     pre, hid, out_t, low_t, scaled, pads, stages, totals, cnt, pool_t, gate_t, save_sems,
     wexp, chan, headt, classes, vecs, gain_e, gain_c, gain_h, gain_s, gain_k, pooled_h, bias_row,
     st_exp, st_chan, st_head, st_class, load_sems, sx, rx, sc, rc, sf, rf, out_sems,
     mask, area, own_rows, firstrow) = refs[:76]
    rest = list(refs[76:])
    edge_l, edge_r = table.at[0], table.at[1]
    n_sh = sizes[1]
    sums = []
    for m in range(2):
        group = []
        for rows in (56, 48, 8, 40):
            near, far = rest[0], rest[1]
            group.append((near, far, rest[2:6], rows))
            rest = rest[6:]
        sums.append(group)

    d, s = lax.axis_index("dp"), lax.axis_index("shard")
    near_peer = s + 1 - 2 * lax.rem(s, 2)
    far_peer = s + 2 - 4 * (s // 2)
    far_near = near_peer + 2 - 4 * (s // 2)
    pieces = [("exp", 0, 0, 0), ("exp", 1, 0, 0), ("vec", 0, 0, 0), ("chan", 0, 0, 0), ("exp", 0, 0, 1), ("exp", 1, 0, 1),
              ("exp", 0, 1, 0), ("exp", 1, 1, 0), ("chan", 0, 1, 0), ("exp", 0, 1, 1), ("exp", 1, 1, 1),
              ("head", 0, 0, 0), ("class", 0, 0, 0), ("class", 1, 0, 0)]
    mats = [k for k, piece in enumerate(pieces) if piece[0] == "exp"]

    def region(k, source):
        kind, m, layer, half = pieces[k]
        if kind == "exp":
            return wexp.at[m, layer, pl.ds(pl.multiple_of(source * 64, 64), 64), half * E : (half + 1) * E]
        if kind == "chan":
            return chan.at[:, layer, :, pl.ds(pl.multiple_of(source * 384, 384), 384)]
        if kind == "vec":
            return vecs.at[source]
        if kind == "head":
            return headt.at[:, pl.ds(pl.multiple_of(source * 320, 320), 320), :]
        return classes.at[m, pl.ds(pl.multiple_of(source * 320, 320), 320), :]

    def loads(k):
        kind, m, layer, half = pieces[k]
        if kind == "exp":
            slot = mats.index(k) % 2
            source = (expand_w, expand_e)[m].at[layer, :, half * E : (half + 1) * E]
            return [pltpu.make_async_copy(source, st_exp.at[slot], load_sems.at[slot])]
        if kind == "chan":
            return [pltpu.make_async_copy((chan_w, chan_e)[i].at[:, layer], st_chan.at[i], load_sems.at[2 + i]) for i in range(2)]
        if kind == "head":
            return [pltpu.make_async_copy((head_w, head_e)[i], st_head.at[i], load_sems.at[4 + i]) for i in range(2)]
        if kind == "class":
            return [pltpu.make_async_copy((class_w, class_e)[m], st_class, load_sems.at[6])]
        return []

    def fetch(k):
        for copy in loads(k):
            copy.start()

    def cast(k):
        kind, m, layer, half = pieces[k]
        for copy in loads(k):
            copy.wait()
        if kind == "exp":
            order = mats.index(k)
            wexp[m, layer, pl.ds(pl.multiple_of(s * 64, 64), 64), half * E : (half + 1) * E] = st_exp[order % 2].astype(BF16)
            if order + 2 < len(mats):
                fetch(mats[order + 2])
        if kind == "chan":
            cols = pl.ds(pl.multiple_of(s * 384, 384), 384)
            for i in range(2):
                padded = jnp.concatenate([st_chan[i, 0:9, :], jnp.zeros((7, 384), F32)], 0)
                chan[i, layer, 0:16, cols] = padded.astype(BF16)
                chan[i, layer, 16:80, cols] = st_chan[i, 9 : 9 + SE, :].astype(BF16)
                chan[i, layer, 80:144, cols] = st_chan[i, 9 + SE : 9 + 2 * SE, :].astype(BF16)
            if layer == 0:
                fetch(pieces.index(("chan", 0, 1, 0)))
        if kind == "head":
            for i in range(2):
                headt[i, pl.ds(pl.multiple_of(s * 320, 320), 320), :] = st_head[i].astype(BF16)
        if kind == "class":
            classes[m, pl.ds(pl.multiple_of(s * 320, 320), 320), :] = st_class[...].astype(BF16)
            if m == 0:
                fetch(k + 1)
        if kind == "vec":
            own_rows[...] = jnp.zeros(own_rows.shape, F32)
            for i in range(2):
                start = 0
                for row, width in enumerate(([384] * 5 + [144]) * L + [320] * 2 + [250]):
                    own_rows[i, row : row + 1, 0:width] = (vec_w, vec_e)[i][0:1, start : start + width]
                    start = start + width
            vecs[s] = own_rows[...].astype(BF16)

    def hop(k, source, target, send, receive):
        return pltpu.make_async_remote_copy(
            region(k, source), region(k, source), send.at[k], receive.at[k],
            device_id=(d, target), device_id_type=MESH)

    def offer(k):
        cast(k)
        hop(k, s, far_peer, sx, rx).start()
        hop(k, s, near_peer, sc, rc).start()

    def forward_on(k):
        hop(k, far_peer, s, sx, rx).wait_recv()
        hop(k, far_peer, near_peer, sf, rf).start()

    def ready(k):
        hop(k, near_peer, s, sc, rc).wait_recv()
        hop(k, far_near, s, sf, rf).wait_recv()

    def settle():
        for k in range(len(pieces)):
            hop(k, s, far_peer, sx, rx).wait_send()
            hop(k, s, near_peer, sc, rc).wait_send()
            hop(k, far_peer, near_peer, sf, rf).wait_send()

    def join(m, row, low, width):
        return jnp.concatenate([vecs[t, m, 0:16, :].astype(F32)[row : row + 1, low : low + width] for t in range(n_sh)], 1)

    def unpack_vectors():
        for m in range(2):
            for layer in range(L):
                for t in range(n_sh):
                    gain_e[m, layer, 0:5, 384 * t : 384 * t + 384] = vecs[t, m].astype(F32)[6 * layer : 6 * layer + 5, :]
                gain_c[m, layer, 0:1, :] = join(m, 6 * layer + 5, 0, 64)
                gain_c[m, layer, 1:2, :] = join(m, 6 * layer + 5, 64, 64)
                gain_s[m, layer, 0:1, :] = join(m, 6 * layer + 5, 128, 16)
            gain_h[m, 0:1, :] = join(m, 12, 0, 320)
            gain_h[m, 1:2, :] = join(m, 13, 0, 320)
            gain_k[m, 0:1, :] = join(m, 14, 0, 250)

    for k in (0, 1, 3, 11, 12):
        fetch(k)
    greet(sizes)
    for k in (0, 1, 2, 3):
        offer(k)
    area_value = fill_mask(mask, table, bucket, counts)
    area[...] = jnp.full((8, LANES), area_value, F32)
    firstrow[...] = jnp.zeros((8, LANES), F32)
    weighted = [[jnp.where(i < counts[b, 0], balance[b, i], 0).astype(F32) for i in range(IMGS)] for b in range(BATCHES)]
    for b in range(BATCHES):
        firstrow[b : b + 1, :] = jnp.full((1, LANES), counts[b, 0].astype(F32) * area_value, F32)
        firstrow[2 + b : 3 + b, :] = jnp.full((1, LANES), sum(weighted[b]), F32)

    def low(m, layer):
        return low_s.at[layer] if m == 0 else low_t

    def out(m, layer):
        return out_s.at[layer] if m == 0 else out_t

    def total_ref(m, kind, layer):
        if m == 0:
            return (tot_e.at[layer, 0], tot_e.at[layer, 1], tot_c.at[layer], tot_h)[kind]
        return totals.at[kind]

    def summer(m, kind, layer):
        near, far, sems, rows = sums[m][kind]
        return Sum(near, far, total_ref(m, kind, layer), sems, sizes, rows)

    def save(src, dst, index):
        return pltpu.make_async_copy(src, dst, save_sems.at[index])

    for slot in range(SLOTS):
        pads[slot, 0:GAP, :] = jnp.zeros((GAP, LANES), F32)
        pads[slot, GAP + ROWS : 2 * GAP + ROWS, :] = jnp.zeros((GAP, LANES), F32)

    def store_wexp(layer):
        return pltpu.make_async_copy(wexp.at[0, layer], wexp_s.at[layer], out_sems.at[layer])

    store_headt = pltpu.make_async_copy(headt.at[0], headt_s, out_sems.at[L])
    store_chan = pltpu.make_async_copy(chan.at[0], chan_s, out_sems.at[L + 1])

    def load_rows(i):
        rows = pl.ds(pl.multiple_of(i * ROWS, ROWS), ROWS)
        for half in range(2):
            cols = slice(half * LANES, half * LANES + LANES)
            value = images[rows, cols].astype(F32) * mask[rows, :]
            hid[0, rows, cols] = value
            hid[1, rows, cols] = value
            low_s[0, rows, cols] = value.astype(BF16)
            low_t[rows, cols] = value.astype(BF16)

    repeat(SLOTS, load_rows)

    def update(m, layer):
        tot = total_ref(m, 2, layer)
        for half in range(2):
            cols = slice(half * LANES, half * LANES + LANES)
            for b in range(BATCHES):
                scale, shift = coefs(tot, 4 * half + 2 * b, cnt[b : b + 1, :], gain_c[m, layer, 0:1, cols], gain_c[m, layer, 1:2, cols])

                def one(i):
                    rows = pl.ds(pl.multiple_of(b * HALF + i * ROWS, ROWS), ROWS)
                    value = hid[m, rows, cols] + mask[rows, :] * (out(m, layer)[rows, cols] * scale + shift)
                    hid[m, rows, cols] = value
                    low(m, layer + 1)[rows, cols] = value.astype(BF16)

                repeat(IMGS, one)

    def put_sums(stage, chunk, b, value):
        stage[pl.ds(4 * chunk + 2 * b, 1), :] = jnp.sum(value, 0, keepdims=True)
        stage[pl.ds(4 * chunk + 2 * b + 1, 1), :] = jnp.sum(value * value, 0, keepdims=True)

    def expand(m, layer, hook=None):
        stage = stages.at[m]

        def body(c):
            weight = wexp[m, layer, :, lanes(c, 256)]
            for b in range(BATCHES):
                value = jnp.dot(low(m, layer)[b * HALF : (b + 1) * HALF, :], weight, preferred_element_type=F32)
                for half in range(2):
                    piece = value[:, half * LANES : (half + 1) * LANES]
                    pre[m, 2 * c + half, b * HALF : (b + 1) * HALF, :] = piece
                    put_sums(stage, 2 * c + half, b, piece)
            if m == 0:
                for half in range(2):
                    save(pre.at[0, 2 * c + half], pre_s.at[layer, 2 * c + half], 2 * c + half).start()

        repeat(E // 256, body, hook)

    def depthwise(m, layer, hook=None):
        stage = stages.at[m]
        tot = total_ref(m, 0, layer)

        def body(c):
            if m == 0:
                save(pre.at[0, c], pre_s.at[layer, c], c).wait()
            tap_rows = chan[m, layer, 0:16, lanes(c)].astype(F32)
            tap = [tap_rows[k : k + 1, :] for k in range(9)]
            for b in range(BATCHES):
                scale, shift = coefs(tot, 4 * c + 2 * b, cnt[b : b + 1, :], gain_e[m, layer, 0:1, lanes(c)], gain_e[m, layer, 1:2, lanes(c)])
                scale, shift = 0.5 * scale, 0.5 * shift
                for i in range(IMGS):
                    slot = b * IMGS + i
                    rows = slice(slot * ROWS, (slot + 1) * ROWS)
                    half = mask[rows, :] * (pre[m, c, rows, :] * scale + shift)
                    pads[slot, GAP : GAP + ROWS, :] = act_half(half)
                first = jnp.zeros((8, LANES), F32)
                second = jnp.zeros((8, LANES), F32)
                for i in range(IMGS):
                    slot = b * IMGS + i
                    for t in range(ROWS // TILE):
                        start = GAP + t * TILE
                        near = [pads[slot, start + o : start + o + TILE, :] for o in OFFSETS]
                        left = near[0] * tap[0] + near[3] * tap[3] + near[6] * tap[6]
                        mid = near[1] * tap[1] + near[4] * tap[4] + near[7] * tap[7]
                        right = near[2] * tap[2] + near[5] * tap[5] + near[8] * tap[8]
                        rows = slice(slot * ROWS + t * TILE, slot * ROWS + (t + 1) * TILE)
                        value = mask[rows, :] * (mid + edge_l[t * TILE : (t + 1) * TILE, :] * left + edge_r[t * TILE : (t + 1) * TILE, :] * right)
                        pre[m, c, rows, :] = value
                        first = first + jnp.sum(value.reshape(TILE // 8, 8, LANES), 0)
                        second = second + jnp.sum((value * value).reshape(TILE // 8, 8, LANES), 0)
                stage[pl.ds(4 * c + 2 * b, 1), :] = jnp.sum(first, 0, keepdims=True)
                stage[pl.ds(4 * c + 2 * b + 1, 1), :] = jnp.sum(second, 0, keepdims=True)
            if m == 0:
                save(pre.at[0, c], mixed_s.at[layer, c], c).start()

        repeat(EC, body, hook)

    def pooling(m, layer, hook=None):
        tot = total_ref(m, 1, layer)
        pool = pool_s.at[layer] if m == 0 else pool_t

        def body(c):
            if m == 0:
                save(pre.at[0, c], mixed_s.at[layer, c], c).wait()
            for b in range(BATCHES):
                scale, shift = coefs(tot, 4 * c + 2 * b, cnt[b : b + 1, :], gain_e[m, layer, 2:3, lanes(c)], gain_e[m, layer, 3:4, lanes(c)])
                scale, shift = 0.5 * scale, 0.5 * shift
                for i in range(IMGS):
                    slot = b * IMGS + i
                    rows = slice(slot * ROWS, (slot + 1) * ROWS)
                    value = act_half(mask[rows, :] * (pre[m, c, rows, :] * scale + shift))
                    pre[m, c, rows, :] = value
                    pool[b * 8 + i : b * 8 + i + 1, lanes(c)] = jnp.sum(value, 0, keepdims=True) / area[0:1, :]

        repeat(EC, body, hook)

    def project(m, layer):
        pool = pool_s.at[layer] if m == 0 else pool_t
        gate = gate_s.at[layer] if m == 0 else gate_t
        units = exact(pool[...], chan[m, layer, 16:80, :], 1) + gain_s[m, layer, 0:1, :]
        if m == 0:
            unit_s[layer] = units
        gate[...] = jax.nn.sigmoid(exact(jax.nn.silu(units), chan[m, layer, 80:144, :], 0) + gain_e[m, layer, 4:5, :])

        def body(c):
            for b in range(BATCHES):
                for i in range(IMGS):
                    rows = slice(b * HALF + i * ROWS, b * HALF + (i + 1) * ROWS)
                    scaled[rows, lanes(c)] = (pre[m, c, rows, :] * gate[b * 8 + i : b * 8 + i + 1, lanes(c)]).astype(BF16)

        repeat(EC, body)
        stage = stages.at[m]
        for b in range(BATCHES):
            rows = slice(b * HALF, (b + 1) * HALF)
            value = contract(scaled[rows, :], wexp[m, layer, :, E : 2 * E], 1, 1)
            out(m, layer)[rows, :] = value
            for half in range(2):
                put_sums(stage, half, b, value[:, half * LANES : (half + 1) * LANES])

    def features(m, hook=None):
        stage = stages.at[m]

        def body(c):
            weight = headt[m, pl.ds(pl.multiple_of(c * 256, 256), 256), :]
            for b in range(BATCHES):
                value = contract(low(m, L)[b * HALF : (b + 1) * HALF, :], weight, 1, 1)
                for half in range(2):
                    piece = value[:, half * LANES : (half + 1) * LANES]
                    pre[m, 2 * c + half, b * HALF : (b + 1) * HALF, :] = piece
                    put_sums(stage, 2 * c + half, b, piece)
            if m == 0:
                for half in range(2):
                    save(pre.at[0, 2 * c + half], feat_s.at[2 * c + half], 2 * c + half).start()

        repeat(HEAD // 256, body, hook)

    def head_pool(m, hook=None):
        tot = total_ref(m, 3, 0)

        def body(c):
            for b in range(BATCHES):
                scale, shift = coefs(tot, 4 * c + 2 * b, cnt[b : b + 1, :], gain_h[m, 0:1, lanes(c)], gain_h[m, 1:2, lanes(c)])
                scale, shift = 0.5 * scale, 0.5 * shift
                for i in range(IMGS):
                    slot = b * IMGS + i
                    rows = slice(slot * ROWS, (slot + 1) * ROWS)
                    value = act_half(mask[rows, :] * (pre[m, c, rows, :] * scale + shift))
                    pooled_h[m, b * 8 + i : b * 8 + i + 1, lanes(c)] = jnp.sum(value, 0, keepdims=True) / area[0:1, :]

        repeat(HC, body, hook)

    for m in range(2):
        stages[m] = jnp.zeros((56, LANES), F32)
    pool_s[...] = jnp.zeros(pool_s.shape, F32)
    pool_t[...] = jnp.zeros(pool_t.shape, F32)
    pooled_h[...] = jnp.zeros(pooled_h.shape, F32)
    stages[0, 48:56, :] = firstrow[...]
    pending = None
    forward_on(0)
    ready(0)
    for layer in range(L):
        s_one, t_one = summer(0, 0, layer), summer(1, 0, layer)
        s_two, t_two = summer(0, 1, layer), summer(1, 1, layer)
        s_three, t_three = summer(0, 2, layer), summer(1, 2, layer)
        if layer > 0:
            update(0, layer - 1)
            ready(6)
        expand(0, layer, None if pending is None else (2, pending.middle))
        s_one.start(stages.at[0])
        if layer == 0:
            forward_on(1)
            ready(1)
            forward_on(2)
            offer(4)
        else:
            forward_on(8)
            pending.finish()
            update(1, layer - 1)
            ready(7)
            offer(10)
        expand(1, layer, (4, s_one.middle))
        t_one.start(stages.at[1])
        if layer == 0:
            forward_on(3)
            ready(2)
            unpack_vectors()
            ready(3)
            offer(5)
        else:
            forward_on(9)
            ready(8)
            offer(11)
        s_one.finish()
        if layer == 0:
            cnt[...] = tot_e[0, 0, 48:56, :]
        depthwise(0, layer, (2, t_one.middle))
        s_two.start(stages.at[0])
        forward_on((4, 10)[layer])
        offer((6, 12)[layer])
        t_one.finish()
        depthwise(1, layer, (5, s_two.middle))
        t_two.start(stages.at[1])
        forward_on((5, 11)[layer])
        if layer == 0:
            offer(7)
        ready((4, 9)[layer])
        s_two.finish()
        pooling(0, layer, (5, t_two.middle))
        project(0, layer)
        s_three.start(stages.at[0])
        forward_on((6, 12)[layer])
        offer((8, 13)[layer])
        ready((5, 10)[layer])
        t_two.finish()
        pooling(1, layer, (6, s_three.middle))
        project(1, layer)
        t_three.start(stages.at[1])
        if layer == 0:
            forward_on(7)
            offer(9)
        s_three.finish()
        pending = t_three
    for layer in range(L):
        store_wexp(layer).start()
    s_head, t_head = summer(0, 3, 0), summer(1, 3, 0)
    update(0, L - 1)
    ready(11)
    features(0, (2, pending.middle))
    s_head.start(stages.at[0])
    pending.finish()
    update(1, L - 1)
    features(1, (4, s_head.middle))
    t_head.start(stages.at[1])
    forward_on(13)
    store_headt.start()
    store_chan.start()
    s_head.finish()
    head_pool(0, (3, t_head.middle))
    ready(12)
    t_head.finish()
    head_pool(1)
    ready(13)

    def class_logits(m):
        low_pool = pooled_h[m].astype(BF16)
        return jnp.dot(low_pool, classes[m], preferred_element_type=F32) + gain_k[m, 0:1, :]

    def log_softmax(value):
        value = value - jnp.max(value, 1, keepdims=True)
        return value - jnp.log(jnp.sum(jnp.exp(value), 1, keepdims=True))

    logp = log_softmax(class_logits(0))
    target = log_softmax(class_logits(1))
    expected = jnp.exp(target)
    row16 = lax.broadcasted_iota(jnp.int32, (16, LANES), 0)
    label_rows = jnp.zeros((16, LANES), jnp.int32)
    weight_rows = jnp.zeros((16, LANES), F32)
    for b in range(BATCHES):
        for i in range(IMGS):
            label_rows = jnp.where(row16 == 8 * b + i, labels[b, i], label_rows)
            weight_rows = jnp.where(row16 == 8 * b + i, weighted[b][i], weight_rows)
    hot = lax.broadcasted_iota(jnp.int32, (16, CLASSES), 1) == label_rows[:, 0:1]
    total_weight = tot_e[0, 0, 50:51, :] + tot_e[0, 0, 51:52, :]
    coef = weight_rows[:, 0:1] / total_weight[:, 0:1]
    per = jnp.sum(expected * (target - logp), 1, keepdims=True) - jnp.sum(jnp.where(hot, logp, 0.0), 1, keepdims=True)
    loss = jnp.sum(coef * per, 0, keepdims=True)
    slope = -coef * (jnp.where(hot, 1.0, 0.0) + expected)
    grad_low = (slope - jnp.exp(logp) * jnp.sum(slope, 1, keepdims=True)).astype(BF16)
    bias_row[...] = jnp.zeros(bias_row.shape, F32)
    bias_row[0:1, 0:CLASSES] = jnp.sum(grad_low.astype(F32), 0, keepdims=True)
    for k in range(8):
        extra[k : k + 1, :] = bias_row[0:1, k * LANES : (k + 1) * LANES]
    extra[8:16, :] = jnp.broadcast_to(loss, (8, LANES))
    dpool_h[...] = contract(grad_low, classes[0], 1, 1) / area[0:1, 0:1]
    facts[...] = jnp.zeros(facts.shape, BF16)
    low_pool = pooled_h[0].astype(BF16)
    for t in range(n_sh):
        facts[t, :, 0:CLASSES] = grad_low
        facts[t, :, CLASS_PAD : CLASS_PAD + 320] = low_pool[:, 320 * t : 320 * t + 320]
    gain_e_s[...] = gain_e[0]
    gain_c_s[...] = gain_c[0]
    gain_h_s[...] = gain_h[0]
    settle()
    for layer in range(L):
        store_wexp(layer).wait()
    store_headt.wait()
    store_chan.wait()
    for c in range(HC):
        save(pre.at[0, c], feat_s.at[c], c).wait()


def run_forward_all(sizes, inputs):
    sds = jax.ShapeDtypeStruct
    vm = pl.BlockSpec(memory_space=pltpu.VMEM)
    hbm = pl.BlockSpec(memory_space=pl.ANY)
    n_sh = sizes[1]
    outs = [
        (sds((L, EC, FULL, LANES), F32), hbm),
        (sds((L, EC, FULL, LANES), F32), hbm),
        (sds((HC, FULL, LANES), F32), hbm),
        (sds((L, FULL, C), F32), vm),
        (sds((L + 1, FULL, C), BF16), vm),
        (sds((L, 16, E), F32), vm),
        (sds((L, 16, SE), F32), vm),
        (sds((L, 16, E), F32), vm),
        (sds((L, 2, 56, LANES), F32), vm),
        (sds((L, 8, LANES), F32), vm),
        (sds((40, LANES), F32), vm),
        (sds((16, HEAD), F32), vm),
        (sds((16, LANES), F32), vm),
        (sds((n_sh, 16, FACT), BF16), vm),
        (sds((L, C, 2 * E), BF16), hbm),
        (sds((HEAD, C), BF16), hbm),
        (sds((L, 144, E), BF16), hbm),
        (sds((L, 8, E), F32), vm),
        (sds((L, 8, C), F32), vm),
        (sds((8, HEAD), F32), vm),
    ]
    scratch = [
        pltpu.VMEM((2, EC, FULL, LANES), F32),
        pltpu.VMEM((2, FULL, C), F32),
        pltpu.VMEM((FULL, C), F32),
        pltpu.VMEM((FULL, C), BF16),
        pltpu.VMEM((FULL, E), BF16),
        pltpu.VMEM((SLOTS, ROWS + 2 * GAP, LANES), F32),
        pltpu.VMEM((2, 56, LANES), F32),
        pltpu.VMEM((4, 56, LANES), F32),
        pltpu.VMEM((8, LANES), F32),
        pltpu.VMEM((16, E), F32),
        pltpu.VMEM((16, E), F32),
        pltpu.SemaphoreType.DMA((EC,)),
        pltpu.VMEM((2, L, C, 2 * E), BF16),
        pltpu.VMEM((2, L, 144, E), BF16),
        pltpu.VMEM((2, HEAD, C), BF16),
        pltpu.VMEM((2, HEAD, CLASSES), BF16),
        pltpu.VMEM((n_sh, 2, 16, 384), BF16),
        pltpu.VMEM((2, L, 8, E), F32),
        pltpu.VMEM((2, L, 8, C), F32),
        pltpu.VMEM((2, 8, HEAD), F32),
        pltpu.VMEM((2, L, 8, SE), F32),
        pltpu.VMEM((2, 8, CLASSES), F32),
        pltpu.VMEM((2, 16, HEAD), F32),
        pltpu.VMEM((8, CLASS_PAD), F32),
        pltpu.VMEM((2, 64, E), F32),
        pltpu.VMEM((2, 137, 384), F32),
        pltpu.VMEM((2, 320, C), F32),
        pltpu.VMEM((320, CLASSES), F32),
        pltpu.SemaphoreType.DMA((7,)),
    ]
    scratch = scratch + [pltpu.SemaphoreType.DMA((14,))] * 6 + [pltpu.SemaphoreType.DMA((L + 2,))]
    scratch = scratch + [
        pltpu.VMEM((FULL, LANES), F32),
        pltpu.VMEM((8, LANES), F32),
        pltpu.VMEM((2, 16, 384), F32),
        pltpu.VMEM((8, LANES), F32),
    ]
    for m in range(2):
        for rows in (56, 48, 8, 40):
            scratch = scratch + sum_scratch(sizes, rows)
    return pl.pallas_call(
        functools.partial(forward_kernel, sizes),
        out_shape=[o[0] for o in outs],
        in_specs=[vm] * 2 + [pl.BlockSpec(memory_space=pltpu.SMEM)] * 4 + [vm] * 2 + [hbm] * 8,
        out_specs=[o[1] for o in outs],
        scratch_shapes=scratch,
        compiler_params=pltpu.CompilerParams(collective_id=1, has_side_effects=True, vmem_limit_bytes=63 * 2**20),
        name="forward",
    )(*inputs)


BACK_ROWS = ((24, 24, 8, 24), (40, 24, 8, 40))


def round_up(value, unit):
    return -(-value // unit) * unit


CHUNKS = 6
MATS = 2 * E // LANES * 8
CHAN = 3 * 18
AT_CHAN = L * MATS
AT_HEAD = AT_CHAN + L * CHAN
AT_END = AT_HEAD + 2 * HEAD // 4 // 8


def packed_blocks(sizes):
    return round_up(AT_END, CHUNKS * 2 * sizes[0])


def backward_kernel(sizes, *refs):
    (dpool_h, extra, table, bucket, counts, wexp, headt, chan, gain_e, gain_c, gain_h,
     pre_s, mixed_s, feat_s, out_s, low_s, pool_s, unit_s, gate_s, tot_e, tot_c, tot_h,
     packed, back_e, back_c, back_h,
     pre, mixed, grad, grad_hid, low_out, low_pre, pads_x, pads_g, slope, dgate, dpool, stages, load_sems,
     held, held_chan, held_exb, held_sqb, out_v, low_v, row_sems, mask, area) = refs[:48]
    rest = list(refs[48:])
    edge_l, edge_r = table.at[0], table.at[1]
    n_dp, n_sh = sizes
    sums = []
    for b in range(BATCHES):
        group = []
        for rows in BACK_ROWS[b]:
            group.append((rest[0], rest[1], rest[2:6], rows))
            rest = rest[6:]
        sums.append(group)

    greet(sizes)

    def back_ref(b, kind, layer):
        return (back_e.at[layer, b, 0], back_e.at[layer, b, 1], back_c.at[layer, b], back_h.at[b])[kind]

    def summer(b, kind, layer):
        near, far, sems, rows = sums[b][kind]
        return Sum(near, far, back_ref(b, kind, layer), sems, sizes, rows)

    def load(b, kind, layer):
        rows = slice(b * HALF, (b + 1) * HALF)
        if kind == 0:
            return pltpu.make_async_copy(pre_s.at[layer, :, rows], pre.at[b], load_sems.at[b, 0])
        if kind == 1:
            return pltpu.make_async_copy(mixed_s.at[layer, :, rows], mixed.at[b], load_sems.at[b, 1])
        return pltpu.make_async_copy(feat_s.at[:, rows], pre.at[b, 0:HC], load_sems.at[b, 0])

    area[...] = jnp.full((8, LANES), fill_mask(mask, table, bucket, counts), F32)

    def load_out(layer):
        return pltpu.make_async_copy(out_s.at[layer], out_v, row_sems.at[0])

    def load_low(layer):
        return pltpu.make_async_copy(low_s.at[layer], low_v, row_sems.at[1])

    for b in range(BATCHES):
        load(b, 2, 0).start()
    load_low(L).start()
    load_out(L - 1).start()
    for b in range(BATCHES):
        load(b, 1, L - 1).start()
    for slot in range(IMGS):
        for pads in (pads_x, pads_g):
            pads[slot, 0:GAP, :] = jnp.zeros((GAP, LANES), F32)
            pads[slot, GAP + ROWS : 2 * GAP + ROWS, :] = jnp.zeros((GAP, LANES), F32)
    dgate[...] = jnp.zeros(dgate.shape, F32)
    stages[...] = jnp.zeros(stages.shape, F32)
    stages[1, 24:40, :] = extra[...]
    held_chan[...] = jnp.zeros(held_chan.shape, F32)
    spare = packed.shape[1] - AT_END
    if spare:
        packed[:, AT_END:] = jnp.zeros((n_sh, spare, 8, LANES), F32)

    def pack(first, c, value):
        for t in range(n_sh):
            for half in range(2):
                piece = value[64 * t : 64 * t + 64, half * LANES : (half + 1) * LANES]
                packed[t, pl.ds(first + 16 * c + 8 * half, 8)] = piece.reshape(8, 8, LANES)

    def pack_chan(layer):
        for k in range(EC):
            first = AT_CHAN + CHAN * layer + 18 * (k % 3)
            packed[k // 3, first : first + 18] = held_chan[:, k * LANES : (k + 1) * LANES].reshape(18, 8, LANES)

    def forward_total(kind, layer):
        return (tot_e.at[layer, 0], tot_e.at[layer, 1], tot_c.at[layer], tot_h)[kind]

    def moments(b, kind, layer, c):
        tot = forward_total(kind, layer)
        count = tot_e[0, 0, 48 + b : 49 + b, :]
        mean = tot[pl.ds(4 * c + 2 * b, 1), :] / count
        square = tot[pl.ds(4 * c + 2 * b + 1, 1), :] / count
        return mean, lax.rsqrt(square - mean * mean + EPS_NORM)

    def half_coefs(b, kind, layer, c, gain, shift):
        mean, scale = moments(b, kind, layer, c)
        scale = scale * gain
        return 0.5 * scale, 0.5 * (shift - mean * scale)

    def back_coefs(b, kind, layer, c, gain):
        mean, scale = moments(b, kind, layer, c)
        count = tot_e[0, 0, 48 + b : 49 + b, :]
        back = back_ref(b, kind, layer)
        plain = back[pl.ds(2 * c, 1), :]
        cross = scale * (back[pl.ds(2 * c + 1, 1), :] - mean * plain)
        first = scale * gain
        third = -first * scale * cross / count
        return first, -first * plain / count - mean * third, third

    def fold(value):
        return jnp.sum(value.reshape(value.shape[0] // 8, 8, LANES), 0)

    def put(stage, c, first, second):
        stage[pl.ds(2 * c, 1), :] = jnp.sum(first, 0, keepdims=True)
        stage[pl.ds(2 * c + 1, 1), :] = jnp.sum(second, 0, keepdims=True)

    def image(b, i):
        return slice(i * ROWS, (i + 1) * ROWS), slice(b * HALF + i * ROWS, b * HALF + (i + 1) * ROWS)

    def bend(half):
        t = jnp.tanh(half)
        return half + half * t, (0.5 + 0.5 * t) * (1.0 + half * (1.0 - t))

    def head_first(b, hook=None):
        stage = stages.at[b]

        def body(c):
            scale, shift = half_coefs(b, 3, 0, c, gain_h[0:1, lanes(c)], gain_h[1:2, lanes(c)])
            first = jnp.zeros((8, LANES), F32)
            second = jnp.zeros((8, LANES), F32)
            for i in range(IMGS):
                rows, full = image(b, i)
                x = pre[b, c, rows, :]
                half = mask[full, :] * (x * scale + shift)
                value = mask[full, :] * dpool_h[b * 8 + i : b * 8 + i + 1, lanes(c)] * bend(half)[1]
                grad[b, c, rows, :] = value
                first = first + fold(value)
                second = second + fold(value * x)
            put(stage, c, first, second)

        repeat(HC, body, hook)

    def norm_back_rows(b, kind, layer, c, gain, source):
        one, two, three = back_coefs(b, kind, layer, c, gain)
        for i in range(IMGS):
            rows, full = image(b, i)
            value = mask[full, :] * (one * grad[b, c, rows, :] + two + three * source[b, c, rows, :])
            low_pre[rows, lanes(c)] = value.astype(BF16)

    def put_hidden_sums(b, layer):
        stage = stages.at[b]
        for half in range(2):
            cols = slice(half * LANES, (half + 1) * LANES)
            first = jnp.zeros((8, LANES), F32)
            second = jnp.zeros((8, LANES), F32)
            for i in range(IMGS):
                full = image(b, i)[1]
                value = grad_hid[full, cols]
                first = first + fold(value)
                second = second + fold(value * out_v[full, cols])
            put(stage, half, first, second)

    def head_second(b, hook=None):
        mine = slice(b * HALF, (b + 1) * HALF)

        def body(c):
            for half in range(2):
                norm_back_rows(b, 3, 0, 2 * c + half, gain_h[0:1, lanes(2 * c + half)], pre)
            value = contract(low_pre[:, lanes(c, 256)], low_v[mine, :], 0, 0)
            if b == 0:
                held[c] = value
            else:
                value = value + held[c]
                for i in range(32):
                    row = 32 * c + i
                    for half in range(2):
                        packed[row // 40, AT_HEAD + 40 * half + lax.rem(row, 40)] = value[8 * i : 8 * i + 8, half * LANES : (half + 1) * LANES]

        repeat(HEAD // 256, body, hook)
        grad_hid[mine, :] = jnp.dot(low_pre[:, 0:HEAD], headt[...], preferred_element_type=F32)
        put_hidden_sums(b, L - 1)

    def block_gate(b, layer, hook=None):
        mine = slice(b * HALF, (b + 1) * HALF)
        eight = slice(b * 8, b * 8 + 8)
        for half in range(2):
            cols = slice(half * LANES, (half + 1) * LANES)
            one, two, three = back_coefs(b, 2, layer, half, gain_c[layer, 0:1, cols])
            for i in range(IMGS):
                rows, full = image(b, i)
                low_out[rows, cols] = (mask[full, :] * (one * grad_hid[full, cols] + two + three * out_v[full, cols])).astype(BF16)

        def body(c):
            value = jnp.dot(low_out[...], wexp[layer, :, lanes(E // 256 + c, 256)], preferred_element_type=F32)
            for part in range(2):
                k = 2 * c + part
                scale, shift = half_coefs(b, 1, layer, k, gain_e[layer, 2:3, lanes(k)], gain_e[layer, 3:4, lanes(k)])
                for i in range(IMGS):
                    rows, full = image(b, i)
                    act = act_half(mask[full, :] * (mixed[b, k, rows, :] * scale + shift))
                    piece = value[rows, part * LANES : (part + 1) * LANES]
                    grad[b, k, rows, :] = piece
                    dgate[i : i + 1, lanes(k)] = jnp.sum(fold(piece * act), 0, keepdims=True)
                    low_pre[rows, lanes(k)] = (act * gate_s[layer, b * 8 + i : b * 8 + i + 1, lanes(k)]).astype(BF16)
            value = contract(low_out[...], low_pre[:, lanes(c, 256)], 0, 0)
            if b == 0:
                held[c] = value
            else:
                pack(MATS * layer + MATS // 2, c, value + held[c])

        repeat(E // 256, body, hook)
        gate = gate_s[layer, eight, :]
        units = unit_s[layer, eight, :]
        sig = jax.nn.sigmoid(units)
        inner = dgate[...] * gate * (1.0 - gate)
        bias_x = jnp.sum(inner, 0, keepdims=True)
        grad_x = exact_outer(units * sig, inner)
        outer = exact(inner, chan[layer, 80:144, :], 1) * (sig * (1.0 + units * (1.0 - sig)))
        bias_r = jnp.sum(outer, 0, keepdims=True)
        grad_r = exact_outer(outer, pool_s[layer, eight, :])
        if b == 0:
            held_exb[0:1, :] = bias_x
            held_chan[9 + SE : 9 + 2 * SE, :] = grad_x
            held_sqb[0:1, 0:SE] = bias_r
            held_chan[9 : 9 + SE, :] = grad_r
        else:
            bias_x = bias_x + held_exb[0:1, :]
            for k in range(EC):
                stages[1, 24 + k : 25 + k, :] = bias_x[:, k * LANES : (k + 1) * LANES]
            stages[1, 24 + EC : 25 + EC, 0:SE] = bias_r + held_sqb[0:1, 0:SE]
            held_chan[9 : 9 + SE, :] = held_chan[9 : 9 + SE, :] + grad_r
            held_chan[9 + SE : 9 + 2 * SE, :] = held_chan[9 + SE : 9 + 2 * SE, :] + grad_x
        dpool[...] = exact(outer, chan[layer, 16:80, :], 0)

    def block_second(b, layer, hook=None):
        stage = stages.at[b]

        def body(c):
            scale, shift = half_coefs(b, 1, layer, c, gain_e[layer, 2:3, lanes(c)], gain_e[layer, 3:4, lanes(c)])
            first = jnp.zeros((8, LANES), F32)
            second = jnp.zeros((8, LANES), F32)
            for i in range(IMGS):
                rows, full = image(b, i)
                x = mixed[b, c, rows, :]
                half = mask[full, :] * (x * scale + shift)
                gate = gate_s[layer, b * 8 + i : b * 8 + i + 1, lanes(c)]
                value = mask[full, :] * (grad[b, c, rows, :] * gate + dpool[i : i + 1, lanes(c)] / area[0:1, :]) * bend(half)[1]
                grad[b, c, rows, :] = value
                first = first + fold(value)
                second = second + fold(value * x)
            put(stage, c, first, second)

        repeat(EC, body, hook)

    def block_spread(b, layer, hook=None):
        stage = stages.at[b]

        def body(c):
            scale, shift = half_coefs(b, 0, layer, c, gain_e[layer, 0:1, lanes(c)], gain_e[layer, 1:2, lanes(c)])
            one, two, three = back_coefs(b, 1, layer, c, gain_e[layer, 2:3, lanes(c)])
            tap_rows = chan[layer, 0:16, lanes(c)].astype(F32)
            tap = [tap_rows[k : k + 1, :] for k in range(9)]
            for i in range(IMGS):
                rows, full = image(b, i)
                act, der = bend(mask[full, :] * (pre[b, c, rows, :] * scale + shift))
                pads_x[i, GAP : GAP + ROWS, :] = act
                slope[rows, :] = mask[full, :] * der
                pads_g[i, GAP : GAP + ROWS, :] = mask[full, :] * (one * grad[b, c, rows, :] + two + three * mixed[b, c, rows, :])
            first = jnp.zeros((8, LANES), F32)
            second = jnp.zeros((8, LANES), F32)
            total = [jnp.zeros((8, LANES), F32) for k in range(9)]
            for i in range(IMGS):
                for t in range(ROWS // TILE_BACK):
                    start = GAP + t * TILE_BACK
                    rows = slice(i * ROWS + t * TILE_BACK, i * ROWS + (t + 1) * TILE_BACK)
                    g = [pads_g[i, start - o : start - o + TILE_BACK, :] for o in OFFSETS]
                    left, right = edge_l[t * TILE_BACK : (t + 1) * TILE_BACK, :], edge_r[t * TILE_BACK : (t + 1) * TILE_BACK, :]
                    wide = (g[1] * tap[1] + g[4] * tap[4] + g[7] * tap[7]
                            + right * (g[0] * tap[0] + g[3] * tap[3] + g[6] * tap[6])
                            + left * (g[2] * tap[2] + g[5] * tap[5] + g[8] * tap[8]))
                    value = wide * slope[rows, :]
                    grad[b, c, rows, :] = value
                    first = first + fold(value)
                    second = second + fold(value * pre[b, c, rows, :])
                    center = g[4]
                    sides = (center * left, center, center * right)
                    for k in range(9):
                        o = OFFSETS[k]
                        total[k] = total[k] + fold(sides[k % 3] * pads_x[i, start + o : start + o + TILE_BACK, :])
            put(stage, c, first, second)
            for k in range(9):
                row = jnp.sum(total[k], 0, keepdims=True)
                if b == 0:
                    held_chan[k : k + 1, lanes(c)] = row
                else:
                    held_chan[k : k + 1, lanes(c)] = held_chan[k : k + 1, lanes(c)] + row

        repeat(EC, body, hook)
        if b == 1:
            pack_chan(layer)

    def block_expand(b, layer, hook=None):
        mine = slice(b * HALF, (b + 1) * HALF)

        def body(c):
            for part in range(2):
                norm_back_rows(b, 0, layer, 2 * c + part, gain_e[layer, 0:1, lanes(2 * c + part)], pre)
            value = contract(low_v[mine, :], low_pre[:, lanes(c, 256)], 0, 0)
            if b == 0:
                held[c] = value
            else:
                pack(MATS * layer, c, value + held[c])

        repeat(E // 256, body, hook)
        if layer > 0:
            grad_hid[mine, :] = grad_hid[mine, :] + contract(low_pre[...], wexp[layer, :, 0:E], 1, 1)
            put_hidden_sums(b, layer - 1)

    heads = [summer(b, 3, 0) for b in range(BATCHES)]
    load(0, 2, 0).wait()
    head_first(0)
    heads[0].start(stages.at[0])
    load(1, 2, 0).wait()
    head_first(1, (5, heads[0].middle))
    heads[1].start(stages.at[1])
    thirds = [summer(b, 2, L - 1) for b in range(BATCHES)]
    heads[0].finish()
    load_low(L).wait()
    load_out(L - 1).wait()
    head_second(0, (2, heads[1].middle))
    load(0, 0, L - 1).start()
    thirds[0].start(stages.at[0])
    heads[1].finish()
    head_second(1, (3, thirds[0].middle))
    load(1, 0, L - 1).start()
    thirds[1].start(stages.at[1])
    load_low(L - 1).start()
    for layer in reversed(range(L)):
        twos = [summer(b, 1, layer) for b in range(BATCHES)]
        ones = [summer(b, 0, layer) for b in range(BATCHES)]
        thirds[0].finish()
        load(0, 1, layer).wait()
        block_gate(0, layer, (3, thirds[1].middle))
        block_second(0, layer)
        twos[0].start(stages.at[0])
        thirds[1].finish()
        load(1, 1, layer).wait()
        block_gate(1, layer, (3, twos[0].middle))
        if layer > 0:
            load_out(layer - 1).start()
        block_second(1, layer)
        twos[1].start(stages.at[1])
        twos[0].finish()
        load(0, 0, layer).wait()
        block_spread(0, layer, (4, twos[1].middle))
        ones[0].start(stages.at[0])
        if layer > 0:
            load(0, 1, layer - 1).start()
        twos[1].finish()
        load(1, 0, layer).wait()
        block_spread(1, layer, (4, ones[0].middle))
        ones[1].start(stages.at[1])
        if layer > 0:
            load(1, 1, layer - 1).start()
        ones[0].finish()
        load_low(layer).wait()
        if layer > 0:
            load_out(layer - 1).wait()
        block_expand(0, layer, (3, ones[1].middle))
        if layer > 0:
            thirds = [summer(b, 2, layer - 1) for b in range(BATCHES)]
            thirds[0].start(stages.at[0])
            load(0, 0, layer - 1).start()
        ones[1].finish()
        block_expand(1, layer, None if layer == 0 else (3, thirds[0].middle))
        if layer > 0:
            thirds[1].start(stages.at[1])
            load(1, 0, layer - 1).start()
            load_low(layer - 1).start()


def run_backward_all(sizes, inputs):
    sds = jax.ShapeDtypeStruct
    vm = pl.BlockSpec(memory_space=pltpu.VMEM)
    hbm = pl.BlockSpec(memory_space=pl.ANY)
    n_dp, n_sh = sizes
    outs = [
        sds((n_sh, packed_blocks(sizes), 8, LANES), F32),
        sds((L, BATCHES, 2, 40, LANES), F32),
        sds((L, BATCHES, 8, LANES), F32),
        sds((BATCHES, 40, LANES), F32),
    ]
    scratch = [
        pltpu.VMEM((BATCHES, EC, HALF, LANES), F32),
        pltpu.VMEM((BATCHES, EC, HALF, LANES), F32),
        pltpu.VMEM((BATCHES, EC, HALF, LANES), F32),
        pltpu.VMEM((FULL, C), F32),
        pltpu.VMEM((HALF, C), BF16),
        pltpu.VMEM((HALF, E), BF16),
        pltpu.VMEM((IMGS, ROWS + 2 * GAP, LANES), F32),
        pltpu.VMEM((IMGS, ROWS + 2 * GAP, LANES), F32),
        pltpu.VMEM((HALF, LANES), F32),
        pltpu.VMEM((8, E), F32),
        pltpu.VMEM((8, E), F32),
        pltpu.VMEM((BATCHES, 40, LANES), F32),
        pltpu.SemaphoreType.DMA((BATCHES, 2)),
        pltpu.VMEM((E // 256, 256, 256), F32),
        pltpu.VMEM((144, E), F32),
        pltpu.VMEM((8, E), F32),
        pltpu.VMEM((8, LANES), F32),
        pltpu.VMEM((FULL, C), F32),
        pltpu.VMEM((FULL, C), BF16),
        pltpu.SemaphoreType.DMA((2,)),
        pltpu.VMEM((FULL, LANES), F32),
        pltpu.VMEM((8, LANES), F32),
    ]
    for b in range(BATCHES):
        for rows in BACK_ROWS[b]:
            scratch = scratch + sum_scratch(sizes, rows)
    specs = [vm] * 3 + [pl.BlockSpec(memory_space=pltpu.SMEM)] * 2 + [vm] * 6 + [hbm] * 5 + [vm] * 6
    return pl.pallas_call(
        functools.partial(backward_kernel, sizes),
        out_shape=outs,
        in_specs=specs,
        out_specs=[vm] * len(outs),
        scratch_shapes=scratch,
        compiler_params=pltpu.CompilerParams(collective_id=2, has_side_effects=True, vmem_limit_bytes=63 * 2**20),
        name="backward",
    )(*inputs)


GROUPS = 12


def update_kernel(sizes, *refs):
    (packed, facts, fixes, tot_e, tot_c, tot_h, back_e, back_c, back_h, *state) = refs[:21]
    state_in = [state[3 * k : 3 * k + 3] for k in range(4)]
    out_refs = refs[21:25]
    gain_grad, norms, peers = refs[25:28]
    (own, near, cross, side, line, full, gathered, g_class, sums_near) = refs[28:37]
    boxes = [refs[37 + 4 * k : 41 + 4 * k] for k in range(4)]
    (core_s, core_r, x_s, x_r, y_s, y_r, z_s, z_r, zz_s, zz_r, yy_s, yy_r,
     fn_s, fn_r, ff_s, ff_r, nn_s, nn_r, load_sems, store_sems, misc) = refs[53:74]
    n_dp, n_sh = sizes
    d, s = lax.axis_index("dp"), lax.axis_index("shard")
    count = packed_blocks(sizes)
    chunk = count // CHUNKS
    half = chunk // 2
    n_z = n_dp // 2
    piece = half // n_z
    bit0, bit1 = lax.rem(s, 2), s // 2
    near_peer = s + 1 - 2 * bit0
    far_peer = s + 2 - 4 * bit1
    yb, zi = lax.rem(d, 2), d // 2
    y_peer = d + 1 - 2 * yb

    greet(sizes)

    def load_own(t):
        return pltpu.make_async_copy(packed.at[t], own.at[t], load_sems.at[16 + t])

    def load(k, i):
        if k == 1:
            return [pltpu.make_async_copy(state_in[1][i].at[:, l], boxes[1][i].at[l], load_sems.at[2 * i + 24 + l]) for l in range(L)]
        return [pltpu.make_async_copy(state_in[k][i], boxes[k][i], load_sems.at[4 * k + i])]

    def store(k):
        if k == 1:
            return [pltpu.make_async_copy(boxes[1][3].at[l], out_refs[1].at[:, l], store_sems.at[4 + l]) for l in range(L)]
        return [pltpu.make_async_copy(boxes[k][3], out_refs[k], store_sems.at[k])]

    def core_copy(k, i):
        rows = pl.ds(k * chunk, chunk)
        return pltpu.make_async_remote_copy(
            packed.at[2 * i + 1 - bit0, rows], near.at[i, rows], core_s.at[k, i], core_r.at[k, i],
            device_id=(d, near_peer), device_id_type=MESH)

    def x_copy(k):
        rows = pl.ds(k * chunk, chunk)
        return pltpu.make_async_remote_copy(
            own.at[far_peer, rows], cross.at[rows], x_s.at[k], x_r.at[k],
            device_id=(d, far_peer), device_id_type=MESH)

    def y_copy(k):
        rows = pl.ds(k * chunk + (1 - yb) * half, half)
        return pltpu.make_async_remote_copy(
            own.at[s, rows], side.at[k], y_s.at[k], y_r.at[k],
            device_id=(y_peer, s), device_id_type=MESH)

    def z_copy(k, step, source, target):
        rows = pl.ds(k * chunk + yb * half + target * piece, piece)
        return pltpu.make_async_remote_copy(
            own.at[s, rows], line.at[k, source], z_s.at[k, step], z_r.at[k, source],
            device_id=(2 * target + yb, s), device_id_type=MESH)

    def zz_copy(k, step, source, target):
        rows = pl.ds(k * (chunk // 2) + yb * (half // 2) + source * (piece // 2), piece // 2)
        return pltpu.make_async_remote_copy(
            full.at[rows], full.at[rows], zz_s.at[k, step], zz_r.at[k, source],
            device_id=(2 * target + yb, s), device_id_type=MESH)

    def yy_copy(k, b):
        rows = pl.ds(k * (chunk // 2) + b * (half // 2), half // 2)
        return pltpu.make_async_remote_copy(
            full.at[rows], full.at[rows], yy_s.at[k], yy_r.at[k],
            device_id=(y_peer, s), device_id_type=MESH)

    def over_z(action):
        def step(j, carry):
            action(j, lax.rem(zi + j, n_z))
            return carry

        lax.fori_loop(1, n_z, step, 0)

    def add_into(t, low, length, other, low_other, unit=8):
        def step(i, carry):
            rows = pl.ds(low + i * unit, unit)
            own[t, rows] = own[t, rows] + other(pl.ds(low_other + i * unit, unit))
            return carry

        lax.fori_loop(0, length // unit, step, 0)

    def stage_core(k):
        for i in range(2):
            core_copy(k, i).start()

    def stage_x(k):
        for i in range(2):
            core_copy(k, i).wait_recv()
        low = k * chunk
        add_into(far_peer, low, chunk, lambda rows: near[1 - bit1, rows], low)
        x_copy(k).start()
        add_into(s, low, chunk, lambda rows: near[bit1, rows], low)

    def stage_y(k):
        x_copy(k).wait_recv()
        low = k * chunk
        give = low + (1 - yb) * half
        keep = low + yb * half
        add_into(s, give, half, lambda rows: cross[rows], give)
        y_copy(k).start()
        add_into(s, keep, half, lambda rows: cross[rows], keep)

    def stage_z(k):
        y_copy(k).wait_recv()
        add_into(s, k * chunk + yb * half, half, lambda rows: side[k, rows], 0)
        over_z(lambda j, t: z_copy(k, j, zi, t).start())

    def stage_zz(k):
        over_z(lambda j, t: z_copy(k, j, t, zi).wait_recv())
        low = k * chunk + yb * half + zi * piece

        def step(i, carry):
            total = own[s, pl.ds(low + 2 * i, 2)]
            for j in range(1, n_z):
                total = total + line[k, lax.rem(zi + j, n_z), pl.ds(2 * i, 2)]
            full[low // 2 + i] = total.reshape(16, LANES).astype(BF16)
            return carry

        lax.fori_loop(0, piece // 2, step, 0)
        over_z(lambda j, t: zz_copy(k, j, zi, t).start())

    def stage_yy(k):
        over_z(lambda j, t: zz_copy(k, j, t, zi).wait_recv())
        yy_copy(k, yb).start()

    def stage_done(k):
        yy_copy(k, 1 - yb).wait_recv()

    def settle(k):
        for i in range(2):
            core_copy(k, i).wait_send()
        x_copy(k).wait_send()
        y_copy(k).wait_send()
        over_z(lambda j, t: z_copy(k, j, zi, t).wait_send())
        over_z(lambda j, t: zz_copy(k, j, zi, t).wait_send())
        yy_copy(k, yb).wait_send()

    def own_facts():
        return pltpu.make_async_copy(facts.at[s], peers.at[d, s], misc.at[0])

    def fact_near(step, source, target):
        return pltpu.make_async_remote_copy(
            facts.at[target], peers.at[d, source], fn_s.at[step], fn_r.at[source],
            device_id=(d, target), device_id_type=MESH)

    def fact_far(step, source, target):
        return pltpu.make_async_remote_copy(
            peers.at[source], peers.at[source], ff_s.at[step], ff_r.at[source],
            device_id=(target, s), device_id_type=MESH)

    def over_dp(action):
        def step(j, carry):
            action(j, lax.rem(d + j, n_dp))
            return carry

        lax.fori_loop(1, n_dp, step, 0)

    def facts_begin():
        own_facts().start()
        for j in range(1, n_sh):
            fact_near(j, s, lax.rem(s + j, n_sh)).start()

    def facts_second():
        for j in range(1, n_sh):
            fact_near(j, lax.rem(s + j, n_sh), s).wait_recv()
            fact_near(j, s, s).wait_send()
        own_facts().wait()
        over_dp(lambda j, t: fact_far(j, d, t).start())

    def facts_third():
        def arrive(j, t):
            fact_far(j, t, d).wait_recv()
            fact_far(j, d, d).wait_send()

        over_dp(arrive)
        for first in range(0, n_dp, 8):
            copy = pltpu.make_async_copy(peers.at[pl.ds(first, 8)], gathered, misc.at[1])
            copy.start()
            copy.wait()
            value = gathered[...].reshape(8 * n_sh * 16, FACT)
            product = contract(value[:, CLASS_PAD:], value[:, :CLASS_PAD], 0, 0)
            g_class[...] = product if first == 0 else g_class[...] + product

    sums_near[s] = jnp.zeros((24, LANES), F32)
    first_fix, second_fix = fixes[0], fixes[1]

    def note(row, value):
        square = value * value
        width = square.shape[1]
        line_sum = jnp.sum(square, 0, keepdims=True)
        total = jnp.zeros((1, LANES), F32)
        for low in range(0, width - width % LANES, LANES):
            total = total + line_sum[:, low : low + LANES]
        tail = width % LANES
        if tail:
            total = total + jnp.concatenate([line_sum[:, width - tail :], jnp.zeros((1, LANES - tail), F32)], 1)
        sums_near[s, row : row + 1, :] = sums_near[s, row : row + 1, :] + total

    def moments(k, index, grad):
        weight, first, second, kept = boxes[k]
        kept[index] = grad
        new_first = BETA_ONE * first[index] + (1.0 - BETA_ONE) * grad
        new_second = BETA_TWO * second[index] + (1.0 - BETA_TWO) * grad * grad
        return new_first / first_fix / (jnp.sqrt(new_second / second_fix) + EPS_ADAM) + DECAY * weight[index]

    def gains_part():
        def norm(tot, back_of, chunk):
            grad, shift = jnp.zeros((1, LANES), F32), jnp.zeros((1, LANES), F32)
            for b in range(BATCHES):
                count = tot_e[0, 0, 48 + b : 49 + b, :]
                mean = tot[pl.ds(4 * chunk + 2 * b, 1), :] / count
                scale = lax.rsqrt(tot[pl.ds(4 * chunk + 2 * b + 1, 1), :] / count - mean * mean + EPS_NORM)
                back = back_of(b)
                plain = back[pl.ds(2 * chunk, 1), :]
                grad = grad + scale * (back[pl.ds(2 * chunk + 1, 1), :] - mean * plain)
                shift = shift + plain
            return grad, shift

        def mine(value, width):
            part = value[:, 0:width]
            for t in range(1, n_sh):
                part = jnp.where(s == t, value[:, t * width : (t + 1) * width], part)
            return part

        start = 0
        for layer in range(L):
            for kind in range(2):
                for q in range(3):
                    pair = norm(tot_e.at[layer, kind], lambda b: back_e.at[layer, b, kind], 3 * s + q)
                    for which in range(2):
                        low = start + 384 * (2 * kind + which) + LANES * q
                        gain_grad[0:1, low : low + LANES] = pair[which]
            for q in range(3):
                low = start + 384 * 4 + LANES * q
                gain_grad[0:1, low : low + LANES] = back_e[layer, 1, 0, pl.ds(24 + 3 * s + q, 1), :]
            low = start + 384 * 5
            pairs = [norm(tot_c.at[layer], lambda b: back_c.at[layer, b], c) for c in range(2)]
            for which in range(2):
                whole = jnp.concatenate([pairs[0][which], pairs[1][which]], 1)
                gain_grad[0:1, low + 64 * which : low + 64 * which + 64] = mine(whole, 64)
            gain_grad[0:1, low + 128 : low + 144] = mine(back_e[layer, 1, 0, 24 + EC : 25 + EC, :], 16)
            start = low + 144
        pairs = [norm(tot_h, lambda b: back_h.at[b], c) for c in range(HC)]
        for which in range(2):
            whole = jnp.concatenate([pair[which] for pair in pairs], 1)
            gain_grad[0:1, start + 320 * which : start + 320 * which + 320] = mine(whole, 320)
        whole = jnp.concatenate([back_h[1, 24 + k : 25 + k, :] for k in range(8)], 1)
        gain_grad[0:1, start + 640 : start + 890] = mine(whole, 250)

    every = slice(None)

    def mats_index(layer, c):
        return (layer, every, lanes(c))

    def weights_squares():
        for layer in range(L):
            for part in range(2):

                def body(c):
                    note(2 * layer + part, boxes[0][0][mats_index(layer, c + part * EC)])

                repeat(EC, body)
            for kk in range(3):
                cols = slice(kk * LANES, (kk + 1) * LANES)
                note(2 * L + 3 * layer, boxes[1][0][layer, 0:9, cols])
                note(2 * L + 3 * layer + 1, boxes[1][0][layer, 9 : 9 + SE, cols])
                note(2 * L + 3 * layer + 2, boxes[1][0][layer, 9 + SE : 9 + 2 * SE, cols])
        note(5 * L, boxes[2][0][...])

        def body(i):
            note(5 * L + 1, boxes[3][0][pl.ds(pl.multiple_of(i * 40, 40), 40), :])

        repeat(8, body)

    def mats_moments(layer):
        for part in range(2):

            def body(c):
                panel = c + part * EC
                grad = full[pl.ds(layer * (MATS // 2) + 4 * panel, 4)].astype(F32).reshape(64, LANES)
                note(GROUPS + 2 * layer + part, moments(0, mats_index(layer, panel), grad))

            repeat(EC, body)

    def chan_moments():
        for layer in range(L):
            for kk in range(3):
                low = (AT_CHAN + CHAN * layer + 18 * kk) // 2
                grad = full[low : low + 9].astype(F32).reshape(144, LANES)[:137]
                value = moments(1, (layer, every, slice(kk * LANES, (kk + 1) * LANES)), grad)
                note(GROUPS + 2 * L + 3 * layer, value[0:9])
                note(GROUPS + 2 * L + 3 * layer + 1, value[9 : 9 + SE])
                note(GROUPS + 2 * L + 3 * layer + 2, value[9 + SE :])

    def head_moments():
        rows = HEAD // 4
        for part in range(2):
            low = (AT_HEAD + part * (rows // 8)) // 2
            grad = full[low : low + rows // 16].astype(F32).reshape(rows, LANES)
            note(GROUPS + 5 * L, moments(2, (every, slice(part * LANES, (part + 1) * LANES)), grad))

    def class_moments():
        def body(i):
            rows = pl.ds(pl.multiple_of(i * 40, 40), 40)
            note(GROUPS + 5 * L + 1, moments(3, (rows, every), g_class[rows, :CLASSES]))

        repeat(8, body)

    def norm_copy(step, source, target):
        return pltpu.make_async_remote_copy(
            sums_near.at[source], sums_near.at[source], nn_s.at[step], nn_r.at[source],
            device_id=(d, target), device_id_type=MESH)

    for k in range(CHUNKS):
        stage_core(k)
    for t in range(n_sh):
        load_own(t).start()
    facts_begin()
    for i in range(3):
        for k in range(4):
            for copy in load(k, i):
                copy.start()
    for t in range(n_sh):
        load_own(t).wait()
    for tau in range(1, CHUNKS + 6):
        stages = (stage_x, stage_y, stage_z, stage_zz, stage_yy, stage_done)
        for age, stage in enumerate(stages):
            k = tau - 1 - age
            if 0 <= k < CHUNKS:
                stage(k)
        if tau == 1:
            facts_second()
            for k in range(4):
                for copy in load(k, 0):
                    copy.wait()
            weights_squares()
        if tau == 2:
            gains_part()
            for i in range(1, 3):
                for k in range(4):
                    for copy in load(k, i):
                        copy.wait()
        if tau == CHUNKS:
            facts_third()
            class_moments()
            for copy in store(3):
                copy.start()
        if tau == CHUNKS + 2:
            mats_moments(0)
        if tau == CHUNKS + 4:
            mats_moments(1)
            for copy in store(0):
                copy.start()
    chan_moments()
    head_moments()
    for j in range(1, n_sh):
        norm_copy(j, s, lax.rem(s + j, n_sh)).start()
    for k in (1, 2):
        for copy in store(k):
            copy.start()
    for k in range(CHUNKS):
        settle(k)
    for j in range(1, n_sh):
        norm_copy(j, lax.rem(s + j, n_sh), s).wait_recv()
        norm_copy(j, s, s).wait_send()
    total = sums_near[0]
    for j in range(1, n_sh):
        total = total + sums_near[j]
    root = jnp.broadcast_to(jnp.sqrt(jnp.sum(total, 1, keepdims=True)), (24, LANES))
    norms[0:24, :] = root
    norms[24:32, :] = back_h[1, 32:40, :]
    for k in range(4):
        for copy in store(k):
            copy.wait()


def run_update(sizes, inputs, states):
    sds = jax.ShapeDtypeStruct
    vm = pl.BlockSpec(memory_space=pltpu.VMEM)
    hbm = pl.BlockSpec(memory_space=pl.ANY)
    n_dp, n_sh = sizes
    count = packed_blocks(sizes)
    chunk = count // CHUNKS
    n_z = n_dp // 2
    sem = pltpu.SemaphoreType.DMA
    outs = [sds(group[0].shape, F32) for group in states]
    gains = sum(([E // n_sh] * 5 + [(2 * C + SE) // n_sh]) * L) + (2 * HEAD + CLASSES) // n_sh
    outs = outs + [sds((1, gains), F32), sds((32, LANES), F32), sds((n_dp, n_sh, 16, FACT), BF16)]
    scratch = [
        pltpu.VMEM((n_sh, count, 8, LANES), F32),
        pltpu.VMEM((2, count, 8, LANES), F32),
        pltpu.VMEM((count, 8, LANES), F32),
        pltpu.VMEM((CHUNKS, chunk // 2, 8, LANES), F32),
        pltpu.VMEM((CHUNKS, n_z, chunk // 2 // n_z, 8, LANES), F32),
        pltpu.VMEM((count // 2, 16, LANES), BF16),
        pltpu.VMEM((8, n_sh, 16, FACT), BF16),
        pltpu.VMEM((FACT - CLASS_PAD, CLASS_PAD), F32),
        pltpu.VMEM((n_sh, 2 * GROUPS, LANES), F32),
    ]
    for k, group in enumerate(states):
        shape = group[0].shape if k != 1 else (L, 137, 384)
        scratch = scratch + [pltpu.VMEM(shape, F32)] * 4
    scratch = scratch + [
        sem((CHUNKS, 2)), sem((CHUNKS, 2)), sem((CHUNKS,)), sem((CHUNKS,)), sem((CHUNKS,)), sem((CHUNKS,)),
        sem((CHUNKS, n_z)), sem((CHUNKS, n_z)), sem((CHUNKS, n_z)), sem((CHUNKS, n_z)), sem((CHUNKS,)), sem((CHUNKS,)),
        sem((n_sh,)), sem((n_sh,)), sem((n_dp,)), sem((n_dp,)), sem((n_sh,)), sem((n_sh,)),
        sem((32,)), sem((24,)), sem((2,)),
    ]
    return pl.pallas_call(
        functools.partial(update_kernel, sizes),
        out_shape=outs,
        in_specs=[hbm, hbm, pl.BlockSpec(memory_space=pltpu.SMEM)] + [vm] * 6 + [hbm] * 12,
        out_specs=[hbm] * 4 + [vm, vm, hbm],
        scratch_shapes=scratch,
        compiler_params=pltpu.CompilerParams(collective_id=3, has_side_effects=True, vmem_limit_bytes=63 * 2**20),
        name="update",
    )(*inputs, *[item for group in states for item in group])


def mats_factor(ratio, value):
    paired = ratio.reshape(-1, 2)
    column = jnp.arange(value.shape[2])
    return jnp.where(column[None, :] < value.shape[2] // 2, paired[:, 0:1], paired[:, 1:2])[
        :, None, :
    ]


def chan_factor(ratio, value):
    triple = ratio.reshape(-1, 3)
    row = jnp.arange(value.shape[1])[None, :]
    return jnp.where(
        row < 9, triple[:, 0:1], jnp.where(row < 9 + SE, triple[:, 1:2], triple[:, 2:3])
    )[:, :, None]


def adapt(first, second, grad, first_fix, second_fix):
    new_first = BETA_ONE * first + (1.0 - BETA_ONE) * grad
    new_second = BETA_TWO * second + (1.0 - BETA_TWO) * grad * grad
    update = new_first / first_fix / (jnp.sqrt(new_second / second_fix) + EPS_ADAM)
    return (new_first, new_second, update)


def per_device(
    images,
    bucket,
    counts,
    balance,
    labels,
    step,
    expand_w,
    expand_m,
    expand_v,
    expand_e,
    chan_w,
    chan_m,
    chan_v,
    chan_e,
    head_w,
    head_m,
    head_v,
    head_e,
    class_w,
    class_m,
    class_v,
    class_e,
    gain_w,
    gain_m,
    gain_v,
    gain_e,
):
    sizes = (lax.axis_size("dp"), lax.axis_size("shard"))
    table = jnp.asarray(tables())
    turned = lambda value: value.transpose(1, 0, 2)
    saved = run_forward_all(
        sizes,
        [
            images.reshape(FULL, C), table, bucket, counts, balance, labels, gain_w, gain_e,
            expand_w, expand_e, turned(chan_w), turned(chan_e), head_w.T, head_e.T, class_w, class_e,
        ],
    )
    kept = saved[:11]
    tot_e, tot_c, tot_h = kept[8:11]
    dpool_h, extra, facts, wexp_s, headt_s, chan_s, vec_e, vec_c, vec_h = saved[11:]
    (packed, back_e, back_c, back_h) = run_backward_all(
        sizes,
        [dpool_h, extra, table, bucket, counts, wexp_s, headt_s, chan_s, vec_e, vec_c, vec_h, *kept],
    )
    power = step[0].astype(F32)
    first_fix = 1.0 - jnp.power(jnp.float32(BETA_ONE), power)
    second_fix = 1.0 - jnp.power(jnp.float32(BETA_TWO), power)
    grads = run_update(
        sizes,
        [packed, facts, jnp.stack([first_fix, second_fix]), tot_e, tot_c, tot_h, back_e, back_c, back_h],
        [
            (expand_w, expand_m, expand_v),
            tuple(turned(item) for item in (chan_w, chan_m, chan_v)),
            tuple(item.T for item in (head_w, head_m, head_v)),
            (class_w, class_m, class_v),
        ],
    )
    roots = grads[5][: 2 * GROUPS, 0].reshape(2, GROUPS)
    ratio = roots[0] / roots[1]
    weights = (expand_w, chan_w, head_w, class_w, gain_w)
    firsts = (expand_m, chan_m, head_m, class_m, gain_m)
    seconds = (expand_v, chan_v, head_v, class_v, gain_v)
    averaged = (expand_e, chan_e, head_e, class_e, gain_e)
    owned = (grads[0], turned(grads[1]), grads[2].T, grads[3], grads[4])
    factors = [
        mats_factor(ratio[: 2 * L], expand_w),
        chan_factor(ratio[2 * L : 5 * L], chan_w),
        ratio[5 * L],
        ratio[5 * L + 1],
    ]
    result = [grads[5][2 * GROUPS, 0]]
    for item in range(5):
        new_first, new_second, update = adapt(firsts[item], seconds[item], owned[item], first_fix, second_fix)
        if item < 4:
            fresh = weights[item] - RATE * factors[item] * (update + DECAY * weights[item])
        else:
            fresh = weights[item] - RATE * update
        result = result + [fresh, new_first, new_second, KEEP * averaged[item] + (1.0 - KEEP) * fresh]
    return tuple(result + [roots])


def solution(mesh):
    in_specs = (
        P(None, ("dp", "shard"), None, None, None),
        P("dp"),
        P(None, ("dp", "shard")),
        P(None, ("dp", "shard")),
        P(None, ("dp", "shard")),
        P(),
        P(None, "shard", None),
        P(None, "shard", None),
        P(None, "shard", None),
        P(None, "shard", None),
        P(None, None, "shard"),
        P(None, None, "shard"),
        P(None, None, "shard"),
        P(None, None, "shard"),
        P(None, "shard"),
        P(None, "shard"),
        P(None, "shard"),
        P(None, "shard"),
        P("shard", None),
        P("shard", None),
        P("shard", None),
        P("shard", None),
        P("shard", None),
        P("shard", None),
        P("shard", None),
        P("shard", None),
    )
    out_specs = (
        P(),
        P(None, "shard", None),
        P(None, "shard", None),
        P(None, "shard", None),
        P(None, "shard", None),
        P(None, None, "shard"),
        P(None, None, "shard"),
        P(None, None, "shard"),
        P(None, None, "shard"),
        P(None, "shard"),
        P(None, "shard"),
        P(None, "shard"),
        P(None, "shard"),
        P("shard", None),
        P("shard", None),
        P("shard", None),
        P("shard", None),
        P("shard", None),
        P("shard", None),
        P("shard", None),
        P("shard", None),
        P(),
    )
    return jax.shard_map(
        per_device, mesh=mesh, in_specs=in_specs, out_specs=out_specs, check_vma=False
    )
```

```python
import functools

import jax
import jax.numpy as jnp
from jax import lax
from jax.experimental import pallas as pl
from jax.experimental.pallas import tpu as pltpu
from jax.sharding import PartitionSpec as P
import numpy as np

C = 256
E = 1536
SE = 64
HEAD = 1280
CLASSES = 1000
L = 2
S = 12


EPS_NORM = 1e-05
BETA_ONE = 0.9
BETA_TWO = 0.99
EPS_ADAM = 1e-08
DECAY = 0.01
RATE = 0.3
KEEP = 0.9


def contract(left, right, left_dim, right_dim):
    return lax.dot_general(
        left, right, (((left_dim,), (right_dim,)), ((), ())), preferred_element_type=jnp.float32
    )


def matmul(left, right):
    return jnp.dot(left, right, precision=lax.Precision.HIGHEST, preferred_element_type=jnp.float32)


def matmul_bt(left, right):
    return lax.dot_general(
        left,
        right,
        (((1,), (1,)), ((), ())),
        precision=lax.Precision.HIGHEST,
        preferred_element_type=jnp.float32,
    )


def matmul_tb(left, right):
    return lax.dot_general(
        left,
        right,
        (((0,), (0,)), ((), ())),
        precision=lax.Precision.HIGHEST,
        preferred_element_type=jnp.float32,
    )


def pack_gains(vectors, rows):
    return jnp.concatenate([vector.reshape(rows, -1) for vector in vectors], 1)


IMGS = 5
ROWS = S * S
BATCHES = 2
HALF = IMGS * ROWS
FULL = BATCHES * HALF
SLOTS = BATCHES * IMGS
LANES = 128
EC = E // LANES
HC = HEAD // LANES
GAP = 16
TILE = 48
TILE_BACK = 48
CLASS_PAD = 1024
FACT = CLASS_PAD + 384
OFFSETS = [S * (a - 1) + (c - 1) for a in range(3) for c in range(3)]
MESH = pl.DeviceIdType.MESH
F32 = jnp.float32
BF16 = jnp.bfloat16


def split(value):
    high = value.astype(BF16).astype(F32)
    rest = value - high
    middle = rest.astype(BF16).astype(F32)
    return jnp.concatenate([high, middle, rest - middle], 0)


def exact(value, low_weight, dim):
    rows = value.shape[0]
    parts = contract(split(value).astype(BF16), low_weight, 1, dim)
    return parts[0:rows] + parts[rows : 2 * rows] + parts[2 * rows : 3 * rows]


def exact_outer(left, right):
    rows = left.shape[0]
    l, r = split(left), split(right)
    pick = lambda value, order: jnp.concatenate([value[k * rows : (k + 1) * rows] for k in order], 0).astype(BF16)
    return contract(pick(l, (0, 0, 1, 1, 0, 2)), pick(r, (0, 1, 0, 1, 2, 0)), 0, 0)


def tables():
    spot = np.arange(ROWS)
    rows = [spot % S > 0, spot % S < S - 1, spot // S, spot % S]
    return np.broadcast_to(np.stack(rows).astype(np.float32)[:, :, None], (4, ROWS, LANES))


def fill_mask(mask, table, bucket, counts):
    code = bucket[0]
    side = jnp.where(code == 0, 7, jnp.where(code == 1, 10, 12)).astype(F32)
    inside = jnp.where((table[2] < side) & (table[3] < side), 1.0, 0.0)
    for b in range(BATCHES):
        for i in range(IMGS):
            low = b * HALF + i * ROWS
            mask[low : low + ROWS, :] = inside * jnp.where(i < counts[b, 0], 1.0, 0.0)
    return side * side


class Sum:
    def __init__(self, near, far, total, sems, sizes, rows):
        self.near, self.far, self.total = near, far, total
        self.sems = sems
        self.n_dp, self.n_sh = sizes
        self.rows = rows

    def copy_near(self, step, slot, target):
        d = lax.axis_index("dp")
        return pltpu.make_async_remote_copy(
            self.near.at[slot], self.near.at[slot],
            self.sems[0].at[step], self.sems[1].at[slot],
            device_id=(d, target), device_id_type=MESH)

    def copy_far(self, step, slot, target):
        s = lax.axis_index("shard")
        return pltpu.make_async_remote_copy(
            self.far.at[slot], self.far.at[slot],
            self.sems[2].at[step], self.sems[3].at[slot],
            device_id=(target, s), device_id_type=MESH)

    def start(self, stage):
        s = lax.axis_index("shard")
        self.near[s] = stage[0 : self.rows]
        for j in range(1, self.n_sh):
            self.copy_near(j, s, lax.rem(s + j, self.n_sh)).start()

    def middle(self):
        s, d = lax.axis_index("shard"), lax.axis_index("dp")
        for j in range(1, self.n_sh):
            self.copy_near(j, lax.rem(s + j, self.n_sh), s).wait_recv()
        for j in range(1, self.n_sh):
            self.copy_near(j, s, s).wait_send()
        part = self.near[0]
        for j in range(1, self.n_sh):
            part = part + self.near[j]
        self.far[d] = part

        def send(j, carry):
            self.copy_far(j, d, lax.rem(d + j, self.n_dp)).start()
            return carry

        lax.fori_loop(1, self.n_dp, send, 0)

    def finish(self):
        d = lax.axis_index("dp")

        def arrive(j, carry):
            self.copy_far(j, lax.rem(d + j, self.n_dp), d).wait_recv()
            self.copy_far(j, d, d).wait_send()
            return carry

        lax.fori_loop(1, self.n_dp, arrive, 0)
        part = self.far[0]
        for j in range(1, self.n_dp):
            part = part + self.far[j]
        self.total[0 : self.rows] = part


def sum_scratch(sizes, rows):
    n_dp, n_sh = sizes
    return [
        pltpu.VMEM((n_sh, rows, LANES), F32),
        pltpu.VMEM((n_dp, rows, LANES), F32),
        pltpu.SemaphoreType.DMA((n_sh,)),
        pltpu.SemaphoreType.DMA((n_sh,)),
        pltpu.SemaphoreType.DMA((n_dp,)),
        pltpu.SemaphoreType.DMA((n_dp,)),
    ]


def greet(sizes):
    n_dp, n_sh = sizes
    d, s = lax.axis_index("dp"), lax.axis_index("shard")
    gate = pltpu.get_barrier_semaphore()
    for j in range(1, n_sh):
        pl.semaphore_signal(gate, inc=1, device_id=(d, lax.rem(s + j, n_sh)), device_id_type=MESH)

    def signal(j, carry):
        pl.semaphore_signal(gate, inc=1, device_id=(lax.rem(d + j, n_dp), s), device_id_type=MESH)
        return carry

    lax.fori_loop(1, n_dp, signal, 0)
    pl.semaphore_wait(gate, n_sh + n_dp - 2)


def repeat(count, body, hook=None):
    def step(i, carry):
        if hook is not None:

            @pl.when(i == hook[0])
            def _():
                hook[1]()

        body(i)
        return carry

    lax.fori_loop(0, count, step, 0)


def lanes(c, width=LANES):
    return pl.ds(pl.multiple_of(c * width, width), width)


def coefs(total, row, count, gain, shift):
    mean = total[pl.ds(row, 1), :] / count
    square = total[pl.ds(row + 1, 1), :] / count
    scale = gain * lax.rsqrt(square - mean * mean + EPS_NORM)
    return scale, shift - mean * scale


def act_half(half):
    return half + half * jnp.tanh(half)


def forward_kernel(sizes, *refs):
    (images, table, bucket, counts, balance, labels, vec_w, vec_e, expand_w, expand_e, chan_w, chan_e,
     head_w, head_e, class_w, class_e,
     pre_s, mixed_s, feat_s, out_s, low_s, pool_s, unit_s, gate_s, tot_e, tot_c, tot_h,
     dpool_h, extra, facts, wexp_s, headt_s, chan_s, gain_e_s, gain_c_s, gain_h_s,
     pre, hid, out_t, low_t, scaled, pads, stages, totals, cnt, pool_t, gate_t, save_sems,
     wexp, chan, headt, classes, vecs, gain_e, gain_c, gain_h, gain_s, gain_k, pooled_h, bias_row,
     st_exp, st_chan, st_head, st_class, load_sems, sx, rx, sc, rc, sf, rf, out_sems,
     mask, area, own_rows, firstrow) = refs[:76]
    rest = list(refs[76:])
    edge_l, edge_r = table.at[0], table.at[1]
    n_sh = sizes[1]
    sums = []
    for m in range(2):
        group = []
        for rows in (56, 48, 8, 40):
            near, far = rest[0], rest[1]
            group.append((near, far, rest[2:6], rows))
            rest = rest[6:]
        sums.append(group)

    d, s = lax.axis_index("dp"), lax.axis_index("shard")
    near_peer = s + 1 - 2 * lax.rem(s, 2)
    far_peer = s + 2 - 4 * (s // 2)
    far_near = near_peer + 2 - 4 * (s // 2)
    pieces = [("exp", 0, 0, 0), ("exp", 1, 0, 0), ("vec", 0, 0, 0), ("chan", 0, 0, 0), ("exp", 0, 0, 1), ("exp", 1, 0, 1),
              ("exp", 0, 1, 0), ("exp", 1, 1, 0), ("chan", 0, 1, 0), ("exp", 0, 1, 1), ("exp", 1, 1, 1),
              ("head", 0, 0, 0), ("class", 0, 0, 0), ("class", 1, 0, 0)]
    mats = [k for k, piece in enumerate(pieces) if piece[0] == "exp"]

    def region(k, source):
        kind, m, layer, half = pieces[k]
        if kind == "exp":
            return wexp.at[m, layer, pl.ds(pl.multiple_of(source * 64, 64), 64), half * E : (half + 1) * E]
        if kind == "chan":
            return chan.at[:, layer, :, pl.ds(pl.multiple_of(source * 384, 384), 384)]
        if kind == "vec":
            return vecs.at[source]
        if kind == "head":
            return headt.at[:, pl.ds(pl.multiple_of(source * 320, 320), 320), :]
        return classes.at[m, pl.ds(pl.multiple_of(source * 320, 320), 320), :]

    def loads(k):
        kind, m, layer, half = pieces[k]
        if kind == "exp":
            slot = mats.index(k) % 2
            source = (expand_w, expand_e)[m].at[layer, :, half * E : (half + 1) * E]
            return [pltpu.make_async_copy(source, st_exp.at[slot], load_sems.at[slot])]
        if kind == "chan":
            return [pltpu.make_async_copy((chan_w, chan_e)[i].at[:, layer], st_chan.at[i], load_sems.at[2 + i]) for i in range(2)]
        if kind == "head":
            return [pltpu.make_async_copy((head_w, head_e)[i], st_head.at[i], load_sems.at[4 + i]) for i in range(2)]
        if kind == "class":
            return [pltpu.make_async_copy((class_w, class_e)[m], st_class, load_sems.at[6])]
        return []

    def fetch(k):
        for copy in loads(k):
            copy.start()

    def cast(k):
        kind, m, layer, half = pieces[k]
        for copy in loads(k):
            copy.wait()
        if kind == "exp":
            order = mats.index(k)
            wexp[m, layer, pl.ds(pl.multiple_of(s * 64, 64), 64), half * E : (half + 1) * E] = st_exp[order % 2].astype(BF16)
            if order + 2 < len(mats):
                fetch(mats[order + 2])
        if kind == "chan":
            cols = pl.ds(pl.multiple_of(s * 384, 384), 384)
            for i in range(2):
                padded = jnp.concatenate([st_chan[i, 0:9, :], jnp.zeros((7, 384), F32)], 0)
                chan[i, layer, 0:16, cols] = padded.astype(BF16)
                chan[i, layer, 16:80, cols] = st_chan[i, 9 : 9 + SE, :].astype(BF16)
                chan[i, layer, 80:144, cols] = st_chan[i, 9 + SE : 9 + 2 * SE, :].astype(BF16)
            if layer == 0:
                fetch(pieces.index(("chan", 0, 1, 0)))
        if kind == "head":
            for i in range(2):
                headt[i, pl.ds(pl.multiple_of(s * 320, 320), 320), :] = st_head[i].astype(BF16)
        if kind == "class":
            classes[m, pl.ds(pl.multiple_of(s * 320, 320), 320), :] = st_class[...].astype(BF16)
            if m == 0:
                fetch(k + 1)
        if kind == "vec":
            own_rows[...] = jnp.zeros(own_rows.shape, F32)
            for i in range(2):
                start = 0
                for row, width in enumerate(([384] * 5 + [144]) * L + [320] * 2 + [250]):
                    own_rows[i, row : row + 1, 0:width] = (vec_w, vec_e)[i][0:1, start : start + width]
                    start = start + width
            vecs[s] = own_rows[...].astype(BF16)

    def hop(k, source, target, send, receive):
        return pltpu.make_async_remote_copy(
            region(k, source), region(k, source), send.at[k], receive.at[k],
            device_id=(d, target), device_id_type=MESH)

    def offer(k):
        cast(k)
        hop(k, s, far_peer, sx, rx).start()
        hop(k, s, near_peer, sc, rc).start()

    def forward_on(k):
        hop(k, far_peer, s, sx, rx).wait_recv()
        hop(k, far_peer, near_peer, sf, rf).start()

    def ready(k):
        hop(k, near_peer, s, sc, rc).wait_recv()
        hop(k, far_near, s, sf, rf).wait_recv()

    def settle():
        for k in range(len(pieces)):
            hop(k, s, far_peer, sx, rx).wait_send()
            hop(k, s, near_peer, sc, rc).wait_send()
            hop(k, far_peer, near_peer, sf, rf).wait_send()

    def join(m, row, low, width):
        return jnp.concatenate([vecs[t, m, 0:16, :].astype(F32)[row : row + 1, low : low + width] for t in range(n_sh)], 1)

    def unpack_vectors():
        for m in range(2):
            for layer in range(L):
                for t in range(n_sh):
                    gain_e[m, layer, 0:5, 384 * t : 384 * t + 384] = vecs[t, m].astype(F32)[6 * layer : 6 * layer + 5, :]
                gain_c[m, layer, 0:1, :] = join(m, 6 * layer + 5, 0, 64)
                gain_c[m, layer, 1:2, :] = join(m, 6 * layer + 5, 64, 64)
                gain_s[m, layer, 0:1, :] = join(m, 6 * layer + 5, 128, 16)
            gain_h[m, 0:1, :] = join(m, 12, 0, 320)
            gain_h[m, 1:2, :] = join(m, 13, 0, 320)
            gain_k[m, 0:1, :] = join(m, 14, 0, 250)

    for k in (0, 1, 3, 11, 12):
        fetch(k)
    greet(sizes)
    for k in (0, 1, 2, 3):
        offer(k)
    area_value = fill_mask(mask, table, bucket, counts)
    area[...] = jnp.full((8, LANES), area_value, F32)
    firstrow[...] = jnp.zeros((8, LANES), F32)
    weighted = [[jnp.where(i < counts[b, 0], balance[b, i], 0).astype(F32) for i in range(IMGS)] for b in range(BATCHES)]
    for b in range(BATCHES):
        firstrow[b : b + 1, :] = jnp.full((1, LANES), counts[b, 0].astype(F32) * area_value, F32)
        firstrow[2 + b : 3 + b, :] = jnp.full((1, LANES), sum(weighted[b]), F32)

    def low(m, layer):
        return low_s.at[layer] if m == 0 else low_t

    def out(m, layer):
        return out_s.at[layer] if m == 0 else out_t

    def total_ref(m, kind, layer):
        if m == 0:
            return (tot_e.at[layer, 0], tot_e.at[layer, 1], tot_c.at[layer], tot_h)[kind]
        return totals.at[kind]

    def summer(m, kind, layer):
        near, far, sems, rows = sums[m][kind]
        return Sum(near, far, total_ref(m, kind, layer), sems, sizes, rows)

    def save(src, dst, index):
        return pltpu.make_async_copy(src, dst, save_sems.at[index])

    for slot in range(SLOTS):
        pads[slot, 0:GAP, :] = jnp.zeros((GAP, LANES), F32)
        pads[slot, GAP + ROWS : 2 * GAP + ROWS, :] = jnp.zeros((GAP, LANES), F32)

    def store_wexp(layer):
        return pltpu.make_async_copy(wexp.at[0, layer], wexp_s.at[layer], out_sems.at[layer])

    store_headt = pltpu.make_async_copy(headt.at[0], headt_s, out_sems.at[L])
    store_chan = pltpu.make_async_copy(chan.at[0], chan_s, out_sems.at[L + 1])

    def load_rows(i):
        rows = pl.ds(pl.multiple_of(i * ROWS, ROWS), ROWS)
        for half in range(2):
            cols = slice(half * LANES, half * LANES + LANES)
            value = images[rows, cols].astype(F32) * mask[rows, :]
            hid[0, rows, cols] = value
            hid[1, rows, cols] = value
            low_s[0, rows, cols] = value.astype(BF16)
            low_t[rows, cols] = value.astype(BF16)

    repeat(SLOTS, load_rows)

    def update(m, layer):
        tot = total_ref(m, 2, layer)
        for half in range(2):
            cols = slice(half * LANES, half * LANES + LANES)
            for b in range(BATCHES):
                scale, shift = coefs(tot, 4 * half + 2 * b, cnt[b : b + 1, :], gain_c[m, layer, 0:1, cols], gain_c[m, layer, 1:2, cols])

                def one(i):
                    rows = pl.ds(pl.multiple_of(b * HALF + i * ROWS, ROWS), ROWS)
                    value = hid[m, rows, cols] + mask[rows, :] * (out(m, layer)[rows, cols] * scale + shift)
                    hid[m, rows, cols] = value
                    low(m, layer + 1)[rows, cols] = value.astype(BF16)

                repeat(IMGS, one)

    def put_sums(stage, chunk, b, value):
        stage[pl.ds(4 * chunk + 2 * b, 1), :] = jnp.sum(value, 0, keepdims=True)
        stage[pl.ds(4 * chunk + 2 * b + 1, 1), :] = jnp.sum(value * value, 0, keepdims=True)

    def expand(m, layer, hook=None):
        stage = stages.at[m]

        def body(c):
            weight = wexp[m, layer, :, lanes(c, 256)]
            for b in range(BATCHES):
                value = jnp.dot(low(m, layer)[b * HALF : (b + 1) * HALF, :], weight, preferred_element_type=F32)
                for half in range(2):
                    piece = value[:, half * LANES : (half + 1) * LANES]
                    pre[m, 2 * c + half, b * HALF : (b + 1) * HALF, :] = piece
                    put_sums(stage, 2 * c + half, b, piece)
            if m == 0:
                for half in range(2):
                    save(pre.at[0, 2 * c + half], pre_s.at[layer, 2 * c + half], 2 * c + half).start()

        repeat(E // 256, body, hook)

    def depthwise(m, layer, hook=None):
        stage = stages.at[m]
        tot = total_ref(m, 0, layer)

        def body(c):
            if m == 0:
                save(pre.at[0, c], pre_s.at[layer, c], c).wait()
            tap_rows = chan[m, layer, 0:16, lanes(c)].astype(F32)
            tap = [tap_rows[k : k + 1, :] for k in range(9)]
            for b in range(BATCHES):
                scale, shift = coefs(tot, 4 * c + 2 * b, cnt[b : b + 1, :], gain_e[m, layer, 0:1, lanes(c)], gain_e[m, layer, 1:2, lanes(c)])
                scale, shift = 0.5 * scale, 0.5 * shift
                for i in range(IMGS):
                    slot = b * IMGS + i
                    rows = slice(slot * ROWS, (slot + 1) * ROWS)
                    half = mask[rows, :] * (pre[m, c, rows, :] * scale + shift)
                    pads[slot, GAP : GAP + ROWS, :] = act_half(half)
                first = jnp.zeros((8, LANES), F32)
                second = jnp.zeros((8, LANES), F32)
                for i in range(IMGS):
                    slot = b * IMGS + i
                    for t in range(ROWS // TILE):
                        start = GAP + t * TILE
                        near = [pads[slot, start + o : start + o + TILE, :] for o in OFFSETS]
                        left = near[0] * tap[0] + near[3] * tap[3] + near[6] * tap[6]
                        mid = near[1] * tap[1] + near[4] * tap[4] + near[7] * tap[7]
                        right = near[2] * tap[2] + near[5] * tap[5] + near[8] * tap[8]
                        rows = slice(slot * ROWS + t * TILE, slot * ROWS + (t + 1) * TILE)
                        value = mask[rows, :] * (mid + edge_l[t * TILE : (t + 1) * TILE, :] * left + edge_r[t * TILE : (t + 1) * TILE, :] * right)
                        pre[m, c, rows, :] = value
                        first = first + jnp.sum(value.reshape(TILE // 8, 8, LANES), 0)
                        second = second + jnp.sum((value * value).reshape(TILE // 8, 8, LANES), 0)
                stage[pl.ds(4 * c + 2 * b, 1), :] = jnp.sum(first, 0, keepdims=True)
                stage[pl.ds(4 * c + 2 * b + 1, 1), :] = jnp.sum(second, 0, keepdims=True)
            if m == 0:
                save(pre.at[0, c], mixed_s.at[layer, c], c).start()

        repeat(EC, body, hook)

    def pooling(m, layer, hook=None):
        tot = total_ref(m, 1, layer)
        pool = pool_s.at[layer] if m == 0 else pool_t

        def body(c):
            if m == 0:
                save(pre.at[0, c], mixed_s.at[layer, c], c).wait()
            for b in range(BATCHES):
                scale, shift = coefs(tot, 4 * c + 2 * b, cnt[b : b + 1, :], gain_e[m, layer, 2:3, lanes(c)], gain_e[m, layer, 3:4, lanes(c)])
                scale, shift = 0.5 * scale, 0.5 * shift
                for i in range(IMGS):
                    slot = b * IMGS + i
                    rows = slice(slot * ROWS, (slot + 1) * ROWS)
                    value = act_half(mask[rows, :] * (pre[m, c, rows, :] * scale + shift))
                    pre[m, c, rows, :] = value
                    pool[b * 8 + i : b * 8 + i + 1, lanes(c)] = jnp.sum(value, 0, keepdims=True) / area[0:1, :]

        repeat(EC, body, hook)

    def project(m, layer):
        pool = pool_s.at[layer] if m == 0 else pool_t
        gate = gate_s.at[layer] if m == 0 else gate_t
        units = exact(pool[...], chan[m, layer, 16:80, :], 1) + gain_s[m, layer, 0:1, :]
        if m == 0:
            unit_s[layer] = units
        gate[...] = jax.nn.sigmoid(exact(jax.nn.silu(units), chan[m, layer, 80:144, :], 0) + gain_e[m, layer, 4:5, :])

        def body(c):
            for b in range(BATCHES):
                for i in range(IMGS):
                    rows = slice(b * HALF + i * ROWS, b * HALF + (i + 1) * ROWS)
                    scaled[rows, lanes(c)] = (pre[m, c, rows, :] * gate[b * 8 + i : b * 8 + i + 1, lanes(c)]).astype(BF16)

        repeat(EC, body)
        stage = stages.at[m]
        for b in range(BATCHES):
            rows = slice(b * HALF, (b + 1) * HALF)
            value = contract(scaled[rows, :], wexp[m, layer, :, E : 2 * E], 1, 1)
            out(m, layer)[rows, :] = value
            for half in range(2):
                put_sums(stage, half, b, value[:, half * LANES : (half + 1) * LANES])

    def features(m, hook=None):
        stage = stages.at[m]

        def body(c):
            weight = headt[m, pl.ds(pl.multiple_of(c * 256, 256), 256), :]
            for b in range(BATCHES):
                value = contract(low(m, L)[b * HALF : (b + 1) * HALF, :], weight, 1, 1)
                for half in range(2):
                    piece = value[:, half * LANES : (half + 1) * LANES]
                    pre[m, 2 * c + half, b * HALF : (b + 1) * HALF, :] = piece
                    put_sums(stage, 2 * c + half, b, piece)
            if m == 0:
                for half in range(2):
                    save(pre.at[0, 2 * c + half], feat_s.at[2 * c + half], 2 * c + half).start()

        repeat(HEAD // 256, body, hook)

    def head_pool(m, hook=None):
        tot = total_ref(m, 3, 0)

        def body(c):
            for b in range(BATCHES):
                scale, shift = coefs(tot, 4 * c + 2 * b, cnt[b : b + 1, :], gain_h[m, 0:1, lanes(c)], gain_h[m, 1:2, lanes(c)])
                scale, shift = 0.5 * scale, 0.5 * shift
                for i in range(IMGS):
                    slot = b * IMGS + i
                    rows = slice(slot * ROWS, (slot + 1) * ROWS)
                    value = act_half(mask[rows, :] * (pre[m, c, rows, :] * scale + shift))
                    pooled_h[m, b * 8 + i : b * 8 + i + 1, lanes(c)] = jnp.sum(value, 0, keepdims=True) / area[0:1, :]

        repeat(HC, body, hook)

    for m in range(2):
        stages[m] = jnp.zeros((56, LANES), F32)
    pool_s[...] = jnp.zeros(pool_s.shape, F32)
    pool_t[...] = jnp.zeros(pool_t.shape, F32)
    pooled_h[...] = jnp.zeros(pooled_h.shape, F32)
    stages[0, 48:56, :] = firstrow[...]
    pending = None
    forward_on(0)
    ready(0)
    for layer in range(L):
        s_one, t_one = summer(0, 0, layer), summer(1, 0, layer)
        s_two, t_two = summer(0, 1, layer), summer(1, 1, layer)
        s_three, t_three = summer(0, 2, layer), summer(1, 2, layer)
        if layer > 0:
            update(0, layer - 1)
            ready(6)
        expand(0, layer, None if pending is None else (2, pending.middle))
        s_one.start(stages.at[0])
        if layer == 0:
            forward_on(1)
            ready(1)
            forward_on(2)
            offer(4)
        else:
            forward_on(8)
            pending.finish()
            update(1, layer - 1)
            ready(7)
            offer(10)
        expand(1, layer, (4, s_one.middle))
        t_one.start(stages.at[1])
        if layer == 0:
            forward_on(3)
            ready(2)
            unpack_vectors()
            ready(3)
            offer(5)
        else:
            forward_on(9)
            ready(8)
            offer(11)
        s_one.finish()
        if layer == 0:
            cnt[...] = tot_e[0, 0, 48:56, :]
        depthwise(0, layer, (2, t_one.middle))
        s_two.start(stages.at[0])
        forward_on((4, 10)[layer])
        offer((6, 12)[layer])
        t_one.finish()
        depthwise(1, layer, (5, s_two.middle))
        t_two.start(stages.at[1])
        forward_on((5, 11)[layer])
        if layer == 0:
            offer(7)
        ready((4, 9)[layer])
        s_two.finish()
        pooling(0, layer, (5, t_two.middle))
        project(0, layer)
        s_three.start(stages.at[0])
        forward_on((6, 12)[layer])
        offer((8, 13)[layer])
        ready((5, 10)[layer])
        t_two.finish()
        pooling(1, layer, (6, s_three.middle))
        project(1, layer)
        t_three.start(stages.at[1])
        if layer == 0:
            forward_on(7)
            offer(9)
        s_three.finish()
        pending = t_three
    for layer in range(L):
        store_wexp(layer).start()
    s_head, t_head = summer(0, 3, 0), summer(1, 3, 0)
    update(0, L - 1)
    ready(11)
    features(0, (2, pending.middle))
    s_head.start(stages.at[0])
    pending.finish()
    update(1, L - 1)
    features(1, (4, s_head.middle))
    t_head.start(stages.at[1])
    forward_on(13)
    store_headt.start()
    store_chan.start()
    s_head.finish()
    head_pool(0, (3, t_head.middle))
    ready(12)
    t_head.finish()
    head_pool(1)
    ready(13)

    def class_logits(m):
        low_pool = pooled_h[m].astype(BF16)
        return jnp.dot(low_pool, classes[m], preferred_element_type=F32) + gain_k[m, 0:1, :]

    def log_softmax(value):
        value = value - jnp.max(value, 1, keepdims=True)
        return value - jnp.log(jnp.sum(jnp.exp(value), 1, keepdims=True))

    logp = log_softmax(class_logits(0))
    target = log_softmax(class_logits(1))
    expected = jnp.exp(target)
    row16 = lax.broadcasted_iota(jnp.int32, (16, LANES), 0)
    label_rows = jnp.zeros((16, LANES), jnp.int32)
    weight_rows = jnp.zeros((16, LANES), F32)
    for b in range(BATCHES):
        for i in range(IMGS):
            label_rows = jnp.where(row16 == 8 * b + i, labels[b, i], label_rows)
            weight_rows = jnp.where(row16 == 8 * b + i, weighted[b][i], weight_rows)
    hot = lax.broadcasted_iota(jnp.int32, (16, CLASSES), 1) == label_rows[:, 0:1]
    total_weight = tot_e[0, 0, 50:51, :] + tot_e[0, 0, 51:52, :]
    coef = weight_rows[:, 0:1] / total_weight[:, 0:1]
    per = jnp.sum(expected * (target - logp), 1, keepdims=True) - jnp.sum(jnp.where(hot, logp, 0.0), 1, keepdims=True)
    loss = jnp.sum(coef * per, 0, keepdims=True)
    slope = -coef * (jnp.where(hot, 1.0, 0.0) + expected)
    grad_low = (slope - jnp.exp(logp) * jnp.sum(slope, 1, keepdims=True)).astype(BF16)
    bias_row[...] = jnp.zeros(bias_row.shape, F32)
    bias_row[0:1, 0:CLASSES] = jnp.sum(grad_low.astype(F32), 0, keepdims=True)
    for k in range(8):
        extra[k : k + 1, :] = bias_row[0:1, k * LANES : (k + 1) * LANES]
    extra[8:16, :] = jnp.broadcast_to(loss, (8, LANES))
    dpool_h[...] = contract(grad_low, classes[0], 1, 1) / area[0:1, 0:1]
    facts[...] = jnp.zeros(facts.shape, BF16)
    low_pool = pooled_h[0].astype(BF16)
    for k in range(8):
        width = min(LANES, CLASSES - k * LANES)
        facts[k, :, 0:width] = grad_low[:, k * LANES : k * LANES + width]
    for t in range(n_sh):
        for q in range(3):
            width = min(LANES, 320 - q * LANES)
            low = 320 * t + q * LANES
            facts[8 + 3 * t + q, :, 0:width] = low_pool[:, low : low + width]
    gain_e_s[...] = gain_e[0]
    gain_c_s[...] = gain_c[0]
    gain_h_s[...] = gain_h[0]
    settle()
    for layer in range(L):
        store_wexp(layer).wait()
    store_headt.wait()
    store_chan.wait()
    for c in range(HC):
        save(pre.at[0, c], feat_s.at[c], c).wait()


def run_forward_all(sizes, inputs):
    sds = jax.ShapeDtypeStruct
    vm = pl.BlockSpec(memory_space=pltpu.VMEM)
    hbm = pl.BlockSpec(memory_space=pl.ANY)
    n_sh = sizes[1]
    outs = [
        (sds((L, EC, FULL, LANES), F32), hbm),
        (sds((L, EC, FULL, LANES), F32), hbm),
        (sds((HC, FULL, LANES), F32), hbm),
        (sds((L, FULL, C), F32), vm),
        (sds((L + 1, FULL, C), BF16), vm),
        (sds((L, 16, E), F32), vm),
        (sds((L, 16, SE), F32), vm),
        (sds((L, 16, E), F32), vm),
        (sds((L, 2, 56, LANES), F32), vm),
        (sds((L, 8, LANES), F32), vm),
        (sds((40, LANES), F32), vm),
        (sds((16, HEAD), F32), vm),
        (sds((16, LANES), F32), vm),
        (sds((8 + 3 * n_sh, 16, LANES), BF16), vm),
        (sds((L, C, 2 * E), BF16), hbm),
        (sds((HEAD, C), BF16), hbm),
        (sds((L, 144, E), BF16), hbm),
        (sds((L, 8, E), F32), vm),
        (sds((L, 8, C), F32), vm),
        (sds((8, HEAD), F32), vm),
    ]
    scratch = [
        pltpu.VMEM((2, EC, FULL, LANES), F32),
        pltpu.VMEM((2, FULL, C), F32),
        pltpu.VMEM((FULL, C), F32),
        pltpu.VMEM((FULL, C), BF16),
        pltpu.VMEM((FULL, E), BF16),
        pltpu.VMEM((SLOTS, ROWS + 2 * GAP, LANES), F32),
        pltpu.VMEM((2, 56, LANES), F32),
        pltpu.VMEM((4, 56, LANES), F32),
        pltpu.VMEM((8, LANES), F32),
        pltpu.VMEM((16, E), F32),
        pltpu.VMEM((16, E), F32),
        pltpu.SemaphoreType.DMA((EC,)),
        pltpu.VMEM((2, L, C, 2 * E), BF16),
        pltpu.VMEM((2, L, 144, E), BF16),
        pltpu.VMEM((2, HEAD, C), BF16),
        pltpu.VMEM((2, HEAD, CLASSES), BF16),
        pltpu.VMEM((n_sh, 2, 16, 384), BF16),
        pltpu.VMEM((2, L, 8, E), F32),
        pltpu.VMEM((2, L, 8, C), F32),
        pltpu.VMEM((2, 8, HEAD), F32),
        pltpu.VMEM((2, L, 8, SE), F32),
        pltpu.VMEM((2, 8, CLASSES), F32),
        pltpu.VMEM((2, 16, HEAD), F32),
        pltpu.VMEM((8, CLASS_PAD), F32),
        pltpu.VMEM((2, 64, E), F32),
        pltpu.VMEM((2, 137, 384), F32),
        pltpu.VMEM((2, 320, C), F32),
        pltpu.VMEM((320, CLASSES), F32),
        pltpu.SemaphoreType.DMA((7,)),
    ]
    scratch = scratch + [pltpu.SemaphoreType.DMA((14,))] * 6 + [pltpu.SemaphoreType.DMA((L + 2,))]
    scratch = scratch + [
        pltpu.VMEM((FULL, LANES), F32),
        pltpu.VMEM((8, LANES), F32),
        pltpu.VMEM((2, 16, 384), F32),
        pltpu.VMEM((8, LANES), F32),
    ]
    for m in range(2):
        for rows in (56, 48, 8, 40):
            scratch = scratch + sum_scratch(sizes, rows)
    return pl.pallas_call(
        functools.partial(forward_kernel, sizes),
        out_shape=[o[0] for o in outs],
        in_specs=[vm] * 2 + [pl.BlockSpec(memory_space=pltpu.SMEM)] * 4 + [vm] * 2 + [hbm] * 8,
        out_specs=[o[1] for o in outs],
        scratch_shapes=scratch,
        compiler_params=pltpu.CompilerParams(collective_id=1, has_side_effects=True, vmem_limit_bytes=63 * 2**20),
        name="forward",
    )(*inputs)


BACK_ROWS = ((24, 24, 8, 24), (40, 24, 8, 40))


def round_up(value, unit):
    return -(-value // unit) * unit


CHUNKS = 6
MATS = 2 * E // LANES * 8
CHAN = 3 * 18
AT_MATS = (MATS + CHAN + 2 * HEAD // 4 // 8, 0)
AT_CHAN = (AT_MATS[0] + MATS, MATS)
AT_HEAD = MATS + CHAN
AT_END = AT_CHAN[0] + CHAN


def packed_blocks(sizes):
    return round_up(AT_END, CHUNKS * 2 * sizes[0])


def late_chunks(sizes):
    return AT_MATS[0] // (packed_blocks(sizes) // CHUNKS)


def backward_kernel(sizes, *refs):
    (dpool_h, extra, table, bucket, counts, wexp, headt, chan, gain_e, gain_c, gain_h,
     pre_s, mixed_s, feat_s, out_s, low_s, pool_s, unit_s, gate_s, tot_e, tot_c, tot_h,
     packed, back_e, back_c, back_h,
     pre, mixed, grad, grad_hid, low_out, low_pre, pads_x, pads_g, slope, dgate, dpool, stages, load_sems,
     held, held_chan, held_exb, held_sqb, out_v, low_v, row_sems, mask, area, near, cross, core_s, core_r, x_s, x_r) = refs[:54]
    rest = list(refs[54:])
    edge_l, edge_r = table.at[0], table.at[1]
    n_dp, n_sh = sizes
    sums = []
    for b in range(BATCHES):
        group = []
        for rows in BACK_ROWS[b]:
            group.append((rest[0], rest[1], rest[2:6], rows))
            rest = rest[6:]
        sums.append(group)

    greet(sizes)

    def back_ref(b, kind, layer):
        return (back_e.at[layer, b, 0], back_e.at[layer, b, 1], back_c.at[layer, b], back_h.at[b])[kind]

    def summer(b, kind, layer):
        near, far, sems, rows = sums[b][kind]
        return Sum(near, far, back_ref(b, kind, layer), sems, sizes, rows)

    def load(b, kind, layer):
        rows = slice(b * HALF, (b + 1) * HALF)
        if kind == 0:
            return pltpu.make_async_copy(pre_s.at[layer, :, rows], pre.at[b], load_sems.at[b, 0])
        if kind == 1:
            return pltpu.make_async_copy(mixed_s.at[layer, :, rows], mixed.at[b], load_sems.at[b, 1])
        return pltpu.make_async_copy(feat_s.at[:, rows], pre.at[b, 0:HC], load_sems.at[b, 0])

    area[...] = jnp.full((8, LANES), fill_mask(mask, table, bucket, counts), F32)

    d, s = lax.axis_index("dp"), lax.axis_index("shard")
    bit0, bit1 = lax.rem(s, 2), s // 2
    near_peer, far_peer = s + 1 - 2 * bit0, s + 2 - 4 * bit1
    late = late_chunks(sizes)
    chunk = packed_blocks(sizes) // CHUNKS

    def core_copy(k, i):
        rows = pl.ds(k * chunk, chunk)
        return pltpu.make_async_remote_copy(
            packed.at[2 * i + 1 - bit0, rows], near.at[i, rows], core_s.at[k, i], core_r.at[k, i],
            device_id=(d, near_peer), device_id_type=MESH)

    def x_copy(k):
        rows = pl.ds(k * chunk, chunk)
        return pltpu.make_async_remote_copy(
            packed.at[far_peer, rows], cross.at[rows], x_s.at[k], x_r.at[k],
            device_id=(d, far_peer), device_id_type=MESH)

    def add_rows(t, k, other):
        def step(i, carry):
            rows = pl.ds(k * chunk + i * 8, 8)
            packed[t, rows] = packed[t, rows] + other(rows)
            return carry

        lax.fori_loop(0, chunk // 8, step, 0)

    def late_core():
        for k in range(late):
            for i in range(2):
                core_copy(k, i).start()

    def late_x(k):
        if k < late:
            for i in range(2):
                core_copy(k, i).wait_recv()
            add_rows(far_peer, k, lambda rows: near[1 - bit1, rows])
            x_copy(k).start()
            add_rows(s, k, lambda rows: near[bit1, rows])

    def late_end():
        for k in range(late):
            x_copy(k).wait_recv()
            add_rows(s, k, lambda rows: cross[rows])
        for k in range(late):
            for i in range(2):
                core_copy(k, i).wait_send()
            x_copy(k).wait_send()

    def then(first, k):
        def run():
            first()
            late_x(k)

        return run

    def load_out(layer):
        return pltpu.make_async_copy(out_s.at[layer], out_v, row_sems.at[0])

    def load_low(layer):
        return pltpu.make_async_copy(low_s.at[layer], low_v, row_sems.at[1])

    for b in range(BATCHES):
        load(b, 2, 0).start()
    load_low(L).start()
    load_out(L - 1).start()
    for b in range(BATCHES):
        load(b, 1, L - 1).start()
    for slot in range(IMGS):
        for pads in (pads_x, pads_g):
            pads[slot, 0:GAP, :] = jnp.zeros((GAP, LANES), F32)
            pads[slot, GAP + ROWS : 2 * GAP + ROWS, :] = jnp.zeros((GAP, LANES), F32)
    dgate[...] = jnp.zeros(dgate.shape, F32)
    stages[...] = jnp.zeros(stages.shape, F32)
    stages[1, 24:40, :] = extra[...]
    held_chan[...] = jnp.zeros(held_chan.shape, F32)
    spare = packed.shape[1] - AT_END
    if spare:
        packed[:, AT_END:] = jnp.zeros((n_sh, spare, 8, LANES), F32)

    def pack(first, c, value):
        for t in range(n_sh):
            for half in range(2):
                piece = value[64 * t : 64 * t + 64, half * LANES : (half + 1) * LANES]
                packed[t, pl.ds(first + 16 * c + 8 * half, 8)] = piece.reshape(8, 8, LANES)

    def pack_chan(layer):
        for k in range(EC):
            first = AT_CHAN[layer] + 18 * (k % 3)
            packed[k // 3, first : first + 18] = held_chan[:, k * LANES : (k + 1) * LANES].reshape(18, 8, LANES)

    def forward_total(kind, layer):
        return (tot_e.at[layer, 0], tot_e.at[layer, 1], tot_c.at[layer], tot_h)[kind]

    def moments(b, kind, layer, c):
        tot = forward_total(kind, layer)
        count = tot_e[0, 0, 48 + b : 49 + b, :]
        mean = tot[pl.ds(4 * c + 2 * b, 1), :] / count
        square = tot[pl.ds(4 * c + 2 * b + 1, 1), :] / count
        return mean, lax.rsqrt(square - mean * mean + EPS_NORM)

    def half_coefs(b, kind, layer, c, gain, shift):
        mean, scale = moments(b, kind, layer, c)
        scale = scale * gain
        return 0.5 * scale, 0.5 * (shift - mean * scale)

    def back_coefs(b, kind, layer, c, gain):
        mean, scale = moments(b, kind, layer, c)
        count = tot_e[0, 0, 48 + b : 49 + b, :]
        back = back_ref(b, kind, layer)
        plain = back[pl.ds(2 * c, 1), :]
        cross = scale * (back[pl.ds(2 * c + 1, 1), :] - mean * plain)
        first = scale * gain
        third = -first * scale * cross / count
        return first, -first * plain / count - mean * third, third

    def fold(value):
        return jnp.sum(value.reshape(value.shape[0] // 8, 8, LANES), 0)

    def put(stage, c, first, second):
        stage[pl.ds(2 * c, 1), :] = jnp.sum(first, 0, keepdims=True)
        stage[pl.ds(2 * c + 1, 1), :] = jnp.sum(second, 0, keepdims=True)

    def image(b, i):
        return slice(i * ROWS, (i + 1) * ROWS), slice(b * HALF + i * ROWS, b * HALF + (i + 1) * ROWS)

    def bend(half):
        t = jnp.tanh(half)
        return half + half * t, (0.5 + 0.5 * t) * (1.0 + half * (1.0 - t))

    def head_first(b, hook=None):
        stage = stages.at[b]

        def body(c):
            scale, shift = half_coefs(b, 3, 0, c, gain_h[0:1, lanes(c)], gain_h[1:2, lanes(c)])
            first = jnp.zeros((8, LANES), F32)
            second = jnp.zeros((8, LANES), F32)
            for i in range(IMGS):
                rows, full = image(b, i)
                x = pre[b, c, rows, :]
                half = mask[full, :] * (x * scale + shift)
                value = mask[full, :] * dpool_h[b * 8 + i : b * 8 + i + 1, lanes(c)] * bend(half)[1]
                grad[b, c, rows, :] = value
                first = first + fold(value)
                second = second + fold(value * x)
            put(stage, c, first, second)

        repeat(HC, body, hook)

    def norm_back_rows(b, kind, layer, c, gain, source):
        one, two, three = back_coefs(b, kind, layer, c, gain)
        for i in range(IMGS):
            rows, full = image(b, i)
            value = mask[full, :] * (one * grad[b, c, rows, :] + two + three * source[b, c, rows, :])
            low_pre[rows, lanes(c)] = value.astype(BF16)

    def put_hidden_sums(b, layer):
        stage = stages.at[b]
        for half in range(2):
            cols = slice(half * LANES, (half + 1) * LANES)
            first = jnp.zeros((8, LANES), F32)
            second = jnp.zeros((8, LANES), F32)
            for i in range(IMGS):
                full = image(b, i)[1]
                value = grad_hid[full, cols]
                first = first + fold(value)
                second = second + fold(value * out_v[full, cols])
            put(stage, half, first, second)

    def head_second(b, hook=None):
        mine = slice(b * HALF, (b + 1) * HALF)

        def body(c):
            for half in range(2):
                norm_back_rows(b, 3, 0, 2 * c + half, gain_h[0:1, lanes(2 * c + half)], pre)
            value = contract(low_pre[:, lanes(c, 256)], low_v[mine, :], 0, 0)
            if b == 0:
                held[c] = value
            else:
                value = value + held[c]
                for i in range(32):
                    row = 32 * c + i
                    for half in range(2):
                        packed[row // 40, AT_HEAD + 40 * half + lax.rem(row, 40)] = value[8 * i : 8 * i + 8, half * LANES : (half + 1) * LANES]

        repeat(HEAD // 256, body, hook)
        grad_hid[mine, :] = jnp.dot(low_pre[:, 0:HEAD], headt[...], preferred_element_type=F32)
        put_hidden_sums(b, L - 1)

    def block_gate(b, layer, hook=None):
        mine = slice(b * HALF, (b + 1) * HALF)
        eight = slice(b * 8, b * 8 + 8)
        for half in range(2):
            cols = slice(half * LANES, (half + 1) * LANES)
            one, two, three = back_coefs(b, 2, layer, half, gain_c[layer, 0:1, cols])
            for i in range(IMGS):
                rows, full = image(b, i)
                low_out[rows, cols] = (mask[full, :] * (one * grad_hid[full, cols] + two + three * out_v[full, cols])).astype(BF16)

        def body(c):
            value = jnp.dot(low_out[...], wexp[layer, :, lanes(E // 256 + c, 256)], preferred_element_type=F32)
            for part in range(2):
                k = 2 * c + part
                scale, shift = half_coefs(b, 1, layer, k, gain_e[layer, 2:3, lanes(k)], gain_e[layer, 3:4, lanes(k)])
                for i in range(IMGS):
                    rows, full = image(b, i)
                    act = act_half(mask[full, :] * (mixed[b, k, rows, :] * scale + shift))
                    piece = value[rows, part * LANES : (part + 1) * LANES]
                    grad[b, k, rows, :] = piece
                    dgate[i : i + 1, lanes(k)] = jnp.sum(fold(piece * act), 0, keepdims=True)
                    low_pre[rows, lanes(k)] = (act * gate_s[layer, b * 8 + i : b * 8 + i + 1, lanes(k)]).astype(BF16)
            value = contract(low_out[...], low_pre[:, lanes(c, 256)], 0, 0)
            if b == 0:
                held[c] = value
            else:
                pack(AT_MATS[layer] + MATS // 2, c, value + held[c])

        repeat(E // 256, body, hook)
        gate = gate_s[layer, eight, :]
        units = unit_s[layer, eight, :]
        sig = jax.nn.sigmoid(units)
        inner = dgate[...] * gate * (1.0 - gate)
        bias_x = jnp.sum(inner, 0, keepdims=True)
        grad_x = exact_outer(units * sig, inner)
        outer = exact(inner, chan[layer, 80:144, :], 1) * (sig * (1.0 + units * (1.0 - sig)))
        bias_r = jnp.sum(outer, 0, keepdims=True)
        grad_r = exact_outer(outer, pool_s[layer, eight, :])
        if b == 0:
            held_exb[0:1, :] = bias_x
            held_chan[9 + SE : 9 + 2 * SE, :] = grad_x
            held_sqb[0:1, 0:SE] = bias_r
            held_chan[9 : 9 + SE, :] = grad_r
        else:
            bias_x = bias_x + held_exb[0:1, :]
            for k in range(EC):
                stages[1, 24 + k : 25 + k, :] = bias_x[:, k * LANES : (k + 1) * LANES]
            stages[1, 24 + EC : 25 + EC, 0:SE] = bias_r + held_sqb[0:1, 0:SE]
            held_chan[9 : 9 + SE, :] = held_chan[9 : 9 + SE, :] + grad_r
            held_chan[9 + SE : 9 + 2 * SE, :] = held_chan[9 + SE : 9 + 2 * SE, :] + grad_x
        dpool[...] = exact(outer, chan[layer, 16:80, :], 0)

    def block_second(b, layer, hook=None):
        stage = stages.at[b]

        def body(c):
            scale, shift = half_coefs(b, 1, layer, c, gain_e[layer, 2:3, lanes(c)], gain_e[layer, 3:4, lanes(c)])
            first = jnp.zeros((8, LANES), F32)
            second = jnp.zeros((8, LANES), F32)
            for i in range(IMGS):
                rows, full = image(b, i)
                x = mixed[b, c, rows, :]
                half = mask[full, :] * (x * scale + shift)
                gate = gate_s[layer, b * 8 + i : b * 8 + i + 1, lanes(c)]
                value = mask[full, :] * (grad[b, c, rows, :] * gate + dpool[i : i + 1, lanes(c)] / area[0:1, :]) * bend(half)[1]
                grad[b, c, rows, :] = value
                first = first + fold(value)
                second = second + fold(value * x)
            put(stage, c, first, second)

        repeat(EC, body, hook)

    def block_spread(b, layer, hook=None):
        stage = stages.at[b]

        def body(c):
            scale, shift = half_coefs(b, 0, layer, c, gain_e[layer, 0:1, lanes(c)], gain_e[layer, 1:2, lanes(c)])
            one, two, three = back_coefs(b, 1, layer, c, gain_e[layer, 2:3, lanes(c)])
            tap_rows = chan[layer, 0:16, lanes(c)].astype(F32)
            tap = [tap_rows[k : k + 1, :] for k in range(9)]
            for i in range(IMGS):
                rows, full = image(b, i)
                act, der = bend(mask[full, :] * (pre[b, c, rows, :] * scale + shift))
                pads_x[i, GAP : GAP + ROWS, :] = act
                slope[rows, :] = mask[full, :] * der
                pads_g[i, GAP : GAP + ROWS, :] = mask[full, :] * (one * grad[b, c, rows, :] + two + three * mixed[b, c, rows, :])
            first = jnp.zeros((8, LANES), F32)
            second = jnp.zeros((8, LANES), F32)
            total = [jnp.zeros((8, LANES), F32) for k in range(9)]
            for i in range(IMGS):
                for t in range(ROWS // TILE_BACK):
                    start = GAP + t * TILE_BACK
                    rows = slice(i * ROWS + t * TILE_BACK, i * ROWS + (t + 1) * TILE_BACK)
                    g = [pads_g[i, start - o : start - o + TILE_BACK, :] for o in OFFSETS]
                    left, right = edge_l[t * TILE_BACK : (t + 1) * TILE_BACK, :], edge_r[t * TILE_BACK : (t + 1) * TILE_BACK, :]
                    wide = (g[1] * tap[1] + g[4] * tap[4] + g[7] * tap[7]
                            + right * (g[0] * tap[0] + g[3] * tap[3] + g[6] * tap[6])
                            + left * (g[2] * tap[2] + g[5] * tap[5] + g[8] * tap[8]))
                    value = wide * slope[rows, :]
                    grad[b, c, rows, :] = value
                    first = first + fold(value)
                    second = second + fold(value * pre[b, c, rows, :])
                    center = g[4]
                    sides = (center * left, center, center * right)
                    for k in range(9):
                        o = OFFSETS[k]
                        total[k] = total[k] + fold(sides[k % 3] * pads_x[i, start + o : start + o + TILE_BACK, :])
            put(stage, c, first, second)
            for k in range(9):
                row = jnp.sum(total[k], 0, keepdims=True)
                if b == 0:
                    held_chan[k : k + 1, lanes(c)] = row
                else:
                    held_chan[k : k + 1, lanes(c)] = held_chan[k : k + 1, lanes(c)] + row

        repeat(EC, body, hook)
        if b == 1:
            pack_chan(layer)

    def block_expand(b, layer, hook=None):
        mine = slice(b * HALF, (b + 1) * HALF)

        def body(c):
            for part in range(2):
                norm_back_rows(b, 0, layer, 2 * c + part, gain_e[layer, 0:1, lanes(2 * c + part)], pre)
            value = contract(low_v[mine, :], low_pre[:, lanes(c, 256)], 0, 0)
            if b == 0:
                held[c] = value
            else:
                pack(AT_MATS[layer], c, value + held[c])

        repeat(E // 256, body, hook)
        if layer > 0:
            grad_hid[mine, :] = grad_hid[mine, :] + contract(low_pre[...], wexp[layer, :, 0:E], 1, 1)
            put_hidden_sums(b, layer - 1)

    heads = [summer(b, 3, 0) for b in range(BATCHES)]
    load(0, 2, 0).wait()
    head_first(0)
    heads[0].start(stages.at[0])
    load(1, 2, 0).wait()
    head_first(1, (5, heads[0].middle))
    heads[1].start(stages.at[1])
    thirds = [summer(b, 2, L - 1) for b in range(BATCHES)]
    heads[0].finish()
    load_low(L).wait()
    load_out(L - 1).wait()
    head_second(0, (2, heads[1].middle))
    load(0, 0, L - 1).start()
    thirds[0].start(stages.at[0])
    heads[1].finish()
    head_second(1, (3, thirds[0].middle))
    load(1, 0, L - 1).start()
    thirds[1].start(stages.at[1])
    load_low(L - 1).start()
    for layer in reversed(range(L)):
        twos = [summer(b, 1, layer) for b in range(BATCHES)]
        ones = [summer(b, 0, layer) for b in range(BATCHES)]
        thirds[0].finish()
        load(0, 1, layer).wait()
        block_gate(0, layer, (3, thirds[1].middle if layer > 0 else then(thirds[1].middle, 0)))
        block_second(0, layer)
        twos[0].start(stages.at[0])
        thirds[1].finish()
        load(1, 1, layer).wait()
        block_gate(1, layer, (3, twos[0].middle if layer > 0 else then(twos[0].middle, 1)))
        if layer > 0:
            load_out(layer - 1).start()
        block_second(1, layer)
        twos[1].start(stages.at[1])
        twos[0].finish()
        load(0, 0, layer).wait()
        block_spread(0, layer, (4, twos[1].middle if layer > 0 else then(twos[1].middle, 2)))
        ones[0].start(stages.at[0])
        if layer > 0:
            load(0, 1, layer - 1).start()
        twos[1].finish()
        load(1, 0, layer).wait()
        block_spread(1, layer, (4, ones[0].middle))
        ones[1].start(stages.at[1])
        if layer > 0:
            load(1, 1, layer - 1).start()
        ones[0].finish()
        load_low(layer).wait()
        if layer > 0:
            load_out(layer - 1).wait()
        block_expand(0, layer, (3, ones[1].middle))
        if layer > 0:
            thirds = [summer(b, 2, layer - 1) for b in range(BATCHES)]
            thirds[0].start(stages.at[0])
            load(0, 0, layer - 1).start()
        ones[1].finish()
        block_expand(1, layer, None if layer == 0 else (3, thirds[0].middle))
        if layer > 0:
            thirds[1].start(stages.at[1])
            late_core()
            load(1, 0, layer - 1).start()
            load_low(layer - 1).start()
    late_end()


def run_backward_all(sizes, inputs):
    sds = jax.ShapeDtypeStruct
    vm = pl.BlockSpec(memory_space=pltpu.VMEM)
    hbm = pl.BlockSpec(memory_space=pl.ANY)
    n_dp, n_sh = sizes
    sem = pltpu.SemaphoreType.DMA
    late = late_chunks(sizes)
    late_blocks = late * packed_blocks(sizes) // CHUNKS
    outs = [
        sds((n_sh, packed_blocks(sizes), 8, LANES), F32),
        sds((L, BATCHES, 2, 40, LANES), F32),
        sds((L, BATCHES, 8, LANES), F32),
        sds((BATCHES, 40, LANES), F32),
    ]
    scratch = [
        pltpu.VMEM((BATCHES, EC, HALF, LANES), F32),
        pltpu.VMEM((BATCHES, EC, HALF, LANES), F32),
        pltpu.VMEM((BATCHES, EC, HALF, LANES), F32),
        pltpu.VMEM((FULL, C), F32),
        pltpu.VMEM((HALF, C), BF16),
        pltpu.VMEM((HALF, E), BF16),
        pltpu.VMEM((IMGS, ROWS + 2 * GAP, LANES), F32),
        pltpu.VMEM((IMGS, ROWS + 2 * GAP, LANES), F32),
        pltpu.VMEM((HALF, LANES), F32),
        pltpu.VMEM((8, E), F32),
        pltpu.VMEM((8, E), F32),
        pltpu.VMEM((BATCHES, 40, LANES), F32),
        pltpu.SemaphoreType.DMA((BATCHES, 2)),
        pltpu.VMEM((E // 256, 256, 256), F32),
        pltpu.VMEM((144, E), F32),
        pltpu.VMEM((8, E), F32),
        pltpu.VMEM((8, LANES), F32),
        pltpu.VMEM((FULL, C), F32),
        pltpu.VMEM((FULL, C), BF16),
        pltpu.SemaphoreType.DMA((2,)),
        pltpu.VMEM((FULL, LANES), F32),
        pltpu.VMEM((8, LANES), F32),
        pltpu.VMEM((2, late_blocks, 8, LANES), F32),
        pltpu.VMEM((late_blocks, 8, LANES), F32),
        sem((late, 2)), sem((late, 2)), sem((late,)), sem((late,)),
    ]
    for b in range(BATCHES):
        for rows in BACK_ROWS[b]:
            scratch = scratch + sum_scratch(sizes, rows)
    specs = [vm] * 3 + [pl.BlockSpec(memory_space=pltpu.SMEM)] * 2 + [vm] * 6 + [hbm] * 5 + [vm] * 6
    return pl.pallas_call(
        functools.partial(backward_kernel, sizes),
        out_shape=outs,
        in_specs=specs,
        out_specs=[vm] * len(outs),
        scratch_shapes=scratch,
        compiler_params=pltpu.CompilerParams(collective_id=2, has_side_effects=True, vmem_limit_bytes=63 * 2**20),
        name="backward",
    )(*inputs)


GROUPS = 12
FACT_STEPS = (0, 3, 8)


def update_kernel(sizes, *refs):
    (packed, facts, fixes, tot_e, tot_c, tot_h, back_e, back_c, back_h, *state) = refs[:21]
    state_in = [state[3 * k : 3 * k + 3] for k in range(4)]
    out_refs = refs[21:25]
    gain_grad, norms, peers, mates = refs[25:29]
    (own, near, cross, side, line, full, gathered, g_class, sums_near) = refs[29:38]
    boxes = [refs[38 + 4 * k : 42 + 4 * k] for k in range(4)]
    (core_s, core_r, x_s, x_r, y_s, y_r, z_s, z_r, zz_s, zz_r, yy_s, yy_r,
     fn_s, fn_r, ff_s, ff_r, nn_s, nn_r, load_sems, store_sems, misc) = refs[54:75]
    n_dp, n_sh = sizes
    d, s = lax.axis_index("dp"), lax.axis_index("shard")
    count = packed_blocks(sizes)
    chunk = count // CHUNKS
    half = chunk // 2
    late = late_chunks(sizes)
    n_z = n_dp // 2
    piece = half // n_z
    bit0, bit1 = lax.rem(s, 2), s // 2
    near_peer = s + 1 - 2 * bit0
    far_peer = s + 2 - 4 * bit1
    yb, zi = lax.rem(d, 2), d // 2
    y_peer = d + 1 - 2 * yb

    greet(sizes)

    def load(k, i):
        if k == 1:
            return [pltpu.make_async_copy(state_in[1][i].at[:, l], boxes[1][i].at[l], load_sems.at[2 * i + 24 + l]) for l in range(L)]
        return [pltpu.make_async_copy(state_in[k][i], boxes[k][i], load_sems.at[4 * k + i])]

    def store(k):
        if k == 1:
            return [pltpu.make_async_copy(boxes[1][3].at[l], out_refs[1].at[:, l], store_sems.at[4 + l]) for l in range(L)]
        return [pltpu.make_async_copy(boxes[k][3], out_refs[k], store_sems.at[k])]

    def core_copy(k, i):
        rows = pl.ds(k * chunk, chunk)
        return pltpu.make_async_remote_copy(
            packed.at[2 * i + 1 - bit0, rows], near.at[i, rows], core_s.at[k, i], core_r.at[k, i],
            device_id=(d, near_peer), device_id_type=MESH)

    def x_copy(k):
        rows = pl.ds(k * chunk, chunk)
        return pltpu.make_async_remote_copy(
            own.at[far_peer, rows], cross.at[rows], x_s.at[k], x_r.at[k],
            device_id=(d, far_peer), device_id_type=MESH)

    def y_copy(k):
        rows = pl.ds(k * chunk + (1 - yb) * half, half)
        return pltpu.make_async_remote_copy(
            own.at[s, rows], side.at[k], y_s.at[k], y_r.at[k],
            device_id=(y_peer, s), device_id_type=MESH)

    def z_copy(k, step, source, target):
        rows = pl.ds(k * chunk + yb * half + target * piece, piece)
        return pltpu.make_async_remote_copy(
            own.at[s, rows], line.at[k, source], z_s.at[k, step], z_r.at[k, source],
            device_id=(2 * target + yb, s), device_id_type=MESH)

    def zz_copy(k, step, source, target):
        rows = pl.ds(k * (chunk // 2) + yb * (half // 2) + source * (piece // 2), piece // 2)
        return pltpu.make_async_remote_copy(
            full.at[rows], full.at[rows], zz_s.at[k, step], zz_r.at[k, source],
            device_id=(2 * target + yb, s), device_id_type=MESH)

    def yy_copy(k, b):
        rows = pl.ds(k * (chunk // 2) + b * (half // 2), half // 2)
        return pltpu.make_async_remote_copy(
            full.at[rows], full.at[rows], yy_s.at[k], yy_r.at[k],
            device_id=(y_peer, s), device_id_type=MESH)

    def over_z(action):
        def step(j, carry):
            action(j, lax.rem(zi + j, n_z))
            return carry

        lax.fori_loop(1, n_z, step, 0)

    def add_into(t, low, length, other, low_other, unit=8):
        def step(i, carry):
            rows = pl.ds(low + i * unit, unit)
            own[t, rows] = own[t, rows] + other(pl.ds(low_other + i * unit, unit))
            return carry

        lax.fori_loop(0, length // unit, step, 0)

    def stage_core(k):
        for i in range(2):
            core_copy(k, i).start()

    def stage_x(k):
        for i in range(2):
            core_copy(k, i).wait_recv()
        low = k * chunk
        add_into(far_peer, low, chunk, lambda rows: near[1 - bit1, rows], low)
        x_copy(k).start()
        add_into(s, low, chunk, lambda rows: near[bit1, rows], low)

    def stage_y(k):
        low = k * chunk
        give = low + (1 - yb) * half
        keep = low + yb * half
        if k >= late:
            x_copy(k).wait_recv()
            add_into(s, give, half, lambda rows: cross[rows], give)
        y_copy(k).start()
        if k >= late:
            add_into(s, keep, half, lambda rows: cross[rows], keep)

    def stage_z(k):
        y_copy(k).wait_recv()
        add_into(s, k * chunk + yb * half, half, lambda rows: side[k, rows], 0)
        over_z(lambda j, t: z_copy(k, j, zi, t).start())

    def stage_zz(k):
        over_z(lambda j, t: z_copy(k, j, t, zi).wait_recv())
        low = k * chunk + yb * half + zi * piece

        def step(i, carry):
            total = own[s, pl.ds(low + 2 * i, 2)]
            for j in range(1, n_z):
                total = total + line[k, lax.rem(zi + j, n_z), pl.ds(2 * i, 2)]
            full[low // 2 + i] = total.reshape(16, LANES).astype(BF16)
            return carry

        lax.fori_loop(0, piece // 2, step, 0)
        over_z(lambda j, t: zz_copy(k, j, zi, t).start())

    def stage_yy(k):
        over_z(lambda j, t: zz_copy(k, j, t, zi).wait_recv())
        yy_copy(k, yb).start()

    def stage_done(k):
        yy_copy(k, 1 - yb).wait_recv()

    def settle(k):
        if k >= late:
            for i in range(2):
                core_copy(k, i).wait_send()
            x_copy(k).wait_send()
        y_copy(k).wait_send()
        over_z(lambda j, t: z_copy(k, j, zi, t).wait_send())
        over_z(lambda j, t: zz_copy(k, j, zi, t).wait_send())
        yy_copy(k, yb).wait_send()

    def own_facts():
        return pltpu.make_async_copy(facts, peers.at[d], misc.at[0])

    def fact_far(step, source, target):
        return pltpu.make_async_remote_copy(
            facts, peers.at[source], ff_s.at[step], ff_r.at[source],
            device_id=(target, s), device_id_type=MESH)

    def fact_parts(t):
        return ((pl.ds(0, 8), pl.ds(0, 8)), (pl.ds(8 + 3 * t, 3), pl.ds(8, 3)))

    def fact_near(step, source, target):
        return [
            pltpu.make_async_remote_copy(
                peers.at[:, low], mates.at[source, :, high], fn_s.at[step, n], fn_r.at[source, n],
                device_id=(d, target), device_id_type=MESH)
            for n, (low, high) in enumerate(fact_parts(target))
        ]

    def fact_mine():
        return [
            pltpu.make_async_copy(peers.at[:, low], mates.at[s, :, high], misc.at[1 + n])
            for n, (low, high) in enumerate(fact_parts(s))
        ]

    def over_dp(action):
        def step(j, carry):
            action(j, lax.rem(d + j, n_dp))
            return carry

        lax.fori_loop(1, n_dp, step, 0)

    def facts_begin():
        own_facts().start()
        over_dp(lambda j, t: fact_far(j, d, t).start())

    def facts_second():
        def arrive(j, t):
            fact_far(j, t, d).wait_recv()
            fact_far(j, d, d).wait_send()

        own_facts().wait()
        over_dp(arrive)
        for copy in fact_mine():
            copy.start()
        for j in range(1, n_sh):
            for copy in fact_near(j, s, lax.rem(s + j, n_sh)):
                copy.start()

    def facts_third():
        for copy in fact_mine():
            copy.wait()
        for j in range(1, n_sh):
            for copy in fact_near(j, lax.rem(s + j, n_sh), s):
                copy.wait_recv()
            for copy in fact_near(j, s, s):
                copy.wait_send()
        for first in range(0, n_dp, 8):
            copy = pltpu.make_async_copy(mates.at[:, pl.ds(first, 8)], gathered, misc.at[0])
            copy.start()
            copy.wait()
            value = [gathered[:, :, k].reshape(8 * n_sh * 16, LANES) for k in range(11)]
            product = contract(jnp.concatenate(value[8:], 1), jnp.concatenate(value[:8], 1), 0, 0)
            g_class[...] = product if first == 0 else g_class[...] + product

    sums_near[s] = jnp.zeros((24, LANES), F32)
    first_fix, second_fix = fixes[0], fixes[1]

    def note(row, value):
        square = value * value
        width = square.shape[1]
        line_sum = jnp.sum(square, 0, keepdims=True)
        total = jnp.zeros((1, LANES), F32)
        for low in range(0, width - width % LANES, LANES):
            total = total + line_sum[:, low : low + LANES]
        tail = width % LANES
        if tail:
            total = total + jnp.concatenate([line_sum[:, width - tail :], jnp.zeros((1, LANES - tail), F32)], 1)
        sums_near[s, row : row + 1, :] = sums_near[s, row : row + 1, :] + total

    def moments(k, index, grad):
        weight, first, second, kept = boxes[k]
        kept[index] = grad
        new_first = BETA_ONE * first[index] + (1.0 - BETA_ONE) * grad
        new_second = BETA_TWO * second[index] + (1.0 - BETA_TWO) * grad * grad
        return new_first / first_fix / (jnp.sqrt(new_second / second_fix) + EPS_ADAM) + DECAY * weight[index]

    def gains_part():
        def norm(tot, back_of, chunk):
            grad, shift = jnp.zeros((1, LANES), F32), jnp.zeros((1, LANES), F32)
            for b in range(BATCHES):
                count = tot_e[0, 0, 48 + b : 49 + b, :]
                mean = tot[pl.ds(4 * chunk + 2 * b, 1), :] / count
                scale = lax.rsqrt(tot[pl.ds(4 * chunk + 2 * b + 1, 1), :] / count - mean * mean + EPS_NORM)
                back = back_of(b)
                plain = back[pl.ds(2 * chunk, 1), :]
                grad = grad + scale * (back[pl.ds(2 * chunk + 1, 1), :] - mean * plain)
                shift = shift + plain
            return grad, shift

        def mine(value, width):
            part = value[:, 0:width]
            for t in range(1, n_sh):
                part = jnp.where(s == t, value[:, t * width : (t + 1) * width], part)
            return part

        start = 0
        for layer in range(L):
            for kind in range(2):
                for q in range(3):
                    pair = norm(tot_e.at[layer, kind], lambda b: back_e.at[layer, b, kind], 3 * s + q)
                    for which in range(2):
                        low = start + 384 * (2 * kind + which) + LANES * q
                        gain_grad[0:1, low : low + LANES] = pair[which]
            for q in range(3):
                low = start + 384 * 4 + LANES * q
                gain_grad[0:1, low : low + LANES] = back_e[layer, 1, 0, pl.ds(24 + 3 * s + q, 1), :]
            low = start + 384 * 5
            pairs = [norm(tot_c.at[layer], lambda b: back_c.at[layer, b], c) for c in range(2)]
            for which in range(2):
                whole = jnp.concatenate([pairs[0][which], pairs[1][which]], 1)
                gain_grad[0:1, low + 64 * which : low + 64 * which + 64] = mine(whole, 64)
            gain_grad[0:1, low + 128 : low + 144] = mine(back_e[layer, 1, 0, 24 + EC : 25 + EC, :], 16)
            start = low + 144
        pairs = [norm(tot_h, lambda b: back_h.at[b], c) for c in range(HC)]
        for which in range(2):
            whole = jnp.concatenate([pair[which] for pair in pairs], 1)
            gain_grad[0:1, start + 320 * which : start + 320 * which + 320] = mine(whole, 320)
        whole = jnp.concatenate([back_h[1, 24 + k : 25 + k, :] for k in range(8)], 1)
        gain_grad[0:1, start + 640 : start + 890] = mine(whole, 250)

    every = slice(None)

    def mats_index(layer, c):
        return (layer, every, lanes(c))

    def weights_squares():
        for layer in range(L):
            for part in range(2):

                def body(c):
                    note(2 * layer + part, boxes[0][0][mats_index(layer, c + part * EC)])

                repeat(EC, body)
            for kk in range(3):
                cols = slice(kk * LANES, (kk + 1) * LANES)
                note(2 * L + 3 * layer, boxes[1][0][layer, 0:9, cols])
                note(2 * L + 3 * layer + 1, boxes[1][0][layer, 9 : 9 + SE, cols])
                note(2 * L + 3 * layer + 2, boxes[1][0][layer, 9 + SE : 9 + 2 * SE, cols])
        note(5 * L, boxes[2][0][...])

        def body(i):
            note(5 * L + 1, boxes[3][0][pl.ds(pl.multiple_of(i * 40, 40), 40), :])

        repeat(8, body)

    def mats_moments(layer, part):
        def body(c):
            panel = c + part * EC
            grad = full[pl.ds(AT_MATS[layer] // 2 + 4 * panel, 4)].astype(F32).reshape(64, LANES)
            note(GROUPS + 2 * layer + part, moments(0, mats_index(layer, panel), grad))

        repeat(EC, body)

    def chan_moments(layer):
        if True:
            for kk in range(3):
                low = (AT_CHAN[layer] + 18 * kk) // 2
                grad = full[low : low + 9].astype(F32).reshape(144, LANES)[:137]
                value = moments(1, (layer, every, slice(kk * LANES, (kk + 1) * LANES)), grad)
                note(GROUPS + 2 * L + 3 * layer, value[0:9])
                note(GROUPS + 2 * L + 3 * layer + 1, value[9 : 9 + SE])
                note(GROUPS + 2 * L + 3 * layer + 2, value[9 + SE :])

    def head_moments():
        rows = HEAD // 4
        for part in range(2):
            low = (AT_HEAD + part * (rows // 8)) // 2
            grad = full[low : low + rows // 16].astype(F32).reshape(rows, LANES)
            note(GROUPS + 5 * L, moments(2, (every, slice(part * LANES, (part + 1) * LANES)), grad))

    def class_moments():
        def body(i):
            rows = pl.ds(pl.multiple_of(i * 40, 40), 40)
            note(GROUPS + 5 * L + 1, moments(3, (rows, every), g_class[rows, :CLASSES]))

        repeat(8, body)

    def norm_copy(step, source, target):
        return pltpu.make_async_remote_copy(
            sums_near.at[source], sums_near.at[source], nn_s.at[step], nn_r.at[source],
            device_id=(d, target), device_id_type=MESH)

    def load_own(which):
        t = (s, far_peer)[which]
        return pltpu.make_async_copy(packed.at[t], own.at[t], load_sems.at[16 + which])

    tasks = [
        (MATS // 2, lambda: mats_moments(1, 0)),
        (MATS, lambda: mats_moments(1, 1)),
        (MATS + CHAN, lambda: chan_moments(1)),
        (AT_MATS[0], head_moments),
        (AT_MATS[0] + MATS // 2, lambda: mats_moments(0, 0)),
        (AT_MATS[0] + MATS, lambda: mats_moments(0, 1)),
        (AT_END, lambda: chan_moments(0)),
    ]
    for k in range(late, CHUNKS):
        stage_core(k)
    for which in range(2):
        load_own(which).start()
    if FACT_STEPS[0] == 0:
        facts_begin()
    for i in range(3):
        for k in range(4):
            for copy in load(k, i):
                copy.start()
    for which in range(2):
        load_own(which).wait()
    stages = (stage_x, stage_y, stage_z, stage_zz, stage_yy, stage_done)
    begins = [(1 + k, 1) if k < late else (1 + k - late, 0) for k in range(CHUNKS)]
    done = set()
    for tau in range(1, 2 + CHUNKS + 6):
        for age, stage in enumerate(stages):
            for k in range(CHUNKS):
                if tau - begins[k][0] + begins[k][1] == age and tau >= begins[k][0]:
                    stage(k)
                    if age == 5:
                        done.add(k)
        if tau == FACT_STEPS[0]:
            facts_begin()
        if tau == FACT_STEPS[1]:
            facts_second()
        if tau == 1:
            for k in range(4):
                for copy in load(k, 0):
                    copy.wait()
            weights_squares()
        if tau == 2:
            gains_part()
            for i in range(1, 3):
                for k in range(4):
                    for copy in load(k, i):
                        copy.wait()
        if tau == FACT_STEPS[2]:
            facts_third()
            class_moments()
            for copy in store(3):
                copy.start()
        while tau >= 3 and tasks and all(k in done for k in range(-(-tasks[0][0] // chunk))):
            tasks.pop(0)[1]()
    for j in range(1, n_sh):
        norm_copy(j, s, lax.rem(s + j, n_sh)).start()
    for k in (0, 1, 2):
        for copy in store(k):
            copy.start()
    for k in range(CHUNKS):
        settle(k)
    for j in range(1, n_sh):
        norm_copy(j, lax.rem(s + j, n_sh), s).wait_recv()
        norm_copy(j, s, s).wait_send()
    total = sums_near[0]
    for j in range(1, n_sh):
        total = total + sums_near[j]
    root = jnp.broadcast_to(jnp.sqrt(jnp.sum(total, 1, keepdims=True)), (24, LANES))
    norms[0:24, :] = root
    norms[24:32, :] = back_h[1, 32:40, :]
    for k in range(4):
        for copy in store(k):
            copy.wait()


def run_update(sizes, inputs, states):
    sds = jax.ShapeDtypeStruct
    vm = pl.BlockSpec(memory_space=pltpu.VMEM)
    hbm = pl.BlockSpec(memory_space=pl.ANY)
    n_dp, n_sh = sizes
    count = packed_blocks(sizes)
    chunk = count // CHUNKS
    n_z = n_dp // 2
    sem = pltpu.SemaphoreType.DMA
    outs = [sds(group[0].shape, F32) for group in states]
    gains = sum(([E // n_sh] * 5 + [(2 * C + SE) // n_sh]) * L) + (2 * HEAD + CLASSES) // n_sh
    outs = outs + [sds((1, gains), F32), sds((32, LANES), F32), sds((n_dp, 8 + 3 * n_sh, 16, LANES), BF16)]
    outs = outs + [sds((n_sh, n_dp, 11, 16, LANES), BF16)]
    scratch = [
        pltpu.VMEM((n_sh, count, 8, LANES), F32),
        pltpu.VMEM((2, count, 8, LANES), F32),
        pltpu.VMEM((count, 8, LANES), F32),
        pltpu.VMEM((CHUNKS, chunk // 2, 8, LANES), F32),
        pltpu.VMEM((CHUNKS, n_z, chunk // 2 // n_z, 8, LANES), F32),
        pltpu.VMEM((count // 2, 16, LANES), BF16),
        pltpu.VMEM((n_sh, 8, 11, 16, LANES), BF16),
        pltpu.VMEM((FACT - CLASS_PAD, CLASS_PAD), F32),
        pltpu.VMEM((n_sh, 2 * GROUPS, LANES), F32),
    ]
    for k, group in enumerate(states):
        shape = group[0].shape if k != 1 else (L, 137, 384)
        scratch = scratch + [pltpu.VMEM(shape, F32)] * 4
    scratch = scratch + [
        sem((CHUNKS, 2)), sem((CHUNKS, 2)), sem((CHUNKS,)), sem((CHUNKS,)), sem((CHUNKS,)), sem((CHUNKS,)),
        sem((CHUNKS, n_z)), sem((CHUNKS, n_z)), sem((CHUNKS, n_z)), sem((CHUNKS, n_z)), sem((CHUNKS,)), sem((CHUNKS,)),
        sem((n_sh, 2)), sem((n_sh, 2)), sem((n_dp,)), sem((n_dp,)), sem((n_sh,)), sem((n_sh,)),
        sem((32,)), sem((24,)), sem((3,)),
    ]
    return pl.pallas_call(
        functools.partial(update_kernel, sizes),
        out_shape=outs,
        in_specs=[hbm, hbm, pl.BlockSpec(memory_space=pltpu.SMEM)] + [vm] * 6 + [hbm] * 12,
        out_specs=[hbm] * 4 + [vm, vm, hbm, hbm],
        scratch_shapes=scratch,
        compiler_params=pltpu.CompilerParams(collective_id=3, has_side_effects=True, vmem_limit_bytes=63 * 2**20),
        name="update",
    )(*inputs, *[item for group in states for item in group])


def mats_factor(ratio, value):
    paired = ratio.reshape(-1, 2)
    column = jnp.arange(value.shape[2])
    return jnp.where(column[None, :] < value.shape[2] // 2, paired[:, 0:1], paired[:, 1:2])[
        :, None, :
    ]


def chan_factor(ratio, value):
    triple = ratio.reshape(-1, 3)
    row = jnp.arange(value.shape[1])[None, :]
    return jnp.where(
        row < 9, triple[:, 0:1], jnp.where(row < 9 + SE, triple[:, 1:2], triple[:, 2:3])
    )[:, :, None]


def adapt(first, second, grad, first_fix, second_fix):
    new_first = BETA_ONE * first + (1.0 - BETA_ONE) * grad
    new_second = BETA_TWO * second + (1.0 - BETA_TWO) * grad * grad
    update = new_first / first_fix / (jnp.sqrt(new_second / second_fix) + EPS_ADAM)
    return (new_first, new_second, update)


def per_device(
    images,
    bucket,
    counts,
    balance,
    labels,
    step,
    expand_w,
    expand_m,
    expand_v,
    expand_e,
    chan_w,
    chan_m,
    chan_v,
    chan_e,
    head_w,
    head_m,
    head_v,
    head_e,
    class_w,
    class_m,
    class_v,
    class_e,
    gain_w,
    gain_m,
    gain_v,
    gain_e,
):
    sizes = (lax.axis_size("dp"), lax.axis_size("shard"))
    table = jnp.asarray(tables())
    turned = lambda value: value.transpose(1, 0, 2)
    saved = run_forward_all(
        sizes,
        [
            images.reshape(FULL, C), table, bucket, counts, balance, labels, gain_w, gain_e,
            expand_w, expand_e, turned(chan_w), turned(chan_e), head_w.T, head_e.T, class_w, class_e,
        ],
    )
    kept = saved[:11]
    tot_e, tot_c, tot_h = kept[8:11]
    dpool_h, extra, facts, wexp_s, headt_s, chan_s, vec_e, vec_c, vec_h = saved[11:]
    (packed, back_e, back_c, back_h) = run_backward_all(
        sizes,
        [dpool_h, extra, table, bucket, counts, wexp_s, headt_s, chan_s, vec_e, vec_c, vec_h, *kept],
    )
    power = step[0].astype(F32)
    first_fix = 1.0 - jnp.power(jnp.float32(BETA_ONE), power)
    second_fix = 1.0 - jnp.power(jnp.float32(BETA_TWO), power)
    grads = run_update(
        sizes,
        [packed, facts, jnp.stack([first_fix, second_fix]), tot_e, tot_c, tot_h, back_e, back_c, back_h],
        [
            (expand_w, expand_m, expand_v),
            tuple(turned(item) for item in (chan_w, chan_m, chan_v)),
            tuple(item.T for item in (head_w, head_m, head_v)),
            (class_w, class_m, class_v),
        ],
    )
    roots = grads[5][: 2 * GROUPS, 0].reshape(2, GROUPS)
    ratio = roots[0] / roots[1]
    weights = (expand_w, chan_w, head_w, class_w, gain_w)
    firsts = (expand_m, chan_m, head_m, class_m, gain_m)
    seconds = (expand_v, chan_v, head_v, class_v, gain_v)
    averaged = (expand_e, chan_e, head_e, class_e, gain_e)
    owned = (grads[0], turned(grads[1]), grads[2].T, grads[3], grads[4])
    factors = [
        mats_factor(ratio[: 2 * L], expand_w),
        chan_factor(ratio[2 * L : 5 * L], chan_w),
        ratio[5 * L],
        ratio[5 * L + 1],
    ]
    result = [grads[5][2 * GROUPS, 0]]
    for item in range(5):
        new_first, new_second, update = adapt(firsts[item], seconds[item], owned[item], first_fix, second_fix)
        if item < 4:
            fresh = weights[item] - RATE * factors[item] * (update + DECAY * weights[item])
        else:
            fresh = weights[item] - RATE * update
        result = result + [fresh, new_first, new_second, KEEP * averaged[item] + (1.0 - KEEP) * fresh]
    return tuple(result + [roots])


def solution(mesh):
    in_specs = (
        P(None, ("dp", "shard"), None, None, None),
        P("dp"),
        P(None, ("dp", "shard")),
        P(None, ("dp", "shard")),
        P(None, ("dp", "shard")),
        P(),
        P(None, "shard", None),
        P(None, "shard", None),
        P(None, "shard", None),
        P(None, "shard", None),
        P(None, None, "shard"),
        P(None, None, "shard"),
        P(None, None, "shard"),
        P(None, None, "shard"),
        P(None, "shard"),
        P(None, "shard"),
        P(None, "shard"),
        P(None, "shard"),
        P("shard", None),
        P("shard", None),
        P("shard", None),
        P("shard", None),
        P("shard", None),
        P("shard", None),
        P("shard", None),
        P("shard", None),
    )
    out_specs = (
        P(),
        P(None, "shard", None),
        P(None, "shard", None),
        P(None, "shard", None),
        P(None, "shard", None),
        P(None, None, "shard"),
        P(None, None, "shard"),
        P(None, None, "shard"),
        P(None, None, "shard"),
        P(None, "shard"),
        P(None, "shard"),
        P(None, "shard"),
        P(None, "shard"),
        P("shard", None),
        P("shard", None),
        P("shard", None),
        P("shard", None),
        P("shard", None),
        P("shard", None),
        P("shard", None),
        P("shard", None),
        P(),
    )
    return jax.shard_map(
        per_device, mesh=mesh, in_specs=in_specs, out_specs=out_specs, check_vma=False
    )
```

```python
import functools

import jax
import jax.numpy as jnp
from jax import lax
from jax.experimental import pallas as pl
from jax.experimental.pallas import tpu as pltpu
from jax.sharding import PartitionSpec as P

C = 256
E = 1536
SE = 64
HEAD = 1280
CLASSES = 1000
L = 2
S = 12


EPS_NORM = 1e-05
BETA_ONE = 0.9
BETA_TWO = 0.99
EPS_ADAM = 1e-08
DECAY = 0.01
RATE = 0.3
KEEP = 0.9


def contract(left, right, left_dim, right_dim):
    return lax.dot_general(
        left, right, (((left_dim,), (right_dim,)), ((), ())), preferred_element_type=jnp.float32
    )


def matmul(left, right):
    return jnp.dot(left, right, precision=lax.Precision.HIGHEST, preferred_element_type=jnp.float32)


def matmul_bt(left, right):
    return lax.dot_general(
        left,
        right,
        (((1,), (1,)), ((), ())),
        precision=lax.Precision.HIGHEST,
        preferred_element_type=jnp.float32,
    )


def matmul_tb(left, right):
    return lax.dot_general(
        left,
        right,
        (((0,), (0,)), ((), ())),
        precision=lax.Precision.HIGHEST,
        preferred_element_type=jnp.float32,
    )


def pack_gains(vectors, rows):
    return jnp.concatenate([vector.reshape(rows, -1) for vector in vectors], 1)


IMGS = 5
ROWS = S * S
BATCHES = 2
HALF = IMGS * ROWS
FULL = BATCHES * HALF
SLOTS = BATCHES * IMGS
LANES = 128
EC = E // LANES
HC = HEAD // LANES
GAP = 16
TILE = 48
TILE_BACK = 48
CLASS_PAD = 1024
FACT = CLASS_PAD + 384
OFFSETS = [S * (a - 1) + (c - 1) for a in range(3) for c in range(3)]
MESH = pl.DeviceIdType.MESH
F32 = jnp.float32
BF16 = jnp.bfloat16


def split(value):
    high = value.astype(BF16).astype(F32)
    rest = value - high
    middle = rest.astype(BF16).astype(F32)
    return jnp.concatenate([high, middle, rest - middle], 0)


def exact(value, low_weight, dim):
    rows = value.shape[0]
    parts = contract(split(value).astype(BF16), low_weight, 1, dim)
    return parts[0:rows] + parts[rows : 2 * rows] + parts[2 * rows : 3 * rows]


def exact_outer(left, right):
    rows = left.shape[0]
    l, r = split(left), split(right)
    pick = lambda value, order: jnp.concatenate([value[k * rows : (k + 1) * rows] for k in order], 0).astype(BF16)
    return contract(pick(l, (0, 0, 1, 1, 0, 2)), pick(r, (0, 1, 0, 1, 2, 0)), 0, 0)


def fill_mask(mask, table, bucket, counts):
    spot = lax.broadcasted_iota(jnp.int32, (ROWS, LANES), 0).astype(F32)
    row = jnp.floor((spot + 0.5) / S)
    column = spot - S * row
    table[0] = jnp.where(column > 0.5, 1.0, 0.0)
    table[1] = jnp.where(column < S - 1.5, 1.0, 0.0)
    code = bucket[0]
    side = jnp.where(code == 0, 7, jnp.where(code == 1, 10, 12)).astype(F32)
    inside = jnp.where((row < side) & (column < side), 1.0, 0.0)
    for b in range(BATCHES):
        for i in range(IMGS):
            low = b * HALF + i * ROWS
            mask[low : low + ROWS, :] = inside * jnp.where(i < counts[b], 1.0, 0.0)
    return side * side


class Sum:
    def __init__(self, near, far, total, sems, sizes, rows):
        self.near, self.far, self.total = near, far, total
        self.sems = sems
        self.n_dp, self.n_sh = sizes
        self.rows = rows

    def copy_near(self, step, slot, target):
        d = lax.axis_index("dp")
        return pltpu.make_async_remote_copy(
            self.near.at[slot], self.near.at[slot],
            self.sems[0].at[step], self.sems[1].at[slot],
            device_id=(d, target), device_id_type=MESH)

    def copy_far(self, step, slot, target):
        s = lax.axis_index("shard")
        return pltpu.make_async_remote_copy(
            self.far.at[slot], self.far.at[slot],
            self.sems[2].at[step], self.sems[3].at[slot],
            device_id=(target, s), device_id_type=MESH)

    def start(self, stage):
        s = lax.axis_index("shard")
        self.near[s] = stage[0 : self.rows]
        for j in range(1, self.n_sh):
            self.copy_near(j, s, lax.rem(s + j, self.n_sh)).start()

    def middle(self):
        s, d = lax.axis_index("shard"), lax.axis_index("dp")
        for j in range(1, self.n_sh):
            self.copy_near(j, lax.rem(s + j, self.n_sh), s).wait_recv()
        for j in range(1, self.n_sh):
            self.copy_near(j, s, s).wait_send()
        part = self.near[0]
        for j in range(1, self.n_sh):
            part = part + self.near[j]
        self.far[d] = part

        def send(j, carry):
            self.copy_far(j, d, lax.rem(d + j, self.n_dp)).start()
            return carry

        lax.fori_loop(1, self.n_dp, send, 0)

    def finish(self):
        d = lax.axis_index("dp")

        def arrive(j, carry):
            self.copy_far(j, lax.rem(d + j, self.n_dp), d).wait_recv()
            self.copy_far(j, d, d).wait_send()
            return carry

        lax.fori_loop(1, self.n_dp, arrive, 0)
        part = self.far[0]
        for j in range(1, self.n_dp):
            part = part + self.far[j]
        self.total[0 : self.rows] = part


def sum_scratch(sizes, rows):
    n_dp, n_sh = sizes
    return [
        pltpu.VMEM((n_sh, rows, LANES), F32),
        pltpu.VMEM((n_dp, rows, LANES), F32),
        pltpu.SemaphoreType.DMA((n_sh,)),
        pltpu.SemaphoreType.DMA((n_sh,)),
        pltpu.SemaphoreType.DMA((n_dp,)),
        pltpu.SemaphoreType.DMA((n_dp,)),
    ]


def greet(sizes):
    n_dp, n_sh = sizes
    d, s = lax.axis_index("dp"), lax.axis_index("shard")
    gate = pltpu.get_barrier_semaphore()
    for j in range(1, n_sh):
        pl.semaphore_signal(gate, inc=1, device_id=(d, lax.rem(s + j, n_sh)), device_id_type=MESH)

    def signal(j, carry):
        pl.semaphore_signal(gate, inc=1, device_id=(lax.rem(d + j, n_dp), s), device_id_type=MESH)
        return carry

    lax.fori_loop(1, n_dp, signal, 0)
    pl.semaphore_wait(gate, n_sh + n_dp - 2)


def repeat(count, body, hook=None):
    def step(i, carry):
        if hook is not None:

            @pl.when(i == hook[0])
            def _():
                hook[1]()

        body(i)
        return carry

    lax.fori_loop(0, count, step, 0)


def lanes(c, width=LANES):
    return pl.ds(pl.multiple_of(c * width, width), width)


def coefs(total, row, count, gain, shift):
    mean = total[pl.ds(row, 1), :] / count
    square = total[pl.ds(row + 1, 1), :] / count
    scale = gain * lax.rsqrt(square - mean * mean + EPS_NORM)
    return scale, shift - mean * scale


def act_half(half):
    return half + half * jnp.tanh(half)


def forward_kernel(sizes, *refs):
    (images, bucket, counts, balance, labels, vec_w, vec_e, expand_w, expand_e, chan_w, chan_e,
     head_w, head_e, class_w, class_e,
     pre_s, mixed_s, feat_s, out_s, low_s, pool_s, unit_s, gate_s, tot_e, tot_c, tot_h,
     dpool_h, extra, facts, wexp_s, headt_s, chan_s, gain_e_s, gain_c_s, gain_h_s,
     pre, hid, out_t, low_t, scaled, pads, stages, totals, cnt, pool_t, gate_t, save_sems,
     wexp, chan, headt, classes, vecs, gain_e, gain_c, gain_h, gain_s, gain_k, pooled_h, bias_row,
     st_exp, st_chan, st_head, st_class, load_sems, sx, rx, sc, rc, sf, rf, out_sems,
     mask, area, own_rows, firstrow, table) = refs[:76]
    rest = list(refs[76:])
    edge_l, edge_r = table.at[0], table.at[1]
    n_sh = sizes[1]
    sums = []
    for m in range(2):
        group = []
        for rows in (56, 48, 8, 40):
            near, far = rest[0], rest[1]
            group.append((near, far, rest[2:6], rows))
            rest = rest[6:]
        sums.append(group)

    d, s = lax.axis_index("dp"), lax.axis_index("shard")
    near_peer = s + 1 - 2 * lax.rem(s, 2)
    far_peer = s + 2 - 4 * (s // 2)
    far_near = near_peer + 2 - 4 * (s // 2)
    pieces = [("exp", 0, 0, 0), ("exp", 1, 0, 0), ("vec", 0, 0, 0), ("chan", 0, 0, 0), ("exp", 0, 0, 1), ("exp", 1, 0, 1),
              ("exp", 0, 1, 0), ("exp", 1, 1, 0), ("chan", 0, 1, 0), ("exp", 0, 1, 1), ("exp", 1, 1, 1),
              ("head", 0, 0, 0), ("class", 0, 0, 0), ("class", 1, 0, 0)]
    mats = [k for k, piece in enumerate(pieces) if piece[0] == "exp"]

    def region(k, source):
        kind, m, layer, half = pieces[k]
        if kind == "exp":
            return wexp.at[m, layer, pl.ds(pl.multiple_of(source * 64, 64), 64), half * E : (half + 1) * E]
        if kind == "chan":
            return chan.at[:, layer, :, pl.ds(pl.multiple_of(source * 384, 384), 384)]
        if kind == "vec":
            return vecs.at[source]
        if kind == "head":
            return headt.at[:, pl.ds(pl.multiple_of(source * 320, 320), 320), :]
        return classes.at[m, pl.ds(pl.multiple_of(source * 320, 320), 320), :]

    def loads(k):
        kind, m, layer, half = pieces[k]
        if kind == "exp":
            slot = mats.index(k) % 2
            source = (expand_w, expand_e)[m].at[layer, :, half * E : (half + 1) * E]
            return [pltpu.make_async_copy(source, st_exp.at[slot], load_sems.at[slot])]
        if kind == "chan":
            return [pltpu.make_async_copy((chan_w, chan_e)[i].at[:, layer], st_chan.at[i], load_sems.at[2 + i]) for i in range(2)]
        if kind == "head":
            return [pltpu.make_async_copy((head_w, head_e)[i], st_head.at[i], load_sems.at[4 + i]) for i in range(2)]
        if kind == "class":
            return [pltpu.make_async_copy((class_w, class_e)[m], st_class, load_sems.at[6])]
        return []

    def fetch(k):
        for copy in loads(k):
            copy.start()

    def cast(k):
        kind, m, layer, half = pieces[k]
        for copy in loads(k):
            copy.wait()
        if kind == "exp":
            order = mats.index(k)
            wexp[m, layer, pl.ds(pl.multiple_of(s * 64, 64), 64), half * E : (half + 1) * E] = st_exp[order % 2].astype(BF16)
            if order + 2 < len(mats):
                fetch(mats[order + 2])
        if kind == "chan":
            cols = pl.ds(pl.multiple_of(s * 384, 384), 384)
            for i in range(2):
                padded = jnp.concatenate([st_chan[i, 0:9, :], jnp.zeros((7, 384), F32)], 0)
                chan[i, layer, 0:16, cols] = padded.astype(BF16)
                chan[i, layer, 16:80, cols] = st_chan[i, 9 : 9 + SE, :].astype(BF16)
                chan[i, layer, 80:144, cols] = st_chan[i, 9 + SE : 9 + 2 * SE, :].astype(BF16)
            if layer == 0:
                fetch(pieces.index(("chan", 0, 1, 0)))
        if kind == "head":
            for i in range(2):
                headt[i, pl.ds(pl.multiple_of(s * 320, 320), 320), :] = st_head[i].astype(BF16)
        if kind == "class":
            classes[m, pl.ds(pl.multiple_of(s * 320, 320), 320), :] = st_class[...].astype(BF16)
            if m == 0:
                fetch(k + 1)
        if kind == "vec":
            own_rows[...] = jnp.zeros(own_rows.shape, F32)
            for i in range(2):
                start = 0
                for row, width in enumerate(([384] * 5 + [144]) * L + [320] * 2 + [250]):
                    own_rows[i, row : row + 1, 0:width] = (vec_w, vec_e)[i][0:1, start : start + width]
                    start = start + width
            vecs[s] = own_rows[...].astype(BF16)

    def hop(k, source, target, send, receive):
        return pltpu.make_async_remote_copy(
            region(k, source), region(k, source), send.at[k], receive.at[k],
            device_id=(d, target), device_id_type=MESH)

    def offer(k):
        cast(k)
        hop(k, s, far_peer, sx, rx).start()
        hop(k, s, near_peer, sc, rc).start()

    def forward_on(k):
        hop(k, far_peer, s, sx, rx).wait_recv()
        hop(k, far_peer, near_peer, sf, rf).start()

    def ready(k):
        hop(k, near_peer, s, sc, rc).wait_recv()
        hop(k, far_near, s, sf, rf).wait_recv()

    def settle():
        for k in range(len(pieces)):
            hop(k, s, far_peer, sx, rx).wait_send()
            hop(k, s, near_peer, sc, rc).wait_send()
            hop(k, far_peer, near_peer, sf, rf).wait_send()

    def join(m, row, low, width):
        return jnp.concatenate([vecs[t, m, 0:16, :].astype(F32)[row : row + 1, low : low + width] for t in range(n_sh)], 1)

    def unpack_vectors():
        for m in range(2):
            for layer in range(L):
                for t in range(n_sh):
                    gain_e[m, layer, 0:5, 384 * t : 384 * t + 384] = vecs[t, m].astype(F32)[6 * layer : 6 * layer + 5, :]
                gain_c[m, layer, 0:1, :] = join(m, 6 * layer + 5, 0, 64)
                gain_c[m, layer, 1:2, :] = join(m, 6 * layer + 5, 64, 64)
                gain_s[m, layer, 0:1, :] = join(m, 6 * layer + 5, 128, 16)
            gain_h[m, 0:1, :] = join(m, 12, 0, 320)
            gain_h[m, 1:2, :] = join(m, 13, 0, 320)
            gain_k[m, 0:1, :] = join(m, 14, 0, 250)

    for k in (0, 1, 3, 11, 12):
        fetch(k)
    greet(sizes)
    for k in (0, 1, 2, 3):
        offer(k)
    area_value = fill_mask(mask, table, bucket, counts)
    area[...] = jnp.full((8, LANES), area_value, F32)
    firstrow[...] = jnp.zeros((8, LANES), F32)
    weighted = [[jnp.where(i < counts[b], balance[b, i], 0).astype(F32) for i in range(IMGS)] for b in range(BATCHES)]
    for b in range(BATCHES):
        firstrow[b : b + 1, :] = jnp.full((1, LANES), counts[b].astype(F32) * area_value, F32)
        firstrow[2 + b : 3 + b, :] = jnp.full((1, LANES), sum(weighted[b]), F32)

    def low(m, layer):
        return low_s.at[layer] if m == 0 else low_t

    def out(m, layer):
        return out_s.at[layer] if m == 0 else out_t

    def total_ref(m, kind, layer):
        if m == 0:
            return (tot_e.at[layer, 0], tot_e.at[layer, 1], tot_c.at[layer], tot_h)[kind]
        return totals.at[kind]

    def summer(m, kind, layer):
        near, far, sems, rows = sums[m][kind]
        return Sum(near, far, total_ref(m, kind, layer), sems, sizes, rows)

    def save(src, dst, index):
        return pltpu.make_async_copy(src, dst, save_sems.at[index])

    for slot in range(SLOTS):
        pads[slot, 0:GAP, :] = jnp.zeros((GAP, LANES), F32)
        pads[slot, GAP + ROWS : 2 * GAP + ROWS, :] = jnp.zeros((GAP, LANES), F32)

    def store_wexp(layer):
        return pltpu.make_async_copy(wexp.at[0, layer], wexp_s.at[layer], out_sems.at[layer])

    store_headt = pltpu.make_async_copy(headt.at[0], headt_s, out_sems.at[L])
    store_chan = pltpu.make_async_copy(chan.at[0], chan_s, out_sems.at[L + 1])

    def load_rows(i):
        rows = pl.ds(pl.multiple_of(i * ROWS, ROWS), ROWS)
        for half in range(2):
            cols = slice(half * LANES, half * LANES + LANES)
            value = images[rows, cols].astype(F32) * mask[rows, :]
            hid[0, rows, cols] = value
            hid[1, rows, cols] = value
            low_s[0, rows, cols] = value.astype(BF16)
            low_t[rows, cols] = value.astype(BF16)

    repeat(SLOTS, load_rows)

    def update(m, layer):
        tot = total_ref(m, 2, layer)
        for half in range(2):
            cols = slice(half * LANES, half * LANES + LANES)
            for b in range(BATCHES):
                scale, shift = coefs(tot, 4 * half + 2 * b, cnt[b : b + 1, :], gain_c[m, layer, 0:1, cols], gain_c[m, layer, 1:2, cols])

                def one(i):
                    rows = pl.ds(pl.multiple_of(b * HALF + i * ROWS, ROWS), ROWS)
                    value = hid[m, rows, cols] + mask[rows, :] * (out(m, layer)[rows, cols] * scale + shift)
                    hid[m, rows, cols] = value
                    low(m, layer + 1)[rows, cols] = value.astype(BF16)

                repeat(IMGS, one)

    def put_sums(stage, chunk, b, value):
        stage[pl.ds(4 * chunk + 2 * b, 1), :] = jnp.sum(value, 0, keepdims=True)
        stage[pl.ds(4 * chunk + 2 * b + 1, 1), :] = jnp.sum(value * value, 0, keepdims=True)

    def expand(m, layer, hook=None):
        stage = stages.at[m]

        def body(c):
            weight = wexp[m, layer, :, lanes(c, 256)]
            for b in range(BATCHES):
                value = jnp.dot(low(m, layer)[b * HALF : (b + 1) * HALF, :], weight, preferred_element_type=F32)
                for half in range(2):
                    piece = value[:, half * LANES : (half + 1) * LANES]
                    pre[m, 2 * c + half, b * HALF : (b + 1) * HALF, :] = piece
                    put_sums(stage, 2 * c + half, b, piece)
            if m == 0:
                for half in range(2):
                    save(pre.at[0, 2 * c + half], pre_s.at[layer, 2 * c + half], 2 * c + half).start()

        repeat(E // 256, body, hook)

    def depthwise(m, layer, hook=None):
        stage = stages.at[m]
        tot = total_ref(m, 0, layer)

        def body(c):
            if m == 0:
                save(pre.at[0, c], pre_s.at[layer, c], c).wait()
            tap_rows = chan[m, layer, 0:16, lanes(c)].astype(F32)
            tap = [tap_rows[k : k + 1, :] for k in range(9)]
            for b in range(BATCHES):
                scale, shift = coefs(tot, 4 * c + 2 * b, cnt[b : b + 1, :], gain_e[m, layer, 0:1, lanes(c)], gain_e[m, layer, 1:2, lanes(c)])
                scale, shift = 0.5 * scale, 0.5 * shift
                for i in range(IMGS):
                    slot = b * IMGS + i
                    rows = slice(slot * ROWS, (slot + 1) * ROWS)
                    half = mask[rows, :] * (pre[m, c, rows, :] * scale + shift)
                    pads[slot, GAP : GAP + ROWS, :] = act_half(half)
                first = jnp.zeros((8, LANES), F32)
                second = jnp.zeros((8, LANES), F32)
                for i in range(IMGS):
                    slot = b * IMGS + i
                    for t in range(ROWS // TILE):
                        start = GAP + t * TILE
                        near = [pads[slot, start + o : start + o + TILE, :] for o in OFFSETS]
                        left = near[0] * tap[0] + near[3] * tap[3] + near[6] * tap[6]
                        mid = near[1] * tap[1] + near[4] * tap[4] + near[7] * tap[7]
                        right = near[2] * tap[2] + near[5] * tap[5] + near[8] * tap[8]
                        rows = slice(slot * ROWS + t * TILE, slot * ROWS + (t + 1) * TILE)
                        value = mask[rows, :] * (mid + edge_l[t * TILE : (t + 1) * TILE, :] * left + edge_r[t * TILE : (t + 1) * TILE, :] * right)
                        pre[m, c, rows, :] = value
                        first = first + jnp.sum(value.reshape(TILE // 8, 8, LANES), 0)
                        second = second + jnp.sum((value * value).reshape(TILE // 8, 8, LANES), 0)
                stage[pl.ds(4 * c + 2 * b, 1), :] = jnp.sum(first, 0, keepdims=True)
                stage[pl.ds(4 * c + 2 * b + 1, 1), :] = jnp.sum(second, 0, keepdims=True)
            if m == 0:
                save(pre.at[0, c], mixed_s.at[layer, c], c).start()

        repeat(EC, body, hook)

    def pooling(m, layer, hook=None):
        tot = total_ref(m, 1, layer)
        pool = pool_s.at[layer] if m == 0 else pool_t

        def body(c):
            if m == 0:
                save(pre.at[0, c], mixed_s.at[layer, c], c).wait()
            for b in range(BATCHES):
                scale, shift = coefs(tot, 4 * c + 2 * b, cnt[b : b + 1, :], gain_e[m, layer, 2:3, lanes(c)], gain_e[m, layer, 3:4, lanes(c)])
                scale, shift = 0.5 * scale, 0.5 * shift
                for i in range(IMGS):
                    slot = b * IMGS + i
                    rows = slice(slot * ROWS, (slot + 1) * ROWS)
                    value = act_half(mask[rows, :] * (pre[m, c, rows, :] * scale + shift))
                    pre[m, c, rows, :] = value
                    pool[b * 8 + i : b * 8 + i + 1, lanes(c)] = jnp.sum(value, 0, keepdims=True) / area[0:1, :]

        repeat(EC, body, hook)

    def project(m, layer):
        pool = pool_s.at[layer] if m == 0 else pool_t
        gate = gate_s.at[layer] if m == 0 else gate_t
        units = exact(pool[...], chan[m, layer, 16:80, :], 1) + gain_s[m, layer, 0:1, :]
        if m == 0:
            unit_s[layer] = units
        gate[...] = jax.nn.sigmoid(exact(jax.nn.silu(units), chan[m, layer, 80:144, :], 0) + gain_e[m, layer, 4:5, :])

        def body(c):
            for b in range(BATCHES):
                for i in range(IMGS):
                    rows = slice(b * HALF + i * ROWS, b * HALF + (i + 1) * ROWS)
                    scaled[rows, lanes(c)] = (pre[m, c, rows, :] * gate[b * 8 + i : b * 8 + i + 1, lanes(c)]).astype(BF16)

        repeat(EC, body)
        stage = stages.at[m]
        for b in range(BATCHES):
            rows = slice(b * HALF, (b + 1) * HALF)
            value = contract(scaled[rows, :], wexp[m, layer, :, E : 2 * E], 1, 1)
            out(m, layer)[rows, :] = value
            for half in range(2):
                put_sums(stage, half, b, value[:, half * LANES : (half + 1) * LANES])

    def features(m, hook=None):
        stage = stages.at[m]

        def body(c):
            weight = headt[m, pl.ds(pl.multiple_of(c * 256, 256), 256), :]
            for b in range(BATCHES):
                value = contract(low(m, L)[b * HALF : (b + 1) * HALF, :], weight, 1, 1)
                for half in range(2):
                    piece = value[:, half * LANES : (half + 1) * LANES]
                    pre[m, 2 * c + half, b * HALF : (b + 1) * HALF, :] = piece
                    put_sums(stage, 2 * c + half, b, piece)
            if m == 0:
                for half in range(2):
                    save(pre.at[0, 2 * c + half], feat_s.at[2 * c + half], 2 * c + half).start()

        repeat(HEAD // 256, body, hook)

    def head_pool(m, hook=None):
        tot = total_ref(m, 3, 0)

        def body(c):
            for b in range(BATCHES):
                scale, shift = coefs(tot, 4 * c + 2 * b, cnt[b : b + 1, :], gain_h[m, 0:1, lanes(c)], gain_h[m, 1:2, lanes(c)])
                scale, shift = 0.5 * scale, 0.5 * shift
                for i in range(IMGS):
                    slot = b * IMGS + i
                    rows = slice(slot * ROWS, (slot + 1) * ROWS)
                    value = act_half(mask[rows, :] * (pre[m, c, rows, :] * scale + shift))
                    pooled_h[m, b * 8 + i : b * 8 + i + 1, lanes(c)] = jnp.sum(value, 0, keepdims=True) / area[0:1, :]

        repeat(HC, body, hook)

    for m in range(2):
        stages[m] = jnp.zeros((56, LANES), F32)
    pool_s[...] = jnp.zeros(pool_s.shape, F32)
    pool_t[...] = jnp.zeros(pool_t.shape, F32)
    pooled_h[...] = jnp.zeros(pooled_h.shape, F32)
    stages[0, 48:56, :] = firstrow[...]
    pending = None
    forward_on(0)
    ready(0)
    for layer in range(L):
        s_one, t_one = summer(0, 0, layer), summer(1, 0, layer)
        s_two, t_two = summer(0, 1, layer), summer(1, 1, layer)
        s_three, t_three = summer(0, 2, layer), summer(1, 2, layer)
        if layer > 0:
            update(0, layer - 1)
            ready(6)
        expand(0, layer, None if pending is None else (2, pending.middle))
        s_one.start(stages.at[0])
        if layer == 0:
            forward_on(1)
            ready(1)
            forward_on(2)
            offer(4)
        else:
            forward_on(8)
            pending.finish()
            update(1, layer - 1)
            ready(7)
            offer(10)
        expand(1, layer, (4, s_one.middle))
        t_one.start(stages.at[1])
        if layer == 0:
            forward_on(3)
            ready(2)
            unpack_vectors()
            ready(3)
            offer(5)
        else:
            forward_on(9)
            ready(8)
            offer(11)
        s_one.finish()
        if layer == 0:
            cnt[...] = tot_e[0, 0, 48:56, :]
        depthwise(0, layer, (2, t_one.middle))
        s_two.start(stages.at[0])
        forward_on((4, 10)[layer])
        offer((6, 12)[layer])
        t_one.finish()
        depthwise(1, layer, (5, s_two.middle))
        t_two.start(stages.at[1])
        forward_on((5, 11)[layer])
        if layer == 0:
            offer(7)
        ready((4, 9)[layer])
        s_two.finish()
        pooling(0, layer, (5, t_two.middle))
        project(0, layer)
        s_three.start(stages.at[0])
        forward_on((6, 12)[layer])
        offer((8, 13)[layer])
        ready((5, 10)[layer])
        t_two.finish()
        pooling(1, layer, (6, s_three.middle))
        project(1, layer)
        t_three.start(stages.at[1])
        if layer == 0:
            forward_on(7)
            offer(9)
        s_three.finish()
        pending = t_three
    for layer in range(L):
        store_wexp(layer).start()
    s_head, t_head = summer(0, 3, 0), summer(1, 3, 0)
    update(0, L - 1)
    ready(11)
    features(0, (2, pending.middle))
    s_head.start(stages.at[0])
    pending.finish()
    update(1, L - 1)
    features(1, (4, s_head.middle))
    t_head.start(stages.at[1])
    forward_on(13)
    store_headt.start()
    store_chan.start()
    s_head.finish()
    head_pool(0, (3, t_head.middle))
    ready(12)
    t_head.finish()
    head_pool(1)
    ready(13)

    def class_logits(m):
        low_pool = pooled_h[m].astype(BF16)
        return jnp.dot(low_pool, classes[m], preferred_element_type=F32) + gain_k[m, 0:1, :]

    def log_softmax(value):
        value = value - jnp.max(value, 1, keepdims=True)
        return value - jnp.log(jnp.sum(jnp.exp(value), 1, keepdims=True))

    logp = log_softmax(class_logits(0))
    target = log_softmax(class_logits(1))
    expected = jnp.exp(target)
    row16 = lax.broadcasted_iota(jnp.int32, (16, LANES), 0)
    label_rows = jnp.zeros((16, LANES), jnp.int32)
    weight_rows = jnp.zeros((16, LANES), F32)
    for b in range(BATCHES):
        for i in range(IMGS):
            label_rows = jnp.where(row16 == 8 * b + i, labels[b, i], label_rows)
            weight_rows = jnp.where(row16 == 8 * b + i, weighted[b][i], weight_rows)
    hot = lax.broadcasted_iota(jnp.int32, (16, CLASSES), 1) == label_rows[:, 0:1]
    total_weight = tot_e[0, 0, 50:51, :] + tot_e[0, 0, 51:52, :]
    coef = weight_rows[:, 0:1] / total_weight[:, 0:1]
    per = jnp.sum(expected * (target - logp), 1, keepdims=True) - jnp.sum(jnp.where(hot, logp, 0.0), 1, keepdims=True)
    loss = jnp.sum(coef * per, 0, keepdims=True)
    slope = -coef * (jnp.where(hot, 1.0, 0.0) + expected)
    grad_low = (slope - jnp.exp(logp) * jnp.sum(slope, 1, keepdims=True)).astype(BF16)
    bias_row[...] = jnp.zeros(bias_row.shape, F32)
    bias_row[0:1, 0:CLASSES] = jnp.sum(grad_low.astype(F32), 0, keepdims=True)
    for k in range(8):
        extra[k : k + 1, :] = bias_row[0:1, k * LANES : (k + 1) * LANES]
    extra[8:16, :] = jnp.broadcast_to(loss, (8, LANES))
    dpool_h[...] = contract(grad_low, classes[0], 1, 1) / area[0:1, 0:1]
    facts[...] = jnp.zeros(facts.shape, BF16)
    low_pool = pooled_h[0].astype(BF16)
    for k in range(8):
        width = min(LANES, CLASSES - k * LANES)
        facts[k, :, 0:width] = grad_low[:, k * LANES : k * LANES + width]
    for t in range(n_sh):
        for q in range(3):
            width = min(LANES, 320 - q * LANES)
            low = 320 * t + q * LANES
            facts[8 + 3 * t + q, :, 0:width] = low_pool[:, low : low + width]
    gain_e_s[...] = gain_e[0]
    gain_c_s[...] = gain_c[0]
    gain_h_s[...] = gain_h[0]
    settle()
    for layer in range(L):
        store_wexp(layer).wait()
    store_headt.wait()
    store_chan.wait()
    for c in range(HC):
        save(pre.at[0, c], feat_s.at[c], c).wait()


def run_forward_all(sizes, inputs):
    sds = jax.ShapeDtypeStruct
    vm = pl.BlockSpec(memory_space=pltpu.VMEM)
    hbm = pl.BlockSpec(memory_space=pl.ANY)
    n_sh = sizes[1]
    outs = [
        (sds((L, EC, FULL, LANES), F32), hbm),
        (sds((L, EC, FULL, LANES), F32), hbm),
        (sds((HC, FULL, LANES), F32), hbm),
        (sds((L, FULL, C), F32), vm),
        (sds((L + 1, FULL, C), BF16), vm),
        (sds((L, 16, E), F32), vm),
        (sds((L, 16, SE), F32), vm),
        (sds((L, 16, E), F32), vm),
        (sds((L, 2, 56, LANES), F32), vm),
        (sds((L, 8, LANES), F32), vm),
        (sds((40, LANES), F32), vm),
        (sds((16, HEAD), F32), vm),
        (sds((16, LANES), F32), vm),
        (sds((8 + 3 * n_sh, 16, LANES), BF16), vm),
        (sds((L, C, 2 * E), BF16), hbm),
        (sds((HEAD, C), BF16), hbm),
        (sds((L, 144, E), BF16), hbm),
        (sds((L, 8, E), F32), vm),
        (sds((L, 8, C), F32), vm),
        (sds((8, HEAD), F32), vm),
    ]
    scratch = [
        pltpu.VMEM((2, EC, FULL, LANES), F32),
        pltpu.VMEM((2, FULL, C), F32),
        pltpu.VMEM((FULL, C), F32),
        pltpu.VMEM((FULL, C), BF16),
        pltpu.VMEM((FULL, E), BF16),
        pltpu.VMEM((SLOTS, ROWS + 2 * GAP, LANES), F32),
        pltpu.VMEM((2, 56, LANES), F32),
        pltpu.VMEM((4, 56, LANES), F32),
        pltpu.VMEM((8, LANES), F32),
        pltpu.VMEM((16, E), F32),
        pltpu.VMEM((16, E), F32),
        pltpu.SemaphoreType.DMA((EC,)),
        pltpu.VMEM((2, L, C, 2 * E), BF16),
        pltpu.VMEM((2, L, 144, E), BF16),
        pltpu.VMEM((2, HEAD, C), BF16),
        pltpu.VMEM((2, HEAD, CLASSES), BF16),
        pltpu.VMEM((n_sh, 2, 16, 384), BF16),
        pltpu.VMEM((2, L, 8, E), F32),
        pltpu.VMEM((2, L, 8, C), F32),
        pltpu.VMEM((2, 8, HEAD), F32),
        pltpu.VMEM((2, L, 8, SE), F32),
        pltpu.VMEM((2, 8, CLASSES), F32),
        pltpu.VMEM((2, 16, HEAD), F32),
        pltpu.VMEM((8, CLASS_PAD), F32),
        pltpu.VMEM((2, 64, E), F32),
        pltpu.VMEM((2, 137, 384), F32),
        pltpu.VMEM((2, 320, C), F32),
        pltpu.VMEM((320, CLASSES), F32),
        pltpu.SemaphoreType.DMA((7,)),
    ]
    scratch = scratch + [pltpu.SemaphoreType.DMA((14,))] * 6 + [pltpu.SemaphoreType.DMA((L + 2,))]
    scratch = scratch + [
        pltpu.VMEM((FULL, LANES), F32),
        pltpu.VMEM((8, LANES), F32),
        pltpu.VMEM((2, 16, 384), F32),
        pltpu.VMEM((8, LANES), F32),
        pltpu.VMEM((2, ROWS, LANES), F32),
    ]
    for m in range(2):
        for rows in (56, 48, 8, 40):
            scratch = scratch + sum_scratch(sizes, rows)
    return pl.pallas_call(
        functools.partial(forward_kernel, sizes),
        out_shape=[o[0] for o in outs],
        in_specs=[vm] + [pl.BlockSpec(memory_space=pltpu.SMEM)] * 4 + [vm] * 2 + [hbm] * 8,
        out_specs=[o[1] for o in outs],
        scratch_shapes=scratch,
        compiler_params=pltpu.CompilerParams(collective_id=1, has_side_effects=True, vmem_limit_bytes=63 * 2**20),
        name="forward",
    )(*inputs)


BACK_ROWS = ((24, 24, 8, 24), (40, 24, 8, 40))


def round_up(value, unit):
    return -(-value // unit) * unit


CHUNKS = 6
MATS = 2 * E // LANES * 8
CHAN = 3 * 18
AT_MATS = (MATS + CHAN + 2 * HEAD // 4 // 8, 0)
AT_CHAN = (AT_MATS[0] + MATS, MATS)
AT_HEAD = MATS + CHAN
AT_END = AT_CHAN[0] + CHAN


def packed_blocks(sizes):
    return round_up(AT_END, CHUNKS * 2 * sizes[0])


def late_chunks(sizes):
    return AT_MATS[0] // (packed_blocks(sizes) // CHUNKS)


def backward_kernel(sizes, *refs):
    (dpool_h, extra, bucket, counts, wexp, headt, chan, gain_e, gain_c, gain_h,
     pre_s, mixed_s, feat_s, out_s, low_s, pool_s, unit_s, gate_s, tot_e, tot_c, tot_h,
     packed, back_e, back_c, back_h,
     pre, mixed, grad, grad_hid, low_out, low_pre, pads_x, pads_g, slope, dgate, dpool, stages, load_sems,
     held, held_chan, held_exb, held_sqb, out_v, low_v, row_sems, mask, area, table, near, cross, core_s, core_r, x_s, x_r) = refs[:54]
    rest = list(refs[54:])
    edge_l, edge_r = table.at[0], table.at[1]
    n_dp, n_sh = sizes
    sums = []
    for b in range(BATCHES):
        group = []
        for rows in BACK_ROWS[b]:
            group.append((rest[0], rest[1], rest[2:6], rows))
            rest = rest[6:]
        sums.append(group)

    greet(sizes)

    def back_ref(b, kind, layer):
        return (back_e.at[layer, b, 0], back_e.at[layer, b, 1], back_c.at[layer, b], back_h.at[b])[kind]

    def summer(b, kind, layer):
        near, far, sems, rows = sums[b][kind]
        return Sum(near, far, back_ref(b, kind, layer), sems, sizes, rows)

    def load(b, kind, layer):
        rows = slice(b * HALF, (b + 1) * HALF)
        if kind == 0:
            return pltpu.make_async_copy(pre_s.at[layer, :, rows], pre.at[b], load_sems.at[b, 0])
        if kind == 1:
            return pltpu.make_async_copy(mixed_s.at[layer, :, rows], mixed.at[b], load_sems.at[b, 1])
        return pltpu.make_async_copy(feat_s.at[:, rows], pre.at[b, 0:HC], load_sems.at[b, 0])

    area[...] = jnp.full((8, LANES), fill_mask(mask, table, bucket, counts), F32)

    d, s = lax.axis_index("dp"), lax.axis_index("shard")
    bit0, bit1 = lax.rem(s, 2), s // 2
    near_peer, far_peer = s + 1 - 2 * bit0, s + 2 - 4 * bit1
    late = late_chunks(sizes)
    chunk = packed_blocks(sizes) // CHUNKS

    def core_copy(k, i):
        rows = pl.ds(k * chunk, chunk)
        return pltpu.make_async_remote_copy(
            packed.at[2 * i + 1 - bit0, rows], near.at[i, rows], core_s.at[k, i], core_r.at[k, i],
            device_id=(d, near_peer), device_id_type=MESH)

    def x_copy(k):
        rows = pl.ds(k * chunk, chunk)
        return pltpu.make_async_remote_copy(
            packed.at[far_peer, rows], cross.at[rows], x_s.at[k], x_r.at[k],
            device_id=(d, far_peer), device_id_type=MESH)

    def add_rows(t, k, other):
        def step(i, carry):
            rows = pl.ds(k * chunk + i * 8, 8)
            packed[t, rows] = packed[t, rows] + other(rows)
            return carry

        lax.fori_loop(0, chunk // 8, step, 0)

    def late_core():
        for k in range(late):
            for i in range(2):
                core_copy(k, i).start()

    def late_x(k):
        if k < late:
            for i in range(2):
                core_copy(k, i).wait_recv()
            add_rows(far_peer, k, lambda rows: near[1 - bit1, rows])
            x_copy(k).start()
            add_rows(s, k, lambda rows: near[bit1, rows])

    def late_end():
        for k in range(late):
            x_copy(k).wait_recv()
            add_rows(s, k, lambda rows: cross[rows])
        for k in range(late):
            for i in range(2):
                core_copy(k, i).wait_send()
            x_copy(k).wait_send()

    def then(first, k):
        def run():
            first()
            late_x(k)

        return run

    def load_out(layer):
        return pltpu.make_async_copy(out_s.at[layer], out_v, row_sems.at[0])

    def load_low(layer):
        return pltpu.make_async_copy(low_s.at[layer], low_v, row_sems.at[1])

    for b in range(BATCHES):
        load(b, 2, 0).start()
    load_low(L).start()
    load_out(L - 1).start()
    for b in range(BATCHES):
        load(b, 1, L - 1).start()
    for slot in range(IMGS):
        for pads in (pads_x, pads_g):
            pads[slot, 0:GAP, :] = jnp.zeros((GAP, LANES), F32)
            pads[slot, GAP + ROWS : 2 * GAP + ROWS, :] = jnp.zeros((GAP, LANES), F32)
    dgate[...] = jnp.zeros(dgate.shape, F32)
    stages[...] = jnp.zeros(stages.shape, F32)
    stages[1, 24:40, :] = extra[...]
    held_chan[...] = jnp.zeros(held_chan.shape, F32)
    spare = packed.shape[1] - AT_END
    if spare:
        packed[:, AT_END:] = jnp.zeros((n_sh, spare, 8, LANES), F32)

    def pack(first, c, value):
        for t in range(n_sh):
            for half in range(2):
                piece = value[64 * t : 64 * t + 64, half * LANES : (half + 1) * LANES]
                packed[t, pl.ds(first + 16 * c + 8 * half, 8)] = piece.reshape(8, 8, LANES)

    def pack_chan(layer):
        for k in range(EC):
            first = AT_CHAN[layer] + 18 * (k % 3)
            packed[k // 3, first : first + 18] = held_chan[:, k * LANES : (k + 1) * LANES].reshape(18, 8, LANES)

    def forward_total(kind, layer):
        return (tot_e.at[layer, 0], tot_e.at[layer, 1], tot_c.at[layer], tot_h)[kind]

    def moments(b, kind, layer, c):
        tot = forward_total(kind, layer)
        count = tot_e[0, 0, 48 + b : 49 + b, :]
        mean = tot[pl.ds(4 * c + 2 * b, 1), :] / count
        square = tot[pl.ds(4 * c + 2 * b + 1, 1), :] / count
        return mean, lax.rsqrt(square - mean * mean + EPS_NORM)

    def half_coefs(b, kind, layer, c, gain, shift):
        mean, scale = moments(b, kind, layer, c)
        scale = scale * gain
        return 0.5 * scale, 0.5 * (shift - mean * scale)

    def back_coefs(b, kind, layer, c, gain):
        mean, scale = moments(b, kind, layer, c)
        count = tot_e[0, 0, 48 + b : 49 + b, :]
        back = back_ref(b, kind, layer)
        plain = back[pl.ds(2 * c, 1), :]
        cross = scale * (back[pl.ds(2 * c + 1, 1), :] - mean * plain)
        first = scale * gain
        third = -first * scale * cross / count
        return first, -first * plain / count - mean * third, third

    def fold(value):
        return jnp.sum(value.reshape(value.shape[0] // 8, 8, LANES), 0)

    def put(stage, c, first, second):
        stage[pl.ds(2 * c, 1), :] = jnp.sum(first, 0, keepdims=True)
        stage[pl.ds(2 * c + 1, 1), :] = jnp.sum(second, 0, keepdims=True)

    def image(b, i):
        return slice(i * ROWS, (i + 1) * ROWS), slice(b * HALF + i * ROWS, b * HALF + (i + 1) * ROWS)

    def bend(half):
        t = jnp.tanh(half)
        return half + half * t, (0.5 + 0.5 * t) * (1.0 + half * (1.0 - t))

    def head_first(b, hook=None):
        stage = stages.at[b]

        def body(c):
            scale, shift = half_coefs(b, 3, 0, c, gain_h[0:1, lanes(c)], gain_h[1:2, lanes(c)])
            first = jnp.zeros((8, LANES), F32)
            second = jnp.zeros((8, LANES), F32)
            for i in range(IMGS):
                rows, full = image(b, i)
                x = pre[b, c, rows, :]
                half = mask[full, :] * (x * scale + shift)
                value = mask[full, :] * dpool_h[b * 8 + i : b * 8 + i + 1, lanes(c)] * bend(half)[1]
                grad[b, c, rows, :] = value
                first = first + fold(value)
                second = second + fold(value * x)
            put(stage, c, first, second)

        repeat(HC, body, hook)

    def norm_back_rows(b, kind, layer, c, gain, source):
        one, two, three = back_coefs(b, kind, layer, c, gain)
        for i in range(IMGS):
            rows, full = image(b, i)
            value = mask[full, :] * (one * grad[b, c, rows, :] + two + three * source[b, c, rows, :])
            low_pre[rows, lanes(c)] = value.astype(BF16)

    def put_hidden_sums(b, layer):
        stage = stages.at[b]
        for half in range(2):
            cols = slice(half * LANES, (half + 1) * LANES)
            first = jnp.zeros((8, LANES), F32)
            second = jnp.zeros((8, LANES), F32)
            for i in range(IMGS):
                full = image(b, i)[1]
                value = grad_hid[full, cols]
                first = first + fold(value)
                second = second + fold(value * out_v[full, cols])
            put(stage, half, first, second)

    def head_second(b, hook=None):
        mine = slice(b * HALF, (b + 1) * HALF)

        def body(c):
            for half in range(2):
                norm_back_rows(b, 3, 0, 2 * c + half, gain_h[0:1, lanes(2 * c + half)], pre)
            value = contract(low_pre[:, lanes(c, 256)], low_v[mine, :], 0, 0)
            if b == 0:
                held[c] = value
            else:
                value = value + held[c]
                for i in range(32):
                    row = 32 * c + i
                    for half in range(2):
                        packed[row // 40, AT_HEAD + 40 * half + lax.rem(row, 40)] = value[8 * i : 8 * i + 8, half * LANES : (half + 1) * LANES]

        repeat(HEAD // 256, body, hook)
        grad_hid[mine, :] = jnp.dot(low_pre[:, 0:HEAD], headt[...], preferred_element_type=F32)
        put_hidden_sums(b, L - 1)

    def block_gate(b, layer, hook=None):
        mine = slice(b * HALF, (b + 1) * HALF)
        eight = slice(b * 8, b * 8 + 8)
        for half in range(2):
            cols = slice(half * LANES, (half + 1) * LANES)
            one, two, three = back_coefs(b, 2, layer, half, gain_c[layer, 0:1, cols])
            for i in range(IMGS):
                rows, full = image(b, i)
                low_out[rows, cols] = (mask[full, :] * (one * grad_hid[full, cols] + two + three * out_v[full, cols])).astype(BF16)

        def body(c):
            value = jnp.dot(low_out[...], wexp[layer, :, lanes(E // 256 + c, 256)], preferred_element_type=F32)
            for part in range(2):
                k = 2 * c + part
                scale, shift = half_coefs(b, 1, layer, k, gain_e[layer, 2:3, lanes(k)], gain_e[layer, 3:4, lanes(k)])
                for i in range(IMGS):
                    rows, full = image(b, i)
                    act = act_half(mask[full, :] * (mixed[b, k, rows, :] * scale + shift))
                    piece = value[rows, part * LANES : (part + 1) * LANES]
                    grad[b, k, rows, :] = piece
                    dgate[i : i + 1, lanes(k)] = jnp.sum(fold(piece * act), 0, keepdims=True)
                    low_pre[rows, lanes(k)] = (act * gate_s[layer, b * 8 + i : b * 8 + i + 1, lanes(k)]).astype(BF16)
            value = contract(low_out[...], low_pre[:, lanes(c, 256)], 0, 0)
            if b == 0:
                held[c] = value
            else:
                pack(AT_MATS[layer] + MATS // 2, c, value + held[c])

        repeat(E // 256, body, hook)
        gate = gate_s[layer, eight, :]
        units = unit_s[layer, eight, :]
        sig = jax.nn.sigmoid(units)
        inner = dgate[...] * gate * (1.0 - gate)
        bias_x = jnp.sum(inner, 0, keepdims=True)
        grad_x = exact_outer(units * sig, inner)
        outer = exact(inner, chan[layer, 80:144, :], 1) * (sig * (1.0 + units * (1.0 - sig)))
        bias_r = jnp.sum(outer, 0, keepdims=True)
        grad_r = exact_outer(outer, pool_s[layer, eight, :])
        if b == 0:
            held_exb[0:1, :] = bias_x
            held_chan[9 + SE : 9 + 2 * SE, :] = grad_x
            held_sqb[0:1, 0:SE] = bias_r
            held_chan[9 : 9 + SE, :] = grad_r
        else:
            bias_x = bias_x + held_exb[0:1, :]
            for k in range(EC):
                stages[1, 24 + k : 25 + k, :] = bias_x[:, k * LANES : (k + 1) * LANES]
            stages[1, 24 + EC : 25 + EC, 0:SE] = bias_r + held_sqb[0:1, 0:SE]
            held_chan[9 : 9 + SE, :] = held_chan[9 : 9 + SE, :] + grad_r
            held_chan[9 + SE : 9 + 2 * SE, :] = held_chan[9 + SE : 9 + 2 * SE, :] + grad_x
        dpool[...] = exact(outer, chan[layer, 16:80, :], 0)

    def block_second(b, layer, hook=None):
        stage = stages.at[b]

        def body(c):
            scale, shift = half_coefs(b, 1, layer, c, gain_e[layer, 2:3, lanes(c)], gain_e[layer, 3:4, lanes(c)])
            first = jnp.zeros((8, LANES), F32)
            second = jnp.zeros((8, LANES), F32)
            for i in range(IMGS):
                rows, full = image(b, i)
                x = mixed[b, c, rows, :]
                half = mask[full, :] * (x * scale + shift)
                gate = gate_s[layer, b * 8 + i : b * 8 + i + 1, lanes(c)]
                value = mask[full, :] * (grad[b, c, rows, :] * gate + dpool[i : i + 1, lanes(c)] / area[0:1, :]) * bend(half)[1]
                grad[b, c, rows, :] = value
                first = first + fold(value)
                second = second + fold(value * x)
            put(stage, c, first, second)

        repeat(EC, body, hook)

    def block_spread(b, layer, hook=None):
        stage = stages.at[b]

        def body(c):
            scale, shift = half_coefs(b, 0, layer, c, gain_e[layer, 0:1, lanes(c)], gain_e[layer, 1:2, lanes(c)])
            one, two, three = back_coefs(b, 1, layer, c, gain_e[layer, 2:3, lanes(c)])
            tap_rows = chan[layer, 0:16, lanes(c)].astype(F32)
            tap = [tap_rows[k : k + 1, :] for k in range(9)]
            for i in range(IMGS):
                rows, full = image(b, i)
                act, der = bend(mask[full, :] * (pre[b, c, rows, :] * scale + shift))
                pads_x[i, GAP : GAP + ROWS, :] = act
                slope[rows, :] = mask[full, :] * der
                pads_g[i, GAP : GAP + ROWS, :] = mask[full, :] * (one * grad[b, c, rows, :] + two + three * mixed[b, c, rows, :])
            first = jnp.zeros((8, LANES), F32)
            second = jnp.zeros((8, LANES), F32)
            total = [jnp.zeros((8, LANES), F32) for k in range(9)]
            for i in range(IMGS):
                for t in range(ROWS // TILE_BACK):
                    start = GAP + t * TILE_BACK
                    rows = slice(i * ROWS + t * TILE_BACK, i * ROWS + (t + 1) * TILE_BACK)
                    g = [pads_g[i, start - o : start - o + TILE_BACK, :] for o in OFFSETS]
                    left, right = edge_l[t * TILE_BACK : (t + 1) * TILE_BACK, :], edge_r[t * TILE_BACK : (t + 1) * TILE_BACK, :]
                    wide = (g[1] * tap[1] + g[4] * tap[4] + g[7] * tap[7]
                            + right * (g[0] * tap[0] + g[3] * tap[3] + g[6] * tap[6])
                            + left * (g[2] * tap[2] + g[5] * tap[5] + g[8] * tap[8]))
                    value = wide * slope[rows, :]
                    grad[b, c, rows, :] = value
                    first = first + fold(value)
                    second = second + fold(value * pre[b, c, rows, :])
                    center = g[4]
                    sides = (center * left, center, center * right)
                    for k in range(9):
                        o = OFFSETS[k]
                        total[k] = total[k] + fold(sides[k % 3] * pads_x[i, start + o : start + o + TILE_BACK, :])
            put(stage, c, first, second)
            for k in range(9):
                row = jnp.sum(total[k], 0, keepdims=True)
                if b == 0:
                    held_chan[k : k + 1, lanes(c)] = row
                else:
                    held_chan[k : k + 1, lanes(c)] = held_chan[k : k + 1, lanes(c)] + row

        repeat(EC, body, hook)
        if b == 1:
            pack_chan(layer)

    def block_expand(b, layer, hook=None):
        mine = slice(b * HALF, (b + 1) * HALF)

        def body(c):
            for part in range(2):
                norm_back_rows(b, 0, layer, 2 * c + part, gain_e[layer, 0:1, lanes(2 * c + part)], pre)
            value = contract(low_v[mine, :], low_pre[:, lanes(c, 256)], 0, 0)
            if b == 0:
                held[c] = value
            else:
                pack(AT_MATS[layer], c, value + held[c])

        repeat(E // 256, body, hook)
        if layer > 0:
            grad_hid[mine, :] = grad_hid[mine, :] + contract(low_pre[...], wexp[layer, :, 0:E], 1, 1)
            put_hidden_sums(b, layer - 1)

    heads = [summer(b, 3, 0) for b in range(BATCHES)]
    load(0, 2, 0).wait()
    head_first(0)
    heads[0].start(stages.at[0])
    load(1, 2, 0).wait()
    head_first(1, (5, heads[0].middle))
    heads[1].start(stages.at[1])
    thirds = [summer(b, 2, L - 1) for b in range(BATCHES)]
    heads[0].finish()
    load_low(L).wait()
    load_out(L - 1).wait()
    head_second(0, (2, heads[1].middle))
    load(0, 0, L - 1).start()
    thirds[0].start(stages.at[0])
    heads[1].finish()
    head_second(1, (3, thirds[0].middle))
    load(1, 0, L - 1).start()
    thirds[1].start(stages.at[1])
    load_low(L - 1).start()
    for layer in reversed(range(L)):
        twos = [summer(b, 1, layer) for b in range(BATCHES)]
        ones = [summer(b, 0, layer) for b in range(BATCHES)]
        thirds[0].finish()
        load(0, 1, layer).wait()
        block_gate(0, layer, (3, thirds[1].middle if layer > 0 else then(thirds[1].middle, 0)))
        block_second(0, layer)
        twos[0].start(stages.at[0])
        thirds[1].finish()
        load(1, 1, layer).wait()
        block_gate(1, layer, (3, twos[0].middle if layer > 0 else then(twos[0].middle, 1)))
        if layer > 0:
            load_out(layer - 1).start()
        block_second(1, layer)
        twos[1].start(stages.at[1])
        twos[0].finish()
        load(0, 0, layer).wait()
        block_spread(0, layer, (4, twos[1].middle if layer > 0 else then(twos[1].middle, 2)))
        ones[0].start(stages.at[0])
        if layer > 0:
            load(0, 1, layer - 1).start()
        twos[1].finish()
        load(1, 0, layer).wait()
        block_spread(1, layer, (4, ones[0].middle))
        ones[1].start(stages.at[1])
        if layer > 0:
            load(1, 1, layer - 1).start()
        ones[0].finish()
        load_low(layer).wait()
        if layer > 0:
            load_out(layer - 1).wait()
        block_expand(0, layer, (3, ones[1].middle))
        if layer > 0:
            thirds = [summer(b, 2, layer - 1) for b in range(BATCHES)]
            thirds[0].start(stages.at[0])
            load(0, 0, layer - 1).start()
        ones[1].finish()
        block_expand(1, layer, None if layer == 0 else (3, thirds[0].middle))
        if layer > 0:
            thirds[1].start(stages.at[1])
            late_core()
            load(1, 0, layer - 1).start()
            load_low(layer - 1).start()
    late_end()


def run_backward_all(sizes, inputs):
    sds = jax.ShapeDtypeStruct
    vm = pl.BlockSpec(memory_space=pltpu.VMEM)
    hbm = pl.BlockSpec(memory_space=pl.ANY)
    n_dp, n_sh = sizes
    sem = pltpu.SemaphoreType.DMA
    late = late_chunks(sizes)
    late_blocks = late * packed_blocks(sizes) // CHUNKS
    outs = [
        sds((n_sh, packed_blocks(sizes), 8, LANES), F32),
        sds((L, BATCHES, 2, 40, LANES), F32),
        sds((L, BATCHES, 8, LANES), F32),
        sds((BATCHES, 40, LANES), F32),
    ]
    scratch = [
        pltpu.VMEM((BATCHES, EC, HALF, LANES), F32),
        pltpu.VMEM((BATCHES, EC, HALF, LANES), F32),
        pltpu.VMEM((BATCHES, EC, HALF, LANES), F32),
        pltpu.VMEM((FULL, C), F32),
        pltpu.VMEM((HALF, C), BF16),
        pltpu.VMEM((HALF, E), BF16),
        pltpu.VMEM((IMGS, ROWS + 2 * GAP, LANES), F32),
        pltpu.VMEM((IMGS, ROWS + 2 * GAP, LANES), F32),
        pltpu.VMEM((HALF, LANES), F32),
        pltpu.VMEM((8, E), F32),
        pltpu.VMEM((8, E), F32),
        pltpu.VMEM((BATCHES, 40, LANES), F32),
        pltpu.SemaphoreType.DMA((BATCHES, 2)),
        pltpu.VMEM((E // 256, 256, 256), F32),
        pltpu.VMEM((144, E), F32),
        pltpu.VMEM((8, E), F32),
        pltpu.VMEM((8, LANES), F32),
        pltpu.VMEM((FULL, C), F32),
        pltpu.VMEM((FULL, C), BF16),
        pltpu.SemaphoreType.DMA((2,)),
        pltpu.VMEM((FULL, LANES), F32),
        pltpu.VMEM((8, LANES), F32),
        pltpu.VMEM((2, ROWS, LANES), F32),
        pltpu.VMEM((2, late_blocks, 8, LANES), F32),
        pltpu.VMEM((late_blocks, 8, LANES), F32),
        sem((late, 2)), sem((late, 2)), sem((late,)), sem((late,)),
    ]
    for b in range(BATCHES):
        for rows in BACK_ROWS[b]:
            scratch = scratch + sum_scratch(sizes, rows)
    specs = [vm] * 2 + [pl.BlockSpec(memory_space=pltpu.SMEM)] * 2 + [vm] * 6 + [hbm] * 5 + [vm] * 6
    return pl.pallas_call(
        functools.partial(backward_kernel, sizes),
        out_shape=outs,
        in_specs=specs,
        out_specs=[vm] * len(outs),
        scratch_shapes=scratch,
        compiler_params=pltpu.CompilerParams(collective_id=2, has_side_effects=True, vmem_limit_bytes=63 * 2**20),
        name="backward",
    )(*inputs)


GROUPS = 12
FACT_STEPS = (0, 3, 8)


def update_kernel(sizes, *refs):
    (packed, facts, fixes, tot_e, tot_c, tot_h, back_e, back_c, back_h, *state) = refs[:21]
    state_in = [state[3 * k : 3 * k + 3] for k in range(4)]
    out_refs = refs[21:25]
    gain_grad, norms, peers, mates = refs[25:29]
    (own, near, cross, side, line, full, gathered, g_class, sums_near) = refs[29:38]
    boxes = [refs[38 + 4 * k : 42 + 4 * k] for k in range(4)]
    (core_s, core_r, x_s, x_r, y_s, y_r, z_s, z_r, zz_s, zz_r, yy_s, yy_r,
     fn_s, fn_r, ff_s, ff_r, nn_s, nn_r, load_sems, store_sems, misc) = refs[54:75]
    n_dp, n_sh = sizes
    d, s = lax.axis_index("dp"), lax.axis_index("shard")
    count = packed_blocks(sizes)
    chunk = count // CHUNKS
    half = chunk // 2
    late = late_chunks(sizes)
    n_z = n_dp // 2
    piece = half // n_z
    bit0, bit1 = lax.rem(s, 2), s // 2
    near_peer = s + 1 - 2 * bit0
    far_peer = s + 2 - 4 * bit1
    yb, zi = lax.rem(d, 2), d // 2
    y_peer = d + 1 - 2 * yb

    greet(sizes)

    def load(k, i):
        if k == 1:
            return [pltpu.make_async_copy(state_in[1][i].at[:, l], boxes[1][i].at[l], load_sems.at[2 * i + 24 + l]) for l in range(L)]
        return [pltpu.make_async_copy(state_in[k][i], boxes[k][i], load_sems.at[4 * k + i])]

    def store(k):
        if k == 1:
            return [pltpu.make_async_copy(boxes[1][3].at[l], out_refs[1].at[:, l], store_sems.at[4 + l]) for l in range(L)]
        return [pltpu.make_async_copy(boxes[k][3], out_refs[k], store_sems.at[k])]

    def core_copy(k, i):
        rows = pl.ds(k * chunk, chunk)
        return pltpu.make_async_remote_copy(
            packed.at[2 * i + 1 - bit0, rows], near.at[i, rows], core_s.at[k, i], core_r.at[k, i],
            device_id=(d, near_peer), device_id_type=MESH)

    def x_copy(k):
        rows = pl.ds(k * chunk, chunk)
        return pltpu.make_async_remote_copy(
            own.at[far_peer, rows], cross.at[rows], x_s.at[k], x_r.at[k],
            device_id=(d, far_peer), device_id_type=MESH)

    def y_copy(k):
        rows = pl.ds(k * chunk + (1 - yb) * half, half)
        return pltpu.make_async_remote_copy(
            own.at[s, rows], side.at[k], y_s.at[k], y_r.at[k],
            device_id=(y_peer, s), device_id_type=MESH)

    def z_copy(k, step, source, target):
        rows = pl.ds(k * chunk + yb * half + target * piece, piece)
        return pltpu.make_async_remote_copy(
            own.at[s, rows], line.at[k, source], z_s.at[k, step], z_r.at[k, source],
            device_id=(2 * target + yb, s), device_id_type=MESH)

    def zz_copy(k, step, source, target):
        rows = pl.ds(k * (chunk // 2) + yb * (half // 2) + source * (piece // 2), piece // 2)
        return pltpu.make_async_remote_copy(
            full.at[rows], full.at[rows], zz_s.at[k, step], zz_r.at[k, source],
            device_id=(2 * target + yb, s), device_id_type=MESH)

    def yy_copy(k, b):
        rows = pl.ds(k * (chunk // 2) + b * (half // 2), half // 2)
        return pltpu.make_async_remote_copy(
            full.at[rows], full.at[rows], yy_s.at[k], yy_r.at[k],
            device_id=(y_peer, s), device_id_type=MESH)

    def over_z(action):
        def step(j, carry):
            action(j, lax.rem(zi + j, n_z))
            return carry

        lax.fori_loop(1, n_z, step, 0)

    def add_into(t, low, length, other, low_other, unit=8):
        def step(i, carry):
            rows = pl.ds(low + i * unit, unit)
            own[t, rows] = own[t, rows] + other(pl.ds(low_other + i * unit, unit))
            return carry

        lax.fori_loop(0, length // unit, step, 0)

    def stage_core(k):
        for i in range(2):
            core_copy(k, i).start()

    def stage_x(k):
        for i in range(2):
            core_copy(k, i).wait_recv()
        low = k * chunk
        add_into(far_peer, low, chunk, lambda rows: near[1 - bit1, rows], low)
        x_copy(k).start()
        add_into(s, low, chunk, lambda rows: near[bit1, rows], low)

    def stage_y(k):
        low = k * chunk
        give = low + (1 - yb) * half
        keep = low + yb * half
        if k >= late:
            x_copy(k).wait_recv()
            add_into(s, give, half, lambda rows: cross[rows], give)
        y_copy(k).start()
        if k >= late:
            add_into(s, keep, half, lambda rows: cross[rows], keep)

    def stage_z(k):
        y_copy(k).wait_recv()
        add_into(s, k * chunk + yb * half, half, lambda rows: side[k, rows], 0)
        over_z(lambda j, t: z_copy(k, j, zi, t).start())

    def stage_zz(k):
        over_z(lambda j, t: z_copy(k, j, t, zi).wait_recv())
        low = k * chunk + yb * half + zi * piece

        def step(i, carry):
            total = own[s, pl.ds(low + 2 * i, 2)]
            for j in range(1, n_z):
                total = total + line[k, lax.rem(zi + j, n_z), pl.ds(2 * i, 2)]
            full[low // 2 + i] = total.reshape(16, LANES).astype(BF16)
            return carry

        lax.fori_loop(0, piece // 2, step, 0)
        over_z(lambda j, t: zz_copy(k, j, zi, t).start())

    def stage_yy(k):
        over_z(lambda j, t: zz_copy(k, j, t, zi).wait_recv())
        yy_copy(k, yb).start()

    def stage_done(k):
        yy_copy(k, 1 - yb).wait_recv()

    def settle(k):
        if k >= late:
            for i in range(2):
                core_copy(k, i).wait_send()
            x_copy(k).wait_send()
        y_copy(k).wait_send()
        over_z(lambda j, t: z_copy(k, j, zi, t).wait_send())
        over_z(lambda j, t: zz_copy(k, j, zi, t).wait_send())
        yy_copy(k, yb).wait_send()

    def own_facts():
        return pltpu.make_async_copy(facts, peers.at[d], misc.at[0])

    def fact_far(step, source, target):
        return pltpu.make_async_remote_copy(
            facts, peers.at[source], ff_s.at[step], ff_r.at[source],
            device_id=(target, s), device_id_type=MESH)

    def fact_parts(t):
        return ((pl.ds(0, 8), pl.ds(0, 8)), (pl.ds(8 + 3 * t, 3), pl.ds(8, 3)))

    def fact_near(step, source, target):
        return [
            pltpu.make_async_remote_copy(
                peers.at[:, low], mates.at[source, :, high], fn_s.at[step, n], fn_r.at[source, n],
                device_id=(d, target), device_id_type=MESH)
            for n, (low, high) in enumerate(fact_parts(target))
        ]

    def fact_mine():
        return [
            pltpu.make_async_copy(peers.at[:, low], mates.at[s, :, high], misc.at[1 + n])
            for n, (low, high) in enumerate(fact_parts(s))
        ]

    def over_dp(action):
        def step(j, carry):
            action(j, lax.rem(d + j, n_dp))
            return carry

        lax.fori_loop(1, n_dp, step, 0)

    def facts_begin():
        own_facts().start()
        over_dp(lambda j, t: fact_far(j, d, t).start())

    def facts_second():
        def arrive(j, t):
            fact_far(j, t, d).wait_recv()
            fact_far(j, d, d).wait_send()

        own_facts().wait()
        over_dp(arrive)
        for copy in fact_mine():
            copy.start()
        for j in range(1, n_sh):
            for copy in fact_near(j, s, lax.rem(s + j, n_sh)):
                copy.start()

    def facts_third():
        for copy in fact_mine():
            copy.wait()
        for j in range(1, n_sh):
            for copy in fact_near(j, lax.rem(s + j, n_sh), s):
                copy.wait_recv()
            for copy in fact_near(j, s, s):
                copy.wait_send()
        for first in range(0, n_dp, 8):
            copy = pltpu.make_async_copy(mates.at[:, pl.ds(first, 8)], gathered, misc.at[0])
            copy.start()
            copy.wait()
            value = [gathered[:, :, k].reshape(8 * n_sh * 16, LANES) for k in range(11)]
            product = contract(jnp.concatenate(value[8:], 1), jnp.concatenate(value[:8], 1), 0, 0)
            g_class[...] = product if first == 0 else g_class[...] + product

    sums_near[s] = jnp.zeros((24, LANES), F32)
    first_fix, second_fix = fixes[0], fixes[1]

    def note(row, value):
        square = value * value
        width = square.shape[1]
        line_sum = jnp.sum(square, 0, keepdims=True)
        total = jnp.zeros((1, LANES), F32)
        for low in range(0, width - width % LANES, LANES):
            total = total + line_sum[:, low : low + LANES]
        tail = width % LANES
        if tail:
            total = total + jnp.concatenate([line_sum[:, width - tail :], jnp.zeros((1, LANES - tail), F32)], 1)
        sums_near[s, row : row + 1, :] = sums_near[s, row : row + 1, :] + total

    def moments(k, index, grad):
        weight, first, second, kept = boxes[k]
        kept[index] = grad
        new_first = BETA_ONE * first[index] + (1.0 - BETA_ONE) * grad
        new_second = BETA_TWO * second[index] + (1.0 - BETA_TWO) * grad * grad
        return new_first * first_fix / (jnp.sqrt(new_second * second_fix) + EPS_ADAM) + DECAY * weight[index]

    def gains_part():
        def norm(tot, back_of, chunk):
            grad, shift = jnp.zeros((1, LANES), F32), jnp.zeros((1, LANES), F32)
            for b in range(BATCHES):
                count = tot_e[0, 0, 48 + b : 49 + b, :]
                mean = tot[pl.ds(4 * chunk + 2 * b, 1), :] / count
                scale = lax.rsqrt(tot[pl.ds(4 * chunk + 2 * b + 1, 1), :] / count - mean * mean + EPS_NORM)
                back = back_of(b)
                plain = back[pl.ds(2 * chunk, 1), :]
                grad = grad + scale * (back[pl.ds(2 * chunk + 1, 1), :] - mean * plain)
                shift = shift + plain
            return grad, shift

        def mine(value, width):
            part = value[:, 0:width]
            for t in range(1, n_sh):
                part = jnp.where(s == t, value[:, t * width : (t + 1) * width], part)
            return part

        start = 0
        for layer in range(L):
            for kind in range(2):
                for q in range(3):
                    pair = norm(tot_e.at[layer, kind], lambda b: back_e.at[layer, b, kind], 3 * s + q)
                    for which in range(2):
                        low = start + 384 * (2 * kind + which) + LANES * q
                        gain_grad[0:1, low : low + LANES] = pair[which]
            for q in range(3):
                low = start + 384 * 4 + LANES * q
                gain_grad[0:1, low : low + LANES] = back_e[layer, 1, 0, pl.ds(24 + 3 * s + q, 1), :]
            low = start + 384 * 5
            pairs = [norm(tot_c.at[layer], lambda b: back_c.at[layer, b], c) for c in range(2)]
            for which in range(2):
                whole = jnp.concatenate([pairs[0][which], pairs[1][which]], 1)
                gain_grad[0:1, low + 64 * which : low + 64 * which + 64] = mine(whole, 64)
            gain_grad[0:1, low + 128 : low + 144] = mine(back_e[layer, 1, 0, 24 + EC : 25 + EC, :], 16)
            start = low + 144
        pairs = [norm(tot_h, lambda b: back_h.at[b], c) for c in range(HC)]
        for which in range(2):
            whole = jnp.concatenate([pair[which] for pair in pairs], 1)
            gain_grad[0:1, start + 320 * which : start + 320 * which + 320] = mine(whole, 320)
        whole = jnp.concatenate([back_h[1, 24 + k : 25 + k, :] for k in range(8)], 1)
        gain_grad[0:1, start + 640 : start + 890] = mine(whole, 250)

    every = slice(None)

    def mats_index(layer, c):
        return (layer, every, lanes(c))

    def weights_squares():
        for layer in range(L):
            for part in range(2):

                def body(c):
                    note(2 * layer + part, boxes[0][0][mats_index(layer, c + part * EC)])

                repeat(EC, body)
            for kk in range(3):
                cols = slice(kk * LANES, (kk + 1) * LANES)
                note(2 * L + 3 * layer, boxes[1][0][layer, 0:9, cols])
                note(2 * L + 3 * layer + 1, boxes[1][0][layer, 9 : 9 + SE, cols])
                note(2 * L + 3 * layer + 2, boxes[1][0][layer, 9 + SE : 9 + 2 * SE, cols])
        note(5 * L, boxes[2][0][...])

        def body(i):
            note(5 * L + 1, boxes[3][0][pl.ds(pl.multiple_of(i * 40, 40), 40), :])

        repeat(8, body)

    def mats_moments(layer, part):
        def body(c):
            panel = c + part * EC
            grad = full[pl.ds(AT_MATS[layer] // 2 + 4 * panel, 4)].astype(F32).reshape(64, LANES)
            note(GROUPS + 2 * layer + part, moments(0, mats_index(layer, panel), grad))

        repeat(EC, body)

    def chan_moments(layer):
        if True:
            for kk in range(3):
                low = (AT_CHAN[layer] + 18 * kk) // 2
                grad = full[low : low + 9].astype(F32).reshape(144, LANES)[:137]
                value = moments(1, (layer, every, slice(kk * LANES, (kk + 1) * LANES)), grad)
                note(GROUPS + 2 * L + 3 * layer, value[0:9])
                note(GROUPS + 2 * L + 3 * layer + 1, value[9 : 9 + SE])
                note(GROUPS + 2 * L + 3 * layer + 2, value[9 + SE :])

    def head_moments():
        rows = HEAD // 4
        for part in range(2):
            low = (AT_HEAD + part * (rows // 8)) // 2
            grad = full[low : low + rows // 16].astype(F32).reshape(rows, LANES)
            note(GROUPS + 5 * L, moments(2, (every, slice(part * LANES, (part + 1) * LANES)), grad))

    def class_moments():
        def body(i):
            rows = pl.ds(pl.multiple_of(i * 40, 40), 40)
            note(GROUPS + 5 * L + 1, moments(3, (rows, every), g_class[rows, :CLASSES]))

        repeat(8, body)

    def norm_copy(step, source, target):
        return pltpu.make_async_remote_copy(
            sums_near.at[source], sums_near.at[source], nn_s.at[step], nn_r.at[source],
            device_id=(d, target), device_id_type=MESH)

    def load_own(which):
        t = (s, far_peer)[which]
        return pltpu.make_async_copy(packed.at[t], own.at[t], load_sems.at[16 + which])

    tasks = [
        (MATS // 2, lambda: mats_moments(1, 0)),
        (MATS, lambda: mats_moments(1, 1)),
        (MATS + CHAN, lambda: chan_moments(1)),
        (AT_MATS[0], head_moments),
        (AT_MATS[0] + MATS // 2, lambda: mats_moments(0, 0)),
        (AT_MATS[0] + MATS, lambda: mats_moments(0, 1)),
        (AT_END, lambda: chan_moments(0)),
    ]
    for k in range(late, CHUNKS):
        stage_core(k)
    for which in range(2):
        load_own(which).start()
    if FACT_STEPS[0] == 0:
        facts_begin()
    for i in range(3):
        for k in range(4):
            for copy in load(k, i):
                copy.start()
    for which in range(2):
        load_own(which).wait()
    stages = (stage_x, stage_y, stage_z, stage_zz, stage_yy, stage_done)
    begins = [(1 + k, 1) if k < late else (1 + k - late, 0) for k in range(CHUNKS)]
    done = set()
    for tau in range(1, 2 + CHUNKS + 6):
        for age, stage in enumerate(stages):
            for k in range(CHUNKS):
                if tau - begins[k][0] + begins[k][1] == age and tau >= begins[k][0]:
                    stage(k)
                    if age == 5:
                        done.add(k)
        if tau == FACT_STEPS[0]:
            facts_begin()
        if tau == FACT_STEPS[1]:
            facts_second()
        if tau == 1:
            for k in range(4):
                for copy in load(k, 0):
                    copy.wait()
            weights_squares()
        if tau == 2:
            gains_part()
            for i in range(1, 3):
                for k in range(4):
                    for copy in load(k, i):
                        copy.wait()
        if tau == FACT_STEPS[2]:
            facts_third()
            class_moments()
            for copy in store(3):
                copy.start()
        while tau >= 3 and tasks and all(k in done for k in range(-(-tasks[0][0] // chunk))):
            tasks.pop(0)[1]()
    for j in range(1, n_sh):
        norm_copy(j, s, lax.rem(s + j, n_sh)).start()
    for k in (0, 1, 2):
        for copy in store(k):
            copy.start()
    for k in range(CHUNKS):
        settle(k)
    for j in range(1, n_sh):
        norm_copy(j, lax.rem(s + j, n_sh), s).wait_recv()
        norm_copy(j, s, s).wait_send()
    total = sums_near[0]
    for j in range(1, n_sh):
        total = total + sums_near[j]
    root = jnp.broadcast_to(jnp.sqrt(jnp.sum(total, 1, keepdims=True)), (24, LANES))
    norms[0:24, :] = root
    norms[24:32, :] = back_h[1, 32:40, :]
    for k in range(4):
        for copy in store(k):
            copy.wait()


def run_update(sizes, inputs, states):
    sds = jax.ShapeDtypeStruct
    vm = pl.BlockSpec(memory_space=pltpu.VMEM)
    hbm = pl.BlockSpec(memory_space=pl.ANY)
    n_dp, n_sh = sizes
    count = packed_blocks(sizes)
    chunk = count // CHUNKS
    n_z = n_dp // 2
    sem = pltpu.SemaphoreType.DMA
    outs = [sds(group[0].shape, F32) for group in states]
    gains = sum(([E // n_sh] * 5 + [(2 * C + SE) // n_sh]) * L) + (2 * HEAD + CLASSES) // n_sh
    outs = outs + [sds((1, gains), F32), sds((32, LANES), F32), sds((n_dp, 8 + 3 * n_sh, 16, LANES), BF16)]
    outs = outs + [sds((n_sh, n_dp, 11, 16, LANES), BF16)]
    scratch = [
        pltpu.VMEM((n_sh, count, 8, LANES), F32),
        pltpu.VMEM((2, count, 8, LANES), F32),
        pltpu.VMEM((count, 8, LANES), F32),
        pltpu.VMEM((CHUNKS, chunk // 2, 8, LANES), F32),
        pltpu.VMEM((CHUNKS, n_z, chunk // 2 // n_z, 8, LANES), F32),
        pltpu.VMEM((count // 2, 16, LANES), BF16),
        pltpu.VMEM((n_sh, 8, 11, 16, LANES), BF16),
        pltpu.VMEM((FACT - CLASS_PAD, CLASS_PAD), F32),
        pltpu.VMEM((n_sh, 2 * GROUPS, LANES), F32),
    ]
    for k, group in enumerate(states):
        shape = group[0].shape if k != 1 else (L, 137, 384)
        scratch = scratch + [pltpu.VMEM(shape, F32)] * 4
    scratch = scratch + [
        sem((CHUNKS, 2)), sem((CHUNKS, 2)), sem((CHUNKS,)), sem((CHUNKS,)), sem((CHUNKS,)), sem((CHUNKS,)),
        sem((CHUNKS, n_z)), sem((CHUNKS, n_z)), sem((CHUNKS, n_z)), sem((CHUNKS, n_z)), sem((CHUNKS,)), sem((CHUNKS,)),
        sem((n_sh, 2)), sem((n_sh, 2)), sem((n_dp,)), sem((n_dp,)), sem((n_sh,)), sem((n_sh,)),
        sem((32,)), sem((24,)), sem((3,)),
    ]
    return pl.pallas_call(
        functools.partial(update_kernel, sizes),
        out_shape=outs,
        in_specs=[hbm, hbm, pl.BlockSpec(memory_space=pltpu.SMEM)] + [vm] * 6 + [hbm] * 12,
        out_specs=[hbm] * 4 + [vm, vm, hbm, hbm],
        scratch_shapes=scratch,
        compiler_params=pltpu.CompilerParams(collective_id=3, has_side_effects=True, vmem_limit_bytes=63 * 2**20),
        name="update",
    )(*inputs, *[item for group in states for item in group])


def mats_factor(ratio, value):
    paired = ratio.reshape(-1, 2)
    column = jnp.arange(value.shape[2])
    return jnp.where(column[None, :] < value.shape[2] // 2, paired[:, 0:1], paired[:, 1:2])[
        :, None, :
    ]


def chan_factor(ratio, value):
    triple = ratio.reshape(-1, 3)
    row = jnp.arange(value.shape[1])[None, :]
    return jnp.where(
        row < 9, triple[:, 0:1], jnp.where(row < 9 + SE, triple[:, 1:2], triple[:, 2:3])
    )[:, :, None]


def adapt(first, second, grad, first_fix, second_fix):
    new_first = BETA_ONE * first + (1.0 - BETA_ONE) * grad
    new_second = BETA_TWO * second + (1.0 - BETA_TWO) * grad * grad
    update = new_first * first_fix / (jnp.sqrt(new_second * second_fix) + EPS_ADAM)
    return (new_first, new_second, update)


def per_device(
    images,
    bucket,
    counts,
    balance,
    labels,
    step,
    expand_w,
    expand_m,
    expand_v,
    expand_e,
    chan_w,
    chan_m,
    chan_v,
    chan_e,
    head_w,
    head_m,
    head_v,
    head_e,
    class_w,
    class_m,
    class_v,
    class_e,
    gain_w,
    gain_m,
    gain_v,
    gain_e,
):
    sizes = (lax.axis_size("dp"), lax.axis_size("shard"))
    counts = counts.reshape(BATCHES)
    turned = lambda value: value.transpose(1, 0, 2)
    saved = run_forward_all(
        sizes,
        [
            images.reshape(FULL, C), bucket, counts, balance, labels, gain_w, gain_e,
            expand_w, expand_e, turned(chan_w), turned(chan_e), head_w.T, head_e.T, class_w, class_e,
        ],
    )
    kept = saved[:11]
    tot_e, tot_c, tot_h = kept[8:11]
    dpool_h, extra, facts, wexp_s, headt_s, chan_s, vec_e, vec_c, vec_h = saved[11:]
    (packed, back_e, back_c, back_h) = run_backward_all(
        sizes,
        [dpool_h, extra, bucket, counts, wexp_s, headt_s, chan_s, vec_e, vec_c, vec_h, *kept],
    )
    power = step[0].astype(F32)
    first_fix = 1.0 / (1.0 - jnp.power(jnp.float32(BETA_ONE), power))
    second_fix = 1.0 / (1.0 - jnp.power(jnp.float32(BETA_TWO), power))
    grads = run_update(
        sizes,
        [packed, facts, jnp.stack([first_fix, second_fix]), tot_e, tot_c, tot_h, back_e, back_c, back_h],
        [
            (expand_w, expand_m, expand_v),
            tuple(turned(item) for item in (chan_w, chan_m, chan_v)),
            tuple(item.T for item in (head_w, head_m, head_v)),
            (class_w, class_m, class_v),
        ],
    )
    roots = grads[5][: 2 * GROUPS, 0].reshape(2, GROUPS)
    ratio = roots[0] / roots[1]
    weights = (expand_w, chan_w, head_w, class_w, gain_w)
    firsts = (expand_m, chan_m, head_m, class_m, gain_m)
    seconds = (expand_v, chan_v, head_v, class_v, gain_v)
    averaged = (expand_e, chan_e, head_e, class_e, gain_e)
    owned = (grads[0], turned(grads[1]), grads[2].T, grads[3], grads[4])
    factors = [
        mats_factor(ratio[: 2 * L], expand_w),
        chan_factor(ratio[2 * L : 5 * L], chan_w),
        ratio[5 * L],
        ratio[5 * L + 1],
    ]
    result = [grads[5][2 * GROUPS, 0]]
    for item in range(5):
        new_first, new_second, update = adapt(firsts[item], seconds[item], owned[item], first_fix, second_fix)
        if item < 4:
            fresh = weights[item] - RATE * factors[item] * (update + DECAY * weights[item])
        else:
            fresh = weights[item] - RATE * update
        result = result + [fresh, new_first, new_second, KEEP * averaged[item] + (1.0 - KEEP) * fresh]
    return tuple(result + [roots])


def solution(mesh):
    in_specs = (
        P(None, ("dp", "shard"), None, None, None),
        P("dp"),
        P(None, ("dp", "shard")),
        P(None, ("dp", "shard")),
        P(None, ("dp", "shard")),
        P(),
        P(None, "shard", None),
        P(None, "shard", None),
        P(None, "shard", None),
        P(None, "shard", None),
        P(None, None, "shard"),
        P(None, None, "shard"),
        P(None, None, "shard"),
        P(None, None, "shard"),
        P(None, "shard"),
        P(None, "shard"),
        P(None, "shard"),
        P(None, "shard"),
        P("shard", None),
        P("shard", None),
        P("shard", None),
        P("shard", None),
        P("shard", None),
        P("shard", None),
        P("shard", None),
        P("shard", None),
    )
    out_specs = (
        P(),
        P(None, "shard", None),
        P(None, "shard", None),
        P(None, "shard", None),
        P(None, "shard", None),
        P(None, None, "shard"),
        P(None, None, "shard"),
        P(None, None, "shard"),
        P(None, None, "shard"),
        P(None, "shard"),
        P(None, "shard"),
        P(None, "shard"),
        P(None, "shard"),
        P("shard", None),
        P("shard", None),
        P("shard", None),
        P("shard", None),
        P("shard", None),
        P("shard", None),
        P("shard", None),
        P("shard", None),
        P(),
    )
    return jax.shard_map(
        per_device, mesh=mesh, in_specs=in_specs, out_specs=out_specs, check_vma=False
    )
```
